32 devices in a mesh: rep: 2 (over core), fsdp: 16 (over z, y, x).
Axes of the slice: x: 2, y: 2, z: 4, core: 2. Of those that a mesh axis runs over, the one named last changes fastest.
Arguments:
- tokens: bfloat16 [20480, 1536], P(('rep', 'fsdp')), may hold values from -6 to 6
- lengths: int32 [32, 4], P(('rep', 'fsdp')), may hold values from 1 to 480, 640 in all within a row
- attn_gain: bfloat16 [1536], P('fsdp'), may hold values from 0.099609375 to 1.8984375
- w_query: bfloat16 [1536, 1536], P('fsdp'), may hold values from -0.15625 to 0.15625
- w_key: bfloat16 [1536, 768], P('fsdp'), may hold values from -0.15625 to 0.15625
- w_value: bfloat16 [1536, 768], P('fsdp'), may hold values from -0.15625 to 0.15625
- w_out: bfloat16 [1536, 1536], P('fsdp'), may hold values from -0.625 to 0.625
- ffn_gain: bfloat16 [1536], P('fsdp'), may hold values from 0.099609375 to 1.8984375
- w_gate: bfloat16 [1536, 4096], P('fsdp'), may hold values from -0.15625 to 0.15625
- w_up: bfloat16 [1536, 4096], P('fsdp'), may hold values from -0.15625 to 0.15625
- w_down: bfloat16 [4096, 1536], P('fsdp'), may hold values from -0.09375 to 0.09375
- cotangent: bfloat16 [20480, 1536], P(('rep', 'fsdp')), may hold values from -6 to 6
Outputs:
- output: bfloat16 [20480, 1536], P(('rep', 'fsdp'))
- grad_tokens: float32 [20480, 1536], P(('rep', 'fsdp'))
- grad_attn_gain: float32 [1536], P('fsdp')
- grad_query: float32 [1536, 1536], P('fsdp')
- grad_key: float32 [1536, 768], P('fsdp')
- grad_value: float32 [1536, 768], P('fsdp')
- grad_out: float32 [1536, 1536], P('fsdp')
- grad_ffn_gain: float32 [1536], P('fsdp')
- grad_gate: float32 [1536, 4096], P('fsdp')
- grad_up: float32 [1536, 4096], P('fsdp')
- grad_down: float32 [4096, 1536], P('fsdp')
The draws below stay inside these ranges and needn't reach their ends.
Inputs may be any that keep to these rules, and one draw needn't show every extreme that they name: Each row holds the lengths of the 4 documents on one device, summing to 640; the longest in each row is exactly 480.
All inputs are finite; a program needn't handle non-finite values.
Results may differ from the reference program's by a relative error of at most 0.015.
Values may be sent and summed in bfloat16 or wider, within the bound.
No kernel may reach another device: no remote copies, remote signals or barrier semaphores. Data moves between devices by JAX's collectives and lax.ppermute only.
A program may use at most 320 MiB of HBM per device.

```python
import math
import jax
import jax.numpy as jnp
import numpy as np
from jax import lax

D = 1536
H = 16
KV = 8
HD = 96
FF = 4096
TOK_DEV = 640
SEQS = 4
MAXLEN = 480
TOKENS = 20480
DEVICES = 32


def levels(stream_key, dims, split, least, largest):
    level = 1.0
    for dim, shards_of in split:
        draws = jax.random.uniform(jax.random.fold_in(jax.random.fold_in(stream_key, 6), dim), (shards_of,), jnp.float32, least / len(split), largest / len(split))
        level = level * jnp.repeat(jnp.exp(draws), dims[dim] // shards_of).reshape((-1,) + (1,) * (len(dims) - 1 - dim))
    return level


def profile(amount, total, most, skew):
    portions = [(1 << 20) // math.isqrt(rank ** skew) + 1 for rank in range(2, amount + 1)]
    surplus, holding = total - most - (amount - 1), [1] * (amount - 1)
    while surplus > 0:
        movable = [i for i in range(amount - 1) if holding[i] < most]
        mass, budget = sum([portions[i] for i in movable]), surplus
        for i in movable:
            extra = min(most - holding[i], max(1, budget * portions[i] // mass), surplus)
            holding[i] = holding[i] + extra
            surplus = surplus - extra
    return np.array([most] + holding)


def uneven(own_key, count, total, limit, lean):
    if count == 2:
        one = jax.random.randint(own_key, (), max(1, total - limit), min(limit, total - 1) + 1)
        return jnp.stack([one, total - one])
    sizes = jnp.asarray(profile(count, total, limit, lean), jnp.int32)
    couples = (count - 1) // 2
    giver, taker = sizes[1:1 + 2 * couples:2], sizes[2:2 + 2 * couples:2]
    slack = jnp.minimum(giver - 1, limit - taker)
    moved = jax.random.randint(jax.random.fold_in(own_key, 1), (couples,), 0, 1 << 20) % (slack + 1)
    sizes = sizes.at[1:1 + 2 * couples:2].set(giver - moved).at[2:2 + 2 * couples:2].set(taker + moved)
    return sizes[jax.random.permutation(jax.random.fold_in(own_key, 2), count)]


def gaussian(rng, shape, width, limit, split=(), held_as=jnp.bfloat16):
    drawn = width * jax.random.normal(rng, shape, jnp.float32)
    if split:
        drawn = drawn * levels(rng, shape, split, -0.22, 0.18)
    return jnp.clip(drawn, -limit, limit).astype(held_as)


def setup_inputs(seed: int = 0) -> dict:
    arg_keys = jax.random.split(jax.random.key(seed), 13)
    tokens = gaussian(arg_keys[0], (TOKENS, D), 1.0, 6.0, ((0, 32),))
    lengths = jax.vmap(lambda own: uneven(own, SEQS, TOK_DEV, MAXLEN, 2))(jax.random.split(arg_keys[1], DEVICES)).reshape((DEVICES, SEQS)).astype(jnp.int32)
    attn_gain = jnp.clip(1.0 + 0.18 * jax.random.normal(arg_keys[2], (D,), jnp.float32), 0.099609375, 1.8984375).astype(jnp.bfloat16)
    w_query = gaussian(arg_keys[3], (D, H * HD), D ** -0.5, 0.15625, ((0, 16),))
    w_key = gaussian(arg_keys[4], (D, KV * HD), D ** -0.5, 0.15625, ((0, 16),))
    w_value = gaussian(arg_keys[5], (D, KV * HD), D ** -0.5, 0.15625, ((0, 16),))
    w_out = gaussian(arg_keys[6], (H * HD, D), HD ** -0.5, 0.625, ((0, 16),))
    ffn_gain = jnp.clip(1.0 + 0.18 * jax.random.normal(arg_keys[7], (D,), jnp.float32), 0.099609375, 1.8984375).astype(jnp.bfloat16)
    w_gate = gaussian(arg_keys[8], (D, FF), D ** -0.5, 0.15625, ((0, 16),))
    w_up = gaussian(arg_keys[9], (D, FF), D ** -0.5, 0.15625, ((0, 16),))
    w_down = gaussian(arg_keys[10], (FF, D), FF ** -0.5, 0.09375, ((0, 16),))
    cotangent = gaussian(arg_keys[11], (TOKENS, D), 1.0, 6.0, ((0, 32),))
    return {"tokens": tokens, "lengths": lengths, "attn_gain": attn_gain, "w_query": w_query, "w_key": w_key, "w_value": w_value, "w_out": w_out, "ffn_gain": ffn_gain, "w_gate": w_gate, "w_up": w_up, "w_down": w_down, "cotangent": cotangent}


epsilon = 1e-05
rope_base = 100000.0
masked_score = -1e+30

@jax.custom_vjp
def low(v):
    return lax.optimization_barrier(v.astype(jnp.bfloat16)).astype(jnp.float32)

@jax.custom_vjp
def low_back(v):
    return v

def low_keep(v):
    return (low(v), None)

def low_pass(kept, grad):
    return (grad,)

def back_keep(v):
    return (v, None)

def back_low(kept, grad):
    return (low(grad),)
low.defvjp(low_keep, low_pass)
low_back.defvjp(back_keep, back_low)

def layout(length_row, count):
    ends = jnp.cumsum(length_row).astype(jnp.int32)
    slots = jnp.arange(count, dtype=jnp.int32)
    passed = (slots[:, None] >= ends[None, :]).astype(jnp.int32)
    segment = lax.optimization_barrier(jnp.sum(passed, axis=1)).astype(jnp.int32)
    position = slots - lax.optimization_barrier(jnp.sum(passed * length_row[None, :], axis=1)).astype(jnp.int32)
    allowed = (segment[:, None] == segment[None, :]) & (slots[None, :] <= slots[:, None])
    return (position, allowed)

def rotation(position):
    half_size = HD // 2
    frequency = rope_base ** (-jnp.arange(half_size, dtype=jnp.float32) * 2.0 / HD)
    angle = position.astype(jnp.float32)[:, None] * frequency[None, :]
    cosine = jnp.concatenate([jnp.cos(angle), jnp.cos(angle)], axis=-1)[:, None, :]
    sine = jnp.concatenate([jnp.sin(angle), jnp.sin(angle)], axis=-1)[:, None, :]
    return (cosine, sine)

def rotate(field, cosine, sine, heads):
    half_size = HD // 2
    shaped = field.reshape(field.shape[0], heads, HD)
    turned = jnp.concatenate([-shaped[..., half_size:], shaped[..., :half_size]], axis=-1)
    return (shaped * cosine + turned * sine).reshape(field.shape)

def normalize(hidden, gain):
    return hidden * lax.rsqrt(lax.optimization_barrier(jnp.mean(hidden * hidden, axis=-1, keepdims=True)) + epsilon) * gain

def matmul(left, right):
    return jnp.dot(left, right, precision=lax.Precision.HIGHEST)

def attend(item):
    queries, keys, values, allowed = item
    count = queries.shape[0]
    shaped_q = queries.reshape(count, KV, H // KV, HD)
    shaped_k = keys.reshape(count, KV, HD)
    shaped_v = values.reshape(count, KV, HD)
    raw = low_back(jnp.einsum('qgrd,kgd->grqk', shaped_q, shaped_k, precision=lax.Precision.HIGHEST))
    scores = jnp.where(allowed[None, None], raw * HD ** (-0.5), masked_score)
    top = lax.optimization_barrier(jnp.max(scores, axis=-1, keepdims=True))
    total = jnp.log(lax.optimization_barrier(jnp.sum(jnp.exp(scores - top), axis=-1, keepdims=True))) + top
    probs = low(jnp.exp(scores - total))
    mixed = jnp.einsum('grqk,kgd->qgrd', probs, shaped_v, precision=lax.Precision.HIGHEST)
    return mixed.reshape(count, H * HD)

def reference(tokens, lengths, attn_gain, w_query, w_key, w_value, w_out, ffn_gain, w_gate, w_up, w_down, cotangent):
    blocks = lengths.shape[0]
    position, allowed = jax.vmap(lambda row: layout(row, TOK_DEV))(lengths)
    cosine, sine = rotation(position.reshape(-1))
    params = tuple((weight.astype(jnp.float32) for weight in (attn_gain, w_query, w_key, w_value, w_out, ffn_gain, w_gate, w_up, w_down)))

    def forward(hidden, gain_one, query_w, key_w, value_w, out_w, gain_two, gate_w, up_w, down_w):
        normed = low(normalize(hidden, gain_one))
        queries = low(rotate(low_back(matmul(normed, query_w)), cosine, sine, H))
        keys = low(rotate(low_back(matmul(normed, key_w)), cosine, sine, KV))
        values = low(low_back(matmul(normed, value_w)))
        attended = lax.map(jax.checkpoint(attend), (queries.reshape(blocks, TOK_DEV, H * HD), keys.reshape(blocks, TOK_DEV, KV * HD), values.reshape(blocks, TOK_DEV, KV * HD), allowed))
        attended = low(low_back(attended.reshape(-1, H * HD)))
        middle = hidden + low_back(matmul(attended, out_w))
        normed_two = low(normalize(middle, gain_two))
        gate = low_back(matmul(normed_two, gate_w))
        upward = low_back(matmul(normed_two, up_w))
        inner = low(jax.nn.silu(gate) * upward)
        return middle + low_back(matmul(inner, down_w))
    result, pull = jax.vjp(forward, tokens.astype(jnp.float32), *params)
    grads = pull(cotangent.astype(jnp.float32))
    return (result.astype(jnp.bfloat16), grads[0], grads[1], grads[2], grads[3], grads[4], grads[5], grads[6], grads[7], grads[8], grads[9])
```

```python
import functools
import math

import jax
import jax.numpy as jnp
from jax import lax
from jax.experimental import pallas as pl
from jax.experimental.pallas import tpu as pltpu
from jax.sharding import PartitionSpec as P

H = 16
KV = 8
HD = 96
LANES = 128
BLOCKS = 16
TILE = 128
SLAB = 512
CHUNKS = 2

epsilon = 1e-05
rope_base = 100000.0
masked_score = -1e30
low = jnp.bfloat16
wide = jnp.float32


class Routes:
    def __init__(self, count):
        self.count = count
        self.direct = count == BLOCKS
        self.fold = count // BLOCKS

    def place(self):
        zero = jnp.int32(0)
        if not self.direct:
            return zero, zero, zero
        index = lax.axis_index("fsdp")
        return index // 4, (index // 2) % 2, index % 2

    def hop(self, array, step):
        pairs = []
        for source in range(BLOCKS):
            z, y, x = source // 4, (source // 2) % 2, source % 2
            z, y, x = (z + step[0]) % 4, (y + step[1]) % 2, (x + step[2]) % 2
            pairs.append((source, (z * 2 + y) * 2 + x))
        return lax.ppermute(array, "fsdp", pairs)

    def regroup(self, blocks, slabs):
        parts, start = [], 0
        for rows in slabs:
            part = blocks[:, start : start + rows]
            parts.append(part.reshape(BLOCKS, self.fold * rows, part.shape[2]))
            start += rows
        return jnp.concatenate(parts, axis=1)

    def ungroup(self, blocks, slabs):
        parts, start = [], 0
        for rows in slabs:
            part = blocks[:, start : start + self.fold * rows]
            parts.append(part.reshape(self.count, rows, part.shape[2]))
            start += self.fold * rows
        return jnp.concatenate(parts, axis=1)

    def gather(self, shard, slabs):
        if not self.direct:
            blocks = self.regroup(lax.all_gather(shard, "fsdp", axis=0), slabs)
            blocks = blocks.reshape(4, 2, 2, *blocks.shape[1:])
            half = blocks.shape[3] // 2
            return (
                blocks[:, 0, 0],
                blocks[:, 0, 1],
                blocks[:, 1, 0],
                blocks[:, 1, 1, :half],
                blocks[:, 1, 1, half:],
            )
        half = shard.shape[0] // 2
        line = jnp.stack([shard] + [self.hop(shard, (-k, 0, 0)) for k in (1, 2, 3)])
        from_x = self.hop(line, (0, 0, 1))
        from_y = self.hop(line, (0, 1, 0))
        far_a = self.hop(from_x[:, :half], (0, 1, 0))
        far_b = self.hop(from_y[:, half:], (0, 0, 1))
        return line, from_x, from_y, far_a, far_b

    def scatter(self, pieces, slabs):
        to_x, to_y, late_x, late_y, own = pieces
        if not self.direct:
            far = jnp.concatenate([to_x[0], to_y[0]], axis=1)
            near_x = jnp.concatenate([to_x[1], late_x], axis=1)
            near_y = jnp.concatenate([late_y, to_y[1]], axis=1)
            blocks = jnp.stack([jnp.stack([own, near_x], 1), jnp.stack([near_y, far], 1)], 1)
            blocks = self.ungroup(blocks.reshape(BLOCKS, *own.shape[1:]), slabs)
            return lax.psum_scatter(blocks, "fsdp", scatter_dimension=0, tiled=True)[0].astype(wide)
        half = own.shape[1] // 2
        got_x = self.hop(to_x, (0, 0, 1))
        got_y = self.hop(to_y, (0, 1, 0))
        more_x = self.hop(late_x + got_y[0], (0, 0, 1))
        more_y = self.hop(late_y + got_x[0], (0, 1, 0))

        def summed(k):
            upper = own[k, :half].astype(wide) + got_x[1, k].astype(wide) + more_y[k].astype(wide)
            lower = own[k, half:].astype(wide) + got_y[1, k].astype(wide) + more_x[k].astype(wide)
            return jnp.concatenate([upper, lower], axis=0)

        total = summed(0)
        for k in (1, 2, 3):
            total = total + self.hop(summed(k).astype(own.dtype), (k, 0, 0)).astype(wide)
        return total


def swap(array):
    return lax.ppermute(array, "rep", [(0, 1), (1, 0)])


def block_index(place_ref, k, dy, dx):
    z, y, x = place_ref[0], place_ref[1], place_ref[2]
    return (lax.rem(z + k, 4) * 2 + (y + dy - 2 * y * dy)) * 2 + (x + dx - 2 * x * dx)


def piece_rows(pieces, k, dy, dx, row, rows, half):
    line, from_x, from_y, far_a, far_b = pieces
    if (dy, dx) == (0, 0):
        return line.at[k, pl.ds(row, rows)]
    if (dy, dx) == (0, 1):
        return from_x.at[k, pl.ds(row, rows)]
    if (dy, dx) == (1, 0):
        return from_y.at[k, pl.ds(row, rows)]
    if row < half:
        return far_a.at[k, pl.ds(row, rows)]
    return far_b.at[k, pl.ds(row - half, rows)]


def grad_rows(outs, k, dy, dx, row, rows, half):
    to_x, to_y, late_x, late_y, own = outs
    first = row < half
    at = pl.ds(row if first else row - half, rows)
    if (dy, dx) == (0, 0):
        return own.at[k, pl.ds(row, rows)]
    if (dy, dx) == (0, 1):
        return to_x.at[1, k, at] if first else late_x.at[k, at]
    if (dy, dx) == (1, 0):
        return late_y.at[k, at] if first else to_y.at[1, k, at]
    return to_x.at[0, k, at] if first else to_y.at[0, k, at]


class Slab:
    def __init__(self, matrix, row, rows, stride, offset, column, width):
        self.matrix, self.row, self.rows = matrix, row, rows
        self.stride, self.offset = stride, offset
        self.column, self.width = column, width

    def of(self, refs, block):
        rows = pl.ds(pl.multiple_of(block * self.stride + self.offset, 16), self.rows)
        return refs[self.matrix].at[rows, pl.ds(self.column, self.width)]


def all_blocks():
    for k in range(4):
        for dy in range(2):
            for dx in range(2):
                yield k, dy, dx


def assemble_kernel(slabs, half, pads, matrices, place_ref, *refs):
    pieces = refs[:5]
    outs = refs[5 : 5 + matrices]
    sems = refs[5 + matrices]
    if pads:
        zeros = jnp.zeros((LANES - HD, outs[0].shape[1]), low)
        for block in range(BLOCKS):
            outs[0][pl.ds(block * LANES + HD, LANES - HD), :] = zeros
    for k, dy, dx in all_blocks():
        block = block_index(place_ref, k, dy, dx)
        for slab in slabs:
            source = piece_rows(pieces, k, dy, dx, slab.row, slab.rows, half)
            pltpu.make_async_copy(source, slab.of(outs, block), sems.at[slab.matrix]).start()
    for index, out in enumerate(outs):
        if pads:
            out = out.at[pl.ds(0, BLOCKS * HD)]
        pltpu.make_async_copy(out, out, sems.at[index]).wait()


def assemble(place, pieces, slabs, shapes, pads=False):
    half = pieces[0].shape[1] // 2
    any_space = pl.BlockSpec(memory_space=pl.ANY)
    whole = [pl.BlockSpec(shape, lambda i, place: (0, 0)) for shape in shapes]
    size = sum(math.prod(shape) for shape in shapes)
    return pl.pallas_call(
        functools.partial(assemble_kernel, slabs, half, pads, len(shapes)),
        grid_spec=pltpu.PrefetchScalarGridSpec(
            num_scalar_prefetch=1,
            grid=(1,),
            in_specs=[any_space] * 5,
            out_specs=whole,
            scratch_shapes=[pltpu.SemaphoreType.DMA((len(shapes),))],
        ),
        out_shape=[jax.ShapeDtypeStruct(shape, low) for shape in shapes],
        compiler_params=pltpu.CompilerParams(vmem_limit_bytes=48 * 2**20),
        cost_estimate=pl.CostEstimate(flops=0, bytes_accessed=4 * size, transcendentals=0),
        name="assemble",
    )(place, *pieces)


def cut_kernel(slabs, half, matrices, place_ref, *refs):
    sources = refs[:matrices]
    outs = refs[matrices : matrices + 5]
    sems = refs[matrices + 5]
    for k, dy, dx in all_blocks():
        block = block_index(place_ref, k, dy, dx)
        for slab in slabs:
            target = grad_rows(outs, k, dy, dx, slab.row, slab.rows, half)
            which = {(0, 0): 4, (0, 1): 0 if slab.row < half else 2}.get((dy, dx))
            if which is None:
                if (dy, dx) == (1, 0):
                    which = 3 if slab.row < half else 1
                else:
                    which = 0 if slab.row < half else 1
            pltpu.make_async_copy(slab.of(sources, block), target, sems.at[which]).start()
    for index, out in enumerate(outs):
        pltpu.make_async_copy(out, out, sems.at[index]).wait()


def cut(place, grads, slabs, rows, width):
    half = rows // 2
    any_space = pl.BlockSpec(memory_space=pl.ANY)
    shapes = [(2, 4, half, width)] * 2 + [(4, half, width)] * 2 + [(4, rows, width)]
    size = sum(math.prod(shape) for shape in shapes)
    return pl.pallas_call(
        functools.partial(cut_kernel, slabs, half, len(grads)),
        grid_spec=pltpu.PrefetchScalarGridSpec(
            num_scalar_prefetch=1,
            grid=(1,),
            in_specs=[pl.BlockSpec(g.shape, lambda i, place: (0, 0)) for g in grads],
            out_specs=[any_space] * 5,
            scratch_shapes=[pltpu.SemaphoreType.DMA((5,))],
        ),
        out_shape=[jax.ShapeDtypeStruct(shape, low) for shape in shapes],
        compiler_params=pltpu.CompilerParams(vmem_limit_bytes=48 * 2**20),
        cost_estimate=pl.CostEstimate(flops=0, bytes_accessed=4 * size, transcendentals=0),
        name="cut",
    )(place, *grads)


def turn_table(position):
    half_size = HD // 2
    frequency = rope_base ** (-jnp.arange(half_size, dtype=wide) * 2.0 / HD)
    angle = position.astype(wide)[:, None] * frequency[None, :]
    gap = jnp.zeros((position.shape[0], LANES // 2 - half_size), wide)
    cosine, sine = jnp.cos(angle), jnp.sin(angle)
    return (
        jnp.concatenate([cosine, gap, cosine, gap], axis=1),
        jnp.concatenate([-sine, gap, sine, gap], axis=1),
    )


def qkv_kernel(x_ref, w_ref, cos_ref, sin_ref, q_ref, k_ref, v_ref):
    half = HD // 2
    gap = jnp.zeros((x_ref.shape[0], LANES // 2 - half), wide)
    heads = q_ref.shape[1] // LANES
    groups = k_ref.shape[1] // LANES
    step = 4
    for first in range(0, heads + 2 * groups, step):
        part = jnp.dot(
            x_ref[...], w_ref[:, first * HD : (first + step) * HD], preferred_element_type=wide
        )
        for index in range(first, first + step):
            at = (index - first) * HD
            if index >= heads + groups:
                column = (index - heads - groups) * LANES
                padded = jnp.concatenate([part[:, at : at + HD], gap, gap], axis=1)
                v_ref[:, column : column + LANES] = padded.astype(low)
                continue
            padded = jnp.concatenate(
                [part[:, at : at + half], gap, part[:, at + half : at + HD], gap], axis=1
            )
            turned = pltpu.roll(padded, LANES // 2, 1)
            padded = (padded * cos_ref[...] + turned * sin_ref[...]).astype(low)
            if index < heads:
                q_ref[:, index * LANES : (index + 1) * LANES] = padded
            else:
                column = (index - heads) * LANES
                k_ref[:, column : column + LANES] = padded


def project_qkv(x, weight, cosine, sine):
    count, depth = x.shape
    tile = 256
    heads, groups = H // 2, KV // 2
    row = lambda width: pl.BlockSpec((tile, width), lambda i: (i, 0))
    return pl.pallas_call(
        qkv_kernel,
        grid=(count // tile,),
        in_specs=[
            row(depth),
            pl.BlockSpec(weight.shape, lambda i: (0, 0)),
            row(LANES),
            row(LANES),
        ],
        out_specs=[row(heads * LANES), row(groups * LANES), row(groups * LANES)],
        out_shape=[
            jax.ShapeDtypeStruct((count, heads * LANES), low),
            jax.ShapeDtypeStruct((count, groups * LANES), low),
            jax.ShapeDtypeStruct((count, groups * LANES), low),
        ],
        compiler_params=pltpu.CompilerParams(vmem_limit_bytes=48 * 2**20),
        cost_estimate=pl.CostEstimate(
            flops=2 * count * depth * weight.shape[1],
            bytes_accessed=2 * (2 * count * depth + weight.size),
            transcendentals=0,
        ),
        name="project_qkv",
    )(x, weight, cosine, sine)


def fill_bias(bias_ref, column_ref, row_ref):
    size = bias_ref.shape[0]
    for start in range(0, size, TILE):
        shape = (TILE, size)
        slots = lax.broadcasted_iota(jnp.int32, shape, 0) + start
        keys = lax.broadcasted_iota(jnp.int32, shape, 1)
        same = column_ref[start : start + TILE, :] == row_ref[0]
        allowed = same & (keys <= slots)
        bias_ref[start : start + TILE, :] = jnp.where(allowed, 0.0, masked_score)


def across(left, right):
    return lax.dot_general(left, right, (((1,), (1,)), ((), ())), preferred_element_type=wide)


def down(left, right):
    return lax.dot_general(left, right, (((0,), (0,)), ((), ())), preferred_element_type=wide)


def attend_kernel(q_ref, k_ref, v_ref, column_ref, row_ref, out_ref, total_ref, bias_ref):
    group = pl.program_id(1)
    size = q_ref.shape[0]

    @pl.when(group == 0)
    def _():
        fill_bias(bias_ref, column_ref, row_ref)
        total_ref[...] = jnp.zeros_like(total_ref)

    lane = lax.broadcasted_iota(jnp.int32, (TILE, LANES), 1)
    for start in range(0, size, TILE):
        stop = start + TILE
        for head in range(2):
            columns = slice(head * LANES, (head + 1) * LANES)
            raw = across(q_ref[start:stop, columns], k_ref[:stop, :])
            scores = raw * HD ** (-0.5) + bias_ref[start:stop, :stop]
            top = jnp.max(scores, axis=-1, keepdims=True)
            powers = jnp.exp(scores - top)
            amount = jnp.sum(powers, axis=-1, keepdims=True)
            probs = (powers * (1.0 / amount)).astype(low)
            mixed = jnp.dot(probs, v_ref[:stop, :], preferred_element_type=wide)
            out_ref[start:stop, columns] = mixed.astype(low)
            total = top + jnp.log(amount)
            total_ref[start:stop, :] = jnp.where(
                lane == 2 * group + head, total, total_ref[start:stop, :]
            )


def attention_specs(size):
    return dict(
        pair=pl.BlockSpec((size, 2 * LANES), lambda b, g: (b, g)),
        one=pl.BlockSpec((size, LANES), lambda b, g: (b, g)),
        shared=pl.BlockSpec((size, LANES), lambda b, g: (b, 0)),
        column=pl.BlockSpec((size, 1), lambda b, g: (b, 0)),
        row=pl.BlockSpec((1, 1, size), lambda b, g: (b, 0, 0)),
    )


def attend(q, k, v, segment):
    blocks, size = segment.shape
    count = blocks * size
    spec = attention_specs(size)
    work = q.shape[1] // LANES * blocks * size * size
    return pl.pallas_call(
        attend_kernel,
        grid=(blocks, k.shape[1] // LANES),
        in_specs=[spec["pair"], spec["one"], spec["one"], spec["column"], spec["row"]],
        out_specs=[spec["pair"], spec["shared"]],
        out_shape=[
            jax.ShapeDtypeStruct(q.shape, low),
            jax.ShapeDtypeStruct((count, LANES), wide),
        ],
        scratch_shapes=[pltpu.VMEM((size, size), wide)],
        compiler_params=pltpu.CompilerParams(vmem_limit_bytes=48 * 2**20),
        cost_estimate=pl.CostEstimate(
            flops=8 * work * LANES, bytes_accessed=4 * q.size, transcendentals=work
        ),
        name="attend",
    )(q, k, v, segment.reshape(count, 1), segment.reshape(blocks, 1, size))


def attend_back_kernel(
    q_ref,
    k_ref,
    v_ref,
    grad_ref,
    total_ref,
    column_ref,
    row_ref,
    cos_ref,
    sin_ref,
    dq_ref,
    dk_ref,
    dv_ref,
    bias_ref,
    dk_sum,
    dv_sum,
):
    group = pl.program_id(1)
    size = q_ref.shape[0]

    @pl.when(group == 0)
    def _():
        fill_bias(bias_ref, column_ref, row_ref)

    def turned_back(grad, rows):
        turned = pltpu.roll(grad, LANES // 2, 1)
        return (grad * cos_ref[rows, :] - turned * sin_ref[rows, :]).astype(low)

    dk_sum[...] = jnp.zeros_like(dk_sum)
    dv_sum[...] = jnp.zeros_like(dv_sum)
    lane = lax.broadcasted_iota(jnp.int32, (TILE, LANES), 1)
    for start in range(0, size, TILE):
        stop = start + TILE
        for head in range(2):
            columns = slice(head * LANES, (head + 1) * LANES)
            queries = q_ref[start:stop, columns]
            grads = grad_ref[start:stop, columns]
            total = jnp.sum(
                jnp.where(lane == 2 * group + head, total_ref[start:stop, :], 0.0),
                axis=-1,
                keepdims=True,
            )
            raw = across(queries, k_ref[:stop, :])
            probs = jnp.exp(raw * HD ** (-0.5) + bias_ref[start:stop, :stop] - total)
            dv_sum[:stop, :] += down(probs.astype(low), grads)
            grad_probs = across(grads, v_ref[:stop, :])
            weighted = probs * grad_probs
            delta = jnp.sum(weighted, axis=-1, keepdims=True)
            grad_raw = ((weighted - probs * delta) * HD ** (-0.5)).astype(low)
            dq = jnp.dot(grad_raw, k_ref[:stop, :], preferred_element_type=wide)
            dq_ref[start:stop, columns] = turned_back(dq, slice(start, stop))
            dk_sum[:stop, :] += down(grad_raw, queries)
    dv_ref[...] = dv_sum[...].astype(low)
    dk_ref[...] = turned_back(dk_sum[...], slice(None))


def attend_back(q, k, v, grad, total, segment, cosine, sine):
    blocks, size = segment.shape
    count = blocks * size
    spec = attention_specs(size)
    work = q.shape[1] // LANES * blocks * size * size
    return pl.pallas_call(
        attend_back_kernel,
        grid=(blocks, k.shape[1] // LANES),
        in_specs=[
            spec["pair"],
            spec["one"],
            spec["one"],
            spec["pair"],
            spec["shared"],
            spec["column"],
            spec["row"],
            spec["shared"],
            spec["shared"],
        ],
        out_specs=[spec["pair"], spec["one"], spec["one"]],
        out_shape=[
            jax.ShapeDtypeStruct(q.shape, low),
            jax.ShapeDtypeStruct(k.shape, low),
            jax.ShapeDtypeStruct(v.shape, low),
        ],
        scratch_shapes=[
            pltpu.VMEM((size, size), wide),
            pltpu.VMEM((size, LANES), wide),
            pltpu.VMEM((size, LANES), wide),
        ],
        compiler_params=pltpu.CompilerParams(vmem_limit_bytes=48 * 2**20),
        cost_estimate=pl.CostEstimate(
            flops=20 * work * LANES, bytes_accessed=10 * q.size, transcendentals=work
        ),
        name="attend_back",
    )(
        q,
        k,
        v,
        grad,
        total,
        segment.reshape(count, 1),
        segment.reshape(blocks, 1, size),
        cosine,
        sine,
    )


def squeeze_kernel(dq_ref, dk_ref, dv_ref, out_ref):
    half = HD // 2
    parts = []
    for ref in (dq_ref, dk_ref):
        for at in range(0, ref.shape[1], LANES):
            head = ref[:, at : at + LANES].astype(wide)
            parts.append(head[:, :half])
            parts.append(head[:, LANES // 2 : LANES // 2 + half])
    for at in range(0, dv_ref.shape[1], LANES):
        parts.append(dv_ref[:, at : at + LANES].astype(wide)[:, :HD])
    out_ref[...] = jnp.concatenate(parts, axis=1).astype(low)


def squeeze(dq, dk, dv):
    count = dq.shape[0]
    tile = 256
    width = (dq.shape[1] + dk.shape[1] + dv.shape[1]) // LANES * HD
    row = lambda columns: pl.BlockSpec((tile, columns), lambda i: (i, 0))
    return pl.pallas_call(
        squeeze_kernel,
        grid=(count // tile,),
        in_specs=[row(dq.shape[1]), row(dk.shape[1]), row(dv.shape[1])],
        out_specs=row(width),
        out_shape=jax.ShapeDtypeStruct((count, width), low),
        cost_estimate=pl.CostEstimate(
            flops=0, bytes_accessed=4 * count * width, transcendentals=0
        ),
        name="squeeze",
    )(dq, dk, dv)


def layout(length_row, count):
    ends = jnp.cumsum(length_row)
    slots = jnp.arange(count, dtype=jnp.int32)
    passed = (slots[:, None] >= ends[None, :]).astype(jnp.int32)
    segment = jnp.sum(passed, axis=1)
    position = slots - jnp.sum(passed * length_row[None, :], axis=1)
    return position, segment


def normalize(hidden, gain):
    scale = lax.rsqrt(jnp.mean(hidden * hidden, axis=-1, keepdims=True) + epsilon)
    return (hidden * scale * gain, scale)


def norm_back(hidden, scale, gain, incoming):
    weighted = incoming * gain
    inner = jnp.mean(weighted * hidden, axis=-1, keepdims=True)
    return (
        scale * weighted - hidden * scale**3 * inner,
        jnp.sum(incoming * hidden * scale, axis=0),
    )


def project(left, weight):
    return jnp.dot(left, weight, preferred_element_type=wide)


def in_order(core, mine, other, axis):
    return jnp.where(
        core == 0,
        jnp.concatenate([mine, other], axis=axis),
        jnp.concatenate([other, mine], axis=axis),
    )


def on_device(
    routes,
    tokens,
    lengths,
    attn_gain,
    w_query,
    w_key,
    w_value,
    w_out,
    ffn_gain,
    w_gate,
    w_up,
    w_down,
    cotangent,
):
    count, width = tokens.shape
    n = routes.count
    owned = attn_gain.shape[0]
    units = w_down.shape[0]
    core = lax.axis_index("rep")
    z, y, x = routes.place()
    place = jnp.stack([z, y, x]).astype(jnp.int32)
    half_width = width // 2
    block_rows = width // BLOCKS
    quarter = units // (2 * CHUNKS)

    qkv_shard = jnp.concatenate(
        [
            lax.dynamic_slice_in_dim(w, core * (w.shape[1] // 2), w.shape[1] // 2, axis=1)
            for w in (w_query, w_key, w_value)
        ],
        axis=1,
    )
    out_shard = lax.dynamic_slice_in_dim(w_out, core * half_width, half_width, axis=1)

    def units_of(weight, chunk):
        split = weight.reshape(weight.shape[0], n, 2 * CHUNKS, quarter)
        part = lax.dynamic_index_in_dim(split, CHUNKS * core + chunk, axis=2, keepdims=False)
        return part.reshape(weight.shape[0], n * quarter)

    def slabs_of(weight):
        return [weight[:, at : at + SLAB] for at in range(0, weight.shape[1], SLAB)]

    ffn_shards = []
    for chunk in range(CHUNKS):
        rows = lax.dynamic_slice_in_dim(w_down, (CHUNKS * core + chunk) * quarter, quarter, axis=0)
        ffn_shards.append(
            jnp.concatenate(
                slabs_of(units_of(w_gate, chunk)) + slabs_of(units_of(w_up, chunk)) + slabs_of(rows),
                axis=0,
            )
        )
    chunk_units = n * quarter
    gate_slabs = chunk_units // SLAB
    down_slabs = width // SLAB
    ffn_parts = [owned] * (2 * gate_slabs) + [quarter] * down_slabs
    ffn_plan, row = [], 0
    for matrix in range(2):
        for at in range(gate_slabs):
            ffn_plan.append(Slab(matrix, row, block_rows, block_rows, 0, at * SLAB, SLAB))
            row += block_rows
    block_units = chunk_units // BLOCKS
    for at in range(down_slabs):
        ffn_plan.append(Slab(2, row, block_units, block_units, 0, at * SLAB, SLAB))
        row += block_units
    ffn_rows = row
    ffn_shapes = [(width, chunk_units), (width, chunk_units), (chunk_units, width)]
    cut_half = block_rows // 2
    square_plan = [
        Slab(0, at, cut_half, block_rows, at, 0, width) for at in (0, cut_half)
    ]
    out_plan = [Slab(0, at, cut_half, LANES, at, 0, half_width) for at in (0, cut_half)]

    other_tokens = swap(tokens)
    both_cotangents = jnp.concatenate([cotangent, swap(cotangent)], axis=0)
    both_lengths = (lengths[0], swap(lengths)[0])
    laid = [layout(row, count) for row in both_lengths]
    segment = jnp.stack([item[1] for item in laid])
    cosine, sine = turn_table(jnp.concatenate([item[0] for item in laid]))

    small = jnp.zeros((8, LANES), wide)
    small = small.at[0, :owned].set(attn_gain.astype(wide))
    small = small.at[4, :owned].set(ffn_gain.astype(wide))
    if routes.direct:
        line, from_x, from_y, far_a, far_b = routes.gather(small, [8])
        far = jnp.concatenate([far_a, far_b], axis=1)
        blocks = jnp.stack([jnp.stack([line, from_x], 1), jnp.stack([from_y, far], 1)], 1)
        blocks = blocks[(jnp.arange(4) - z) % 4]
        blocks = blocks[:, jnp.arange(2) ^ y]
        blocks = blocks[:, :, jnp.arange(2) ^ x].reshape(BLOCKS, 8, LANES)
    else:
        blocks = lax.all_gather(small, "fsdp", axis=0)
    gain_one = blocks[:, 0, :owned].reshape(width)
    gain_two = blocks[:, 4, :owned].reshape(width)

    qkv_pieces = routes.gather(qkv_shard, [owned])
    out_pieces = routes.gather(out_shard, [owned])
    ffn_pieces = [routes.gather(shard, ffn_parts) for shard in ffn_shards]

    hidden = tokens.astype(wide)
    normed, scale_one = normalize(hidden, gain_one)
    other_normed, _ = normalize(other_tokens.astype(wide), gain_one)
    normed_low = jnp.concatenate([normed.astype(low), other_normed.astype(low)], axis=0)
    (qkv_full,) = assemble(place, qkv_pieces, square_plan, [(width, width)])
    queries, keys, values = project_qkv(normed_low, qkv_full, cosine, sine)
    attended, total = attend(queries, keys, values, segment)
    other_attended = swap(attended)
    (out_mine,) = assemble(place, out_pieces, out_plan, [(H * LANES, half_width)], pads=True)
    out_full = in_order(core, out_mine, swap(out_mine), 1)
    attended_own = in_order(core, attended[:count], other_attended[count:], 1)
    attended_other = in_order(core, attended[count:], other_attended[:count], 1)
    middle = hidden + project(attended_own, out_full)
    normed_two, scale_two = normalize(middle, gain_two)
    normed_two_own = normed_two.astype(low)
    normed_two_low = jnp.concatenate([normed_two_own, swap(normed_two_own)], axis=0)

    output_part, normed_part = None, None
    ffn_owned = []
    for chunk in range(CHUNKS):
        gate_w, up_w, down_w = assemble(place, ffn_pieces[chunk], ffn_plan, ffn_shapes)
        gate = project(normed_two_low, gate_w)
        upward = project(normed_two_low, up_w)
        sigma = jax.nn.sigmoid(gate)
        inner_low = (gate * sigma * upward).astype(low)
        grad_inner = across(both_cotangents, down_w)
        grad_gate_low = (grad_inner * upward * sigma * (1.0 + gate * (1.0 - sigma))).astype(low)
        grad_up_low = (grad_inner * gate * sigma).astype(low)
        grads = (
            down(normed_two_low, grad_gate_low).astype(low),
            down(normed_two_low, grad_up_low).astype(low),
            down(inner_low, both_cotangents).astype(low),
        )
        ffn_owned.append(
            routes.scatter(cut(place, grads, ffn_plan, ffn_rows, SLAB), ffn_parts)
        )
        out_term = project(inner_low, down_w)
        normed_term = across(grad_gate_low, gate_w) + across(grad_up_low, up_w)
        output_part = out_term if output_part is None else output_part + out_term
        normed_part = normed_term if normed_part is None else normed_part + normed_term
    output = (middle + output_part[:count] + swap(output_part[count:])).astype(low)
    grad_normed_two = normed_part[:count] + swap(normed_part[count:])

    middle_part, grad_ffn_gain = norm_back(middle, scale_two, gain_two, grad_normed_two)
    grad_middle = cotangent.astype(wide) + middle_part
    grad_branch = grad_middle.astype(low)

    branch_mine = lax.dynamic_slice_in_dim(grad_branch, core * half_width, half_width, axis=1)
    branch_sent = lax.dynamic_slice_in_dim(grad_branch, (1 - core) * half_width, half_width, axis=1)
    branch_columns = jnp.concatenate([branch_mine, swap(branch_sent)], axis=0)
    grad_out = down(jnp.concatenate([attended_own, attended_other], axis=0), branch_columns)
    out_owned = routes.scatter(
        cut(place, (grad_out.astype(low),), out_plan, block_rows, half_width), [owned]
    )
    grad_attended = across(grad_branch, out_full).astype(low)
    half_heads = H // 2 * LANES
    attended_mine = lax.dynamic_slice_in_dim(grad_attended, core * half_heads, half_heads, axis=1)
    attended_sent = lax.dynamic_slice_in_dim(
        grad_attended, (1 - core) * half_heads, half_heads, axis=1
    )
    grad_heads = jnp.concatenate([attended_mine, swap(attended_sent)], axis=0)
    grad_qkv = squeeze(
        *attend_back(queries, keys, values, grad_heads, total, segment, cosine, sine)
    )
    qkv_owned = routes.scatter(
        cut(place, (down(normed_low, grad_qkv).astype(low),), square_plan, block_rows, width),
        [owned],
    )
    normed_part = across(grad_qkv, qkv_full)
    grad_normed = normed_part[:count] + swap(normed_part[count:])
    hidden_part, grad_attn_gain = norm_back(hidden, scale_one, gain_one, grad_normed)
    grad_tokens = grad_middle + hidden_part

    gains = jnp.zeros((n, 8, LANES), wide)
    gains = gains.at[:, 0, :owned].set(grad_attn_gain.reshape(n, owned))
    gains = gains.at[:, 4, :owned].set(grad_ffn_gain.reshape(n, owned))
    gains = gains + swap(gains)
    if routes.direct:
        blocks = gains.reshape(4, 2, 2, 8, LANES)[(jnp.arange(4) + z) % 4]
        blocks = blocks[:, jnp.arange(2) ^ y][:, :, jnp.arange(2) ^ x]
        far, near_x, near_y = blocks[:, 1, 1], blocks[:, 0, 1], blocks[:, 1, 0]
        pieces = (
            jnp.stack([far[:, :4], near_x[:, :4]]),
            jnp.stack([far[:, 4:], near_y[:, 4:]]),
            near_x[:, 4:],
            near_y[:, :4],
            blocks[:, 0, 0],
        )
        gains = routes.scatter(pieces, [8])
    else:
        gains = lax.psum_scatter(gains, "fsdp", scatter_dimension=0, tiled=True)[0]

    def both(mine):
        other = swap(mine.astype(low)).astype(wide)
        return jnp.where(core == 0, mine, other), jnp.where(core == 0, other, mine)

    qkv_halves = both(qkv_owned)
    q_columns, k_columns = w_query.shape[1] // 2, w_key.shape[1] // 2
    at = 0
    attn_grads = []
    for columns in (q_columns, k_columns, k_columns):
        attn_grads.append(
            jnp.concatenate([item[:, at : at + columns] for item in qkv_halves], axis=1)
        )
        at += columns
    grad_out_rows = jnp.concatenate(both(out_owned), axis=1)
    ffn_halves = [both(item) for item in ffn_owned]
    quarters = [ffn_halves[chunk][part] for part in range(2) for chunk in range(CHUNKS)]
    span = owned * gate_slabs

    def matrix_rows(packed, start, rows, slabs):
        return jnp.concatenate(
            [packed[start + s * rows : start + (s + 1) * rows] for s in range(slabs)], axis=1
        )

    def unit_columns(start):
        parts = [
            matrix_rows(item, start, owned, gate_slabs).reshape(owned, n, quarter)
            for item in quarters
        ]
        return jnp.stack(parts, axis=2).reshape(owned, n * units)

    grad_gate = unit_columns(0)
    grad_up = unit_columns(span)
    grad_down = jnp.concatenate(
        [matrix_rows(item, 2 * span, quarter, down_slabs) for item in quarters], axis=0
    )
    return (
        output,
        grad_tokens,
        gains[0, :owned],
        attn_grads[0],
        attn_grads[1],
        attn_grads[2],
        grad_out_rows,
        gains[4, :owned],
        grad_gate,
        grad_up,
        grad_down,
    )


def solution(mesh):
    rows = P(("rep", "fsdp"), None)
    split = P("fsdp", None)
    gain = P("fsdp")
    return jax.shard_map(
        functools.partial(on_device, Routes(mesh.shape["fsdp"])),
        mesh=mesh,
        in_specs=(rows, rows, gain) + (split,) * 4 + (gain,) + (split,) * 3 + (rows,),
        out_specs=(rows, rows, gain) + (split,) * 4 + (gain,) + (split,) * 3,
        check_vma=False,
    )
```

```python
import functools

import jax
import jax.numpy as jnp
from jax import lax
from jax.experimental import pallas as pl
from jax.experimental.pallas import tpu as pltpu
from jax.sharding import PartitionSpec as P

H = 16
KV = 8
HD = 96
HALF = HD // 2
LANES = 128
BLOCKS = 16
TILE = 128
SLAB = 512
CHUNKS = 2
COST_SCALE = 0.001

epsilon = 1e-05
rope_base = 100000.0
masked_score = -1e30
low = jnp.bfloat16
wide = jnp.float32


def whole(array, buffers=1):
    zeros = (0,) * array.ndim
    mode = pl.Buffered(buffers)
    return pl.BlockSpec(array.shape, lambda *at: zeros, pipeline_mode=mode)


def rows_of(tile, width, first=0):
    return pl.BlockSpec((tile, width), lambda i, place: (first + i, 0))


def shaped(shape, dtype):
    return jax.ShapeDtypeStruct(shape, dtype)


anywhere = pl.BlockSpec(memory_space=pl.ANY)


def run(kernel, name, place, grid, operands, outs, scratch=(), after=(), vmem=56, us=4):
    after = [item for item in after if isinstance(item, jax.Array)]
    count, extra = len(operands), len(after)

    def body(place_ref, *refs):
        kernel(place_ref, *refs[:count], *refs[count + extra :])

    return pl.pallas_call(
        body,
        grid_spec=pltpu.PrefetchScalarGridSpec(
            num_scalar_prefetch=1,
            grid=grid,
            in_specs=[spec for _, spec in operands] + [anywhere] * extra,
            out_specs=[spec for _, spec in outs],
            scratch_shapes=list(scratch),
        ),
        out_shape=[shape for shape, _ in outs],
        compiler_params=pltpu.CompilerParams(vmem_limit_bytes=vmem * 2**20),
        cost_estimate=pl.CostEstimate(
            flops=0, bytes_accessed=int(us * COST_SCALE * 3.3e6), transcendentals=0
        ),
        name=name,
    )(place, *[array for array, _ in operands], *after)


def across(left, right):
    return lax.dot_general(left, right, (((1,), (1,)), ((), ())), preferred_element_type=wide)


def down(left, right):
    return lax.dot_general(left, right, (((0,), (0,)), ((), ())), preferred_element_type=wide)


def project(left, right):
    return jnp.dot(left, right, preferred_element_type=wide)


class Slab:
    def __init__(self, matrix, row, rows, stride, offset, column, width=SLAB, lane=0):
        self.matrix, self.row, self.rows = matrix, row, rows
        self.stride, self.offset = stride, offset
        self.column, self.width, self.lane = column, width, lane

    def of(self, refs, block):
        rows = pl.ds(pl.multiple_of(block * self.stride + self.offset, 16), self.rows)
        return refs[self.matrix].at[rows, pl.ds(self.column, self.width)]

    def lanes(self):
        return pl.ds(self.lane, self.width)


FIRST_HALF, FFN_HALF, QKV_HALF, OUT_HALF = 224, 288, 160, 80


def square_plan(half):
    plan = []
    for slab in range(3):
        top, bottom = slab * 96, slab * 96 + 96
        for first, last in ((top, min(bottom, half)), (max(top, half), bottom)):
            if first < last:
                plan.append(Slab(0, first, last - first, 96, first - top, slab * SLAB))
    return plan


def out_plan(start, half):
    plan = []
    for first, last in ((start, min(start + 96, half)), (max(start, half), start + 96)):
        if first < last:
            plan.append(Slab(0, first, last - first, LANES, first - start, 0))
    for part in range(2):
        plan.append(Slab(0, start + 96, 48, LANES, part * 48, SLAB, 256, part * 256))
    return plan


GAINS = 288
GAIN_SLAB = Slab(1, GAINS, 16, 16, 0, 0)
FIRST_QKV_PLAN = square_plan(FIRST_HALF) + [GAIN_SLAB]
FIRST_OUT_PLAN = out_plan(GAINS + 16, FIRST_HALF)
QKV_PLAN = square_plan(QKV_HALF) + [GAIN_SLAB]
OUT_PLAN = out_plan(0, OUT_HALF)
FFN_PLAN = [
    Slab(0, 0, 96, 96, 0, 0),
    Slab(0, 96, 96, 96, 0, SLAB),
    Slab(1, 192, 96, 96, 0, 0),
    Slab(1, 288, 96, 96, 0, SLAB),
    Slab(2, 384, 64, 64, 0, 0),
    Slab(2, 448, 64, 64, 0, SLAB),
    Slab(2, 512, 64, 64, 0, 2 * SLAB),
]


def block_index(place_ref, k, dy, dx):
    z, y, x = place_ref[0], place_ref[1], place_ref[2]
    return ((z ^ k) * 2 + (y ^ dy)) * 2 + (x ^ dx)


def fetch(place_ref, pieces, plan, half, matrices, sems):
    for k in range(4):
        for dy in range(2):
            for dx in range(2):
                block = block_index(place_ref, k, dy, dx)
                for slab in plan:
                    at = pl.ds(slab.row, slab.rows)
                    source = pieces[dy * 2 + dx]
                    if dy and dx:
                        part = int(slab.row >= half)
                        at = pl.ds(slab.row - part * half, slab.rows)
                        source = pieces[3 + part]
                    copy = pltpu.make_async_copy(
                        source.at[k, at, slab.lanes()],
                        slab.of(matrices, block),
                        sems.at[slab.matrix],
                    )
                    copy.start()


def send_off(place_ref, k, matrices, stride_base, plan, half, outs, sems):
    to_x, to_y, late_x, late_y, own = range(5)
    for dy in range(2):
        for dx in range(2):
            block = block_index(place_ref, place_ref[0], dy, dx) + stride_base
            for slab in plan:
                part = int(slab.row >= half)
                at = pl.ds(slab.row - part * half, slab.rows)
                if (dy, dx) == (0, 0):
                    which, index = own, (k, part)
                elif dy and dx:
                    which, index = (to_y if part else to_x), (0, k)
                elif part == dy:
                    which, index = (to_y if dy else to_x), (1, k)
                else:
                    which, index = (late_y if dy else late_x), (k,)
                target = outs[which].at[(*index, at, slab.lanes())]
                pltpu.make_async_copy(slab.of(matrices, block), target, sems.at[which]).start()


def fill_spare(source, row, rows, half, outs, sems):
    at = pl.ds(row - half, rows)
    for k in range(4):
        for which, index in ((1, (0, k)), (1, (1, k)), (2, (k,)), (4, (k, 1))):
            target = outs[which].at[(*index, at)]
            pltpu.make_async_copy(source, target, sems.at[which]).start()


def drain(refs, sems):
    for index, ref in enumerate(refs):
        pltpu.make_async_copy(ref, ref, sems.at[index]).wait()


def sent_shapes(half, width):
    shapes = [(2, 4, half, width)] * 2 + [(4, half, width)] * 2 + [(4, 2, half, width)]
    return [(shaped(shape, low), anywhere) for shape in shapes]


def pair_kernel(place_ref, own, far, out, sems):
    copies = [
        pltpu.make_async_copy(ref, out.at[k], sems.at[k]) for k, ref in enumerate((own, far))
    ]
    for copy in copies:
        copy.start()
    for copy in copies:
        copy.wait()


def pair_up(place, own, far, after=()):
    out = shaped((2, *own.shape), low)
    return run(
        pair_kernel,
        "pair",
        place,
        (1,),
        [(own, anywhere), (far, anywhere)],
        [(out, whole(out))],
        [pltpu.SemaphoreType.DMA((2,))],
        after,
        us=2,
    )[0]


def line_kernel(place_ref, pair, near, out, sems):
    copies = []
    for k in range(4):
        ref = near if k % 2 else pair
        copies.append(pltpu.make_async_copy(ref.at[k // 2], out.at[k], sems.at[k]))
        copies[-1].start()
    for copy in copies:
        copy.wait()


def line_up(place, pair, near, after=()):
    _, rows, width = pair.shape
    out = shaped((4, rows, width), low)
    return run(
        line_kernel,
        "line",
        place,
        (1,),
        [(pair, anywhere), (near, anywhere)],
        [(out, whole(out))],
        [pltpu.SemaphoreType.DMA((4,))],
        after,
        us=4,
    )[0]


def halves_kernel(place_ref, from_x, from_y, upper, lower, sems):
    half = upper.shape[1]
    copies = (
        pltpu.make_async_copy(from_x.at[:, pl.ds(0, half)], upper, sems.at[0]),
        pltpu.make_async_copy(from_y.at[:, pl.ds(half, half)], lower, sems.at[1]),
    )
    for copy in copies:
        copy.start()
    for copy in copies:
        copy.wait()


def halves(place, from_x, from_y, after):
    count, rows, width = from_x.shape
    out = shaped((count, rows // 2, width), low)
    return run(
        halves_kernel,
        "halves",
        place,
        (1,),
        [(from_x, anywhere), (from_y, anywhere)],
        [(out, whole(out))] * 2,
        [pltpu.SemaphoreType.DMA((2,))],
        after,
        us=2,
    )


def step_rows(half):
    return next(rows for rows in (96, 80, 48) if half % rows == 0)


def merge_kernel(place_ref, late_x, late_y, got_x, got_y, out_x, out_y):
    out_x[...] = (late_x[...].astype(wide) + got_y[0].astype(wide)).astype(low)
    out_y[...] = (late_y[...].astype(wide) + got_x[0].astype(wide)).astype(low)


def merge(place, late_x, late_y, got_x, got_y, after):
    shape = late_x.shape
    rows = step_rows(shape[1])
    spec = pl.BlockSpec((4, rows, shape[2]), lambda i, place: (0, i, 0))
    got = pl.BlockSpec((1, 4, rows, shape[2]), lambda i, place: (0, 0, i, 0))
    return run(
        merge_kernel,
        "merge",
        place,
        (shape[1] // rows,),
        [(late_x, spec), (late_y, spec), (got_x, got), (got_y, got)],
        [(shaped(shape, low), spec)] * 2,
        after=after,
    )


def sum_kernel(groups, place_ref, *refs):
    ins, (kept, kept_far, sent) = refs[: 5 * groups], refs[5 * groups :]
    row = 0
    for group in range(groups):
        own, got_x, got_y, more_x, more_y = ins[5 * group : 5 * group + 5]
        rows = own.shape[2]
        at = slice(row, row + rows)
        for k in range(4):
            upper = own[k, 0].astype(wide) + got_x[0, k].astype(wide) + more_y[k].astype(wide)
            lower = own[k, 1].astype(wide) + got_y[0, k].astype(wide) + more_x[k].astype(wide)
            if k % 2:
                sent[k // 2, 0, at, :] = upper.astype(low)
                sent[k // 2, 1, at, :] = lower.astype(low)
            else:
                ref = kept_far if k else kept
                ref[0, at, :], ref[1, at, :] = upper, lower
        row += rows


def sum_plane(place, groups, after):
    halves = [group[0].shape[2] for group in groups]
    width = groups[0][0].shape[3]
    steps = halves[0] // step_rows(halves[0]) if len(groups) == 1 else 1
    total, rows = sum(halves), sum(halves) // steps
    operands = []
    for group, half in zip(groups, halves):
        own, got_x, got_y, more_x, more_y = group
        part = half // steps
        got = pl.BlockSpec((1, 4, part, width), lambda i, place: (1, 0, i, 0))
        more = pl.BlockSpec((4, part, width), lambda i, place: (0, i, 0))
        operands += [
            (own, pl.BlockSpec((4, 2, part, width), lambda i, place: (0, 0, i, 0))),
            (got_x, got),
            (got_y, got),
            (more_x, more),
            (more_y, more),
        ]
    out = pl.BlockSpec((2, rows, width), lambda i, place: (0, i, 0))
    both = pl.BlockSpec((2, 2, rows, width), lambda i, place: (0, 0, i, 0))
    return run(
        functools.partial(sum_kernel, len(groups)),
        "sum_plane",
        place,
        (steps,),
        operands,
        [(shaped((2, total, width), wide), out)] * 2
        + [(shaped((2, 2, total, width), low), both)],
        after=after,
        us=5,
    )


def pass_kernel(place_ref, kept_far, near, out):
    out[...] = (kept_far[...] + near[0].astype(wide)).astype(low)


def sum_pass(place, kept_far, near, after):
    _, half, width = kept_far.shape
    rows = step_rows(half)
    spec = pl.BlockSpec((2, rows, width), lambda i, place: (0, i, 0))
    second = pl.BlockSpec((1, 2, rows, width), lambda i, place: (1, 0, i, 0))
    return run(
        pass_kernel,
        "sum_pass",
        place,
        (half // rows,),
        [(kept_far, spec), (near, second)],
        [(shaped(kept_far.shape, low), spec)],
        after=after,
        us=3,
    )[0]


def total_kernel(place_ref, kept, near, far, out, out_low):
    total = kept[...] + near[0].astype(wide) + far[...].astype(wide)
    out[...] = total
    out_low[...] = total.astype(low)


def sum_line(place, kept, near, far, after):
    _, half, width = kept.shape
    rows = step_rows(half)
    spec = pl.BlockSpec((2, rows, width), lambda i, place: (0, i, 0))
    first = pl.BlockSpec((1, 2, rows, width), lambda i, place: (0, 0, i, 0))
    total, total_low = run(
        total_kernel,
        "sum_line",
        place,
        (half // rows,),
        [(kept, spec), (near, first), (far, spec)],
        [(shaped(kept.shape, wide), spec), (shaped(kept.shape, low), spec)],
        after=after,
        us=4,
    )
    return total.reshape(2 * half, width), total_low.reshape(2 * half, width)


def pack_first_kernel(place_ref, query, key, value, square, gain_one, gain_two, out):
    core = place_ref[3]

    def mine(ref):
        columns = ref.shape[1] // 2
        return ref[:, pl.ds(pl.multiple_of(core * columns, LANES), columns)]

    packed = jnp.concatenate([mine(query), mine(key), mine(value)], axis=1)
    rows = packed.shape[0]
    for slab in range(3):
        out[slab * rows : (slab + 1) * rows, :] = packed[:, slab * SLAB : (slab + 1) * SLAB]
    row = lax.broadcasted_iota(jnp.int32, (16, LANES), 0)
    gap = jnp.zeros((16, LANES - rows), wide)
    out[GAINS : GAINS + 16, :] = jnp.zeros((16, SLAB), low)
    for index, gain in enumerate((gain_one, gain_two)):
        spread = jnp.broadcast_to(gain[...].astype(wide), (16, rows))
        spread = jnp.where(row == 0, jnp.concatenate([spread, gap], axis=1), 0.0)
        out[GAINS : GAINS + 16, index * LANES : (index + 1) * LANES] = spread.astype(low)
    at, packed = GAINS + 16, mine(square)
    out[at : at + rows, :] = packed[:, :SLAB]
    for part in range(2):
        out[at + rows :, part * 256 : (part + 1) * 256] = packed[
            part * rows // 2 : (part + 1) * rows // 2, SLAB:
        ]


def pack_first(place, query, key, value, square, gain_one, gain_two):
    operands = [query, key, value, square, gain_one.reshape(1, -1), gain_two.reshape(1, -1)]
    out = shaped((2 * FIRST_HALF, SLAB), low)
    return run(
        pack_first_kernel,
        "pack_first",
        place,
        (1,),
        [(item, whole(item)) for item in operands],
        [(out, whole(out))],
    )[0]


def interleave(even, odd):
    lane = lax.broadcasted_iota(jnp.int32, even.shape, 1)
    left = jnp.where(lane < LANES // 2, even, pltpu.roll(odd, LANES // 2, 1))
    right = jnp.where(lane < LANES // 2, pltpu.roll(even, LANES // 2, 1), odd)
    return left, right


def pack_ffn_kernel(chunk, place_ref, gate, up, down_w, out):
    core = place_ref[3]
    rows = gate.shape[0]
    for matrix, ref in enumerate((gate, up)):
        for pair in range(8):
            windows = [
                ref[:, pl.ds(pl.multiple_of((2 * pair + odd) * 256 + core * LANES, LANES), LANES)]
                for odd in range(2)
            ]
            packed = interleave(windows[0].astype(wide), windows[1].astype(wide))[chunk]
            at = (matrix * 2 + pair // 4) * rows
            column = pair % 4 * LANES
            out[at : at + rows, column : column + LANES] = packed.astype(low)
    units = down_w[pl.ds(pl.multiple_of(core * LANES + chunk * 64, 64), 64), :]
    for slab in range(3):
        at = 4 * rows + slab * 64
        out[at : at + 64, :] = units[:, slab * SLAB : (slab + 1) * SLAB]


def pack_ffn(place, chunk, gate, up, down_w, after):
    out = shaped((2 * FFN_HALF, SLAB), low)
    return run(
        functools.partial(pack_ffn_kernel, chunk),
        "pack_ffn",
        place,
        (1,),
        [(item, whole(item)) for item in (gate, up, down_w)],
        [(out, whole(out))],
        after=after,
    )[0]


def unpack_ffn_kernel(place_ref, mine_0, mine_1, other_0, other_1, gate, up, down_w):
    core = place_ref[3]
    rows = gate.shape[0]
    for owner, chunks in ((core, (mine_0, mine_1)), (1 - core, (other_0, other_1))):
        for matrix, ref in enumerate((gate, up)):
            for pair in range(8):
                at = (matrix * 2 + pair // 4) * rows
                column = pair % 4 * LANES
                parts = [
                    chunk[at : at + rows, column : column + LANES].astype(wide)
                    for chunk in chunks
                ]
                for odd, window in enumerate(interleave(*parts)):
                    place = (2 * pair + odd) * 256 + owner * LANES
                    ref[:, pl.ds(pl.multiple_of(place, LANES), LANES)] = window
        for index, chunk in enumerate(chunks):
            for slab in range(3):
                at = 4 * rows + slab * 64
                place = pl.multiple_of(owner * LANES + index * 64, 64)
                down_w[pl.ds(place, 64), slab * SLAB : (slab + 1) * SLAB] = chunk[
                    at : at + 64, :
                ].astype(wide)


def unpack_ffn(place, mine, other, shapes, after):
    outs = [shaped(shape, wide) for shape in shapes]
    return run(
        unpack_ffn_kernel,
        "unpack_ffn",
        place,
        (1,),
        [(item, whole(item)) for item in (*mine, *other)],
        [(out, whole(out)) for out in outs],
        after=after,
    )


def unpack_first_kernel(place_ref, mine, other, query, key, value, square):
    core = place_ref[3]
    rows = query.shape[0]
    half = QKV_HALF + OUT_HALF

    def put(ref, owner, part):
        columns = ref.shape[1] // 2
        at = pl.ds(pl.multiple_of(owner * columns, LANES), columns)
        ref[:, at] = part.astype(wide)

    for owner, ref in ((core, mine), (1 - core, other)):
        qkv = jnp.concatenate([ref[:QKV_HALF, :], ref[half : half + QKV_HALF, :]], axis=0)
        out = jnp.concatenate([ref[QKV_HALF:half, :], ref[half + QKV_HALF :, :]], axis=0)
        slabs = [qkv[slab * rows : (slab + 1) * rows, :] for slab in range(3)]
        put(query, owner, jnp.concatenate([slabs[0], slabs[1][:, :256]], axis=1))
        put(key, owner, jnp.concatenate([slabs[1][:, 256:], slabs[2][:, :128]], axis=1))
        put(value, owner, slabs[2][:, 128:])
        rest = out[rows : rows + rows // 2, :]
        rest = jnp.concatenate([rest[:, :256], rest[:, 256:]], axis=0)
        put(square, owner, jnp.concatenate([out[:rows, :], rest], axis=1))


def unpack_first(place, mine, other, shapes):
    outs = [shaped(shape, wide) for shape in shapes]
    return run(
        unpack_first_kernel,
        "unpack_first",
        place,
        (1,),
        [(item, whole(item)) for item in (mine, other)],
        [(out, whole(out)) for out in outs],
    )


def turn_table(position):
    frequency = rope_base ** (-jnp.arange(HALF, dtype=wide) * 2.0 / HD)
    angle = position.astype(wide)[:, None] * frequency[None, :]
    gap = jnp.zeros((position.shape[0], LANES // 2 - HALF), wide)
    cosine, sine = jnp.cos(angle), jnp.sin(angle)
    return (
        jnp.concatenate([cosine, gap, cosine, gap], axis=1),
        jnp.concatenate([-sine, gap, sine, gap], axis=1),
    )


def qkv_kernel(tiles, place_ref, own_ref, far_ref, cos_ref, sin_ref, *refs):
    pieces = refs[:5]
    normed_ref, q_ref, k_ref, v_ref, w_ref, gain_ref, gain_rows, x_ref, sems = refs[5:]
    step = pl.program_id(0)

    @pl.when(step < tiles)
    def _():
        x_ref[...] = own_ref[...]

    @pl.when(step >= tiles)
    def _():
        x_ref[...] = far_ref[...]

    @pl.when(pl.program_id(0) == 0)
    def _():
        fetch(place_ref, pieces, FIRST_QKV_PLAN, FIRST_HALF, (w_ref, gain_rows), sems)
        drain((w_ref, gain_rows), sems)
        for index in range(2):
            parts = [
                gain_rows[16 * block : 16 * block + 16, index * LANES : (index + 1) * LANES]
                for block in range(BLOCKS)
            ]
            parts = [part.astype(wide)[:8, :HD] for part in parts]
            gain_ref[8 * index : 8 * index + 8, :] = jnp.concatenate(parts, axis=1)

    hidden = x_ref[...].astype(wide)
    scale = lax.rsqrt(jnp.mean(hidden * hidden, axis=-1, keepdims=True) + epsilon)
    normed = (hidden * scale * gain_ref[0:1, :]).astype(low)
    normed_ref[...] = normed
    gap = jnp.zeros((x_ref.shape[0], LANES // 2 - HALF), wide)
    heads = q_ref.shape[1] // LANES
    groups = k_ref.shape[1] // LANES
    count = 4
    for first in range(0, heads + 2 * groups, count):
        part = project(normed, w_ref[:, first * HD : (first + count) * HD])
        for index in range(first, first + count):
            at = (index - first) * HD
            if index >= heads + groups:
                column = (index - heads - groups) * LANES
                padded = jnp.concatenate([part[:, at : at + HD], gap, gap], axis=1)
                v_ref[:, column : column + LANES] = padded.astype(low)
                continue
            padded = jnp.concatenate(
                [part[:, at : at + HALF], gap, part[:, at + HALF : at + HD], gap], axis=1
            )
            turned = pltpu.roll(padded, LANES // 2, 1)
            padded = (padded * cos_ref[...] + turned * sin_ref[...]).astype(low)
            if index < heads:
                q_ref[:, index * LANES : (index + 1) * LANES] = padded
            else:
                column = (index - heads) * LANES
                k_ref[:, column : column + LANES] = padded


def project_qkv(place, own, far, cosine, sine, pieces, after):
    count, width = own.shape
    tile = 320
    tiles = count // tile
    count = 2 * count
    heads, groups = H // 2 * LANES, KV // 2 * LANES
    weight, gains = shaped((width, width), low), shaped((16, width), wide)
    early = pl.BlockSpec((tile, width), lambda i, place: (jnp.minimum(i, tiles - 1), 0))
    late = pl.BlockSpec((tile, width), lambda i, place: (jnp.maximum(i - tiles, 0), 0))
    return run(
        functools.partial(qkv_kernel, tiles),
        "project_qkv",
        place,
        (count // tile,),
        [
            (own, early),
            (far, late),
            (cosine, rows_of(tile, LANES)),
            (sine, rows_of(tile, LANES)),
        ]
        + [(piece, anywhere) for piece in pieces],
        [
            (shaped((count, width), low), rows_of(tile, width)),
            (shaped((count, heads), low), rows_of(tile, heads)),
            (shaped((count, groups), low), rows_of(tile, groups)),
            (shaped((count, groups), low), rows_of(tile, groups)),
            (weight, whole(weight)),
            (gains, whole(gains)),
        ],
        [
            pltpu.VMEM((BLOCKS * 16, SLAB), low),
            pltpu.VMEM((tile, width), low),
            pltpu.SemaphoreType.DMA((2,)),
        ],
        after,
        us=18,
    )


def fill_bias(bias_ref, column_ref, row_ref):
    size = bias_ref.shape[0]
    for start in range(0, size, TILE):
        shape = (TILE, size)
        slots = lax.broadcasted_iota(jnp.int32, shape, 0) + start
        keys = lax.broadcasted_iota(jnp.int32, shape, 1)
        same = column_ref[start : start + TILE, :] == row_ref[0]
        allowed = same & (keys <= slots)
        bias_ref[start : start + TILE, :] = jnp.where(allowed, 0.0, masked_score)


def attend_kernel(
    place_ref, q_ref, k_ref, v_ref, column_ref, row_ref, out_ref, total_ref, bias_ref
):
    group = pl.program_id(0)
    size = q_ref.shape[0]

    @pl.when(group == 0)
    def _():
        fill_bias(bias_ref, column_ref, row_ref)
        total_ref[...] = jnp.zeros_like(total_ref)

    lane = lax.broadcasted_iota(jnp.int32, (TILE, LANES), 1)
    for start in range(0, size, TILE):
        stop = start + TILE
        for head in range(2):
            columns = slice(head * LANES, (head + 1) * LANES)
            raw = across(q_ref[start:stop, columns], k_ref[:stop, :])
            scores = raw * HD ** (-0.5) + bias_ref[start:stop, :stop]
            top = jnp.max(scores, axis=-1, keepdims=True)
            powers = jnp.exp(scores - top)
            amount = jnp.sum(powers, axis=-1, keepdims=True)
            probs = (powers * (1.0 / amount)).astype(low)
            out_ref[start:stop, columns] = project(probs, v_ref[:stop, :]).astype(low)
            total = top + jnp.log(amount)
            total_ref[start:stop, :] = jnp.where(
                lane == 2 * group + head, total, total_ref[start:stop, :]
            )


def attention_specs(size, block):
    return dict(
        pair=pl.BlockSpec((size, 2 * LANES), lambda g, place: (block, g)),
        one=pl.BlockSpec((size, LANES), lambda g, place: (block, g)),
        pair_alone=pl.BlockSpec((size, 2 * LANES), lambda g, place: (0, g)),
        one_alone=pl.BlockSpec((size, LANES), lambda g, place: (0, g)),
        shared=pl.BlockSpec((size, LANES), lambda g, place: (block, 0)),
        alone=pl.BlockSpec((size, LANES), lambda g, place: (0, 0)),
        column=pl.BlockSpec((size, 1), lambda g, place: (block, 0)),
        row=pl.BlockSpec((1, 1, size), lambda g, place: (block, 0, 0)),
    )


def attend(place, q, k, v, segment, block, after=()):
    blocks, size = segment.shape
    spec = attention_specs(size, block)
    return run(
        attend_kernel,
        "attend",
        place,
        (k.shape[1] // LANES,),
        [
            (q, spec["pair"]),
            (k, spec["one"]),
            (v, spec["one"]),
            (segment.reshape(blocks * size, 1), spec["column"]),
            (segment.reshape(blocks, 1, size), spec["row"]),
        ],
        [
            (shaped((size, q.shape[1]), low), spec["pair_alone"]),
            (shaped((size, LANES), wide), spec["alone"]),
        ],
        [pltpu.VMEM((size, size), wide)],
        after,
        us=17,
    )


def attend_back_kernel(
    place_ref,
    q_ref,
    k_ref,
    v_ref,
    grad_ref,
    total_ref,
    column_ref,
    row_ref,
    cos_ref,
    sin_ref,
    dq_ref,
    dk_ref,
    dv_ref,
    bias_ref,
    dk_sum,
    dv_sum,
):
    group = pl.program_id(0)
    size = q_ref.shape[0]

    @pl.when(group == 0)
    def _():
        fill_bias(bias_ref, column_ref, row_ref)

    def turned_back(grad, rows):
        turned = pltpu.roll(grad, LANES // 2, 1)
        return (grad * cos_ref[rows, :] - turned * sin_ref[rows, :]).astype(low)

    dk_sum[...] = jnp.zeros_like(dk_sum)
    dv_sum[...] = jnp.zeros_like(dv_sum)
    lane = lax.broadcasted_iota(jnp.int32, (TILE, LANES), 1)
    for start in range(0, size, TILE):
        stop = start + TILE
        for head in range(2):
            columns = slice(head * LANES, (head + 1) * LANES)
            queries = q_ref[start:stop, columns]
            grads = grad_ref[start:stop, columns]
            total = jnp.sum(
                jnp.where(lane == 2 * group + head, total_ref[start:stop, :], 0.0),
                axis=-1,
                keepdims=True,
            )
            raw = across(queries, k_ref[:stop, :])
            probs = jnp.exp(raw * HD ** (-0.5) + bias_ref[start:stop, :stop] - total)
            dv_sum[:stop, :] += down(probs.astype(low), grads)
            grad_probs = across(grads, v_ref[:stop, :])
            weighted = probs * grad_probs
            delta = jnp.sum(weighted, axis=-1, keepdims=True)
            grad_raw = ((weighted - probs * delta) * HD ** (-0.5)).astype(low)
            dq = project(grad_raw, k_ref[:stop, :])
            dq_ref[start:stop, columns] = turned_back(dq, slice(start, stop))
            dk_sum[:stop, :] += down(grad_raw, queries)
    dv_ref[...] = dv_sum[...].astype(low)
    dk_ref[...] = turned_back(dk_sum[...], slice(None))


def attend_back(place, q, k, v, grad, total, segment, cosine, sine, block, after=()):
    blocks, size = segment.shape
    spec = attention_specs(size, block)
    return run(
        attend_back_kernel,
        "attend_back",
        place,
        (k.shape[1] // LANES,),
        [
            (q, spec["pair"]),
            (k, spec["one"]),
            (v, spec["one"]),
            (grad, spec["pair_alone"]),
            (total, spec["alone"]),
            (segment.reshape(blocks * size, 1), spec["column"]),
            (segment.reshape(blocks, 1, size), spec["row"]),
            (cosine, spec["shared"]),
            (sine, spec["shared"]),
        ],
        [
            (shaped((size, q.shape[1]), low), spec["pair_alone"]),
            (shaped((size, k.shape[1]), low), spec["one_alone"]),
            (shaped((size, v.shape[1]), low), spec["one_alone"]),
        ],
        [
            pltpu.VMEM((size, size), wide),
            pltpu.VMEM((size, LANES), wide),
            pltpu.VMEM((size, LANES), wide),
        ],
        after,
        us=21,
    )


def out_weight_kernel(place_ref, *refs):
    pieces, weight, sems = refs[:5], refs[5], refs[6]
    fetch(place_ref, pieces, FIRST_OUT_PLAN, FIRST_HALF, (weight,), sems)
    zeros = jnp.zeros((LANES - HD, weight.shape[1]), low)
    for block in range(BLOCKS):
        weight[pl.ds(block * LANES + HD, LANES - HD), :] = zeros
    drain((weight.at[pl.ds(0, BLOCKS * HD)],), sems)


def out_weight(place, pieces, width, after):
    out = shaped((H * LANES, width // 2), low)
    return run(
        out_weight_kernel,
        "out_weight",
        place,
        (1,),
        [(piece, anywhere) for piece in pieces],
        [(out, whole(out))],
        [pltpu.SemaphoreType.DMA((1,))],
        after,
    )[0]


def middle_kernel(
    place_ref, x_ref, mine_ref, other_ref, w_mine, w_other, gain_ref, middle_ref, out_ref, heads
):
    core = place_ref[3]
    span = mine_ref.shape[1]
    heads[:, pl.ds(pl.multiple_of(core * span, LANES), span)] = mine_ref[...]
    heads[:, pl.ds(pl.multiple_of((1 - core) * span, LANES), span)] = other_ref[...]
    columns = w_mine.shape[1]
    for owner, weight in ((core, w_mine), (1 - core, w_other)):
        at = pl.ds(pl.multiple_of(owner * columns, LANES), columns)
        middle_ref[:, at] = x_ref[:, at].astype(wide) + project(heads[...], weight[...])
    hidden = middle_ref[...]
    scale = lax.rsqrt(jnp.mean(hidden * hidden, axis=-1, keepdims=True) + epsilon)
    out_ref[...] = (hidden * scale * gain_ref[8:9, :]).astype(low)


def middle_of(place, x, mine, other, w_mine, w_other, gains, after=()):
    count, width = x.shape
    tile, span = count // 2, mine.shape[1]
    return run(
        middle_kernel,
        "middle",
        place,
        (2,),
        [
            (x, rows_of(tile, width)),
            (mine, rows_of(tile, span)),
            (other, rows_of(tile, span)),
            (w_mine, whole(w_mine)),
            (w_other, whole(w_other)),
            (gains, whole(gains)),
        ],
        [
            (shaped((count, width), wide), rows_of(tile, width)),
            (shaped((count, width), low), rows_of(tile, width)),
        ],
        [pltpu.VMEM((tile, 2 * span), low)],
        after,
        us=11,
    )


def middle_back_kernel(
    place_ref,
    middle_ref,
    mine_0,
    mine_1,
    other_0,
    other_1,
    cotangent_ref,
    gain_ref,
    w_mine,
    w_other,
    grad_ref,
    branch_mine,
    branch_other,
    heads_mine,
    heads_other,
    gain_grad,
    branch,
    heads,
):
    core = place_ref[3]
    hidden = middle_ref[...]
    scale = lax.rsqrt(jnp.mean(hidden * hidden, axis=-1, keepdims=True) + epsilon)
    incoming = mine_0[...] + mine_1[...] + other_0[...].astype(wide) + other_1[...].astype(wide)
    weighted = incoming * gain_ref[8:9, :]
    inner = jnp.mean(weighted * hidden, axis=-1, keepdims=True)
    grad = cotangent_ref[...].astype(wide) + (scale * weighted - hidden * scale**3 * inner)
    grad_ref[...] = grad
    branch[...] = grad.astype(low)

    @pl.when(pl.program_id(0) == 0)
    def _():
        gain_grad[...] = jnp.zeros_like(gain_grad)

    summed = jnp.sum(incoming * hidden * scale, axis=0, keepdims=True)
    gain_grad[...] += jnp.broadcast_to(summed, gain_grad.shape)
    columns, span = w_mine.shape[1], heads_mine.shape[1]

    def part(ref, owner, size):
        return ref[:, pl.ds(pl.multiple_of(owner * size, LANES), size)]

    branch_mine[...] = part(branch, core, columns)
    branch_other[...] = part(branch, 1 - core, columns)
    for at in range(0, 2 * span, SLAB):
        heads[:, at : at + SLAB] = (
            across(branch_mine[...], w_mine[at : at + SLAB, :])
            + across(branch_other[...], w_other[at : at + SLAB, :])
        ).astype(low)
    heads_mine[...] = part(heads, core, span)
    heads_other[...] = part(heads, 1 - core, span)


def middle_back(place, middle, parts, cotangent, gains, w_mine, w_other, after=()):
    count, width = middle.shape
    tile, columns, span = count // 2, w_mine.shape[1], w_mine.shape[0] // 2
    gain_grad = shaped((8, width), wide)
    return run(
        middle_back_kernel,
        "middle_back",
        place,
        (2,),
        [
            *[(item, rows_of(tile, width)) for item in (middle, *parts, cotangent)],
            (gains, whole(gains)),
            (w_mine, whole(w_mine)),
            (w_other, whole(w_other)),
        ],
        [
            (shaped((count, width), wide), rows_of(tile, width)),
            (shaped((count, columns), low), rows_of(tile, columns)),
            (shaped((count, columns), low), rows_of(tile, columns)),
            (shaped((count, span), low), rows_of(tile, span)),
            (shaped((count, span), low), rows_of(tile, span)),
            (gain_grad, whole(gain_grad)),
        ],
        [pltpu.VMEM((tile, width), low), pltpu.VMEM((tile, 2 * span), low)],
        after,
        us=15,
    )


def out_grad_kernel(
    place_ref,
    own_mine,
    own_other,
    far_mine,
    far_other,
    branch_own,
    branch_far,
    *refs,
):
    outs, (grad, sems) = refs[:5], refs[5:]
    core = place_ref[3]
    span = own_mine.shape[1]
    for owner, own, far in ((core, own_mine, far_mine), (1 - core, own_other, far_other)):
        for at in range(0, span, SLAB):
            part = down(own[:, at : at + SLAB], branch_own[...])
            part = part + down(far[:, at : at + SLAB], branch_far[...])
            grad[pl.ds(pl.multiple_of(owner * span + at, LANES), SLAB), :] = part.astype(low)
    for k in range(4):
        base = (place_ref[0] ^ k) * 4
        send_off(place_ref, k, (grad,), base, OUT_PLAN, OUT_HALF, outs, sems)
    fill_spare(grad.at[pl.ds(0, 16), pl.ds(0, SLAB)], 144, 16, OUT_HALF, outs, sems)
    drain(outs, sems)


def out_grad(place, own_mine, own_other, far_mine, far_other, branch_own, branch_far, after=()):
    columns = branch_own.shape[1]
    operands = (own_mine, own_other, far_mine, far_other, branch_own, branch_far)
    return run(
        out_grad_kernel,
        "out_grad",
        place,
        (1,),
        [(item, whole(item)) for item in operands],
        sent_shapes(OUT_HALF, SLAB),
        [pltpu.VMEM((H * LANES, columns), low), pltpu.SemaphoreType.DMA((5,))],
        after,
        us=10,
    )


FFN_TILE = 320
FFN_STEP = 256
FFN_SPAN = 768


def load_tokens(x_ref, c_ref, x_own, x_far, c_own, c_far, sems):
    count = x_far.shape[0]
    for index, (ref, far, own) in enumerate(((x_ref, x_far, x_own), (c_ref, c_far, c_own))):
        for part, source in enumerate((far, own)):
            target = ref.at[pl.ds(part * count, count)]
            pltpu.make_async_copy(source, target, sems.at[index]).start()


def ffn_forward(step, tiles, x_ref, c_ref, weights, sums, middles, at_rows):
    gate_w, up_w, down_w = weights
    inner, grad_gate, grad_up = middles
    units, width = gate_w.shape[1], gate_w.shape[0]
    rows = pl.ds(pl.multiple_of(step * FFN_TILE, FFN_TILE), FFN_TILE)

    @pl.loop(0, units // FFN_STEP)
    def _(index):
        at = pl.ds(pl.multiple_of(index * FFN_STEP, FFN_STEP), FFN_STEP)
        gate = project(x_ref[rows, :], gate_w[:, at])
        upward = project(x_ref[rows, :], up_w[:, at])
        grad_inner = across(c_ref[rows, :], down_w[at, :])
        sigma = 1.0 / (1.0 + jnp.exp(-gate))
        silu = gate * sigma
        inner[at_rows, at] = (silu * upward).astype(low)
        grad_up[at_rows, at] = (grad_inner * silu).astype(low)
        grad_gate[at_rows, at] = (
            grad_inner * upward * sigma * (1.0 + gate * (1.0 - sigma))
        ).astype(low)

    for part in range(2):

        @pl.when((step >= part * tiles // 2) & (step < (part + 1) * tiles // 2))
        def _():
            out_ref, normed_ref = sums[2 * part : 2 * part + 2]

            @pl.loop(0, width // SLAB)
            def _(index):
                at = pl.ds(pl.multiple_of(index * SLAB, SLAB), SLAB)
                out = project(inner[at_rows, :], down_w[:, at])
                normed = across(grad_gate[at_rows, :], gate_w[at, :])
                normed = normed + across(grad_up[at_rows, :], up_w[at, :])
                out_ref[:, at] = out.astype(out_ref.dtype)
                normed_ref[:, at] = normed.astype(normed_ref.dtype)


def ffn_backward(place_ref, k, x_ref, c_ref, middles, stages, turned, turned_units, sent, sems):
    inner, grad_gate, grad_up = middles
    stage_gate, stage_up, stage_down = stages
    width, units = x_ref.shape[1], inner.shape[1]
    depth = place_ref[0] ^ k
    rows, span = width // 4, units // 4
    here = pl.ds(pl.multiple_of(depth * rows, LANES), rows)
    there = pl.ds(pl.multiple_of(depth * span, LANES), span)
    turned[...] = x_ref[:, here].T
    to = pl.ds(pl.multiple_of(k * rows, 16), rows)
    to_units = pl.ds(pl.multiple_of(k * span, 16), span)
    stage_gate[to, :] = project(turned[...], grad_gate[...]).astype(low)
    stage_up[to, :] = project(turned[...], grad_up[...]).astype(low)
    turned_units[...] = inner[:, there].T

    @pl.loop(0, width // FFN_SPAN)
    def _(index):
        at = pl.ds(pl.multiple_of(index * FFN_SPAN, FFN_SPAN), FFN_SPAN)
        stage_down[to_units, at] = project(turned_units[...], c_ref[:, at]).astype(low)

    send_off(place_ref, k, stages, k * 4, FFN_PLAN, FFN_HALF, sent, sems)


def ffn_kernel(tiles, place_ref, *refs):
    tokens, pieces, sums, sent = refs[:4], refs[4:9], refs[9:13], refs[13:18]
    x_ref, c_ref, *rest = refs[18:]
    weights, middles, stages, rest = rest[:3], rest[3:6], rest[6:9], rest[9:]
    turned, turned_units, x_sems, in_sems, out_sems = rest
    step = pl.program_id(0)

    @pl.when(step == 0)
    def _():
        load_tokens(x_ref, c_ref, *tokens, x_sems)
        fetch(place_ref, pieces, FFN_PLAN, FFN_HALF, weights, in_sems)
        drain((x_ref, c_ref), x_sems)
        drain(weights, in_sems)

    @pl.when(step < tiles)
    def _():
        rows = pl.ds(pl.multiple_of(step * FFN_TILE, FFN_TILE), FFN_TILE)
        ffn_forward(step, tiles, x_ref, c_ref, weights, sums, middles, rows)

    @pl.when(step >= tiles)
    def _():
        k = step - tiles
        ffn_backward(
            place_ref, k, x_ref, c_ref, middles, stages, turned, turned_units, sent, out_sems
        )

    @pl.when(step == tiles + 3)
    def _():
        drain(sent, out_sems)


def ffn_forward_kernel(tiles, place_ref, *refs):
    tokens, pieces, sums, middles = refs[:4], refs[4:9], refs[9:13], refs[13:16]
    x_ref, c_ref, *weights, x_sems, in_sems = refs[16:]
    step = pl.program_id(0)

    @pl.when(step == 0)
    def _():
        load_tokens(x_ref, c_ref, *tokens, x_sems)
        fetch(place_ref, pieces, FFN_PLAN, FFN_HALF, weights, in_sems)
        drain((x_ref, c_ref), x_sems)
        drain(weights, in_sems)

    ffn_forward(step, tiles, x_ref, c_ref, weights, sums, middles, slice(None))


def ffn_backward_kernel(place_ref, *refs):
    tokens, sources, sent = refs[:4], refs[4:7], refs[7:12]
    x_ref, c_ref, *rest = refs[12:]
    middles, stages, rest = rest[:3], rest[3:6], rest[6:]
    turned, turned_units, x_sems, in_sems, out_sems = rest
    k = pl.program_id(0)

    @pl.when(k == 0)
    def _():
        load_tokens(x_ref, c_ref, *tokens, x_sems)
        for index in (1, 2, 0):
            pltpu.make_async_copy(sources[index], middles[index], in_sems.at[index]).start()
        drain((x_ref, c_ref), x_sems)
        drain(middles, in_sems)

    ffn_backward(
        place_ref, k, x_ref, c_ref, middles, stages, turned, turned_units, sent, out_sems
    )

    @pl.when(k == 3)
    def _():
        drain(sent, out_sems)


FFN_UNITS = 1024


def ffn_sums(count, width):
    last = count // FFN_TILE - 1
    early = pl.BlockSpec((FFN_TILE, width), lambda i, place: (jnp.minimum(i, last), 0))
    late = pl.BlockSpec(
        (FFN_TILE, width), lambda i, place: (jnp.clip(i - last - 1, 0, last), 0)
    )
    pairs = ((low, early), (low, early), (wide, late), (wide, late))
    return [(shaped((count, width), kind), spec) for kind, spec in pairs]


def ffn_scratch(count, width, weights=True, middles=True, stages=True):
    weight = [pltpu.VMEM((width, FFN_UNITS), low)] * 2 + [pltpu.VMEM((FFN_UNITS, width), low)]
    shapes = [pltpu.VMEM((count, width), low)] * 2
    shapes += weight if weights else []
    shapes += [pltpu.VMEM((count, FFN_UNITS), low)] * 3 if middles else []
    if stages:
        shapes += weight
        shapes += [pltpu.VMEM((width // 4, count), low)]
        shapes += [pltpu.VMEM((FFN_UNITS // 4, count), low)]
    shapes += [pltpu.SemaphoreType.DMA((2,)), pltpu.SemaphoreType.DMA((3,))]
    return shapes + ([pltpu.SemaphoreType.DMA((5,))] if stages else [])


def ffn_chunk(place, tokens, pieces, after=()):
    count, width = tokens[0].shape
    tiles = 2 * count // FFN_TILE
    results = run(
        functools.partial(ffn_kernel, tiles),
        "ffn",
        place,
        (tiles + 4,),
        [(item, anywhere) for item in (*tokens, *pieces)],
        ffn_sums(count, width) + sent_shapes(FFN_HALF, SLAB),
        ffn_scratch(2 * count, width),
        after,
        us=60,
    )
    return results[:4], results[4:]


def ffn_chunk_forward(place, tokens, pieces, after=()):
    count, width = tokens[0].shape
    tiles = 2 * count // FFN_TILE
    middle = pl.BlockSpec((FFN_TILE, FFN_UNITS), lambda i, place: (i, 0))
    results = run(
        functools.partial(ffn_forward_kernel, tiles),
        "ffn_forward",
        place,
        (tiles,),
        [(item, anywhere) for item in (*tokens, *pieces)],
        ffn_sums(count, width) + [(shaped((2 * count, FFN_UNITS), low), middle)] * 3,
        ffn_scratch(2 * count, width, middles=False, stages=False),
        after,
        us=36,
    )
    return results[:4], results[4:]


def ffn_chunk_backward(place, tokens, middles, after=()):
    count, width = tokens[0].shape
    return run(
        ffn_backward_kernel,
        "ffn_backward",
        place,
        (4,),
        [(item, anywhere) for item in (*tokens, *middles)],
        sent_shapes(FFN_HALF, SLAB),
        ffn_scratch(2 * count, width, weights=False),
        after,
        us=22,
    )


def input_back_kernel(
    tiles, place_ref, own_q, own_k, own_v, far_q, far_k, far_v, x_own, x_far, w_ref, *refs
):
    grad_ref, own_ref, far_ref, gain_grad = refs
    step = pl.program_id(0)

    @pl.when(step == 0)
    def _():
        gain_grad[...] = jnp.zeros_like(gain_grad)

    def squeezed(query, key, value):
        parts = []
        for ref in (query, key):
            for at in range(0, ref.shape[1], LANES):
                head = ref[:, at : at + LANES].astype(wide)
                parts.append(head[:, :HALF])
                parts.append(head[:, LANES // 2 : LANES // 2 + HALF])
        for at in range(0, value.shape[1], LANES):
            parts.append(value[:, at : at + LANES].astype(wide)[:, :HD])
        return jnp.concatenate(parts, axis=1).astype(low)

    def rest(x_ref, incoming):
        hidden = x_ref[...].astype(wide)
        scale = lax.rsqrt(jnp.mean(hidden * hidden, axis=-1, keepdims=True) + epsilon)
        summed = jnp.sum(incoming * hidden * scale, axis=0, keepdims=True)
        gain_grad[...] += jnp.broadcast_to(summed, gain_grad.shape)

    @pl.when(step < tiles)
    def _():
        grad_ref[...] = squeezed(far_q, far_k, far_v)
        incoming = across(grad_ref[...], w_ref[...])
        far_ref[...] = incoming.astype(low)
        rest(x_far, incoming)

    @pl.when(step >= tiles)
    def _():
        grad_ref[...] = squeezed(own_q, own_k, own_v)
        incoming = across(grad_ref[...], w_ref[...])
        own_ref[...] = incoming
        rest(x_own, incoming)


def input_back(place, own, far, x_own, x_far, weight, after=()):
    count, width = 2 * x_own.shape[0], x_own.shape[1]
    tile = 320
    tiles = count // 2 // tile
    gain_grad = shaped((8, width), wide)

    def late(columns):
        return pl.BlockSpec((tile, columns), lambda i, place: (jnp.maximum(i - tiles, 0), 0))

    def early(columns):
        return pl.BlockSpec((tile, columns), lambda i, place: (jnp.minimum(i, tiles - 1), 0))

    def both(columns):
        return pl.BlockSpec((tile, columns), lambda i, place: (lax.rem(i + tiles, 2 * tiles), 0))

    return run(
        functools.partial(input_back_kernel, tiles),
        "input_back",
        place,
        (2 * tiles,),
        [(item, late(item.shape[1])) for item in own]
        + [(item, early(item.shape[1])) for item in far]
        + [(x_own, late(width)), (x_far, early(width)), (weight, whole(weight))],
        [
            (shaped((count, width), low), both(width)),
            (shaped((count // 2, width), wide), late(width)),
            (shaped((count // 2, width), low), early(width)),
            (gain_grad, whole(gain_grad)),
        ],
        after=after,
        us=15,
    )


def qkv_grad_kernel(place_ref, x_ref, grad_ref, gain_one, gain_two, *refs):
    outs, (stage, gain_rows, turned, sems) = refs[:5], refs[5:]
    k = pl.program_id(0)
    width = grad_ref.shape[1]

    @pl.when(k == 0)
    def _():
        gap = jnp.zeros((8, LANES - HD), wide)
        row = lax.broadcasted_iota(jnp.int32, (16, LANES), 0)
        gain_rows[...] = jnp.zeros_like(gain_rows)
        for block in range(BLOCKS):
            for index, gain in enumerate((gain_one, gain_two)):
                part = jnp.concatenate([gain[:, block * HD : (block + 1) * HD], gap], axis=1)
                part = jnp.where(row == 0, jnp.concatenate([part, part], axis=0), 0.0)
                gain_rows[
                    16 * block : 16 * block + 16, index * LANES : (index + 1) * LANES
                ] = part.astype(low)

    depth = place_ref[0] ^ k
    rows = width // 4
    turned[...] = x_ref[:, pl.ds(pl.multiple_of(depth * rows, LANES), rows)].T
    to = pl.ds(pl.multiple_of(depth * rows, 16), rows)

    @pl.loop(0, width // SLAB)
    def _(index):
        at = pl.ds(pl.multiple_of(index * SLAB, SLAB), SLAB)
        stage[to, at] = project(turned[...], grad_ref[:, at]).astype(low)

    send_off(place_ref, k, (stage, gain_rows), depth * 4, QKV_PLAN, QKV_HALF, outs, sems)

    @pl.when(k == 3)
    def _():
        fill_spare(gain_rows.at[pl.ds(0, 16)], GAINS + 16, 16, QKV_HALF, outs, sems)
        drain(outs, sems)


def qkv_grad(place, x, grad, gain_one, gain_two, after=()):
    count, width = x.shape
    operands = (x, grad, gain_one, gain_two)
    return run(
        qkv_grad_kernel,
        "qkv_grad",
        place,
        (4,),
        [(item, whole(item)) for item in operands],
        sent_shapes(QKV_HALF, SLAB),
        [
            pltpu.VMEM((width, width), low),
            pltpu.VMEM((BLOCKS * 16, SLAB), low),
            pltpu.VMEM((width // 4, count), low),
            pltpu.SemaphoreType.DMA((5,)),
        ],
        after,
        us=15,
    )


def tokens_grad_kernel(place_ref, x_ref, middle_ref, mine_ref, other_ref, gain_ref, out_ref):
    hidden = x_ref[...].astype(wide)
    scale = lax.rsqrt(jnp.mean(hidden * hidden, axis=-1, keepdims=True) + epsilon)
    weighted = (mine_ref[...] + other_ref[...].astype(wide)) * gain_ref[0:1, :]
    inner = jnp.mean(weighted * hidden, axis=-1, keepdims=True)
    out_ref[...] = middle_ref[...] + (scale * weighted - hidden * scale**3 * inner)


def tokens_grad(place, x, grad_middle, mine, other, gains, after=()):
    count, width = x.shape
    tile = 128
    return run(
        tokens_grad_kernel,
        "tokens_grad",
        place,
        (count // tile,),
        [(item, rows_of(tile, width)) for item in (x, grad_middle, mine, other)]
        + [(gains, whole(gains))],
        [(shaped((count, width), wide), rows_of(tile, width))],
        after=after,
    )[0]


def output_kernel(place_ref, middle_ref, mine_0, mine_1, other_0, other_1, out_ref):
    total = middle_ref[...] + mine_0[...] + mine_1[...]
    total = total + other_0[...].astype(wide) + other_1[...].astype(wide)
    out_ref[...] = total.astype(low)


def output_of(place, middle, parts, after=()):
    count, width = middle.shape
    tile = 128
    return run(
        output_kernel,
        "output",
        place,
        (count // tile,),
        [(item, rows_of(tile, width)) for item in (middle, *parts)],
        [(shaped((count, width), low), rows_of(tile, width))],
        after=after,
    )[0]


def swap(array):
    return lax.ppermute(array, "rep", [(0, 1), (1, 0)])


def hop(array, z_flip, y_flip, x_flip):
    flip = (z_flip * 2 + y_flip) * 2 + x_flip
    return lax.ppermute(array, "fsdp", [(chip, chip ^ flip) for chip in range(BLOCKS)])


def hop_x(array):
    return hop(array, 0, 0, 1)


def hop_y(array):
    return hop(array, 0, 1, 0)


def near(line):
    return hop_x(line), hop_y(line)


def pieces_of(blocks):
    cut = blocks.reshape(4, 2, 2, *blocks.shape[1:])
    half = blocks.shape[1] // 2
    far = cut[:, 1, 1]
    return cut[:, 0, 0], cut[:, 0, 1], cut[:, 1, 0], far[:, :half], far[:, half:]


def blocks_of(sent):
    to_x, to_y, late_x, late_y, own = sent
    near_x = jnp.stack([to_x[1], late_x], axis=1)
    near_y = jnp.stack([late_y, to_y[1]], axis=1)
    far = jnp.stack([to_x[0], to_y[0]], axis=1)
    cut = jnp.stack([jnp.stack([own, near_x], 1), jnp.stack([near_y, far], 1)], 1)
    return cut.reshape(BLOCKS, 2 * own.shape[2], own.shape[3])


def layout(length_row, count):
    ends = jnp.cumsum(length_row)
    slots = jnp.arange(count, dtype=jnp.int32)
    passed = (slots[:, None] >= ends[None, :]).astype(jnp.int32)
    segment = jnp.sum(passed, axis=1)
    position = slots - jnp.sum(passed * length_row[None, :], axis=1)
    return position, segment


class Direct:
    def __init__(self, place, weights):
        self.place = place
        self.weights = weights

    def pack_first(self):
        return pack_first(self.place, *self.weights[:4], *self.weights[7:])

    def pack_ffn(self, chunk, after):
        return pack_ffn(self.place, chunk, *self.weights[4:7], after)

    def step_1(self, shard, after=()):
        return pair_up(self.place, shard, hop(shard, 2, 0, 0), after)

    def step_2(self, pair, after=()):
        return line_up(self.place, pair, hop(pair, 1, 0, 0), after)

    def step_3(self, line):
        return near(line)

    def step_4(self, line, sides, after=()):
        upper, lower = halves(self.place, *sides, after)
        return line, *sides, hop_y(upper), hop_x(lower)

    def scatter_1(self, sent):
        return hop_x(sent[0]), hop_y(sent[1])

    def scatter_2(self, sent, got, after):
        late_x, late_y = merge(self.place, sent[2], sent[3], got[0], got[1], after)
        return late_x, (hop_x(late_x), hop_y(late_y))

    def scatter_3(self, groups, after):
        groups = [(sent[4], *got, *more) for sent, got, more in groups]
        kept, kept_far, part = sum_plane(self.place, groups, after)
        return kept, (kept_far, hop(part, 1, 0, 0))

    def scatter_4(self, kept, parts, after):
        kept_far, near = parts
        token = sum_pass(self.place, kept_far, near, after)
        return token, (near, hop(token, 2, 0, 0))

    def scatter_5(self, kept, parts, after):
        total, total_low = sum_line(self.place, kept, parts[0], parts[1], after)
        return total, swap(total_low)

    def finish_ffn(self, mine, other, shapes, after):
        return unpack_ffn(self.place, mine, other, shapes, after)

    def finish_first(self, mine, other, shapes, owned):
        grads = unpack_first(self.place, mine, other, shapes)
        row = GAINS + OUT_HALF
        both = mine[row, : 2 * LANES] + other[row, : 2 * LANES].astype(wide)
        return grads, (both[:owned], both[LANES : LANES + owned])


def on_device(
    direct,
    tokens,
    lengths,
    attn_gain,
    w_query,
    w_key,
    w_value,
    w_out,
    ffn_gain,
    w_gate,
    w_up,
    w_down,
    cotangent,
):
    count, width = tokens.shape
    owned = attn_gain.shape[0]
    core = lax.axis_index("rep")
    if direct:
        index = lax.axis_index("fsdp")
        spot = (index // 4, (index // 2) % 2, index % 2)
    else:
        spot = (0, 0, 0)
    place = jnp.stack([jnp.int32(item) for item in (*spot, core)])
    weights = (w_query, w_key, w_value, w_out, w_gate, w_up, w_down, attn_gain, ffn_gain)
    routes = Direct(place, weights) if direct else Whole(place, weights)

    first = routes.pack_first()
    far_tokens, far_cotangent = swap(tokens), swap(cotangent)
    laid = [layout(row, count) for row in (lengths[0], swap(lengths)[0])]
    segment = jnp.stack([item[1] for item in laid])
    cosine, sine = turn_table(jnp.concatenate([item[0] for item in laid]))

    pair_first = routes.step_1(first)
    line_first = routes.step_2(pair_first, (far_tokens, far_cotangent, segment, cosine, sine))
    sides_first = routes.step_3(line_first)
    chunk_0 = routes.pack_ffn(0, (line_first,))
    pair_0 = routes.step_1(chunk_0)
    pieces_first = routes.step_4(line_first, sides_first)
    line_0 = routes.step_2(pair_0, (pair_0, *sides_first))
    sides_0 = routes.step_3(line_0)
    w_mine = out_weight(place, pieces_first, tokens.shape[1], (line_0,))
    w_other = swap(w_mine)
    normed_low, queries, keys, values, w_qkv, gains = project_qkv(
        place, tokens, far_tokens, cosine, sine, pieces_first, (w_mine,)
    )
    chunk_1 = routes.pack_ffn(1, (keys,))
    far_mine, far_total = attend(place, queries, keys, values, segment, 1, (chunk_1,))
    own_other = swap(far_mine)
    pair_1 = routes.step_1(chunk_1, (far_mine,))
    pieces_0 = routes.step_4(line_0, sides_0)
    own_mine, own_total = attend(
        place, queries, keys, values, segment, 0, (pair_1, *sides_0)
    )
    far_other = swap(own_mine)
    middle, normed_own = middle_of(
        place, tokens, own_mine, own_other, w_mine, w_other, gains
    )
    normed_far = swap(normed_own)
    line_1 = routes.step_2(pair_1, (normed_own, *pieces_0[3:]))
    sides_1 = routes.step_3(line_1)

    inputs = (normed_own, normed_far, cotangent, far_cotangent)
    sums_0, middles_0 = ffn_chunk_forward(place, inputs, pieces_0, (line_1, far_other))
    out_far_0, norm_far_0 = swap(sums_0[0]), swap(sums_0[1])
    pieces_1 = routes.step_4(line_1, sides_1, (sums_0[0],))
    sent_0 = ffn_chunk_backward(place, inputs, middles_0, (pieces_1[0],))
    got_0 = routes.scatter_1(sent_0)
    sums_1, sent_1 = ffn_chunk(place, inputs, pieces_1)
    out_far_1, norm_far_1 = swap(sums_1[0]), swap(sums_1[1])
    got_1 = routes.scatter_1(sent_1)

    norms = (sums_0[3], sums_1[3], norm_far_0, norm_far_1)
    grad_middle, branch_mine, branch_sent, heads_mine, heads_sent, ffn_gain_grad = middle_back(
        place, middle, norms, cotangent, gains, w_mine, w_other, got_0
    )
    branch_far, heads_far = swap(branch_sent), swap(heads_sent)
    own_grads = attend_back(
        place, queries, keys, values, heads_mine, own_total, segment, cosine, sine, 0
    )
    token, more_0 = routes.scatter_2(sent_0, got_0, (own_grads[0],))
    far_grads = attend_back(
        place,
        queries,
        keys,
        values,
        heads_far,
        far_total,
        segment,
        cosine,
        sine,
        1,
        (token,),
    )
    token, more_1 = routes.scatter_2(sent_1, got_1, (far_grads[0],))
    sent_out = out_grad(
        place,
        own_mine,
        own_other,
        far_mine,
        far_other,
        branch_mine,
        branch_far,
        (token,),
    )
    got_out = routes.scatter_1(sent_out)
    kept_0, parts_0 = routes.scatter_3([(sent_0, got_0, more_0)], (sent_out[4],))
    grad_qkv, own_part, far_part, attn_gain_grad = input_back(
        place, own_grads, far_grads, tokens, far_tokens, w_qkv, (kept_0,)
    )
    own_rest = swap(far_part)
    sent_qkv = qkv_grad(place, normed_low, grad_qkv, attn_gain_grad, ffn_gain_grad)
    got_qkv = routes.scatter_1(sent_qkv)

    token, more_out = routes.scatter_2(sent_out, got_out, (sent_qkv[4],))
    token, parts_0 = routes.scatter_4(kept_0, parts_0, (token,))
    kept_1, parts_1 = routes.scatter_3([(sent_1, got_1, more_1)], (token,))
    token, more_qkv = routes.scatter_2(sent_qkv, got_qkv, (kept_1,))
    owned_0, other_0 = routes.scatter_5(kept_0, parts_0, (token,))
    token, parts_1 = routes.scatter_4(kept_1, parts_1, (owned_0,))
    groups = [(sent_qkv, got_qkv, more_qkv), (sent_out, got_out, more_out)]
    kept_qkv, parts_qkv = routes.scatter_3(groups, (token,))
    outs = (sums_0[2], sums_1[2], out_far_0, out_far_1)
    output = output_of(place, middle, outs, (kept_qkv,))
    owned_1, other_1 = routes.scatter_5(kept_1, parts_1, (output,))
    token, parts_qkv = routes.scatter_4(kept_qkv, parts_qkv, (owned_1,))
    grad_tokens = tokens_grad(place, tokens, grad_middle, own_part, own_rest, gains, (token,))
    shapes = [w_gate.shape, w_up.shape, w_down.shape]
    grad_gate, grad_up, grad_down = routes.finish_ffn(
        (owned_0, owned_1), (other_0, other_1), shapes, (grad_tokens,)
    )
    owned_qkv, other_qkv = routes.scatter_5(kept_qkv, parts_qkv, (grad_gate,))
    shapes = [w_query.shape, w_key.shape, w_value.shape, w_out.shape]
    grads, gain_grads = routes.finish_first(owned_qkv, other_qkv, shapes, owned)
    return (
        output,
        grad_tokens,
        gain_grads[0],
        *grads,
        gain_grads[1],
        grad_gate,
        grad_up,
        grad_down,
    )


class Whole:
    def __init__(self, place, weights):
        self.place = place
        query, key, value, out, gate, up, down_w, gain_one, gain_two = weights
        core = place[3]
        self.core = core
        count = query.shape[1] // query.shape[0]
        self.count = count
        rows = query.shape[1] // BLOCKS

        def full(shard):
            return lax.all_gather(shard, "fsdp", axis=0, tiled=True)

        def mine(weight):
            columns = weight.shape[1] // 2
            return lax.dynamic_slice_in_dim(weight, core * columns, columns, axis=1)

        def slabs(weight):
            blocks = weight.reshape(BLOCKS, -1, weight.shape[1])
            return [blocks[:, :, at : at + SLAB] for at in range(0, weight.shape[1], SLAB)]

        qkv = full(jnp.concatenate([mine(query), mine(key), mine(value)], axis=1))
        gain_rows = jnp.zeros((BLOCKS, 16, SLAB), low)
        for index, gain in enumerate((gain_one, gain_two)):
            part = full(gain).reshape(BLOCKS, rows)
            gain_rows = gain_rows.at[:, 0, index * LANES : index * LANES + rows].set(part)
        square = full(mine(out)).reshape(BLOCKS, rows, -1)
        rest = square[:, :, SLAB:]
        rest = jnp.concatenate([rest[:, : rows // 2], rest[:, rows // 2 :]], axis=2)
        parts = slabs(qkv) + [gain_rows, square[:, :, :SLAB], rest]
        self.first = pieces_of(jnp.concatenate(parts, axis=1))
        quarter = down_w.shape[0] // (2 * CHUNKS)
        self.quarter = quarter

        def units(weight, chunk):
            split = weight.reshape(weight.shape[0], count, 2 * CHUNKS, quarter)
            part = lax.dynamic_index_in_dim(split, CHUNKS * core + chunk, 2, keepdims=False)
            return full(part.reshape(weight.shape[0], count * quarter))

        chunks = []
        for chunk in range(CHUNKS):
            at = (CHUNKS * core + chunk) * quarter
            part = full(lax.dynamic_slice_in_dim(down_w, at, quarter, axis=0))
            parts = slabs(units(gate, chunk)) + slabs(units(up, chunk)) + slabs(part)
            chunks.append(pieces_of(jnp.concatenate(parts, axis=1)))
        self.ffn_0, self.ffn_1 = chunks

    def pack_first(self):
        return self.first

    def pack_ffn(self, chunk, after):
        return (self.ffn_0, self.ffn_1)[chunk]

    def step_1(self, shard, after=()):
        return shard

    def step_2(self, pair, after=()):
        return pair

    def step_3(self, line):
        return ()

    def step_4(self, line, sides, after=()):
        return line

    def scatter_1(self, sent):
        return blocks_of(sent)

    def scatter_2(self, sent, got, after):
        return got, got

    def scatter_3(self, groups, after):
        blocks = jnp.concatenate([got for _, got, _ in groups], axis=1)
        return blocks, blocks

    def scatter_4(self, kept, parts, after):
        return kept, kept

    def scatter_5(self, kept, parts, after):
        return kept, kept

    def split(self, blocks, widths):
        parts, row = [], 0
        for rows, slabs in widths:
            taken = []
            for _ in range(slabs):
                taken.append(blocks[:, row : row + rows])
                row += rows
            part = jnp.concatenate(taken, axis=2)
            part = part.reshape(BLOCKS * rows, part.shape[2])
            parts.append(lax.psum_scatter(part, "fsdp", scatter_dimension=0, tiled=True))
        return parts

    def ordered(self, part):
        other = swap(part).astype(wide)
        part = part.astype(wide)
        first = jnp.where(self.core == 0, part, other)
        return first, jnp.where(self.core == 0, other, part)

    def finish_ffn(self, mine, other, shapes, after):
        gates, ups, downs = [], [], []
        for blocks in mine:
            gate, up, down_w = self.split(blocks, ((96, 2), (96, 2), (64, 3)))
            gates.append(self.ordered(gate))
            ups.append(self.ordered(up))
            downs.append(self.ordered(down_w))

        def columns(pairs):
            parts = [pairs[chunk][owner] for owner in range(2) for chunk in range(CHUNKS)]
            rows = parts[0].shape[0]
            parts = [part.reshape(rows, self.count, self.quarter) for part in parts]
            return jnp.stack(parts, axis=2).reshape(rows, -1)

        grad_down = [downs[chunk][owner] for owner in range(2) for chunk in range(CHUNKS)]
        return columns(gates), columns(ups), jnp.concatenate(grad_down, axis=0)

    def finish_first(self, mine, other, shapes, owned):
        (qkv,) = self.split(mine[:, :GAINS], ((96, 3),))
        blocks = mine[:, 2 * QKV_HALF :]
        rest = blocks[:, 96:144]
        rest = jnp.concatenate([rest[:, :, :256], rest[:, :, 256:]], axis=1)
        (square,) = self.split(jnp.concatenate([blocks[:, :96], rest], axis=2), ((96, 1),))
        pair = self.ordered(qkv)
        grads, at = [], 0
        for shape in shapes[:3]:
            columns = shape[1] // 2
            grads.append(jnp.concatenate([item[:, at : at + columns] for item in pair], axis=1))
            at += columns
        grads.append(jnp.concatenate(self.ordered(square), axis=1))
        rows = mine[:, GAINS, : 2 * LANES].astype(wide)
        rows = rows + swap(rows)
        gains = []
        for index in range(2):
            gain = rows[:, index * LANES : index * LANES + 96].reshape(-1)
            gains.append(lax.psum_scatter(gain, "fsdp", scatter_dimension=0, tiled=True))
        return grads, gains


def solution(mesh):
    rows = P(("rep", "fsdp"), None)
    split = P("fsdp", None)
    gain = P("fsdp")
    return jax.shard_map(
        functools.partial(on_device, mesh.shape["fsdp"] == BLOCKS),
        mesh=mesh,
        in_specs=(rows, rows, gain) + (split,) * 4 + (gain,) + (split,) * 3 + (rows,),
        out_specs=(rows, rows, gain) + (split,) * 4 + (gain,) + (split,) * 3,
        check_vma=False,
    )
```

```python
import functools

import jax
import jax.numpy as jnp
from jax import lax
from jax.experimental import pallas as pl
from jax.experimental.pallas import tpu as pltpu
from jax.sharding import PartitionSpec as P

H = 16
KV = 8
HD = 96
HALF = HD // 2
LANES = 128
BLOCKS = 16
TILE = 128
SLAB = 512
CHUNKS = 2
COST_SCALE = 0.001

epsilon = 1e-05
rope_base = 100000.0
masked_score = -1e30
low = jnp.bfloat16
wide = jnp.float32


def whole(array, buffers=1):
    zeros = (0,) * array.ndim
    mode = pl.Buffered(buffers)
    return pl.BlockSpec(array.shape, lambda *at: zeros, pipeline_mode=mode)


def rows_of(tile, width, first=0):
    return pl.BlockSpec((tile, width), lambda i, place: (first + i, 0))


def shaped(shape, dtype):
    return jax.ShapeDtypeStruct(shape, dtype)


anywhere = pl.BlockSpec(memory_space=pl.ANY)


def run(kernel, name, place, grid, operands, outs, scratch=(), after=(), vmem=56, us=4):
    after = [item for item in after if isinstance(item, jax.Array)]
    count, extra = len(operands), len(after)

    def body(place_ref, *refs):
        kernel(place_ref, *refs[:count], *refs[count + extra :])

    return pl.pallas_call(
        body,
        grid_spec=pltpu.PrefetchScalarGridSpec(
            num_scalar_prefetch=1,
            grid=grid,
            in_specs=[spec for _, spec in operands] + [anywhere] * extra,
            out_specs=[spec for _, spec in outs],
            scratch_shapes=list(scratch),
        ),
        out_shape=[shape for shape, _ in outs],
        compiler_params=pltpu.CompilerParams(vmem_limit_bytes=vmem * 2**20),
        cost_estimate=pl.CostEstimate(
            flops=0, bytes_accessed=int(us * COST_SCALE * 3.3e6), transcendentals=0
        ),
        name=name,
    )(place, *[array for array, _ in operands], *after)


def across(left, right):
    return lax.dot_general(left, right, (((1,), (1,)), ((), ())), preferred_element_type=wide)


def down(left, right):
    return lax.dot_general(left, right, (((0,), (0,)), ((), ())), preferred_element_type=wide)


def project(left, right):
    return jnp.dot(left, right, preferred_element_type=wide)


class Slab:
    def __init__(self, matrix, row, rows, stride, offset, column, width=SLAB, lane=0):
        self.matrix, self.row, self.rows = matrix, row, rows
        self.stride, self.offset = stride, offset
        self.column, self.width, self.lane = column, width, lane

    def of(self, refs, block):
        rows = pl.ds(pl.multiple_of(block * self.stride + self.offset, 16), self.rows)
        return refs[self.matrix].at[rows, pl.ds(self.column, self.width)]

    def lanes(self):
        return pl.ds(self.lane, self.width)


FIRST_HALF, FFN_HALF, QKV_HALF, OUT_HALF = 224, 288, 160, 80


def square_plan(half):
    plan = []
    for slab in range(3):
        top, bottom = slab * 96, slab * 96 + 96
        for first, last in ((top, min(bottom, half)), (max(top, half), bottom)):
            if first < last:
                plan.append(Slab(0, first, last - first, 96, first - top, slab * SLAB))
    return plan


def out_plan(start, half):
    plan = []
    for first, last in ((start, min(start + 96, half)), (max(start, half), start + 96)):
        if first < last:
            plan.append(Slab(0, first, last - first, LANES, first - start, 0))
    for part in range(2):
        plan.append(Slab(0, start + 96, 48, LANES, part * 48, SLAB, 256, part * 256))
    return plan


GAINS = 288
GAIN_SLAB = Slab(1, GAINS, 16, 16, 0, 0)
FIRST_QKV_PLAN = square_plan(FIRST_HALF) + [GAIN_SLAB]
FIRST_OUT_PLAN = out_plan(GAINS + 16, FIRST_HALF)
QKV_PLAN = square_plan(QKV_HALF) + [GAIN_SLAB]
OUT_PLAN = out_plan(0, OUT_HALF)
FFN_PLAN = [
    Slab(0, 0, 96, 96, 0, 0),
    Slab(0, 96, 96, 96, 0, SLAB),
    Slab(1, 192, 96, 96, 0, 0),
    Slab(1, 288, 96, 96, 0, SLAB),
    Slab(2, 384, 64, 64, 0, 0),
    Slab(2, 448, 64, 64, 0, SLAB),
    Slab(2, 512, 64, 64, 0, 2 * SLAB),
]
UPPER_ROWS = 384
UPPER_PLAN, LOWER_PLAN = FFN_PLAN[:4], [
    Slab(2, slab * 64, 64, 64, 0, slab * SLAB) for slab in range(3)
]


def block_index(place_ref, k, dy, dx):
    z, y, x = place_ref[0], place_ref[1], place_ref[2]
    return ((z ^ k) * 2 + (y ^ dy)) * 2 + (x ^ dx)


def from_pieces(pieces, half):
    def source(k, dy, dx, slab):
        at = pl.ds(slab.row, slab.rows)
        piece = pieces[dy * 2 + dx]
        if dy and dx:
            part = int(slab.row >= half)
            at = pl.ds(slab.row - part * half, slab.rows)
            piece = pieces[3 + part]
        return piece.at[k, at, slab.lanes()]

    return source


def from_planes(pair, other):
    def source(k, dy, dx, slab):
        planes = other if k % 2 else pair
        return planes.at[k // 2, dy * 2 + dx, pl.ds(slab.row, slab.rows), slab.lanes()]

    return source


def fetch(place_ref, source, plan, matrices, sems):
    for k in range(4):
        for dy in range(2):
            for dx in range(2):
                block = block_index(place_ref, k, dy, dx)
                for slab in plan:
                    pltpu.make_async_copy(
                        source(k, dy, dx, slab), slab.of(matrices, block), sems.at[slab.matrix]
                    ).start()


def send_off(place_ref, k, matrices, stride_base, plan, half, outs, sems):
    to_x, to_y, late_x, late_y, own = range(5)
    for dy in range(2):
        for dx in range(2):
            block = block_index(place_ref, place_ref[0], dy, dx) + stride_base
            for slab in plan:
                part = int(slab.row >= half)
                at = pl.ds(slab.row - part * half, slab.rows)
                if (dy, dx) == (0, 0):
                    which, index = own, (k, part)
                elif dy and dx:
                    which, index = (to_y if part else to_x), (0, k)
                elif part == dy:
                    which, index = (to_y if dy else to_x), (1, k)
                else:
                    which, index = (late_y if dy else late_x), (k,)
                target = outs[which].at[(*index, at, slab.lanes())]
                pltpu.make_async_copy(slab.of(matrices, block), target, sems.at[which]).start()


def fill_spare(source, row, rows, half, outs, sems):
    at = pl.ds(row - half, rows)
    for k in range(4):
        for which, index in ((1, (0, k)), (1, (1, k)), (2, (k,)), (4, (k, 1))):
            target = outs[which].at[(*index, at)]
            pltpu.make_async_copy(source, target, sems.at[which]).start()


def drain(refs, sems):
    for index, ref in enumerate(refs):
        pltpu.make_async_copy(ref, ref, sems.at[index]).wait()


def sent_shapes(half, width):
    shapes = [(2, 4, half, width)] * 2 + [(4, half, width)] * 2 + [(4, 2, half, width)]
    return [(shaped(shape, low), anywhere) for shape in shapes]


def gate_kernel(place_ref, *refs):
    pass


def gate(place, arrays, after):
    count, extra = len(arrays), len(after)
    return pl.pallas_call(
        gate_kernel,
        grid_spec=pltpu.PrefetchScalarGridSpec(
            num_scalar_prefetch=1,
            grid=(1,),
            in_specs=[anywhere] * (count + extra),
            out_specs=[anywhere] * count,
        ),
        out_shape=[shaped(array.shape, array.dtype) for array in arrays],
        input_output_aliases={1 + index: index for index in range(count)},
        cost_estimate=pl.CostEstimate(flops=0, bytes_accessed=0, transcendentals=0),
        name="gate",
    )(place, *arrays, *after)


def pair_kernel(place_ref, own, far, out, sems):
    copies = [
        pltpu.make_async_copy(ref, out.at[k], sems.at[k]) for k, ref in enumerate((own, far))
    ]
    for copy in copies:
        copy.start()
    for copy in copies:
        copy.wait()


def pair_up(place, own, far, after=()):
    out = shaped((2, *own.shape), low)
    return run(
        pair_kernel,
        "pair",
        place,
        (1,),
        [(own, anywhere), (far, anywhere)],
        [(out, whole(out))],
        [pltpu.SemaphoreType.DMA((2,))],
        after,
        us=2,
    )[0]


def line_kernel(place_ref, pair, near, out, sems):
    copies = []
    for k in range(4):
        ref = near if k % 2 else pair
        copies.append(pltpu.make_async_copy(ref.at[k // 2], out.at[k], sems.at[k]))
        copies[-1].start()
    for copy in copies:
        copy.wait()


def line_up(place, pair, near, after=()):
    _, rows, width = pair.shape
    out = shaped((4, rows, width), low)
    return run(
        line_kernel,
        "line",
        place,
        (1,),
        [(pair, anywhere), (near, anywhere)],
        [(out, whole(out))],
        [pltpu.SemaphoreType.DMA((4,))],
        after,
        us=4,
    )[0]


def plane_kernel(place_ref, own, from_x, from_y, upper, lower, out, sems):
    half = upper.shape[1]
    parts = [
        (own, out.at[pl.ds(0, 1)]),
        (from_x, out.at[pl.ds(1, 1)]),
        (from_y, out.at[pl.ds(2, 1)]),
        (upper, out.at[pl.ds(3, 1), pl.ds(0, half)]),
        (lower, out.at[pl.ds(3, 1), pl.ds(half, half)]),
    ]
    copies = [
        pltpu.make_async_copy(source, target, sems.at[index])
        for index, (source, target) in enumerate(parts)
    ]
    for copy in copies:
        copy.start()
    for copy in copies:
        copy.wait()


def plane_up(place, parts, after):
    _, rows, width = parts[0].shape
    out = shaped((4, rows, width), low)
    return run(
        plane_kernel,
        "plane",
        place,
        (1,),
        [(part, anywhere) for part in parts],
        [(out, whole(out))],
        [pltpu.SemaphoreType.DMA((5,))],
        after,
        us=2,
    )[0]


def halves_kernel(place_ref, from_x, from_y, upper, lower, sems):
    half = upper.shape[1]
    copies = (
        pltpu.make_async_copy(from_x.at[:, pl.ds(0, half)], upper, sems.at[0]),
        pltpu.make_async_copy(from_y.at[:, pl.ds(half, half)], lower, sems.at[1]),
    )
    for copy in copies:
        copy.start()
    for copy in copies:
        copy.wait()


def halves(place, from_x, from_y, after):
    count, rows, width = from_x.shape
    out = shaped((count, rows // 2, width), low)
    return run(
        halves_kernel,
        "halves",
        place,
        (1,),
        [(from_x, anywhere), (from_y, anywhere)],
        [(out, whole(out))] * 2,
        [pltpu.SemaphoreType.DMA((2,))],
        after,
        us=2,
    )


def step_rows(half):
    return next(rows for rows in (96, 80, 48, 368) if half % rows == 0)


def merge_kernel(place_ref, late_x, late_y, got_x, got_y, out_x, out_y):
    out_x[...] = (late_x[...].astype(wide) + got_y[0].astype(wide)).astype(low)
    out_y[...] = (late_y[...].astype(wide) + got_x[0].astype(wide)).astype(low)


def merge(place, late_x, late_y, got_x, got_y, after):
    shape = late_x.shape
    rows = step_rows(shape[1])
    spec = pl.BlockSpec((4, rows, shape[2]), lambda i, place: (0, i, 0))
    got = pl.BlockSpec((1, 4, rows, shape[2]), lambda i, place: (0, 0, i, 0))
    return run(
        merge_kernel,
        "merge",
        place,
        (shape[1] // rows,),
        [(late_x, spec), (late_y, spec), (got_x, got), (got_y, got)],
        [(shaped(shape, low), spec)] * 2,
        after=after,
    )


def sum_kernel(direct, groups, place_ref, *refs):
    ins, (kept, *outs) = refs[: 5 * groups], refs[5 * groups :]
    step = pl.program_id(0)
    for k in range(4):

        @pl.when(step == k)
        def _():
            row = 0
            for group in range(groups):
                own, got_x, got_y, more_x, more_y = ins[5 * group : 5 * group + 5]
                at = slice(row, row + own.shape[2])
                row += own.shape[2]
                upper = own[0, 0].astype(wide) + got_x[0, 0].astype(wide)
                upper = upper + more_y[0].astype(wide)
                lower = own[0, 1].astype(wide) + got_y[0, 0].astype(wide)
                lower = lower + more_x[0].astype(wide)
                if k == 0:
                    ref = kept
                elif direct:
                    ref = outs[k - 1]
                else:
                    ref = outs[1].at[0] if k % 2 else outs[0]
                ref[0, at, :], ref[1, at, :] = upper.astype(ref.dtype), lower.astype(ref.dtype)


def sum_plane(place, groups, direct, after):
    operands = []
    for own, got_x, got_y, more_x, more_y in groups:
        _, _, half, width = own.shape
        got = pl.BlockSpec((1, 1, half, width), lambda k, place: (1, k, 0, 0))
        more = pl.BlockSpec((1, half, width), lambda k, place: (k, 0, 0))
        operands += [
            (own, pl.BlockSpec((1, 2, half, width), lambda k, place: (k, 0, 0, 0))),
            (got_x, got),
            (got_y, got),
            (more_x, more),
            (more_y, more),
        ]
    half = sum(group[0].shape[2] for group in groups)
    out = pl.BlockSpec((2, half, width), lambda k, place: (0, 0, 0))
    both = pl.BlockSpec((1, 2, half, width), lambda k, place: (k // 2, 0, 0, 0))
    outs = [(shaped((2, half, width), wide), out)]
    if direct:
        outs += [(shaped((2, half, width), low), out)] * 3
    else:
        outs += [(shaped((2, half, width), wide), out)]
        outs += [(shaped((2, 2, half, width), low), both)]
    return run(
        functools.partial(sum_kernel, direct, len(groups)),
        "sum_plane",
        place,
        (4,),
        operands,
        outs,
        after=after,
        us=5,
    )


def pass_kernel(place_ref, kept_far, near, out):
    out[...] = (kept_far[...] + near[0].astype(wide)).astype(low)


def sum_pass(place, kept_far, near, after):
    _, half, width = kept_far.shape
    rows = step_rows(half)
    spec = pl.BlockSpec((2, rows, width), lambda i, place: (0, i, 0))
    second = pl.BlockSpec((1, 2, rows, width), lambda i, place: (1, 0, i, 0))
    return run(
        pass_kernel,
        "sum_pass",
        place,
        (half // rows,),
        [(kept_far, spec), (near, second)],
        [(shaped(kept_far.shape, low), spec)],
        after=after,
        us=3,
    )[0]


def total_kernel(place_ref, kept, *refs):
    *received, out, out_low = refs
    total = kept[...]
    for ref in received:
        part = ref[0] if len(ref.shape) > len(kept.shape) else ref[...]
        total = total + part.astype(wide)
    out[...] = total
    out_low[...] = total.astype(low)


def sum_line(place, kept, received, after):
    _, half, width = kept.shape
    rows = step_rows(half)
    spec = pl.BlockSpec((2, rows, width), lambda i, place: (0, i, 0))
    first = pl.BlockSpec((1, 2, rows, width), lambda i, place: (0, 0, i, 0))
    total, total_low = run(
        total_kernel,
        "sum_line",
        place,
        (half // rows,),
        [(kept, spec)] + [(item, first if item.ndim == 4 else spec) for item in received],
        [(shaped(kept.shape, wide), spec), (shaped(kept.shape, low), spec)],
        after=after,
        us=4,
    )
    return total.reshape(2 * half, width), total_low.reshape(2 * half, width)


def pack_first_kernel(place_ref, query, key, value, square, gain_one, gain_two, out):
    core = place_ref[3]

    def mine(ref):
        columns = ref.shape[1] // 2
        return ref[:, pl.ds(pl.multiple_of(core * columns, LANES), columns)]

    packed = jnp.concatenate([mine(query), mine(key), mine(value)], axis=1)
    rows = packed.shape[0]
    for slab in range(3):
        out[slab * rows : (slab + 1) * rows, :] = packed[:, slab * SLAB : (slab + 1) * SLAB]
    row = lax.broadcasted_iota(jnp.int32, (16, LANES), 0)
    gap = jnp.zeros((16, LANES - rows), wide)
    out[GAINS : GAINS + 16, :] = jnp.zeros((16, SLAB), low)
    for index, gain in enumerate((gain_one, gain_two)):
        spread = jnp.broadcast_to(gain[...].astype(wide), (16, rows))
        spread = jnp.where(row == 0, jnp.concatenate([spread, gap], axis=1), 0.0)
        out[GAINS : GAINS + 16, index * LANES : (index + 1) * LANES] = spread.astype(low)
    at, packed = GAINS + 16, mine(square)
    out[at : at + rows, :] = packed[:, :SLAB]
    for part in range(2):
        out[at + rows :, part * 256 : (part + 1) * 256] = packed[
            part * rows // 2 : (part + 1) * rows // 2, SLAB:
        ]


def pack_first(place, query, key, value, square, gain_one, gain_two):
    operands = [query, key, value, square, gain_one.reshape(1, -1), gain_two.reshape(1, -1)]
    out = shaped((2 * FIRST_HALF, SLAB), low)
    return run(
        pack_first_kernel,
        "pack_first",
        place,
        (1,),
        [(item, whole(item)) for item in operands],
        [(out, whole(out))],
    )[0]


def interleave(even, odd):
    lane = lax.broadcasted_iota(jnp.int32, even.shape, 1)
    left = jnp.where(lane < LANES // 2, even, pltpu.roll(odd, LANES // 2, 1))
    right = jnp.where(lane < LANES // 2, pltpu.roll(even, LANES // 2, 1), odd)
    return left, right


def pack_ffn_kernel(chunk, place_ref, gate, up, down_w, *outs):
    core = place_ref[3]
    rows = gate.shape[0]

    def put(at, size, column, part):
        span, width = outs[0].shape[0], part.shape[1]
        out, at = (outs[0], at) if at < span else (outs[1], at - span)
        out[at : at + size, column : column + width] = part

    for matrix, ref in enumerate((gate, up)):
        for pair in range(8):
            windows = [
                ref[:, pl.ds(pl.multiple_of((2 * pair + odd) * 256 + core * LANES, LANES), LANES)]
                for odd in range(2)
            ]
            packed = interleave(windows[0].astype(wide), windows[1].astype(wide))[chunk]
            at = (matrix * 2 + pair // 4) * rows
            column = pair % 4 * LANES
            put(at, rows, column, packed.astype(low))
    units = down_w[pl.ds(pl.multiple_of(core * LANES + chunk * 64, 64), 64), :]
    for slab in range(3):
        at = 4 * rows + slab * 64
        put(at, 64, 0, units[:, slab * SLAB : (slab + 1) * SLAB])


def pack_ffn(place, chunk, parts, gate, up, down_w, after):
    outs = [shaped((rows, SLAB), low) for rows in parts]
    return run(
        functools.partial(pack_ffn_kernel, chunk),
        "pack_ffn",
        place,
        (1,),
        [(item, whole(item)) for item in (gate, up, down_w)],
        [(out, whole(out)) for out in outs],
        after=after,
    )


def rows_in(ref, at, rows):
    if at >= FFN_HALF:
        at += ref.shape[0] // 2 - FFN_HALF
    return ref[at : at + rows, :]


def unpack_ffn_kernel(place_ref, mine_0, mine_1, other_0, other_1, gate, up, down_w):
    core = place_ref[3]
    rows = gate.shape[0]
    for owner, chunks in ((core, (mine_0, mine_1)), (1 - core, (other_0, other_1))):
        for matrix, ref in enumerate((gate, up)):
            for pair in range(8):
                at = (matrix * 2 + pair // 4) * rows
                column = pair % 4 * LANES
                parts = [
                    rows_in(chunk, at, rows)[:, column : column + LANES].astype(wide)
                    for chunk in chunks
                ]
                for odd, window in enumerate(interleave(*parts)):
                    place = (2 * pair + odd) * 256 + owner * LANES
                    ref[:, pl.ds(pl.multiple_of(place, LANES), LANES)] = window
        for index, chunk in enumerate(chunks):
            for slab in range(3):
                at = 4 * rows + slab * 64
                place = pl.multiple_of(owner * LANES + index * 64, 64)
                part = rows_in(chunk, at, 64).astype(wide)
                down_w[pl.ds(place, 64), slab * SLAB : (slab + 1) * SLAB] = part


def unpack_ffn(place, mine, other, shapes, after):
    outs = [shaped(shape, wide) for shape in shapes]
    return run(
        unpack_ffn_kernel,
        "unpack_ffn",
        place,
        (1,),
        [(item, whole(item)) for item in (*mine, *other)],
        [(out, whole(out)) for out in outs],
        after=after,
    )


def unpack_first_kernel(
    place_ref, mine, other, joint_mine, joint_other, query, key, value, square
):
    core = place_ref[3]
    rows = query.shape[0]

    def put(ref, owner, part):
        columns = ref.shape[1] // 2
        at = pl.ds(pl.multiple_of(owner * columns, LANES), columns)
        ref[:, at] = part.astype(wide)

    for owner, qkv, joint in ((core, mine, joint_mine), (1 - core, other, joint_other)):
        slabs = [qkv[slab * rows : (slab + 1) * rows, :] for slab in range(3)]
        put(query, owner, jnp.concatenate([slabs[0], slabs[1][:, :256]], axis=1))
        put(key, owner, jnp.concatenate([slabs[1][:, 256:], slabs[2][:, :128]], axis=1))
        put(value, owner, slabs[2][:, 128:])
        half = FFN_HALF + OUT_HALF
        out = [joint[part * half + FFN_HALF : (part + 1) * half, :] for part in range(2)]
        out = jnp.concatenate(out, axis=0)
        rest = out[rows : rows + rows // 2, :]
        rest = jnp.concatenate([rest[:, :256], rest[:, 256:]], axis=0)
        put(square, owner, jnp.concatenate([out[:rows, :], rest], axis=1))


def unpack_first(place, parts, shapes, after):
    outs = [shaped(shape, wide) for shape in shapes]
    return run(
        unpack_first_kernel,
        "unpack_first",
        place,
        (1,),
        [(item, whole(item)) for item in parts],
        [(out, whole(out)) for out in outs],
        after=after,
    )


def turn_table(position):
    frequency = rope_base ** (-jnp.arange(HALF, dtype=wide) * 2.0 / HD)
    angle = position.astype(wide)[:, None] * frequency[None, :]
    gap = jnp.zeros((position.shape[0], LANES // 2 - HALF), wide)
    cosine, sine = jnp.cos(angle), jnp.sin(angle)
    return (
        jnp.concatenate([cosine, gap, cosine, gap], axis=1),
        jnp.concatenate([-sine, gap, sine, gap], axis=1),
    )


def qkv_kernel(tiles, place_ref, own_ref, far_ref, cos_ref, sin_ref, *refs):
    pieces = refs[:5]
    normed_ref, q_ref, k_ref, v_ref, w_ref, gain_ref, gain_rows, x_ref, sems = refs[5:]
    step = pl.program_id(0)

    @pl.when(step < tiles)
    def _():
        x_ref[...] = own_ref[...]

    @pl.when(step >= tiles)
    def _():
        x_ref[...] = far_ref[...]

    @pl.when(pl.program_id(0) == 0)
    def _():
        fetch(
            place_ref, from_pieces(pieces, FIRST_HALF), FIRST_QKV_PLAN, (w_ref, gain_rows), sems
        )
        drain((w_ref, gain_rows), sems)
        for index in range(2):
            parts = [
                gain_rows[16 * block : 16 * block + 16, index * LANES : (index + 1) * LANES]
                for block in range(BLOCKS)
            ]
            parts = [part.astype(wide)[:8, :HD] for part in parts]
            gain_ref[8 * index : 8 * index + 8, :] = jnp.concatenate(parts, axis=1)

    hidden = x_ref[...].astype(wide)
    scale = lax.rsqrt(jnp.mean(hidden * hidden, axis=-1, keepdims=True) + epsilon)
    normed = (hidden * scale * gain_ref[0:1, :]).astype(low)
    normed_ref[...] = normed
    gap = jnp.zeros((x_ref.shape[0], LANES // 2 - HALF), wide)
    heads = q_ref.shape[1] // LANES
    groups = k_ref.shape[1] // LANES
    count = 4
    for first in range(0, heads + 2 * groups, count):
        part = project(normed, w_ref[:, first * HD : (first + count) * HD])
        for index in range(first, first + count):
            at = (index - first) * HD
            if index >= heads + groups:
                column = (index - heads - groups) * LANES
                padded = jnp.concatenate([part[:, at : at + HD], gap, gap], axis=1)
                v_ref[:, column : column + LANES] = padded.astype(low)
                continue
            padded = jnp.concatenate(
                [part[:, at : at + HALF], gap, part[:, at + HALF : at + HD], gap], axis=1
            )
            turned = pltpu.roll(padded, LANES // 2, 1)
            padded = (padded * cos_ref[...] + turned * sin_ref[...]).astype(low)
            if index < heads:
                q_ref[:, index * LANES : (index + 1) * LANES] = padded
            else:
                column = (index - heads) * LANES
                k_ref[:, column : column + LANES] = padded


def project_qkv(place, own, far, cosine, sine, pieces, after):
    count, width = own.shape
    tile = 320
    tiles = count // tile
    count = 2 * count
    heads, groups = H // 2 * LANES, KV // 2 * LANES
    weight, gains = shaped((width, width), low), shaped((16, width), wide)
    early = pl.BlockSpec((tile, width), lambda i, place: (jnp.minimum(i, tiles - 1), 0))
    late = pl.BlockSpec((tile, width), lambda i, place: (jnp.maximum(i - tiles, 0), 0))
    return run(
        functools.partial(qkv_kernel, tiles),
        "project_qkv",
        place,
        (count // tile,),
        [
            (own, early),
            (far, late),
            (cosine, rows_of(tile, LANES)),
            (sine, rows_of(tile, LANES)),
        ]
        + [(piece, anywhere) for piece in pieces],
        [
            (shaped((count, width), low), rows_of(tile, width)),
            (shaped((count, heads), low), rows_of(tile, heads)),
            (shaped((count, groups), low), rows_of(tile, groups)),
            (shaped((count, groups), low), rows_of(tile, groups)),
            (weight, whole(weight)),
            (gains, whole(gains)),
        ],
        [
            pltpu.VMEM((BLOCKS * 16, SLAB), low),
            pltpu.VMEM((tile, width), low),
            pltpu.SemaphoreType.DMA((2,)),
        ],
        after,
        us=18,
    )


def fill_bias(bias_ref, column_ref, row_ref):
    size = bias_ref.shape[0]
    for start in range(0, size, TILE):
        shape = (TILE, size)
        slots = lax.broadcasted_iota(jnp.int32, shape, 0) + start
        keys = lax.broadcasted_iota(jnp.int32, shape, 1)
        same = column_ref[start : start + TILE, :] == row_ref[0]
        allowed = same & (keys <= slots)
        bias_ref[start : start + TILE, :] = jnp.where(allowed, 0.0, masked_score)


LOG2_E = 1.4426950408889634


def both_heads(ref, start):
    rows = slice(start, start + TILE)
    return jnp.concatenate([ref[rows, :LANES], ref[rows, LANES:]], axis=0)


def attend_kernel(
    place_ref, q_ref, k_ref, v_ref, column_ref, row_ref, out_ref, total_ref, bias_ref
):
    group = pl.program_id(0)
    size = q_ref.shape[0]

    @pl.when(group == 0)
    def _():
        fill_bias(bias_ref, column_ref, row_ref)
        total_ref[...] = jnp.zeros_like(total_ref)

    lane = lax.broadcasted_iota(jnp.int32, (TILE, LANES), 1)
    for start in range(0, size, TILE):
        stop = start + TILE
        raw = across(both_heads(q_ref, start), k_ref[:stop, :])
        bias = bias_ref[start:stop, :stop]
        scores = raw * (HD ** (-0.5) * LOG2_E) + jnp.concatenate([bias, bias], axis=0)
        top = jnp.max(scores, axis=-1, keepdims=True)
        powers = jnp.exp2(scores - top)
        amount = jnp.sum(powers, axis=-1, keepdims=True)
        probs = (powers * (1.0 / amount)).astype(low)
        mixed = project(probs, v_ref[:stop, :]).astype(low)
        total = top + jnp.log2(amount)
        kept = total_ref[start:stop, :]
        for head in range(2):
            rows = slice(head * TILE, (head + 1) * TILE)
            out_ref[start:stop, head * LANES : (head + 1) * LANES] = mixed[rows]
            kept = jnp.where(lane == 2 * group + head, total[rows], kept)
        total_ref[start:stop, :] = kept


def attention_specs(size, block):
    return dict(
        pair=pl.BlockSpec((size, 2 * LANES), lambda g, place: (block, g)),
        one=pl.BlockSpec((size, LANES), lambda g, place: (block, g)),
        pair_alone=pl.BlockSpec((size, 2 * LANES), lambda g, place: (0, g)),
        one_alone=pl.BlockSpec((size, LANES), lambda g, place: (0, g)),
        shared=pl.BlockSpec((size, LANES), lambda g, place: (block, 0)),
        alone=pl.BlockSpec((size, LANES), lambda g, place: (0, 0)),
        column=pl.BlockSpec((size, 1), lambda g, place: (block, 0)),
        row=pl.BlockSpec((1, 1, size), lambda g, place: (block, 0, 0)),
    )


def attend(place, q, k, v, segment, block, after=()):
    blocks, size = segment.shape
    spec = attention_specs(size, block)
    return run(
        attend_kernel,
        "attend",
        place,
        (k.shape[1] // LANES,),
        [
            (q, spec["pair"]),
            (k, spec["one"]),
            (v, spec["one"]),
            (segment.reshape(blocks * size, 1), spec["column"]),
            (segment.reshape(blocks, 1, size), spec["row"]),
        ],
        [
            (shaped((size, q.shape[1]), low), spec["pair_alone"]),
            (shaped((size, LANES), wide), spec["alone"]),
        ],
        [pltpu.VMEM((size, size), wide)],
        after,
        us=17,
    )


def attend_back_kernel(
    place_ref,
    q_ref,
    k_ref,
    v_ref,
    grad_ref,
    out_ref,
    total_ref,
    column_ref,
    row_ref,
    cos_ref,
    sin_ref,
    dq_ref,
    dk_ref,
    dv_ref,
    bias_ref,
    dk_sum,
    dv_sum,
):
    group = pl.program_id(0)
    size = q_ref.shape[0]

    @pl.when(group == 0)
    def _():
        fill_bias(bias_ref, column_ref, row_ref)

    def turned_back(grad, rows):
        turned = pltpu.roll(grad, LANES // 2, 1)
        return (grad * cos_ref[rows, :] - turned * sin_ref[rows, :]).astype(low)

    dk_sum[...] = jnp.zeros_like(dk_sum)
    dv_sum[...] = jnp.zeros_like(dv_sum)
    lane = lax.broadcasted_iota(jnp.int32, (TILE, LANES), 1)
    scale = HD ** (-0.5)
    for start in range(0, size, TILE):
        stop = start + TILE
        queries, grads = both_heads(q_ref, start), both_heads(grad_ref, start)
        mixed = both_heads(out_ref, start)
        delta = jnp.sum(grads.astype(wide) * mixed.astype(wide), axis=-1, keepdims=True)
        totals = [
            jnp.sum(
                jnp.where(lane == 2 * group + head, total_ref[start:stop, :], 0.0),
                axis=-1,
                keepdims=True,
            )
            for head in range(2)
        ]
        bias = bias_ref[start:stop, :stop]
        raw = across(queries, k_ref[:stop, :])
        scores = raw * (scale * LOG2_E) + jnp.concatenate([bias, bias], axis=0)
        probs = jnp.exp2(scores - jnp.concatenate(totals, axis=0))
        dv_sum[:stop, :] += down(probs.astype(low), grads)
        grad_probs = across(grads, v_ref[:stop, :])
        grad_raw = (probs * (grad_probs - delta)).astype(low)
        dq = project(grad_raw, k_ref[:stop, :]) * scale
        for head in range(2):
            part = turned_back(dq[head * TILE : (head + 1) * TILE], slice(start, stop))
            dq_ref[start:stop, head * LANES : (head + 1) * LANES] = part
        dk_sum[:stop, :] += down(grad_raw, queries)
    dv_ref[...] = dv_sum[...].astype(low)
    dk_ref[...] = turned_back(dk_sum[...] * scale, slice(None))


def attend_back(place, q, k, v, grad, out, total, segment, cosine, sine, block, after=()):
    blocks, size = segment.shape
    spec = attention_specs(size, block)
    return run(
        attend_back_kernel,
        "attend_back",
        place,
        (k.shape[1] // LANES,),
        [
            (q, spec["pair"]),
            (k, spec["one"]),
            (v, spec["one"]),
            (grad, spec["pair_alone"]),
            (out, spec["pair_alone"]),
            (total, spec["alone"]),
            (segment.reshape(blocks * size, 1), spec["column"]),
            (segment.reshape(blocks, 1, size), spec["row"]),
            (cosine, spec["shared"]),
            (sine, spec["shared"]),
        ],
        [
            (shaped((size, q.shape[1]), low), spec["pair_alone"]),
            (shaped((size, k.shape[1]), low), spec["one_alone"]),
            (shaped((size, v.shape[1]), low), spec["one_alone"]),
        ],
        [
            pltpu.VMEM((size, size), wide),
            pltpu.VMEM((size, LANES), wide),
            pltpu.VMEM((size, LANES), wide),
        ],
        after,
        us=21,
    )


def out_weight_kernel(place_ref, *refs):
    pieces, weights, whole_weight, sems = refs[:5], refs[5:7], refs[7], refs[8]
    fetch(place_ref, from_pieces(pieces, FIRST_HALF), FIRST_OUT_PLAN, (whole_weight,), sems)
    zeros = jnp.zeros((LANES - HD, whole_weight.shape[1]), low)
    for block in range(BLOCKS):
        whole_weight[pl.ds(block * LANES + HD, LANES - HD), :] = zeros
    drain((whole_weight.at[pl.ds(0, BLOCKS * HD)],), sems)
    rows = weights[0].shape[0]
    for part in range(2):
        weights[part][...] = whole_weight[part * rows : (part + 1) * rows, :]


def out_weight(place, pieces, width, after):
    out = shaped((H // 2 * LANES, width // 2), low)
    return run(
        out_weight_kernel,
        "out_weight",
        place,
        (1,),
        [(piece, anywhere) for piece in pieces],
        [(out, whole(out))] * 2,
        [pltpu.VMEM((H * LANES, width // 2), low), pltpu.SemaphoreType.DMA((1,))],
        after,
    )


def middle_kernel(
    place_ref, x_ref, mine_ref, other_ref, *refs
):
    w_mine, w_other, (gain_ref, middle_ref, out_ref, heads) = refs[:2], refs[2:4], refs[4:]
    core = place_ref[3]
    span = mine_ref.shape[1]
    heads[:, pl.ds(pl.multiple_of(core * span, LANES), span)] = mine_ref[...]
    heads[:, pl.ds(pl.multiple_of((1 - core) * span, LANES), span)] = other_ref[...]
    columns = w_mine[0].shape[1]
    for owner, weight in ((core, w_mine), (1 - core, w_other)):
        at = pl.ds(pl.multiple_of(owner * columns, LANES), columns)
        branch = project(heads[:, :span], weight[0][...])
        branch = branch + project(heads[:, span:], weight[1][...])
        middle_ref[:, at] = x_ref[:, at].astype(wide) + branch
    hidden = middle_ref[...]
    scale = lax.rsqrt(jnp.mean(hidden * hidden, axis=-1, keepdims=True) + epsilon)
    out_ref[...] = (hidden * scale * gain_ref[8:9, :]).astype(low)


def middle_of(place, x, mine, other, w_mine, w_other, gains, after=()):
    count, width = x.shape
    tile, span = count // 2, mine.shape[1]
    return run(
        middle_kernel,
        "middle",
        place,
        (2,),
        [
            (x, rows_of(tile, width)),
            (mine, rows_of(tile, span)),
            (other, rows_of(tile, span)),
            *[(item, whole(item)) for item in (*w_mine, *w_other, gains)],
        ],
        [
            (shaped((count, width), wide), rows_of(tile, width)),
            (shaped((count, width), low), rows_of(tile, width)),
        ],
        [pltpu.VMEM((tile, 2 * span), low)],
        after,
        us=11,
    )


def middle_back_kernel(
    place_ref,
    middle_ref,
    mine_0,
    mine_1,
    other_0,
    other_1,
    cotangent_ref,
    gain_ref,
    *refs,
):
    w_mine, w_other, refs = refs[:2], refs[2:4], refs[4:]
    grad_ref, branch_mine, branch_other, heads_mine, heads_other, gain_grad, branch, heads = refs
    core = place_ref[3]
    hidden = middle_ref[...]
    scale = lax.rsqrt(jnp.mean(hidden * hidden, axis=-1, keepdims=True) + epsilon)
    incoming = mine_0[...] + mine_1[...] + other_0[...].astype(wide) + other_1[...].astype(wide)
    weighted = incoming * gain_ref[8:9, :]
    inner = jnp.mean(weighted * hidden, axis=-1, keepdims=True)
    grad = cotangent_ref[...].astype(wide) + (scale * weighted - hidden * scale**3 * inner)
    grad_ref[...] = grad
    branch[...] = grad.astype(low)

    @pl.when(pl.program_id(0) == 0)
    def _():
        gain_grad[...] = jnp.zeros_like(gain_grad)

    summed = jnp.sum(incoming * hidden * scale, axis=0, keepdims=True)
    gain_grad[...] += jnp.broadcast_to(summed, gain_grad.shape)
    columns, span = w_mine[0].shape[1], heads_mine.shape[1]

    def part(ref, owner, size):
        return ref[:, pl.ds(pl.multiple_of(owner * size, LANES), size)]

    branch_mine[...] = part(branch, core, columns)
    branch_other[...] = part(branch, 1 - core, columns)
    for at in range(0, 2 * span, SLAB):
        index, rows = at // span, slice(at % span, at % span + SLAB)
        heads[:, at : at + SLAB] = (
            across(branch_mine[...], w_mine[index][rows, :])
            + across(branch_other[...], w_other[index][rows, :])
        ).astype(low)
    heads_mine[...] = part(heads, core, span)
    heads_other[...] = part(heads, 1 - core, span)


def middle_back(place, middle, parts, cotangent, gains, w_mine, w_other, after=()):
    count, width = middle.shape
    tile, columns, span = count // 2, w_mine[0].shape[1], w_mine[0].shape[0]
    gain_grad = shaped((8, width), wide)
    return run(
        middle_back_kernel,
        "middle_back",
        place,
        (2,),
        [
            *[(item, rows_of(tile, width)) for item in (middle, *parts, cotangent)],
            *[(item, whole(item)) for item in (gains, *w_mine, *w_other)],
        ],
        [
            (shaped((count, width), wide), rows_of(tile, width)),
            (shaped((count, columns), low), rows_of(tile, columns)),
            (shaped((count, columns), low), rows_of(tile, columns)),
            (shaped((count, span), low), rows_of(tile, span)),
            (shaped((count, span), low), rows_of(tile, span)),
            (gain_grad, whole(gain_grad)),
        ],
        [pltpu.VMEM((tile, width), low), pltpu.VMEM((tile, 2 * span), low)],
        after,
        us=15,
    )


def out_grad_kernel(
    place_ref,
    own_mine,
    own_other,
    far_mine,
    far_other,
    branch_own,
    branch_far,
    *refs,
):
    outs, (grad, sems) = refs[:5], refs[5:]
    core = place_ref[3]
    span = own_mine.shape[1]
    for owner, own, far in ((core, own_mine, far_mine), (1 - core, own_other, far_other)):
        for at in range(0, span, SLAB):
            part = down(own[:, at : at + SLAB], branch_own[...])
            part = part + down(far[:, at : at + SLAB], branch_far[...])
            grad[pl.ds(pl.multiple_of(owner * span + at, LANES), SLAB), :] = part.astype(low)
    for k in range(4):
        base = (place_ref[0] ^ k) * 4
        send_off(place_ref, k, (grad,), base, OUT_PLAN, OUT_HALF, outs, sems)
    fill_spare(grad.at[pl.ds(0, 16), pl.ds(0, SLAB)], 144, 16, OUT_HALF, outs, sems)
    drain(outs, sems)


def out_grad(place, own_mine, own_other, far_mine, far_other, branch_own, branch_far, after=()):
    columns = branch_own.shape[1]
    operands = (own_mine, own_other, far_mine, far_other, branch_own, branch_far)
    return run(
        out_grad_kernel,
        "out_grad",
        place,
        (1,),
        [(item, whole(item)) for item in operands],
        sent_shapes(OUT_HALF, SLAB),
        [pltpu.VMEM((H * LANES, columns), low), pltpu.SemaphoreType.DMA((5,))],
        after,
        us=10,
    )


FFN_TILE = 320
FFN_STEP = 256
FFN_SPAN = 768


def load_tokens(x_ref, c_ref, x_own, x_far, c_own, c_far, sems):
    count = x_far.shape[0]
    for index, (ref, far, own) in enumerate(((x_ref, x_far, x_own), (c_ref, c_far, c_own))):
        for part, source in enumerate((far, own)):
            target = ref.at[pl.ds(part * count, count)]
            pltpu.make_async_copy(source, target, sems.at[index]).start()


def ffn_forward(step, tiles, x_ref, c_ref, weights, sums, middles, at_rows):
    gate_w, up_w, down_w = weights
    inner, grad_gate, grad_up = middles
    units, width = gate_w.shape[1], gate_w.shape[0]
    rows = pl.ds(pl.multiple_of(step * FFN_TILE, FFN_TILE), FFN_TILE)

    @pl.loop(0, units // FFN_STEP)
    def _(index):
        at = pl.ds(pl.multiple_of(index * FFN_STEP, FFN_STEP), FFN_STEP)
        gate = project(x_ref[rows, :], gate_w[:, at])
        upward = project(x_ref[rows, :], up_w[:, at])
        grad_inner = across(c_ref[rows, :], down_w[at, :])
        sigma = 1.0 / (1.0 + jnp.exp(-gate))
        silu = gate * sigma
        inner[at_rows, at] = (silu * upward).astype(low)
        grad_up[at_rows, at] = (grad_inner * silu).astype(low)
        grad_gate[at_rows, at] = (
            grad_inner * upward * sigma * (1.0 + gate * (1.0 - sigma))
        ).astype(low)

    for part in range(2):

        @pl.when((step >= part * tiles // 2) & (step < (part + 1) * tiles // 2))
        def _():
            out_ref, normed_ref = sums[2 * part : 2 * part + 2]

            @pl.loop(0, width // SLAB)
            def _(index):
                at = pl.ds(pl.multiple_of(index * SLAB, SLAB), SLAB)
                out = project(inner[at_rows, :], down_w[:, at])
                normed = across(grad_gate[at_rows, :], gate_w[at, :])
                normed = normed + across(grad_up[at_rows, :], up_w[at, :])
                out_ref[:, at] = out.astype(out_ref.dtype)
                normed_ref[:, at] = normed.astype(normed_ref.dtype)


def ffn_backward(place_ref, k, x_ref, c_ref, middles, stages, turned, turned_units, sent, sems):
    inner, grad_gate, grad_up = middles
    stage_gate, stage_up, stage_down = stages
    width, units = x_ref.shape[1], inner.shape[1]
    depth = place_ref[0] ^ k
    rows, span = width // 4, units // 4
    here = pl.ds(pl.multiple_of(depth * rows, LANES), rows)
    there = pl.ds(pl.multiple_of(depth * span, LANES), span)
    turned[...] = x_ref[:, here].T
    to = pl.ds(pl.multiple_of(k * rows, 16), rows)
    to_units = pl.ds(pl.multiple_of(k * span, 16), span)
    stage_gate[to, :] = project(turned[...], grad_gate[...]).astype(low)
    stage_up[to, :] = project(turned[...], grad_up[...]).astype(low)
    turned_units[...] = inner[:, there].T

    @pl.loop(0, width // FFN_SPAN)
    def _(index):
        at = pl.ds(pl.multiple_of(index * FFN_SPAN, FFN_SPAN), FFN_SPAN)
        stage_down[to_units, at] = project(turned_units[...], c_ref[:, at]).astype(low)

    send_off(place_ref, k, stages, k * 4, FFN_PLAN, FFN_HALF, sent, sems)


def ffn_forward_kernel(tiles, pieces, place_ref, *refs):
    tokens, pieces, refs = refs[:4], refs[4 : 4 + pieces], refs[4 + pieces :]
    sums, middles = refs[:4], refs[4:7]
    x_ref, c_ref, *weights, x_sems, in_sems = refs[7:]
    step = pl.program_id(0)

    @pl.when(step == 0)
    def _():
        load_tokens(x_ref, c_ref, *tokens, x_sems)
        if len(pieces) == 5:
            fetch(place_ref, from_pieces(pieces, FFN_HALF), FFN_PLAN, weights, in_sems)
        else:
            source = from_pieces(pieces[:5], UPPER_ROWS // 2)
            fetch(place_ref, source, UPPER_PLAN, weights, in_sems)
            fetch(place_ref, from_planes(*pieces[5:]), LOWER_PLAN, weights, in_sems)
        drain((x_ref, c_ref), x_sems)
        drain(weights, in_sems)

    ffn_forward(step, tiles, x_ref, c_ref, weights, sums, middles, slice(None))


def ffn_backward_kernel(place_ref, *refs):
    tokens, sources, sent = refs[:4], refs[4:7], refs[7:12]
    x_ref, c_ref, *rest = refs[12:]
    middles, stages, rest = rest[:3], rest[3:6], rest[6:]
    turned, turned_units, x_sems, in_sems, out_sems = rest
    k = pl.program_id(0)

    @pl.when(k == 0)
    def _():
        load_tokens(x_ref, c_ref, *tokens, x_sems)
        for index in (1, 2, 0):
            pltpu.make_async_copy(sources[index], middles[index], in_sems.at[index]).start()
        drain((x_ref, c_ref), x_sems)
        drain(middles, in_sems)

    ffn_backward(
        place_ref, k, x_ref, c_ref, middles, stages, turned, turned_units, sent, out_sems
    )

    @pl.when(k == 3)
    def _():
        drain(sent, out_sems)


FFN_UNITS = 1024


def ffn_sums(count, width):
    last = count // FFN_TILE - 1
    early = pl.BlockSpec((FFN_TILE, width), lambda i, place: (jnp.minimum(i, last), 0))
    late = pl.BlockSpec(
        (FFN_TILE, width), lambda i, place: (jnp.clip(i - last - 1, 0, last), 0)
    )
    pairs = ((low, early), (low, early), (wide, late), (wide, late))
    return [(shaped((count, width), kind), spec) for kind, spec in pairs]


def ffn_scratch(count, width, weights=True, middles=True, stages=True):
    weight = [pltpu.VMEM((width, FFN_UNITS), low)] * 2 + [pltpu.VMEM((FFN_UNITS, width), low)]
    shapes = [pltpu.VMEM((count, width), low)] * 2
    shapes += weight if weights else []
    shapes += [pltpu.VMEM((count, FFN_UNITS), low)] * 3 if middles else []
    if stages:
        shapes += weight
        shapes += [pltpu.VMEM((width // 4, count), low)]
        shapes += [pltpu.VMEM((FFN_UNITS // 4, count), low)]
    shapes += [pltpu.SemaphoreType.DMA((2,)), pltpu.SemaphoreType.DMA((3,))]
    return shapes + ([pltpu.SemaphoreType.DMA((5,))] if stages else [])


def ffn_chunk_forward(place, tokens, pieces, after=()):
    count, width = tokens[0].shape
    tiles = 2 * count // FFN_TILE
    middle = pl.BlockSpec((FFN_TILE, FFN_UNITS), lambda i, place: (i, 0))
    results = run(
        functools.partial(ffn_forward_kernel, tiles, len(pieces)),
        "ffn_forward",
        place,
        (tiles,),
        [(item, anywhere) for item in (*tokens, *pieces)],
        ffn_sums(count, width) + [(shaped((2 * count, FFN_UNITS), low), middle)] * 3,
        ffn_scratch(2 * count, width, middles=False, stages=False),
        after,
        us=36,
    )
    return results[:4], results[4:]


def ffn_chunk_backward(place, tokens, middles, after=()):
    count, width = tokens[0].shape
    return run(
        ffn_backward_kernel,
        "ffn_backward",
        place,
        (4,),
        [(item, anywhere) for item in (*tokens, *middles)],
        sent_shapes(FFN_HALF, SLAB),
        ffn_scratch(2 * count, width, weights=False),
        after,
        us=22,
    )


def input_back_kernel(
    tiles, place_ref, own_q, own_k, own_v, far_q, far_k, far_v, x_own, x_far, w_ref, *refs
):
    grad_ref, own_ref, far_ref, gain_grad = refs
    step = pl.program_id(0)

    @pl.when(step == 0)
    def _():
        gain_grad[...] = jnp.zeros_like(gain_grad)

    def squeezed(query, key, value):
        parts = []
        for ref in (query, key):
            for at in range(0, ref.shape[1], LANES):
                head = ref[:, at : at + LANES].astype(wide)
                parts.append(head[:, :HALF])
                parts.append(head[:, LANES // 2 : LANES // 2 + HALF])
        for at in range(0, value.shape[1], LANES):
            parts.append(value[:, at : at + LANES].astype(wide)[:, :HD])
        return jnp.concatenate(parts, axis=1).astype(low)

    def rest(x_ref, incoming):
        hidden = x_ref[...].astype(wide)
        scale = lax.rsqrt(jnp.mean(hidden * hidden, axis=-1, keepdims=True) + epsilon)
        summed = jnp.sum(incoming * hidden * scale, axis=0, keepdims=True)
        gain_grad[...] += jnp.broadcast_to(summed, gain_grad.shape)

    @pl.when(step < tiles)
    def _():
        grad_ref[...] = squeezed(far_q, far_k, far_v)
        incoming = across(grad_ref[...], w_ref[...])
        far_ref[...] = incoming.astype(low)
        rest(x_far, incoming)

    @pl.when(step >= tiles)
    def _():
        grad_ref[...] = squeezed(own_q, own_k, own_v)
        incoming = across(grad_ref[...], w_ref[...])
        own_ref[...] = incoming
        rest(x_own, incoming)


def input_back(place, own, far, x_own, x_far, weight, after=()):
    count, width = 2 * x_own.shape[0], x_own.shape[1]
    tile = 320
    tiles = count // 2 // tile
    gain_grad = shaped((8, width), wide)

    def late(columns):
        return pl.BlockSpec((tile, columns), lambda i, place: (jnp.maximum(i - tiles, 0), 0))

    def early(columns):
        return pl.BlockSpec((tile, columns), lambda i, place: (jnp.minimum(i, tiles - 1), 0))

    def both(columns):
        return pl.BlockSpec((tile, columns), lambda i, place: (lax.rem(i + tiles, 2 * tiles), 0))

    return run(
        functools.partial(input_back_kernel, tiles),
        "input_back",
        place,
        (2 * tiles,),
        [(item, late(item.shape[1])) for item in own]
        + [(item, early(item.shape[1])) for item in far]
        + [(x_own, late(width)), (x_far, early(width)), (weight, whole(weight))],
        [
            (shaped((count, width), low), both(width)),
            (shaped((count // 2, width), wide), late(width)),
            (shaped((count // 2, width), low), early(width)),
            (gain_grad, whole(gain_grad)),
        ],
        after=after,
        us=15,
    )


def qkv_grad_kernel(place_ref, x_ref, grad_ref, gain_one, gain_two, *refs):
    outs, (stage, gain_rows, turned, sems) = refs[:5], refs[5:]
    k = pl.program_id(0)
    width = grad_ref.shape[1]

    @pl.when(k == 0)
    def _():
        gap = jnp.zeros((8, LANES - HD), wide)
        row = lax.broadcasted_iota(jnp.int32, (16, LANES), 0)
        gain_rows[...] = jnp.zeros_like(gain_rows)
        for block in range(BLOCKS):
            for index, gain in enumerate((gain_one, gain_two)):
                part = jnp.concatenate([gain[:, block * HD : (block + 1) * HD], gap], axis=1)
                part = jnp.where(row == 0, jnp.concatenate([part, part], axis=0), 0.0)
                gain_rows[
                    16 * block : 16 * block + 16, index * LANES : (index + 1) * LANES
                ] = part.astype(low)

    depth = place_ref[0] ^ k
    rows = width // 4
    turned[...] = x_ref[:, pl.ds(pl.multiple_of(depth * rows, LANES), rows)].T
    to = pl.ds(pl.multiple_of(depth * rows, 16), rows)

    @pl.loop(0, width // SLAB)
    def _(index):
        at = pl.ds(pl.multiple_of(index * SLAB, SLAB), SLAB)
        stage[to, at] = project(turned[...], grad_ref[:, at]).astype(low)

    send_off(place_ref, k, (stage, gain_rows), depth * 4, QKV_PLAN, QKV_HALF, outs, sems)

    @pl.when(k == 3)
    def _():
        fill_spare(gain_rows.at[pl.ds(0, 16)], GAINS + 16, 16, QKV_HALF, outs, sems)
        drain(outs, sems)


def qkv_grad(place, x, grad, gain_one, gain_two, after=()):
    count, width = x.shape
    operands = (x, grad, gain_one, gain_two)
    return run(
        qkv_grad_kernel,
        "qkv_grad",
        place,
        (4,),
        [(item, whole(item)) for item in operands],
        sent_shapes(QKV_HALF, SLAB),
        [
            pltpu.VMEM((width, width), low),
            pltpu.VMEM((BLOCKS * 16, SLAB), low),
            pltpu.VMEM((width // 4, count), low),
            pltpu.SemaphoreType.DMA((5,)),
        ],
        after,
        us=15,
    )


def tokens_grad_kernel(place_ref, x_ref, middle_ref, mine_ref, other_ref, gain_ref, out_ref):
    hidden = x_ref[...].astype(wide)
    scale = lax.rsqrt(jnp.mean(hidden * hidden, axis=-1, keepdims=True) + epsilon)
    weighted = (mine_ref[...] + other_ref[...].astype(wide)) * gain_ref[0:1, :]
    inner = jnp.mean(weighted * hidden, axis=-1, keepdims=True)
    out_ref[...] = middle_ref[...] + (scale * weighted - hidden * scale**3 * inner)


def tokens_grad(place, x, grad_middle, mine, other, gains, after=()):
    count, width = x.shape
    tile = 128
    return run(
        tokens_grad_kernel,
        "tokens_grad",
        place,
        (count // tile,),
        [(item, rows_of(tile, width)) for item in (x, grad_middle, mine, other)]
        + [(gains, whole(gains))],
        [(shaped((count, width), wide), rows_of(tile, width))],
        after=after,
    )[0]


def output_kernel(place_ref, middle_ref, mine_0, mine_1, other_0, other_1, out_ref):
    total = middle_ref[...] + mine_0[...] + mine_1[...]
    total = total + other_0[...].astype(wide) + other_1[...].astype(wide)
    out_ref[...] = total.astype(low)


def output_of(place, middle, parts, after=()):
    count, width = middle.shape
    tile = 128
    return run(
        output_kernel,
        "output",
        place,
        (count // tile,),
        [(item, rows_of(tile, width)) for item in (middle, *parts)],
        [(shaped((count, width), low), rows_of(tile, width))],
        after=after,
    )[0]


def swap(array):
    return lax.ppermute(array, "rep", [(0, 1), (1, 0)])


def hop(array, z_flip, y_flip, x_flip):
    flip = (z_flip * 2 + y_flip) * 2 + x_flip
    return lax.ppermute(array, "fsdp", [(chip, chip ^ flip) for chip in range(BLOCKS)])


def hop_x(array):
    return hop(array, 0, 0, 1)


def hop_y(array):
    return hop(array, 0, 1, 0)


def near(line):
    return hop_x(line), hop_y(line)


def pieces_of(blocks):
    cut = blocks.reshape(4, 2, 2, *blocks.shape[1:])
    half = blocks.shape[1] // 2
    far = cut[:, 1, 1]
    return cut[:, 0, 0], cut[:, 0, 1], cut[:, 1, 0], far[:, :half], far[:, half:]


def blocks_of(sent):
    to_x, to_y, late_x, late_y, own = sent
    near_x = jnp.stack([to_x[1], late_x], axis=1)
    near_y = jnp.stack([late_y, to_y[1]], axis=1)
    far = jnp.stack([to_x[0], to_y[0]], axis=1)
    cut = jnp.stack([jnp.stack([own, near_x], 1), jnp.stack([near_y, far], 1)], 1)
    return cut.reshape(BLOCKS, 2 * own.shape[2], own.shape[3])


def layout(length_row, count):
    ends = jnp.cumsum(length_row)
    slots = jnp.arange(count, dtype=jnp.int32)
    passed = (slots[:, None] >= ends[None, :]).astype(jnp.int32)
    segment = jnp.sum(passed, axis=1)
    position = slots - jnp.sum(passed * length_row[None, :], axis=1)
    return position, segment


class Direct:
    def __init__(self, place, weights):
        self.place = place
        self.weights = weights

    def pack_first(self):
        return pack_first(self.place, *self.weights[:4], *self.weights[7:])

    def pack_ffn(self, chunk, parts, after):
        return pack_ffn(self.place, chunk, parts, *self.weights[4:7], after)

    def step_0(self, shard):
        return hop(shard, 2, 0, 0)

    def step_1(self, shard, received, after=()):
        return pair_up(self.place, shard, received, after)

    def step_2(self, pair):
        return hop(pair, 1, 0, 0)

    def step_3(self, pair, received, after=()):
        return line_up(self.place, pair, received, after)

    def step_4(self, line):
        return near(line)

    def step_5(self, line, sides, after=()):
        upper, lower = halves(self.place, *sides, after)
        return (line, *sides, hop_y(upper), hop_x(lower)), upper

    def plane(self, parts, after):
        return plane_up(self.place, parts, after)

    def gate(self, sent, pieces):
        return (*gate(self.place, sent[:2], (*pieces[3:5], pieces[6])), *sent[2:])

    def scatter_1(self, sent):
        return hop_x(sent[0]), hop_y(sent[1])

    def scatter_2(self, sent, got, after):
        late_x, late_y = merge(self.place, sent[2], sent[3], got[0], got[1], after)
        return late_x, (hop_x(late_x), hop_y(late_y))

    def scatter_3(self, groups, after):
        groups = [(sent[4], *got, *more) for sent, got, more in groups]
        kept, kept_far, part = sum_plane(self.place, groups, False, after)
        return kept, (kept_far, hop(part, 1, 0, 0))

    def scatter_4(self, kept, parts, after):
        kept_far, near = parts
        token = sum_pass(self.place, kept_far, near, after)
        return token, (near, hop(token, 2, 0, 0))

    def scatter_34(self, sent, got, more, after):
        kept, *parts = sum_plane(self.place, [(sent[4], *got, *more)], True, after)
        return kept, tuple(hop(part, k + 1, 0, 0) for k, part in enumerate(parts))

    def scatter_5(self, kept, parts, after):
        total, total_low = sum_line(self.place, kept, parts, after)
        return total, swap(total_low)

    def pins(self, arrays):
        return tuple(arrays)

    def finish_ffn(self, chunk_0, chunk_1, shapes, after):
        mine, other = zip(chunk_0, chunk_1)
        return unpack_ffn(self.place, mine, other, shapes, after)

    def finish_first(self, first, chunk_1, shapes, owned, after):
        grads = unpack_first(self.place, (*first, *chunk_1), shapes, after)
        both = first[0][GAINS, : 2 * LANES] + first[1][GAINS, : 2 * LANES].astype(wide)
        return grads, (both[:owned], both[LANES : LANES + owned])


def on_device(
    direct,
    tokens,
    lengths,
    attn_gain,
    w_query,
    w_key,
    w_value,
    w_out,
    ffn_gain,
    w_gate,
    w_up,
    w_down,
    cotangent,
):
    count, width = tokens.shape
    owned = attn_gain.shape[0]
    core = lax.axis_index("rep")
    if direct:
        index = lax.axis_index("fsdp")
        spot = (index // 4, (index // 2) % 2, index % 2)
    else:
        spot = (0, 0, 0)
    place = jnp.stack([jnp.int32(item) for item in (*spot, core)])
    weights = (w_query, w_key, w_value, w_out, w_gate, w_up, w_down, attn_gain, ffn_gain)
    routes = Direct(place, weights) if direct else Whole(place, weights)

    first = routes.pack_first()
    far_tokens, far_cotangent = swap(tokens), swap(cotangent)
    laid = [layout(row, count) for row in (lengths[0], swap(lengths)[0])]
    segment = jnp.stack([item[1] for item in laid])
    cosine, sine = turn_table(jnp.concatenate([item[0] for item in laid]))

    received_first = routes.step_0(first)
    whole_rows = 2 * FFN_HALF
    chunk_a, chunk_b = routes.pack_ffn(1, (UPPER_ROWS, whole_rows - UPPER_ROWS), (first,))
    if direct:
        chunk_b = chunk_b.reshape(1, *chunk_b.shape)
    sides_b = routes.step_4(chunk_b)
    parts_b, token = routes.step_5(chunk_b, sides_b)
    pair_first = routes.step_1(first, received_first, (token,))
    near_first = routes.step_2(pair_first)
    (chunk_0,) = routes.pack_ffn(0, (whole_rows,), (pair_first,))
    received_0 = routes.step_0(chunk_0)
    plane_b = routes.plane(parts_b, (chunk_0,))
    tables = (far_tokens, far_cotangent, segment, cosine, sine)
    line_first = routes.step_3(pair_first, near_first, (*tables, plane_b))
    sides_first = routes.step_4(line_first)
    pair_0 = routes.step_1(chunk_0, received_0, (line_first,))
    near_0 = routes.step_2(pair_0)
    received_a = routes.step_0(chunk_a)
    received_b = routes.step_0(plane_b)
    pieces_first, token = routes.step_5(line_first, sides_first, (pair_0,))
    line_0 = routes.step_3(pair_0, near_0, (token,))
    sides_0 = routes.step_4(line_0)
    w_mine = out_weight(place, pieces_first, tokens.shape[1], (line_0,))
    w_other = [swap(part) for part in w_mine]
    normed_low, queries, keys, values, w_qkv, gains = project_qkv(
        place, tokens, far_tokens, cosine, sine, pieces_first, (w_mine[0],)
    )
    far_mine, far_total = attend(place, queries, keys, values, segment, 1, (keys,))
    own_other = swap(far_mine)
    own_mine, own_total = attend(
        place, queries, keys, values, segment, 0, (far_mine, *w_other)
    )
    far_other = swap(own_mine)
    pair_b = routes.step_1(plane_b, received_b, (own_mine,))
    near_b = routes.step_2(pair_b)
    pieces_0, token = routes.step_5(line_0, sides_0, (pair_b, received_a))
    pair_a = routes.step_1(chunk_a, received_a, (token,))
    near_a = routes.step_2(pair_a)
    middle, normed_own = middle_of(
        place, tokens, own_mine, own_other, w_mine, w_other, gains, (pair_a,)
    )
    normed_far = swap(normed_own)
    line_a = routes.step_3(pair_a, near_a, (normed_own, far_other, *pieces_0[3:]))
    sides_a = routes.step_4(line_a)

    inputs = (normed_own, normed_far, cotangent, far_cotangent)
    sums_0, middles_0 = ffn_chunk_forward(place, inputs, pieces_0, (line_a,))
    out_far_0, norm_far_0 = swap(sums_0[0]), swap(sums_0[1])
    pieces_a, token = routes.step_5(line_a, sides_a, (sums_0[0],))
    planes_b = (pair_b, near_b) if direct else chunk_b
    pieces_1 = (*pieces_a, *planes_b)
    sent_0 = ffn_chunk_backward(place, inputs, middles_0, (token,))
    sent_0 = routes.gate(sent_0, pieces_1)
    got_0 = routes.scatter_1(sent_0)
    sums_1, middles_1 = ffn_chunk_forward(place, inputs, pieces_1, (sent_0[0],))
    out_far_1, norm_far_1 = swap(sums_1[0]), swap(sums_1[1])
    token, more_0 = routes.scatter_2(sent_0, got_0, (sums_1[0], out_far_0))
    sent_1 = ffn_chunk_backward(place, inputs, middles_1, (token,))
    got_1 = routes.scatter_1(sent_1)

    norms = (sums_0[3], sums_1[3], norm_far_0, norm_far_1)
    grad_middle, branch_mine, branch_sent, heads_mine, heads_sent, ffn_gain_grad = middle_back(
        place, middle, norms, cotangent, gains, w_mine, w_other, (sent_1[4], *more_0)
    )
    branch_far, heads_far = swap(branch_sent), swap(heads_sent)
    attended = (queries, keys, values)
    tables = (segment, cosine, sine)
    own_grads = attend_back(place, *attended, heads_mine, own_mine, own_total, *tables, 0)
    sent_out = out_grad(
        place,
        own_mine,
        own_other,
        far_mine,
        far_other,
        branch_mine,
        branch_far,
        (own_grads[0],),
    )
    got_out = routes.scatter_1(sent_out)
    kept_0, parts_0 = routes.scatter_3([(sent_0, got_0, more_0)], (sent_out[4],))
    far_grads = attend_back(
        place, *attended, heads_far, far_mine, far_total, *tables, 1, (kept_0, out_far_1)
    )
    token, more_1 = routes.scatter_2(sent_1, got_1, (far_grads[0], *routes.pins(got_out)))
    token, more_out = routes.scatter_2(sent_out, got_out, (token,))
    token, parts_0 = routes.scatter_4(kept_0, parts_0, (token,))
    grad_qkv, own_part, far_part, attn_gain_grad = input_back(
        place, own_grads, far_grads, tokens, far_tokens, w_qkv, (token,)
    )
    own_rest = swap(far_part)
    groups = [(sent_1, got_1, more_1), (sent_out, got_out, more_out)]
    kept_1, parts_1 = routes.scatter_3(groups, (grad_qkv,))
    pins = (kept_1, *routes.pins(parts_0[1:]))
    sent_qkv = qkv_grad(place, normed_low, grad_qkv, attn_gain_grad, ffn_gain_grad, pins)
    got_qkv = routes.scatter_1(sent_qkv)

    owned_0 = routes.scatter_5(kept_0, parts_0, (sent_qkv[4],))
    outs = (sums_0[2], sums_1[2], out_far_0, out_far_1)
    output = output_of(place, middle, outs, (owned_0[0],))
    token, parts_1 = routes.scatter_4(kept_1, parts_1, (output,))
    token, more_qkv = routes.scatter_2(sent_qkv, got_qkv, (token,))
    grad_tokens = tokens_grad(place, tokens, grad_middle, own_part, own_rest, gains, (token,))
    kept_qkv, parts_qkv = routes.scatter_34(sent_qkv, got_qkv, more_qkv, (grad_tokens,))
    owned_1 = routes.scatter_5(kept_1, parts_1, (kept_qkv,))
    owned_qkv = routes.scatter_5(kept_qkv, parts_qkv, (owned_1[0],))
    shapes = [w_gate.shape, w_up.shape, w_down.shape]
    grad_gate, grad_up, grad_down = routes.finish_ffn(owned_0, owned_1, shapes, (owned_qkv[0],))
    shapes = [w_query.shape, w_key.shape, w_value.shape, w_out.shape]
    grads, gain_grads = routes.finish_first(owned_qkv, owned_1, shapes, owned, (grad_gate,))
    return (
        output,
        grad_tokens,
        gain_grads[0],
        *grads,
        gain_grads[1],
        grad_gate,
        grad_up,
        grad_down,
    )


class Whole:
    def __init__(self, place, weights):
        self.place = place
        query, key, value, out, gate, up, down_w, gain_one, gain_two = weights
        core = place[3]
        self.core = core
        count = query.shape[1] // query.shape[0]
        self.count = count
        rows = query.shape[1] // BLOCKS

        def full(shard):
            return lax.all_gather(shard, "fsdp", axis=0, tiled=True)

        def mine(weight):
            columns = weight.shape[1] // 2
            return lax.dynamic_slice_in_dim(weight, core * columns, columns, axis=1)

        def slabs(weight):
            blocks = weight.reshape(BLOCKS, -1, weight.shape[1])
            return [blocks[:, :, at : at + SLAB] for at in range(0, weight.shape[1], SLAB)]

        qkv = full(jnp.concatenate([mine(query), mine(key), mine(value)], axis=1))
        gain_rows = jnp.zeros((BLOCKS, 16, SLAB), low)
        for index, gain in enumerate((gain_one, gain_two)):
            part = full(gain).reshape(BLOCKS, rows)
            gain_rows = gain_rows.at[:, 0, index * LANES : index * LANES + rows].set(part)
        square = full(mine(out)).reshape(BLOCKS, rows, -1)
        rest = square[:, :, SLAB:]
        rest = jnp.concatenate([rest[:, : rows // 2], rest[:, rows // 2 :]], axis=2)
        parts = slabs(qkv) + [gain_rows, square[:, :, :SLAB], rest]
        self.first = pieces_of(jnp.concatenate(parts, axis=1))
        quarter = down_w.shape[0] // (2 * CHUNKS)
        self.quarter = quarter

        def units(weight, chunk):
            split = weight.reshape(weight.shape[0], count, 2 * CHUNKS, quarter)
            part = lax.dynamic_index_in_dim(split, CHUNKS * core + chunk, 2, keepdims=False)
            return full(part.reshape(weight.shape[0], count * quarter))

        chunks = []
        for chunk in range(CHUNKS):
            at = (CHUNKS * core + chunk) * quarter
            part = full(lax.dynamic_slice_in_dim(down_w, at, quarter, axis=0))
            parts = slabs(units(gate, chunk)) + slabs(units(up, chunk)) + slabs(part)
            chunks.append(jnp.concatenate(parts, axis=1))
        planes = chunks[1][:, UPPER_ROWS:].reshape(4, 4, -1, SLAB)
        self.ffn_0 = (pieces_of(chunks[0]),)
        self.ffn_1 = pieces_of(chunks[1][:, :UPPER_ROWS]), (planes[0::2], planes[1::2])

    def pack_first(self):
        return self.first

    def pack_ffn(self, chunk, parts, after):
        return (self.ffn_0, self.ffn_1)[chunk]

    def step_0(self, shard):
        return shard

    def step_1(self, shard, received, after=()):
        return shard

    def step_2(self, pair):
        return pair

    def step_3(self, pair, received, after=()):
        return pair

    def step_4(self, line):
        return ()

    def step_5(self, line, sides, after=()):
        return line, line

    def plane(self, parts, after):
        return parts

    def gate(self, sent, pieces):
        return sent

    def scatter_1(self, sent):
        return blocks_of(sent)

    def scatter_2(self, sent, got, after):
        return got, got

    def scatter_3(self, groups, after):
        blocks = jnp.concatenate([got for _, got, _ in groups], axis=1)
        return blocks, blocks

    def scatter_34(self, sent, got, more, after):
        return got, ()

    def scatter_4(self, kept, parts, after):
        return kept, kept

    def scatter_5(self, kept, parts, after):
        return kept, kept

    def split(self, blocks, widths):
        parts, row = [], 0
        for rows, slabs in widths:
            taken = []
            for _ in range(slabs):
                taken.append(blocks[:, row : row + rows])
                row += rows
            part = jnp.concatenate(taken, axis=2)
            part = part.reshape(BLOCKS * rows, part.shape[2])
            parts.append(lax.psum_scatter(part, "fsdp", scatter_dimension=0, tiled=True))
        return parts

    def ordered(self, part):
        other = swap(part).astype(wide)
        part = part.astype(wide)
        first = jnp.where(self.core == 0, part, other)
        return first, jnp.where(self.core == 0, other, part)

    def pins(self, arrays):
        return ()

    def finish_ffn(self, chunk_0, chunk_1, shapes, after):
        gates, ups, downs = [], [], []
        for blocks, _ in (chunk_0, chunk_1):
            gate, up, down_w = self.split(blocks, ((96, 2), (96, 2), (64, 3)))
            gates.append(self.ordered(gate))
            ups.append(self.ordered(up))
            downs.append(self.ordered(down_w))

        def columns(pairs):
            parts = [pairs[chunk][owner] for owner in range(2) for chunk in range(CHUNKS)]
            rows = parts[0].shape[0]
            parts = [part.reshape(rows, self.count, self.quarter) for part in parts]
            return jnp.stack(parts, axis=2).reshape(rows, -1)

        grad_down = [downs[chunk][owner] for owner in range(2) for chunk in range(CHUNKS)]
        return columns(gates), columns(ups), jnp.concatenate(grad_down, axis=0)

    def finish_first(self, first, chunk_1, shapes, owned, after):
        mine = first[0]
        (qkv,) = self.split(mine[:, :GAINS], ((96, 3),))
        blocks = chunk_1[0][:, 2 * FFN_HALF :]
        rest = blocks[:, 96:144]
        rest = jnp.concatenate([rest[:, :, :256], rest[:, :, 256:]], axis=1)
        (square,) = self.split(jnp.concatenate([blocks[:, :96], rest], axis=2), ((96, 1),))
        pair = self.ordered(qkv)
        grads, at = [], 0
        for shape in shapes[:3]:
            columns = shape[1] // 2
            grads.append(jnp.concatenate([item[:, at : at + columns] for item in pair], axis=1))
            at += columns
        grads.append(jnp.concatenate(self.ordered(square), axis=1))
        rows = mine[:, GAINS, : 2 * LANES].astype(wide)
        rows = rows + swap(rows)
        gains = []
        for index in range(2):
            gain = rows[:, index * LANES : index * LANES + 96].reshape(-1)
            gains.append(lax.psum_scatter(gain, "fsdp", scatter_dimension=0, tiled=True))
        return grads, gains


def solution(mesh):
    rows = P(("rep", "fsdp"), None)
    split = P("fsdp", None)
    gain = P("fsdp")
    return jax.shard_map(
        functools.partial(on_device, mesh.shape["fsdp"] == BLOCKS),
        mesh=mesh,
        in_specs=(rows, rows, gain) + (split,) * 4 + (gain,) + (split,) * 3 + (rows,),
        out_specs=(rows, rows, gain) + (split,) * 4 + (gain,) + (split,) * 3,
        check_vma=False,
    )
```

```python
import functools

import jax
import jax.numpy as jnp
from jax import lax
from jax.experimental import pallas as pl
from jax.experimental.pallas import tpu as pltpu
from jax.sharding import PartitionSpec as P

H = 16
KV = 8
HD = 96
HALF = HD // 2
LANES = 128
BLOCKS = 16
TILE = 128
SLAB = 512
CHUNKS = 2
COST_SCALE = 0.001

epsilon = 1e-05
rope_base = 100000.0
masked_score = -1e30
low = jnp.bfloat16
wide = jnp.float32


def whole(array, buffers=1):
    zeros = (0,) * array.ndim
    mode = pl.Buffered(buffers)
    return pl.BlockSpec(array.shape, lambda *at: zeros, pipeline_mode=mode)


def rows_of(tile, width, first=0):
    return pl.BlockSpec((tile, width), lambda i, place: (first + i, 0))


def shaped(shape, dtype):
    return jax.ShapeDtypeStruct(shape, dtype)


anywhere = pl.BlockSpec(memory_space=pl.ANY)


def run(kernel, name, place, grid, operands, outs, scratch=(), after=(), vmem=56, us=4):
    after = [item for item in after if isinstance(item, jax.Array)]
    count, extra = len(operands), len(after)

    def body(place_ref, *refs):
        kernel(place_ref, *refs[:count], *refs[count + extra :])

    return pl.pallas_call(
        body,
        grid_spec=pltpu.PrefetchScalarGridSpec(
            num_scalar_prefetch=1,
            grid=grid,
            in_specs=[spec for _, spec in operands] + [anywhere] * extra,
            out_specs=[spec for _, spec in outs],
            scratch_shapes=list(scratch),
        ),
        out_shape=[shape for shape, _ in outs],
        compiler_params=pltpu.CompilerParams(vmem_limit_bytes=vmem * 2**20),
        cost_estimate=pl.CostEstimate(
            flops=0, bytes_accessed=int(us * COST_SCALE * 3.3e6), transcendentals=0
        ),
        name=name,
    )(place, *[array for array, _ in operands], *after)


def across(left, right):
    return lax.dot_general(left, right, (((1,), (1,)), ((), ())), preferred_element_type=wide)


def down(left, right):
    return lax.dot_general(left, right, (((0,), (0,)), ((), ())), preferred_element_type=wide)


def project(left, right):
    return jnp.dot(left, right, preferred_element_type=wide)


class Slab:
    def __init__(self, matrix, row, rows, stride, offset, column, width=SLAB, lane=0):
        self.matrix, self.row, self.rows = matrix, row, rows
        self.stride, self.offset = stride, offset
        self.column, self.width, self.lane = column, width, lane

    def of(self, refs, block):
        rows = pl.ds(pl.multiple_of(block * self.stride + self.offset, 16), self.rows)
        return refs[self.matrix].at[rows, pl.ds(self.column, self.width)]

    def lanes(self):
        return pl.ds(self.lane, self.width)


FIRST_HALF, FFN_HALF, QKV_HALF, OUT_HALF = 224, 288, 160, 80


def square_plan(half):
    plan = []
    for slab in range(3):
        top, bottom = slab * 96, slab * 96 + 96
        for first, last in ((top, min(bottom, half)), (max(top, half), bottom)):
            if first < last:
                plan.append(Slab(0, first, last - first, 96, first - top, slab * SLAB))
    return plan


def out_plan(start, half):
    plan = []
    for first, last in ((start, min(start + 96, half)), (max(start, half), start + 96)):
        if first < last:
            plan.append(Slab(0, first, last - first, LANES, first - start, 0))
    for part in range(2):
        plan.append(Slab(0, start + 96, 48, LANES, part * 48, SLAB, 256, part * 256))
    return plan


GAINS = 288
GAIN_SLAB = Slab(1, GAINS, 16, 16, 0, 0)
FIRST_QKV_PLAN = square_plan(FIRST_HALF) + [GAIN_SLAB]
FIRST_OUT_PLAN = out_plan(GAINS + 16, FIRST_HALF)
QKV_PLAN = square_plan(QKV_HALF) + [GAIN_SLAB]
OUT_PLAN = out_plan(0, OUT_HALF)
FFN_PLAN = [
    Slab(0, 0, 96, 96, 0, 0),
    Slab(0, 96, 96, 96, 0, SLAB),
    Slab(1, 192, 96, 96, 0, 0),
    Slab(1, 288, 96, 96, 0, SLAB),
    Slab(2, 384, 64, 64, 0, 0),
    Slab(2, 448, 64, 64, 0, SLAB),
    Slab(2, 512, 64, 64, 0, 2 * SLAB),
]
UPPER_ROWS = 384
UPPER_PLAN, LOWER_PLAN = FFN_PLAN[:4], [
    Slab(2, slab * 64, 64, 64, 0, slab * SLAB) for slab in range(3)
]


def block_index(place_ref, k, dy, dx):
    z, y, x = place_ref[0], place_ref[1], place_ref[2]
    return ((z ^ k) * 2 + (y ^ dy)) * 2 + (x ^ dx)


def from_pieces(pieces, half):
    def source(k, dy, dx, slab):
        at = pl.ds(slab.row, slab.rows)
        piece = pieces[dy * 2 + dx]
        if dy and dx:
            part = int(slab.row >= half)
            at = pl.ds(slab.row - part * half, slab.rows)
            piece = pieces[3 + part]
        return piece.at[k, at, slab.lanes()]

    return source


def from_planes(pair, other):
    def source(k, dy, dx, slab):
        planes = other if k % 2 else pair
        return planes.at[k // 2, dy * 2 + dx, pl.ds(slab.row, slab.rows), slab.lanes()]

    return source


def fetch(place_ref, source, plan, matrices, sems):
    for k in range(4):
        for dy in range(2):
            for dx in range(2):
                block = block_index(place_ref, k, dy, dx)
                for slab in plan:
                    pltpu.make_async_copy(
                        source(k, dy, dx, slab), slab.of(matrices, block), sems.at[slab.matrix]
                    ).start()


def send_off(place_ref, k, matrices, stride_base, plan, half, outs, sems):
    to_x, to_y, late_x, late_y, own = range(5)
    for dy in range(2):
        for dx in range(2):
            block = block_index(place_ref, place_ref[0], dy, dx) + stride_base
            for slab in plan:
                part = int(slab.row >= half)
                at = pl.ds(slab.row - part * half, slab.rows)
                if (dy, dx) == (0, 0):
                    which, index = own, (k, part)
                elif dy and dx:
                    which, index = (to_y if part else to_x), (0, k)
                elif part == dy:
                    which, index = (to_y if dy else to_x), (1, k)
                else:
                    which, index = (late_y if dy else late_x), (k,)
                target = outs[which].at[(*index, at, slab.lanes())]
                pltpu.make_async_copy(slab.of(matrices, block), target, sems.at[which]).start()


def fill_spare(source, row, rows, half, outs, sems):
    at = pl.ds(row - half, rows)
    for k in range(4):
        for which, index in ((1, (0, k)), (1, (1, k)), (2, (k,)), (4, (k, 1))):
            target = outs[which].at[(*index, at)]
            pltpu.make_async_copy(source, target, sems.at[which]).start()


def drain(refs, sems):
    for index, ref in enumerate(refs):
        pltpu.make_async_copy(ref, ref, sems.at[index]).wait()


def sent_shapes(half, width):
    shapes = [(2, 4, half, width)] * 2 + [(4, half, width)] * 2 + [(4, 2, half, width)]
    return [(shaped(shape, low), anywhere) for shape in shapes]


def gate_kernel(place_ref, *refs):
    pass


def gate(place, arrays, after):
    count, extra = len(arrays), len(after)
    return pl.pallas_call(
        gate_kernel,
        grid_spec=pltpu.PrefetchScalarGridSpec(
            num_scalar_prefetch=1,
            grid=(1,),
            in_specs=[anywhere] * (count + extra),
            out_specs=[anywhere] * count,
        ),
        out_shape=[shaped(array.shape, array.dtype) for array in arrays],
        input_output_aliases={1 + index: index for index in range(count)},
        cost_estimate=pl.CostEstimate(flops=0, bytes_accessed=0, transcendentals=0),
        name="gate",
    )(place, *arrays, *after)


def pair_kernel(place_ref, own, far, out, sems):
    copies = [
        pltpu.make_async_copy(ref, out.at[k], sems.at[k]) for k, ref in enumerate((own, far))
    ]
    for copy in copies:
        copy.start()
    for copy in copies:
        copy.wait()


def pair_up(place, own, far, after=()):
    out = shaped((2, *own.shape), low)
    return run(
        pair_kernel,
        "pair",
        place,
        (1,),
        [(own, anywhere), (far, anywhere)],
        [(out, whole(out))],
        [pltpu.SemaphoreType.DMA((2,))],
        after,
        us=2,
    )[0]


def line_kernel(place_ref, pair, near, out, sems):
    copies = []
    for k in range(4):
        ref = near if k % 2 else pair
        copies.append(pltpu.make_async_copy(ref.at[k // 2], out.at[k], sems.at[k]))
        copies[-1].start()
    for copy in copies:
        copy.wait()


def line_up(place, pair, near, after=()):
    _, rows, width = pair.shape
    out = shaped((4, rows, width), low)
    return run(
        line_kernel,
        "line",
        place,
        (1,),
        [(pair, anywhere), (near, anywhere)],
        [(out, whole(out))],
        [pltpu.SemaphoreType.DMA((4,))],
        after,
        us=4,
    )[0]


def plane_kernel(place_ref, own, from_x, from_y, upper, lower, out, sems):
    half = upper.shape[1]
    parts = [
        (own, out.at[pl.ds(0, 1)]),
        (from_x, out.at[pl.ds(1, 1)]),
        (from_y, out.at[pl.ds(2, 1)]),
        (upper, out.at[pl.ds(3, 1), pl.ds(0, half)]),
        (lower, out.at[pl.ds(3, 1), pl.ds(half, half)]),
    ]
    copies = [
        pltpu.make_async_copy(source, target, sems.at[index])
        for index, (source, target) in enumerate(parts)
    ]
    for copy in copies:
        copy.start()
    for copy in copies:
        copy.wait()


def plane_up(place, parts, after):
    _, rows, width = parts[0].shape
    out = shaped((4, rows, width), low)
    return run(
        plane_kernel,
        "plane",
        place,
        (1,),
        [(part, anywhere) for part in parts],
        [(out, whole(out))],
        [pltpu.SemaphoreType.DMA((5,))],
        after,
        us=2,
    )[0]


def halves_kernel(place_ref, from_x, from_y, upper, lower, sems):
    half = upper.shape[1]
    copies = (
        pltpu.make_async_copy(from_x.at[:, pl.ds(0, half)], upper, sems.at[0]),
        pltpu.make_async_copy(from_y.at[:, pl.ds(half, half)], lower, sems.at[1]),
    )
    for copy in copies:
        copy.start()
    for copy in copies:
        copy.wait()


def halves(place, from_x, from_y, after):
    count, rows, width = from_x.shape
    out = shaped((count, rows // 2, width), low)
    return run(
        halves_kernel,
        "halves",
        place,
        (1,),
        [(from_x, anywhere), (from_y, anywhere)],
        [(out, whole(out))] * 2,
        [pltpu.SemaphoreType.DMA((2,))],
        after,
        us=2,
    )


def step_rows(half):
    return next(rows for rows in (96, 80, 48, 368) if half % rows == 0)


def merge_kernel(place_ref, late_x, late_y, got_x, got_y, out_x, out_y):
    out_x[...] = late_x[...] + got_y[0]
    out_y[...] = late_y[...] + got_x[0]


def merge(place, late_x, late_y, got_x, got_y, after):
    shape = late_x.shape
    rows = step_rows(shape[1])
    spec = pl.BlockSpec((4, rows, shape[2]), lambda i, place: (0, i, 0))
    got = pl.BlockSpec((1, 4, rows, shape[2]), lambda i, place: (0, 0, i, 0))
    return run(
        merge_kernel,
        "merge",
        place,
        (shape[1] // rows,),
        [(late_x, spec), (late_y, spec), (got_x, got), (got_y, got)],
        [(shaped(shape, low), spec)] * 2,
        after=after,
    )


def sum_kernel(direct, groups, place_ref, *refs):
    ins, (kept, *outs) = refs[: 5 * groups], refs[5 * groups :]
    step = pl.program_id(0)
    for k in range(4):

        @pl.when(step == k)
        def _():
            row = 0
            for group in range(groups):
                own, got_x, got_y, more_x, more_y = ins[5 * group : 5 * group + 5]
                at = slice(row, row + own.shape[2])
                row += own.shape[2]
                upper = own[0, 0].astype(wide) + got_x[0, 0].astype(wide)
                upper = upper + more_y[0].astype(wide)
                lower = own[0, 1].astype(wide) + got_y[0, 0].astype(wide)
                lower = lower + more_x[0].astype(wide)
                if k == 0:
                    ref = kept
                elif direct:
                    ref = outs[k - 1]
                else:
                    ref = outs[1].at[0] if k % 2 else outs[0]
                ref[0, at, :], ref[1, at, :] = upper.astype(ref.dtype), lower.astype(ref.dtype)


def sum_plane(place, groups, direct, after):
    operands = []
    for own, got_x, got_y, more_x, more_y in groups:
        _, _, half, width = own.shape
        got = pl.BlockSpec((1, 1, half, width), lambda k, place: (1, k, 0, 0))
        more = pl.BlockSpec((1, half, width), lambda k, place: (k, 0, 0))
        operands += [
            (own, pl.BlockSpec((1, 2, half, width), lambda k, place: (k, 0, 0, 0))),
            (got_x, got),
            (got_y, got),
            (more_x, more),
            (more_y, more),
        ]
    half = sum(group[0].shape[2] for group in groups)
    out = pl.BlockSpec((2, half, width), lambda k, place: (0, 0, 0))
    both = pl.BlockSpec((1, 2, half, width), lambda k, place: (k // 2, 0, 0, 0))
    outs = [(shaped((2, half, width), wide), out)]
    if direct:
        outs += [(shaped((2, half, width), low), out)] * 3
    else:
        outs += [(shaped((2, half, width), wide), out)]
        outs += [(shaped((2, 2, half, width), low), both)]
    return run(
        functools.partial(sum_kernel, direct, len(groups)),
        "sum_plane",
        place,
        (4,),
        operands,
        outs,
        after=after,
        us=5,
    )


def pass_kernel(place_ref, kept_far, near, out):
    out[...] = (kept_far[...] + near[0].astype(wide)).astype(low)


def sum_pass(place, kept_far, near, after):
    _, half, width = kept_far.shape
    rows = step_rows(half)
    spec = pl.BlockSpec((2, rows, width), lambda i, place: (0, i, 0))
    second = pl.BlockSpec((1, 2, rows, width), lambda i, place: (1, 0, i, 0))
    return run(
        pass_kernel,
        "sum_pass",
        place,
        (half // rows,),
        [(kept_far, spec), (near, second)],
        [(shaped(kept_far.shape, low), spec)],
        after=after,
        us=3,
    )[0]


def total_kernel(place_ref, kept, *refs):
    *received, out, out_low = refs
    total = kept[...]
    for ref in received:
        part = ref[0] if len(ref.shape) > len(kept.shape) else ref[...]
        total = total + part.astype(wide)
    out[...] = total
    out_low[...] = total.astype(low)


def sum_line(place, kept, received, after):
    _, half, width = kept.shape
    rows = step_rows(half)
    spec = pl.BlockSpec((2, rows, width), lambda i, place: (0, i, 0))
    first = pl.BlockSpec((1, 2, rows, width), lambda i, place: (0, 0, i, 0))
    total, total_low = run(
        total_kernel,
        "sum_line",
        place,
        (half // rows,),
        [(kept, spec)] + [(item, first if item.ndim == 4 else spec) for item in received],
        [(shaped(kept.shape, wide), spec), (shaped(kept.shape, low), spec)],
        after=after,
        us=4,
    )
    return total.reshape(2 * half, width), total_low.reshape(2 * half, width)


def pack_first_kernel(place_ref, query, key, value, square, gain_one, gain_two, out):
    core = place_ref[3]

    def mine(ref):
        columns = ref.shape[1] // 2
        return ref[:, pl.ds(pl.multiple_of(core * columns, LANES), columns)]

    packed = jnp.concatenate([mine(query), mine(key), mine(value)], axis=1)
    rows = packed.shape[0]
    for slab in range(3):
        out[slab * rows : (slab + 1) * rows, :] = packed[:, slab * SLAB : (slab + 1) * SLAB]
    row = lax.broadcasted_iota(jnp.int32, (16, LANES), 0)
    gap = jnp.zeros((16, LANES - rows), wide)
    out[GAINS : GAINS + 16, :] = jnp.zeros((16, SLAB), low)
    for index, gain in enumerate((gain_one, gain_two)):
        spread = jnp.broadcast_to(gain[...].astype(wide), (16, rows))
        spread = jnp.where(row == 0, jnp.concatenate([spread, gap], axis=1), 0.0)
        out[GAINS : GAINS + 16, index * LANES : (index + 1) * LANES] = spread.astype(low)
    at, packed = GAINS + 16, mine(square)
    out[at : at + rows, :] = packed[:, :SLAB]
    for part in range(2):
        out[at + rows :, part * 256 : (part + 1) * 256] = packed[
            part * rows // 2 : (part + 1) * rows // 2, SLAB:
        ]


def pack_first(place, query, key, value, square, gain_one, gain_two):
    operands = [query, key, value, square, gain_one.reshape(1, -1), gain_two.reshape(1, -1)]
    out = shaped((2 * FIRST_HALF, SLAB), low)
    return run(
        pack_first_kernel,
        "pack_first",
        place,
        (1,),
        [(item, whole(item)) for item in operands],
        [(out, whole(out))],
    )[0]


def interleave(even, odd):
    lane = lax.broadcasted_iota(jnp.int32, even.shape, 1)
    left = jnp.where(lane < LANES // 2, even, pltpu.roll(odd, LANES // 2, 1))
    right = jnp.where(lane < LANES // 2, pltpu.roll(even, LANES // 2, 1), odd)
    return left, right


def pack_ffn_kernel(chunk, place_ref, gate, up, down_w, *outs):
    core = place_ref[3]
    rows = gate.shape[0]

    def put(at, size, column, part):
        span, width = outs[0].shape[0], part.shape[1]
        out, at = (outs[0], at) if at < span else (outs[1], at - span)
        out[at : at + size, column : column + width] = part

    for matrix, ref in enumerate((gate, up)):
        for pair in range(8):
            windows = [
                ref[:, pl.ds(pl.multiple_of((2 * pair + odd) * 256 + core * LANES, LANES), LANES)]
                for odd in range(2)
            ]
            packed = interleave(windows[0].astype(wide), windows[1].astype(wide))[chunk]
            at = (matrix * 2 + pair // 4) * rows
            column = pair % 4 * LANES
            put(at, rows, column, packed.astype(low))
    units = down_w[pl.ds(pl.multiple_of(core * LANES + chunk * 64, 64), 64), :]
    for slab in range(3):
        at = 4 * rows + slab * 64
        put(at, 64, 0, units[:, slab * SLAB : (slab + 1) * SLAB])


def pack_ffn(place, chunk, parts, gate, up, down_w, after):
    outs = [shaped((rows, SLAB), low) for rows in parts]
    return run(
        functools.partial(pack_ffn_kernel, chunk),
        "pack_ffn",
        place,
        (1,),
        [(item, whole(item)) for item in (gate, up, down_w)],
        [(out, whole(out)) for out in outs],
        after=after,
    )


def rows_in(ref, at, rows):
    if at >= FFN_HALF:
        at += ref.shape[0] // 2 - FFN_HALF
    return ref[at : at + rows, :]


def unpack_ffn_kernel(place_ref, mine_0, mine_1, other_0, other_1, gate, up, down_w):
    core = place_ref[3]
    rows = gate.shape[0]
    for owner, chunks in ((core, (mine_0, mine_1)), (1 - core, (other_0, other_1))):
        for matrix, ref in enumerate((gate, up)):
            for pair in range(8):
                at = (matrix * 2 + pair // 4) * rows
                column = pair % 4 * LANES
                parts = [
                    rows_in(chunk, at, rows)[:, column : column + LANES].astype(wide)
                    for chunk in chunks
                ]
                for odd, window in enumerate(interleave(*parts)):
                    place = (2 * pair + odd) * 256 + owner * LANES
                    ref[:, pl.ds(pl.multiple_of(place, LANES), LANES)] = window
        for index, chunk in enumerate(chunks):
            for slab in range(3):
                at = 4 * rows + slab * 64
                place = pl.multiple_of(owner * LANES + index * 64, 64)
                part = rows_in(chunk, at, 64).astype(wide)
                down_w[pl.ds(place, 64), slab * SLAB : (slab + 1) * SLAB] = part


def unpack_ffn(place, mine, other, shapes, after):
    outs = [shaped(shape, wide) for shape in shapes]
    return run(
        unpack_ffn_kernel,
        "unpack_ffn",
        place,
        (1,),
        [(item, whole(item)) for item in (*mine, *other)],
        [(out, whole(out)) for out in outs],
        after=after,
    )


def unpack_first_kernel(
    place_ref, mine, other, joint_mine, joint_other, query, key, value, square
):
    core = place_ref[3]
    rows = query.shape[0]

    def put(ref, owner, part):
        columns = ref.shape[1] // 2
        at = pl.ds(pl.multiple_of(owner * columns, LANES), columns)
        ref[:, at] = part.astype(wide)

    for owner, qkv, joint in ((core, mine, joint_mine), (1 - core, other, joint_other)):
        slabs = [qkv[slab * rows : (slab + 1) * rows, :] for slab in range(3)]
        put(query, owner, jnp.concatenate([slabs[0], slabs[1][:, :256]], axis=1))
        put(key, owner, jnp.concatenate([slabs[1][:, 256:], slabs[2][:, :128]], axis=1))
        put(value, owner, slabs[2][:, 128:])
        half = FFN_HALF + OUT_HALF
        out = [joint[part * half + FFN_HALF : (part + 1) * half, :] for part in range(2)]
        out = jnp.concatenate(out, axis=0)
        rest = out[rows : rows + rows // 2, :]
        rest = jnp.concatenate([rest[:, :256], rest[:, 256:]], axis=0)
        put(square, owner, jnp.concatenate([out[:rows, :], rest], axis=1))


def unpack_first(place, parts, shapes, after):
    outs = [shaped(shape, wide) for shape in shapes]
    return run(
        unpack_first_kernel,
        "unpack_first",
        place,
        (1,),
        [(item, whole(item)) for item in parts],
        [(out, whole(out)) for out in outs],
        after=after,
    )


def turn_table(position):
    frequency = rope_base ** (-jnp.arange(HALF, dtype=wide) * 2.0 / HD)
    angle = position.astype(wide)[:, None] * frequency[None, :]
    gap = jnp.zeros((position.shape[0], LANES // 2 - HALF), wide)
    cosine, sine = jnp.cos(angle), jnp.sin(angle)
    return (
        jnp.concatenate([cosine, gap, cosine, gap], axis=1),
        jnp.concatenate([-sine, gap, sine, gap], axis=1),
    )


def qkv_kernel(tiles, place_ref, own_ref, far_ref, cos_ref, sin_ref, *refs):
    pieces = refs[:5]
    normed_ref, q_ref, k_ref, v_ref, w_ref, gain_ref, gain_rows, x_ref, sems = refs[5:]
    step = pl.program_id(0)

    @pl.when(step < tiles)
    def _():
        x_ref[...] = own_ref[...]

    @pl.when(step >= tiles)
    def _():
        x_ref[...] = far_ref[...]

    @pl.when(pl.program_id(0) == 0)
    def _():
        fetch(
            place_ref, from_pieces(pieces, FIRST_HALF), FIRST_QKV_PLAN, (w_ref, gain_rows), sems
        )
        drain((w_ref, gain_rows), sems)
        for index in range(2):
            parts = [
                gain_rows[16 * block : 16 * block + 16, index * LANES : (index + 1) * LANES]
                for block in range(BLOCKS)
            ]
            parts = [part.astype(wide)[:8, :HD] for part in parts]
            gain_ref[8 * index : 8 * index + 8, :] = jnp.concatenate(parts, axis=1)

    hidden = x_ref[...].astype(wide)
    scale = lax.rsqrt(jnp.mean(hidden * hidden, axis=-1, keepdims=True) + epsilon)
    normed = (hidden * scale * gain_ref[0:1, :]).astype(low)
    normed_ref[...] = normed
    gap = jnp.zeros((x_ref.shape[0], LANES // 2 - HALF), wide)
    heads = q_ref.shape[1] // LANES
    groups = k_ref.shape[1] // LANES
    count = 4
    for first in range(0, heads + 2 * groups, count):
        part = project(normed, w_ref[:, first * HD : (first + count) * HD])
        for index in range(first, first + count):
            at = (index - first) * HD
            if index >= heads + groups:
                column = (index - heads - groups) * LANES
                padded = jnp.concatenate([part[:, at : at + HD], gap, gap], axis=1)
                v_ref[:, column : column + LANES] = padded.astype(low)
                continue
            padded = jnp.concatenate(
                [part[:, at : at + HALF], gap, part[:, at + HALF : at + HD], gap], axis=1
            )
            turned = pltpu.roll(padded, LANES // 2, 1)
            padded = (padded * cos_ref[...] + turned * sin_ref[...]).astype(low)
            if index < heads:
                q_ref[:, index * LANES : (index + 1) * LANES] = padded
            else:
                column = (index - heads) * LANES
                k_ref[:, column : column + LANES] = padded


def project_qkv(place, own, far, cosine, sine, pieces, after):
    count, width = own.shape
    tile = 320
    tiles = count // tile
    count = 2 * count
    heads, groups = H // 2 * LANES, KV // 2 * LANES
    weight, gains = shaped((width, width), low), shaped((16, width), wide)
    early = pl.BlockSpec((tile, width), lambda i, place: (jnp.minimum(i, tiles - 1), 0))
    late = pl.BlockSpec((tile, width), lambda i, place: (jnp.maximum(i - tiles, 0), 0))
    return run(
        functools.partial(qkv_kernel, tiles),
        "project_qkv",
        place,
        (count // tile,),
        [
            (own, early),
            (far, late),
            (cosine, rows_of(tile, LANES)),
            (sine, rows_of(tile, LANES)),
        ]
        + [(piece, anywhere) for piece in pieces],
        [
            (shaped((count, width), low), rows_of(tile, width)),
            (shaped((count, heads), low), rows_of(tile, heads)),
            (shaped((count, groups), low), rows_of(tile, groups)),
            (shaped((count, groups), low), rows_of(tile, groups)),
            (weight, whole(weight)),
            (gains, whole(gains)),
        ],
        [
            pltpu.VMEM((BLOCKS * 16, SLAB), low),
            pltpu.VMEM((tile, width), low),
            pltpu.SemaphoreType.DMA((2,)),
        ],
        after,
        us=18,
    )


def fill_bias(bias_ref, column_ref, row_ref):
    size = bias_ref.shape[0]
    for start in range(0, size, TILE):
        shape = (TILE, size)
        slots = lax.broadcasted_iota(jnp.int32, shape, 0) + start
        keys = lax.broadcasted_iota(jnp.int32, shape, 1)
        same = column_ref[start : start + TILE, :] == row_ref[0]
        allowed = same & (keys <= slots)
        bias_ref[start : start + TILE, :] = jnp.where(allowed, 0.0, masked_score)


LOG2_E = 1.4426950408889634


def both_heads(ref, start):
    rows = slice(start, start + TILE)
    return jnp.concatenate([ref[rows, :LANES], ref[rows, LANES:]], axis=0)


def attend_kernel(
    place_ref, q_ref, k_ref, v_ref, column_ref, row_ref, out_ref, total_ref, bias_ref
):
    group = pl.program_id(0)
    size = q_ref.shape[0]

    @pl.when(group == 0)
    def _():
        fill_bias(bias_ref, column_ref, row_ref)
        total_ref[...] = jnp.zeros_like(total_ref)

    lane = lax.broadcasted_iota(jnp.int32, (TILE, LANES), 1)
    for start in range(0, size, TILE):
        stop = start + TILE
        raw = across(both_heads(q_ref, start), k_ref[:stop, :])
        bias = bias_ref[start:stop, :stop]
        scores = raw * (HD ** (-0.5) * LOG2_E) + jnp.concatenate([bias, bias], axis=0)
        top = jnp.max(scores, axis=-1, keepdims=True)
        powers = jnp.exp2(scores - top)
        amount = jnp.sum(powers, axis=-1, keepdims=True)
        probs = (powers * (1.0 / amount)).astype(low)
        mixed = project(probs, v_ref[:stop, :]).astype(low)
        total = top + jnp.log2(amount)
        kept = total_ref[start:stop, :]
        for head in range(2):
            rows = slice(head * TILE, (head + 1) * TILE)
            out_ref[start:stop, head * LANES : (head + 1) * LANES] = mixed[rows]
            kept = jnp.where(lane == 2 * group + head, total[rows], kept)
        total_ref[start:stop, :] = kept


def attention_specs(size, block):
    return dict(
        pair=pl.BlockSpec((size, 2 * LANES), lambda g, place: (block, g)),
        one=pl.BlockSpec((size, LANES), lambda g, place: (block, g)),
        pair_alone=pl.BlockSpec((size, 2 * LANES), lambda g, place: (0, g)),
        one_alone=pl.BlockSpec((size, LANES), lambda g, place: (0, g)),
        shared=pl.BlockSpec((size, LANES), lambda g, place: (block, 0)),
        alone=pl.BlockSpec((size, LANES), lambda g, place: (0, 0)),
        column=pl.BlockSpec((size, 1), lambda g, place: (block, 0)),
        row=pl.BlockSpec((1, 1, size), lambda g, place: (block, 0, 0)),
    )


def attend(place, q, k, v, segment, block, after=()):
    blocks, size = segment.shape
    spec = attention_specs(size, block)
    return run(
        attend_kernel,
        "attend",
        place,
        (k.shape[1] // LANES,),
        [
            (q, spec["pair"]),
            (k, spec["one"]),
            (v, spec["one"]),
            (segment.reshape(blocks * size, 1), spec["column"]),
            (segment.reshape(blocks, 1, size), spec["row"]),
        ],
        [
            (shaped((size, q.shape[1]), low), spec["pair_alone"]),
            (shaped((size, LANES), wide), spec["alone"]),
        ],
        [pltpu.VMEM((size, size), wide)],
        after,
        us=17,
    )


def attend_back_kernel(
    place_ref,
    q_ref,
    k_ref,
    v_ref,
    grad_ref,
    out_ref,
    total_ref,
    column_ref,
    row_ref,
    cos_ref,
    sin_ref,
    dq_ref,
    dk_ref,
    dv_ref,
    bias_ref,
    dk_sum,
    dv_sum,
):
    group = pl.program_id(0)
    size = q_ref.shape[0]

    @pl.when(group == 0)
    def _():
        fill_bias(bias_ref, column_ref, row_ref)

    def turned_back(grad, rows):
        turned = pltpu.roll(grad, LANES // 2, 1)
        return (grad * cos_ref[rows, :] - turned * sin_ref[rows, :]).astype(low)

    dk_sum[...] = jnp.zeros_like(dk_sum)
    dv_sum[...] = jnp.zeros_like(dv_sum)
    lane = lax.broadcasted_iota(jnp.int32, (TILE, LANES), 1)
    scale = HD ** (-0.5)
    for start in range(0, size, TILE):
        stop = start + TILE
        queries, grads = both_heads(q_ref, start), both_heads(grad_ref, start)
        mixed = both_heads(out_ref, start)
        delta = jnp.sum(grads.astype(wide) * mixed.astype(wide), axis=-1, keepdims=True)
        totals = [
            jnp.sum(
                jnp.where(lane == 2 * group + head, total_ref[start:stop, :], 0.0),
                axis=-1,
                keepdims=True,
            )
            for head in range(2)
        ]
        bias = bias_ref[start:stop, :stop]
        raw = across(queries, k_ref[:stop, :])
        scores = raw * (scale * LOG2_E) + jnp.concatenate([bias, bias], axis=0)
        probs = jnp.exp2(scores - jnp.concatenate(totals, axis=0))
        dv_sum[:stop, :] += down(probs.astype(low), grads)
        grad_probs = across(grads, v_ref[:stop, :])
        grad_raw = (probs * (grad_probs - delta)).astype(low)
        dq = project(grad_raw, k_ref[:stop, :]) * scale
        for head in range(2):
            part = turned_back(dq[head * TILE : (head + 1) * TILE], slice(start, stop))
            dq_ref[start:stop, head * LANES : (head + 1) * LANES] = part
        dk_sum[:stop, :] += down(grad_raw, queries)
    dv_ref[...] = dv_sum[...].astype(low)
    dk_ref[...] = turned_back(dk_sum[...] * scale, slice(None))


def attend_back(place, q, k, v, grad, out, total, segment, cosine, sine, block, after=()):
    blocks, size = segment.shape
    spec = attention_specs(size, block)
    return run(
        attend_back_kernel,
        "attend_back",
        place,
        (k.shape[1] // LANES,),
        [
            (q, spec["pair"]),
            (k, spec["one"]),
            (v, spec["one"]),
            (grad, spec["pair_alone"]),
            (out, spec["pair_alone"]),
            (total, spec["alone"]),
            (segment.reshape(blocks * size, 1), spec["column"]),
            (segment.reshape(blocks, 1, size), spec["row"]),
            (cosine, spec["shared"]),
            (sine, spec["shared"]),
        ],
        [
            (shaped((size, q.shape[1]), low), spec["pair_alone"]),
            (shaped((size, k.shape[1]), low), spec["one_alone"]),
            (shaped((size, v.shape[1]), low), spec["one_alone"]),
        ],
        [
            pltpu.VMEM((size, size), wide),
            pltpu.VMEM((size, LANES), wide),
            pltpu.VMEM((size, LANES), wide),
        ],
        after,
        us=21,
    )


def out_weight_kernel(place_ref, *refs):
    pieces, weights, whole_weight, sems = refs[:5], refs[5:7], refs[7], refs[8]
    fetch(place_ref, from_pieces(pieces, FIRST_HALF), FIRST_OUT_PLAN, (whole_weight,), sems)
    zeros = jnp.zeros((LANES - HD, whole_weight.shape[1]), low)
    for block in range(BLOCKS):
        whole_weight[pl.ds(block * LANES + HD, LANES - HD), :] = zeros
    drain((whole_weight.at[pl.ds(0, BLOCKS * HD)],), sems)
    rows = weights[0].shape[0]
    for part in range(2):
        weights[part][...] = whole_weight[part * rows : (part + 1) * rows, :]


def out_weight(place, pieces, width, after):
    out = shaped((H // 2 * LANES, width // 2), low)
    return run(
        out_weight_kernel,
        "out_weight",
        place,
        (1,),
        [(piece, anywhere) for piece in pieces],
        [(out, whole(out))] * 2,
        [pltpu.VMEM((H * LANES, width // 2), low), pltpu.SemaphoreType.DMA((1,))],
        after,
    )


def middle_kernel(
    place_ref, x_ref, mine_ref, other_ref, *refs
):
    w_mine, w_other, (gain_ref, middle_ref, out_ref, heads) = refs[:2], refs[2:4], refs[4:]
    core = place_ref[3]
    span = mine_ref.shape[1]
    heads[:, pl.ds(pl.multiple_of(core * span, LANES), span)] = mine_ref[...]
    heads[:, pl.ds(pl.multiple_of((1 - core) * span, LANES), span)] = other_ref[...]
    columns = w_mine[0].shape[1]
    for owner, weight in ((core, w_mine), (1 - core, w_other)):
        at = pl.ds(pl.multiple_of(owner * columns, LANES), columns)
        branch = project(heads[:, :span], weight[0][...])
        branch = branch + project(heads[:, span:], weight[1][...])
        middle_ref[:, at] = x_ref[:, at].astype(wide) + branch
    hidden = middle_ref[...]
    scale = lax.rsqrt(jnp.mean(hidden * hidden, axis=-1, keepdims=True) + epsilon)
    out_ref[...] = (hidden * scale * gain_ref[8:9, :]).astype(low)


def middle_of(place, x, mine, other, w_mine, w_other, gains, after=()):
    count, width = x.shape
    tile, span = count // 2, mine.shape[1]
    return run(
        middle_kernel,
        "middle",
        place,
        (2,),
        [
            (x, rows_of(tile, width)),
            (mine, rows_of(tile, span)),
            (other, rows_of(tile, span)),
            *[(item, whole(item)) for item in (*w_mine, *w_other, gains)],
        ],
        [
            (shaped((count, width), wide), rows_of(tile, width)),
            (shaped((count, width), low), rows_of(tile, width)),
        ],
        [pltpu.VMEM((tile, 2 * span), low)],
        after,
        us=11,
    )


def middle_back_kernel(
    place_ref,
    middle_ref,
    mine_0,
    mine_1,
    other_0,
    other_1,
    cotangent_ref,
    gain_ref,
    *refs,
):
    w_mine, w_other, refs = refs[:2], refs[2:4], refs[4:]
    grad_ref, branch_mine, branch_other, heads_mine, heads_other, gain_grad, branch, heads = refs
    core = place_ref[3]
    hidden = middle_ref[...]
    scale = lax.rsqrt(jnp.mean(hidden * hidden, axis=-1, keepdims=True) + epsilon)
    parts = (mine_0, mine_1, other_0, other_1)
    incoming = sum(ref[...].astype(wide) for ref in parts)
    weighted = incoming * gain_ref[8:9, :]
    inner = jnp.mean(weighted * hidden, axis=-1, keepdims=True)
    grad = cotangent_ref[...].astype(wide) + (scale * weighted - hidden * scale**3 * inner)
    grad_ref[...] = grad
    branch[...] = grad.astype(low)

    @pl.when(pl.program_id(0) == 0)
    def _():
        gain_grad[...] = jnp.zeros_like(gain_grad)

    summed = jnp.sum(incoming * hidden * scale, axis=0, keepdims=True)
    gain_grad[...] += jnp.broadcast_to(summed, gain_grad.shape)
    columns, span = w_mine[0].shape[1], heads_mine.shape[1]

    def part(ref, owner, size):
        return ref[:, pl.ds(pl.multiple_of(owner * size, LANES), size)]

    branch_mine[...] = part(branch, core, columns)
    branch_other[...] = part(branch, 1 - core, columns)
    for at in range(0, 2 * span, SLAB):
        index, rows = at // span, slice(at % span, at % span + SLAB)
        heads[:, at : at + SLAB] = (
            across(branch_mine[...], w_mine[index][rows, :])
            + across(branch_other[...], w_other[index][rows, :])
        ).astype(low)
    heads_mine[...] = part(heads, core, span)
    heads_other[...] = part(heads, 1 - core, span)


def middle_back(place, middle, parts, cotangent, gains, w_mine, w_other, after=()):
    count, width = middle.shape
    tile, columns, span = count // 2, w_mine[0].shape[1], w_mine[0].shape[0]
    gain_grad = shaped((8, width), wide)
    return run(
        middle_back_kernel,
        "middle_back",
        place,
        (2,),
        [
            *[(item, rows_of(tile, width)) for item in (middle, *parts, cotangent)],
            *[(item, whole(item)) for item in (gains, *w_mine, *w_other)],
        ],
        [
            (shaped((count, width), wide), rows_of(tile, width)),
            (shaped((count, columns), low), rows_of(tile, columns)),
            (shaped((count, columns), low), rows_of(tile, columns)),
            (shaped((count, span), low), rows_of(tile, span)),
            (shaped((count, span), low), rows_of(tile, span)),
            (gain_grad, whole(gain_grad)),
        ],
        [pltpu.VMEM((tile, width), low), pltpu.VMEM((tile, 2 * span), low)],
        after,
        us=15,
    )


def out_grad_kernel(
    place_ref,
    own_mine,
    own_other,
    far_mine,
    far_other,
    branch_own,
    branch_far,
    *refs,
):
    outs, (grad, sems) = refs[:5], refs[5:]
    core = place_ref[3]
    span = own_mine.shape[1]
    for owner, own, far in ((core, own_mine, far_mine), (1 - core, own_other, far_other)):
        for at in range(0, span, SLAB):
            part = down(own[:, at : at + SLAB], branch_own[...])
            part = part + down(far[:, at : at + SLAB], branch_far[...])
            grad[pl.ds(pl.multiple_of(owner * span + at, LANES), SLAB), :] = part.astype(low)
    for k in range(4):
        base = (place_ref[0] ^ k) * 4
        send_off(place_ref, k, (grad,), base, OUT_PLAN, OUT_HALF, outs, sems)
    fill_spare(grad.at[pl.ds(0, 16), pl.ds(0, SLAB)], 144, 16, OUT_HALF, outs, sems)
    drain(outs, sems)


def out_grad(place, own_mine, own_other, far_mine, far_other, branch_own, branch_far, after=()):
    columns = branch_own.shape[1]
    operands = (own_mine, own_other, far_mine, far_other, branch_own, branch_far)
    return run(
        out_grad_kernel,
        "out_grad",
        place,
        (1,),
        [(item, whole(item)) for item in operands],
        sent_shapes(OUT_HALF, SLAB),
        [pltpu.VMEM((H * LANES, columns), low), pltpu.SemaphoreType.DMA((5,))],
        after,
        us=10,
    )


FFN_TILE = 640
FFN_STEP = 256
FFN_SPAN = 768


def load_tokens(ref, own, far, sem):
    count = far.shape[0]
    for part, source in enumerate((far, own)):
        pltpu.make_async_copy(source, ref.at[pl.ds(part * count, count)], sem).start()


def ffn_forward(step, tiles, x_ref, c_ref, weights, sums, middles, at_rows):
    gate_w, up_w, down_w = weights
    inner, grad_gate, grad_up = middles
    units, width = gate_w.shape[1], gate_w.shape[0]
    rows = pl.ds(pl.multiple_of(step * FFN_TILE, FFN_TILE), FFN_TILE)

    @pl.loop(0, units // FFN_STEP)
    def _(index):
        at = pl.ds(pl.multiple_of(index * FFN_STEP, FFN_STEP), FFN_STEP)
        gate = project(x_ref[rows, :], gate_w[:, at])
        upward = project(x_ref[rows, :], up_w[:, at])
        grad_inner = across(c_ref[rows, :], down_w[at, :])
        sigma = 1.0 / (1.0 + jnp.exp(-gate))
        silu = gate * sigma
        inner[at_rows, at] = (silu * upward).astype(low)
        grad_up[at_rows, at] = (grad_inner * silu).astype(low)
        grad_gate[at_rows, at] = (
            grad_inner * upward * sigma * (1.0 + gate * (1.0 - sigma))
        ).astype(low)

    for part in range(2):

        @pl.when((step >= part * tiles // 2) & (step < (part + 1) * tiles // 2))
        def _():
            out_ref, normed_ref = sums[2 * part : 2 * part + 2]

            @pl.loop(0, width // SLAB)
            def _(index):
                at = pl.ds(pl.multiple_of(index * SLAB, SLAB), SLAB)
                out = project(inner[at_rows, :], down_w[:, at])
                normed = across(grad_gate[at_rows, :], gate_w[at, :])
                normed = normed + across(grad_up[at_rows, :], up_w[at, :])
                out_ref[:, at] = out.astype(out_ref.dtype)
                normed_ref[:, at] = normed.astype(normed_ref.dtype)


def ffn_backward(
    place_ref, k, x_ref, c_ref, middles, stages, turned, turned_units, sent, sems, wait
):
    inner, grad_gate, grad_up = middles
    stage_gate, stage_up, stage_down = stages
    width, units = x_ref.shape[1], inner.shape[1]
    depth = place_ref[0] ^ k
    rows, span = width // 4, units // 4
    here = pl.ds(pl.multiple_of(depth * rows, LANES), rows)
    there = pl.ds(pl.multiple_of(depth * span, LANES), span)
    wait(x_ref, grad_gate)
    turned[...] = x_ref[:, here].T
    to = pl.ds(pl.multiple_of(k * rows, 16), rows)
    to_units = pl.ds(pl.multiple_of(k * span, 16), span)
    stage_gate[to, :] = project(turned[...], grad_gate[...]).astype(low)
    wait(grad_up)
    stage_up[to, :] = project(turned[...], grad_up[...]).astype(low)
    wait(inner, c_ref)
    turned_units[...] = inner[:, there].T

    @pl.loop(0, width // FFN_SPAN)
    def _(index):
        at = pl.ds(pl.multiple_of(index * FFN_SPAN, FFN_SPAN), FFN_SPAN)
        stage_down[to_units, at] = project(turned_units[...], c_ref[:, at]).astype(low)

    send_off(place_ref, k, stages, k * 4, FFN_PLAN, FFN_HALF, sent, sems)


def ffn_forward_kernel(tiles, pieces, place_ref, *refs):
    tokens, pieces, refs = refs[:4], refs[4 : 4 + pieces], refs[4 + pieces :]
    sums, middles = refs[:4], refs[4:7]
    x_ref, c_ref, *weights, x_sems, in_sems = refs[7:]
    step = pl.program_id(0)

    @pl.when(step == 0)
    def _():
        x_own, x_far, c_own, c_far = tokens
        load_tokens(x_ref, x_own, x_far, x_sems.at[0])
        load_tokens(c_ref, c_own, c_far, x_sems.at[1])
        if len(pieces) == 5:
            fetch(place_ref, from_pieces(pieces, FFN_HALF), FFN_PLAN, weights, in_sems)
        else:
            source = from_pieces(pieces[:5], UPPER_ROWS // 2)
            fetch(place_ref, source, UPPER_PLAN, weights, in_sems)
            fetch(place_ref, from_planes(*pieces[5:]), LOWER_PLAN, weights, in_sems)
        drain((x_ref, c_ref), x_sems)
        drain(weights, in_sems)

    ffn_forward(step, tiles, x_ref, c_ref, weights, sums, middles, slice(None))


def ffn_backward_kernel(place_ref, *refs):
    tokens, sources, sent = refs[:4], refs[4:7], refs[7:12]
    x_ref, c_ref, *rest = refs[12:]
    middles, stages, rest = rest[:3], rest[3:6], rest[6:]
    turned, turned_units, x_sems, in_sems, out_sems = rest
    k = pl.program_id(0)

    x_own, x_far, c_own, c_far = tokens

    def middle(index):
        pltpu.make_async_copy(sources[index], middles[index], in_sems.at[index]).start()

    @pl.when(k == 0)
    def _():
        load_tokens(x_ref, x_own, x_far, x_sems.at[0])
        middle(1)
        middle(2)
        middle(0)
        load_tokens(c_ref, c_own, c_far, x_sems.at[1])

    arrived = [(x_ref, x_sems.at[0]), (c_ref, x_sems.at[1])]
    arrived += [(ref, in_sems.at[index]) for index, ref in enumerate(middles)]

    def wait(*refs):
        @pl.when(k == 0)
        def _():
            for ref, sem in arrived:
                if any(ref is other for other in refs):
                    pltpu.make_async_copy(ref, ref, sem).wait()

    ffn_backward(
        place_ref, k, x_ref, c_ref, middles, stages, turned, turned_units, sent, out_sems, wait
    )

    @pl.when(k == 3)
    def _():
        drain(sent, out_sems)


FFN_UNITS = 1024


def ffn_sums(count, width):
    last = count // FFN_TILE - 1
    early = pl.BlockSpec((FFN_TILE, width), lambda i, place: (jnp.minimum(i, last), 0))
    late = pl.BlockSpec(
        (FFN_TILE, width), lambda i, place: (jnp.clip(i - last - 1, 0, last), 0)
    )
    return [(shaped((count, width), low), spec) for spec in (early, early, late, late)]


def ffn_scratch(count, width, weights=True, middles=True, stages=True):
    weight = [pltpu.VMEM((width, FFN_UNITS), low)] * 2 + [pltpu.VMEM((FFN_UNITS, width), low)]
    shapes = [pltpu.VMEM((count, width), low)] * 2
    shapes += weight if weights else []
    shapes += [pltpu.VMEM((count, FFN_UNITS), low)] * 3 if middles else []
    if stages:
        shapes += weight
        shapes += [pltpu.VMEM((width // 4, count), low)]
        shapes += [pltpu.VMEM((FFN_UNITS // 4, count), low)]
    shapes += [pltpu.SemaphoreType.DMA((2,)), pltpu.SemaphoreType.DMA((3,))]
    return shapes + ([pltpu.SemaphoreType.DMA((5,))] if stages else [])


def ffn_chunk_forward(place, tokens, pieces, after=()):
    count, width = tokens[0].shape
    tiles = 2 * count // FFN_TILE
    middle = pl.BlockSpec((FFN_TILE, FFN_UNITS), lambda i, place: (i, 0))
    results = run(
        functools.partial(ffn_forward_kernel, tiles, len(pieces)),
        "ffn_forward",
        place,
        (tiles,),
        [(item, anywhere) for item in (*tokens, *pieces)],
        ffn_sums(count, width) + [(shaped((2 * count, FFN_UNITS), low), middle)] * 3,
        ffn_scratch(2 * count, width, middles=False, stages=False),
        after,
        us=36,
    )
    return results[:4], results[4:]


def ffn_chunk_backward(place, tokens, middles, after=()):
    count, width = tokens[0].shape
    return run(
        ffn_backward_kernel,
        "ffn_backward",
        place,
        (4,),
        [(item, anywhere) for item in (*tokens, *middles)],
        sent_shapes(FFN_HALF, SLAB),
        ffn_scratch(2 * count, width, weights=False),
        after,
        us=22,
    )


def input_back_kernel(
    tiles, place_ref, own_q, own_k, own_v, far_q, far_k, far_v, x_own, x_far, w_ref, *refs
):
    grad_ref, own_ref, far_ref, gain_grad = refs
    step = pl.program_id(0)

    @pl.when(step == 0)
    def _():
        gain_grad[...] = jnp.zeros_like(gain_grad)

    def squeezed(query, key, value):
        parts = []
        for ref in (query, key):
            for at in range(0, ref.shape[1], LANES):
                head = ref[:, at : at + LANES].astype(wide)
                parts.append(head[:, :HALF])
                parts.append(head[:, LANES // 2 : LANES // 2 + HALF])
        for at in range(0, value.shape[1], LANES):
            parts.append(value[:, at : at + LANES].astype(wide)[:, :HD])
        return jnp.concatenate(parts, axis=1).astype(low)

    def rest(x_ref, incoming):
        hidden = x_ref[...].astype(wide)
        scale = lax.rsqrt(jnp.mean(hidden * hidden, axis=-1, keepdims=True) + epsilon)
        summed = jnp.sum(incoming * hidden * scale, axis=0, keepdims=True)
        gain_grad[...] += jnp.broadcast_to(summed, gain_grad.shape)

    @pl.when(step < tiles)
    def _():
        grad_ref[...] = squeezed(far_q, far_k, far_v)
        incoming = across(grad_ref[...], w_ref[...])
        far_ref[...] = incoming.astype(low)
        rest(x_far, incoming)

    @pl.when(step >= tiles)
    def _():
        grad_ref[...] = squeezed(own_q, own_k, own_v)
        incoming = across(grad_ref[...], w_ref[...])
        own_ref[...] = incoming.astype(low)
        rest(x_own, incoming)


def input_back(place, own, far, x_own, x_far, weight, after=()):
    count, width = 2 * x_own.shape[0], x_own.shape[1]
    tile = 320
    tiles = count // 2 // tile
    gain_grad = shaped((8, width), wide)

    def late(columns):
        return pl.BlockSpec((tile, columns), lambda i, place: (jnp.maximum(i - tiles, 0), 0))

    def early(columns):
        return pl.BlockSpec((tile, columns), lambda i, place: (jnp.minimum(i, tiles - 1), 0))

    def both(columns):
        return pl.BlockSpec((tile, columns), lambda i, place: (lax.rem(i + tiles, 2 * tiles), 0))

    return run(
        functools.partial(input_back_kernel, tiles),
        "input_back",
        place,
        (2 * tiles,),
        [(item, late(item.shape[1])) for item in own]
        + [(item, early(item.shape[1])) for item in far]
        + [(x_own, late(width)), (x_far, early(width)), (weight, whole(weight))],
        [
            (shaped((count, width), low), both(width)),
            (shaped((count // 2, width), low), late(width)),
            (shaped((count // 2, width), low), early(width)),
            (gain_grad, whole(gain_grad)),
        ],
        after=after,
        us=15,
    )


def qkv_grad_kernel(place_ref, x_ref, grad_ref, gain_one, gain_two, *refs):
    outs, (stage, gain_rows, sems) = refs[:5], refs[5:]
    k = pl.program_id(0)
    width = grad_ref.shape[1]

    @pl.when(k == 0)
    def _():
        gap = jnp.zeros((8, LANES - HD), wide)
        row = lax.broadcasted_iota(jnp.int32, (16, LANES), 0)
        gain_rows[...] = jnp.zeros_like(gain_rows)
        for block in range(BLOCKS):
            for index, gain in enumerate((gain_one, gain_two)):
                part = jnp.concatenate([gain[:, block * HD : (block + 1) * HD], gap], axis=1)
                part = jnp.where(row == 0, jnp.concatenate([part, part], axis=0), 0.0)
                gain_rows[
                    16 * block : 16 * block + 16, index * LANES : (index + 1) * LANES
                ] = part.astype(low)

    depth = place_ref[0] ^ k
    rows = width // 4
    to = pl.ds(pl.multiple_of(depth * rows, 16), rows)
    stage[to, :] = project(x_ref[...].T, grad_ref[...]).astype(low)
    send_off(place_ref, k, (stage, gain_rows), depth * 4, QKV_PLAN, QKV_HALF, outs, sems)

    @pl.when(k == 3)
    def _():
        fill_spare(gain_rows.at[pl.ds(0, 16)], GAINS + 16, 16, QKV_HALF, outs, sems)
        drain(outs, sems)


def qkv_grad(place, x, grad, gain_one, gain_two, after=()):
    count, width = x.shape
    column = pl.BlockSpec((count, width // 4), lambda k, place: (0, place[0] ^ k))
    return run(
        qkv_grad_kernel,
        "qkv_grad",
        place,
        (4,),
        [(x, column)] + [(item, whole(item)) for item in (grad, gain_one, gain_two)],
        sent_shapes(QKV_HALF, SLAB),
        [
            pltpu.VMEM((width, width), low),
            pltpu.VMEM((BLOCKS * 16, SLAB), low),
            pltpu.SemaphoreType.DMA((5,)),
        ],
        after,
        us=15,
    )


def tokens_grad_kernel(place_ref, x_ref, middle_ref, mine_ref, other_ref, gain_ref, out_ref):
    hidden = x_ref[...].astype(wide)
    scale = lax.rsqrt(jnp.mean(hidden * hidden, axis=-1, keepdims=True) + epsilon)
    incoming = mine_ref[...].astype(wide) + other_ref[...].astype(wide)
    weighted = incoming * gain_ref[0:1, :]
    inner = jnp.mean(weighted * hidden, axis=-1, keepdims=True)
    out_ref[...] = middle_ref[...] + (scale * weighted - hidden * scale**3 * inner)


def tokens_grad(place, x, grad_middle, mine, other, gains, after=()):
    count, width = x.shape
    tile = 128
    return run(
        tokens_grad_kernel,
        "tokens_grad",
        place,
        (count // tile,),
        [(item, rows_of(tile, width)) for item in (x, grad_middle, mine, other)]
        + [(gains, whole(gains))],
        [(shaped((count, width), wide), rows_of(tile, width))],
        after=after,
    )[0]


def output_kernel(place_ref, middle_ref, mine_0, mine_1, other_0, other_1, out_ref):
    parts = (mine_0, mine_1, other_0, other_1)
    total = middle_ref[...] + sum(ref[...].astype(wide) for ref in parts)
    out_ref[...] = total.astype(low)


def output_of(place, middle, parts, after=()):
    count, width = middle.shape
    tile = 128
    return run(
        output_kernel,
        "output",
        place,
        (count // tile,),
        [(item, rows_of(tile, width)) for item in (middle, *parts)],
        [(shaped((count, width), low), rows_of(tile, width))],
        after=after,
    )[0]


def swap(array):
    return lax.ppermute(array, "rep", [(0, 1), (1, 0)])


def hop(array, z_flip, y_flip, x_flip):
    flip = (z_flip * 2 + y_flip) * 2 + x_flip
    return lax.ppermute(array, "fsdp", [(chip, chip ^ flip) for chip in range(BLOCKS)])


def hop_x(array):
    return hop(array, 0, 0, 1)


def hop_y(array):
    return hop(array, 0, 1, 0)


def near(line):
    return hop_x(line), hop_y(line)


def pieces_of(blocks):
    cut = blocks.reshape(4, 2, 2, *blocks.shape[1:])
    half = blocks.shape[1] // 2
    far = cut[:, 1, 1]
    return cut[:, 0, 0], cut[:, 0, 1], cut[:, 1, 0], far[:, :half], far[:, half:]


def blocks_of(sent):
    to_x, to_y, late_x, late_y, own = sent
    near_x = jnp.stack([to_x[1], late_x], axis=1)
    near_y = jnp.stack([late_y, to_y[1]], axis=1)
    far = jnp.stack([to_x[0], to_y[0]], axis=1)
    cut = jnp.stack([jnp.stack([own, near_x], 1), jnp.stack([near_y, far], 1)], 1)
    return cut.reshape(BLOCKS, 2 * own.shape[2], own.shape[3])


def layout(length_row, count):
    ends = jnp.cumsum(length_row)
    slots = jnp.arange(count, dtype=jnp.int32)
    passed = (slots[:, None] >= ends[None, :]).astype(jnp.int32)
    segment = jnp.sum(passed, axis=1)
    position = slots - jnp.sum(passed * length_row[None, :], axis=1)
    return position, segment


class Direct:
    def __init__(self, place, weights):
        self.place = place
        self.weights = weights

    def pack_first(self):
        return pack_first(self.place, *self.weights[:4], *self.weights[7:])

    def pack_ffn(self, chunk, parts, after):
        return pack_ffn(self.place, chunk, parts, *self.weights[4:7], after)

    def step_0(self, shard):
        return hop(shard, 2, 0, 0)

    def step_1(self, shard, received, after=()):
        return pair_up(self.place, shard, received, after)

    def step_2(self, pair):
        return hop(pair, 1, 0, 0)

    def step_3(self, pair, received, after=()):
        return line_up(self.place, pair, received, after)

    def step_4(self, line):
        return near(line)

    def step_5(self, line, sides, after=()):
        upper, lower = halves(self.place, *sides, after)
        return (line, *sides, hop_y(upper), hop_x(lower)), upper

    def plane(self, parts, after):
        return plane_up(self.place, parts, after)

    def gate(self, sent, pieces):
        return (*gate(self.place, sent[:2], (*pieces[3:5], pieces[6])), *sent[2:])

    def scatter_1(self, sent):
        return hop_x(sent[0]), hop_y(sent[1])

    def scatter_2(self, sent, got, after):
        late_x, late_y = merge(self.place, sent[2], sent[3], got[0], got[1], after)
        return late_x, (hop_x(late_x), hop_y(late_y))

    def scatter_3(self, groups, after):
        groups = [(sent[4], *got, *more) for sent, got, more in groups]
        kept, kept_far, part = sum_plane(self.place, groups, False, after)
        return kept, (kept_far, hop(part, 1, 0, 0))

    def scatter_4(self, kept, parts, after):
        kept_far, near = parts
        token = sum_pass(self.place, kept_far, near, after)
        return token, (near, hop(token, 2, 0, 0))

    def scatter_34(self, sent, got, more, after):
        kept, *parts = sum_plane(self.place, [(sent[4], *got, *more)], True, after)
        return kept, tuple(hop(part, k + 1, 0, 0) for k, part in enumerate(parts))

    def scatter_5(self, kept, parts, after):
        total, total_low = sum_line(self.place, kept, parts, after)
        return total, swap(total_low)

    def pins(self, arrays):
        return tuple(arrays)

    def finish_ffn(self, chunk_0, chunk_1, shapes, after):
        mine, other = zip(chunk_0, chunk_1)
        return unpack_ffn(self.place, mine, other, shapes, after)

    def finish_first(self, first, chunk_1, shapes, owned, after):
        grads = unpack_first(self.place, (*first, *chunk_1), shapes, after)
        both = first[0][GAINS, : 2 * LANES] + first[1][GAINS, : 2 * LANES].astype(wide)
        return grads, (both[:owned], both[LANES : LANES + owned])


def on_device(
    direct,
    tokens,
    lengths,
    attn_gain,
    w_query,
    w_key,
    w_value,
    w_out,
    ffn_gain,
    w_gate,
    w_up,
    w_down,
    cotangent,
):
    count, width = tokens.shape
    owned = attn_gain.shape[0]
    core = lax.axis_index("rep")
    if direct:
        index = lax.axis_index("fsdp")
        spot = (index // 4, (index // 2) % 2, index % 2)
    else:
        spot = (0, 0, 0)
    place = jnp.stack([jnp.int32(item) for item in (*spot, core)])
    weights = (w_query, w_key, w_value, w_out, w_gate, w_up, w_down, attn_gain, ffn_gain)
    routes = Direct(place, weights) if direct else Whole(place, weights)

    first = routes.pack_first()
    far_tokens, far_cotangent = swap(tokens), swap(cotangent)
    laid = [layout(row, count) for row in (lengths[0], swap(lengths)[0])]
    segment = jnp.stack([item[1] for item in laid])
    cosine, sine = turn_table(jnp.concatenate([item[0] for item in laid]))

    received_first = routes.step_0(first)
    whole_rows = 2 * FFN_HALF
    chunk_a, chunk_b = routes.pack_ffn(1, (UPPER_ROWS, whole_rows - UPPER_ROWS), (first,))
    if direct:
        chunk_b = chunk_b.reshape(1, *chunk_b.shape)
    sides_b = routes.step_4(chunk_b)
    parts_b, token = routes.step_5(chunk_b, sides_b)
    pair_first = routes.step_1(first, received_first, (token,))
    near_first = routes.step_2(pair_first)
    (chunk_0,) = routes.pack_ffn(0, (whole_rows,), (pair_first,))
    received_0 = routes.step_0(chunk_0)
    plane_b = routes.plane(parts_b, (chunk_0,))
    tables = (far_tokens, far_cotangent, segment, cosine, sine)
    line_first = routes.step_3(pair_first, near_first, (*tables, plane_b))
    sides_first = routes.step_4(line_first)
    pair_0 = routes.step_1(chunk_0, received_0, (line_first,))
    near_0 = routes.step_2(pair_0)
    received_a = routes.step_0(chunk_a)
    received_b = routes.step_0(plane_b)
    pieces_first, token = routes.step_5(line_first, sides_first, (pair_0,))
    line_0 = routes.step_3(pair_0, near_0, (token,))
    sides_0 = routes.step_4(line_0)
    w_mine = out_weight(place, pieces_first, tokens.shape[1], (line_0,))
    w_other = [swap(part) for part in w_mine]
    normed_low, queries, keys, values, w_qkv, gains = project_qkv(
        place, tokens, far_tokens, cosine, sine, pieces_first, (w_mine[0],)
    )
    far_mine, far_total = attend(place, queries, keys, values, segment, 1, (keys,))
    own_other = swap(far_mine)
    own_mine, own_total = attend(
        place, queries, keys, values, segment, 0, (far_mine, *w_other)
    )
    far_other = swap(own_mine)
    pair_b = routes.step_1(plane_b, received_b, (own_mine,))
    near_b = routes.step_2(pair_b)
    pieces_0, token = routes.step_5(line_0, sides_0, (pair_b, received_a))
    pair_a = routes.step_1(chunk_a, received_a, (token,))
    near_a = routes.step_2(pair_a)
    middle, normed_own = middle_of(
        place, tokens, own_mine, own_other, w_mine, w_other, gains, (pair_a,)
    )
    normed_far = swap(normed_own)
    line_a = routes.step_3(pair_a, near_a, (normed_own, far_other, *pieces_0[3:]))
    sides_a = routes.step_4(line_a)

    inputs = (normed_own, normed_far, cotangent, far_cotangent)
    sums_0, middles_0 = ffn_chunk_forward(place, inputs, pieces_0, (line_a,))
    out_far_0, norm_far_0 = swap(sums_0[0]), swap(sums_0[1])
    pieces_a, token = routes.step_5(line_a, sides_a, (sums_0[0],))
    planes_b = (pair_b, near_b) if direct else chunk_b
    pieces_1 = (*pieces_a, *planes_b)
    sent_0 = ffn_chunk_backward(place, inputs, middles_0, (token,))
    sent_0 = routes.gate(sent_0, pieces_1)
    got_0 = routes.scatter_1(sent_0)
    sums_1, middles_1 = ffn_chunk_forward(place, inputs, pieces_1, (sent_0[0],))
    out_far_1, norm_far_1 = swap(sums_1[0]), swap(sums_1[1])
    token, more_0 = routes.scatter_2(sent_0, got_0, (sums_1[0], out_far_0))
    sent_1 = ffn_chunk_backward(place, inputs, middles_1, (token,))
    got_1 = routes.scatter_1(sent_1)

    norms = (sums_0[3], sums_1[3], norm_far_0, norm_far_1)
    grad_middle, branch_mine, branch_sent, heads_mine, heads_sent, ffn_gain_grad = middle_back(
        place, middle, norms, cotangent, gains, w_mine, w_other, (sent_1[4], *more_0)
    )
    branch_far, heads_far = swap(branch_sent), swap(heads_sent)
    attended = (queries, keys, values)
    tables = (segment, cosine, sine)
    own_grads = attend_back(place, *attended, heads_mine, own_mine, own_total, *tables, 0)
    sent_out = out_grad(
        place,
        own_mine,
        own_other,
        far_mine,
        far_other,
        branch_mine,
        branch_far,
        (own_grads[0],),
    )
    got_out = routes.scatter_1(sent_out)
    kept_0, parts_0 = routes.scatter_3([(sent_0, got_0, more_0)], (sent_out[4],))
    token, more_1 = routes.scatter_2(sent_1, got_1, (kept_0,))
    far_grads = attend_back(
        place, *attended, heads_far, far_mine, far_total, *tables, 1, (token, out_far_1)
    )
    token, more_out = routes.scatter_2(sent_out, got_out, (far_grads[0],))
    token, parts_0 = routes.scatter_4(kept_0, parts_0, (token,))
    grad_qkv, own_part, far_part, attn_gain_grad = input_back(
        place, own_grads, far_grads, tokens, far_tokens, w_qkv, (token,)
    )
    own_rest = swap(far_part)
    sent_qkv = qkv_grad(place, normed_low, grad_qkv, attn_gain_grad, ffn_gain_grad)
    got_qkv = routes.scatter_1(sent_qkv)
    groups = [(sent_1, got_1, more_1), (sent_out, got_out, more_out)]
    kept_1, parts_1 = routes.scatter_3(groups, (sent_qkv[4], *routes.pins(parts_0[1:])))

    owned_0 = routes.scatter_5(kept_0, parts_0, (kept_1,))
    outs = (sums_0[2], sums_1[2], out_far_0, out_far_1)
    output = output_of(place, middle, outs, (owned_0[0],))
    token, more_qkv = routes.scatter_2(sent_qkv, got_qkv, (output,))
    token, parts_1 = routes.scatter_4(kept_1, parts_1, (token,))
    grad_tokens = tokens_grad(place, tokens, grad_middle, own_part, own_rest, gains, (token,))
    kept_qkv, parts_qkv = routes.scatter_34(sent_qkv, got_qkv, more_qkv, (grad_tokens,))
    owned_1 = routes.scatter_5(kept_1, parts_1, (kept_qkv,))
    owned_qkv = routes.scatter_5(kept_qkv, parts_qkv, (owned_1[0],))
    shapes = [w_gate.shape, w_up.shape, w_down.shape]
    grad_gate, grad_up, grad_down = routes.finish_ffn(owned_0, owned_1, shapes, (owned_qkv[0],))
    shapes = [w_query.shape, w_key.shape, w_value.shape, w_out.shape]
    grads, gain_grads = routes.finish_first(owned_qkv, owned_1, shapes, owned, (grad_gate,))
    return (
        output,
        grad_tokens,
        gain_grads[0],
        *grads,
        gain_grads[1],
        grad_gate,
        grad_up,
        grad_down,
    )


class Whole:
    def __init__(self, place, weights):
        self.place = place
        query, key, value, out, gate, up, down_w, gain_one, gain_two = weights
        core = place[3]
        self.core = core
        count = query.shape[1] // query.shape[0]
        self.count = count
        rows = query.shape[1] // BLOCKS

        def full(shard):
            return lax.all_gather(shard, "fsdp", axis=0, tiled=True)

        def mine(weight):
            columns = weight.shape[1] // 2
            return lax.dynamic_slice_in_dim(weight, core * columns, columns, axis=1)

        def slabs(weight):
            blocks = weight.reshape(BLOCKS, -1, weight.shape[1])
            return [blocks[:, :, at : at + SLAB] for at in range(0, weight.shape[1], SLAB)]

        qkv = full(jnp.concatenate([mine(query), mine(key), mine(value)], axis=1))
        gain_rows = jnp.zeros((BLOCKS, 16, SLAB), low)
        for index, gain in enumerate((gain_one, gain_two)):
            part = full(gain).reshape(BLOCKS, rows)
            gain_rows = gain_rows.at[:, 0, index * LANES : index * LANES + rows].set(part)
        square = full(mine(out)).reshape(BLOCKS, rows, -1)
        rest = square[:, :, SLAB:]
        rest = jnp.concatenate([rest[:, : rows // 2], rest[:, rows // 2 :]], axis=2)
        parts = slabs(qkv) + [gain_rows, square[:, :, :SLAB], rest]
        self.first = pieces_of(jnp.concatenate(parts, axis=1))
        quarter = down_w.shape[0] // (2 * CHUNKS)
        self.quarter = quarter

        def units(weight, chunk):
            split = weight.reshape(weight.shape[0], count, 2 * CHUNKS, quarter)
            part = lax.dynamic_index_in_dim(split, CHUNKS * core + chunk, 2, keepdims=False)
            return full(part.reshape(weight.shape[0], count * quarter))

        chunks = []
        for chunk in range(CHUNKS):
            at = (CHUNKS * core + chunk) * quarter
            part = full(lax.dynamic_slice_in_dim(down_w, at, quarter, axis=0))
            parts = slabs(units(gate, chunk)) + slabs(units(up, chunk)) + slabs(part)
            chunks.append(jnp.concatenate(parts, axis=1))
        planes = chunks[1][:, UPPER_ROWS:].reshape(4, 4, -1, SLAB)
        self.ffn_0 = (pieces_of(chunks[0]),)
        self.ffn_1 = pieces_of(chunks[1][:, :UPPER_ROWS]), (planes[0::2], planes[1::2])

    def pack_first(self):
        return self.first

    def pack_ffn(self, chunk, parts, after):
        return (self.ffn_0, self.ffn_1)[chunk]

    def step_0(self, shard):
        return shard

    def step_1(self, shard, received, after=()):
        return shard

    def step_2(self, pair):
        return pair

    def step_3(self, pair, received, after=()):
        return pair

    def step_4(self, line):
        return ()

    def step_5(self, line, sides, after=()):
        return line, line

    def plane(self, parts, after):
        return parts

    def gate(self, sent, pieces):
        return sent

    def scatter_1(self, sent):
        return blocks_of(sent)

    def scatter_2(self, sent, got, after):
        return got, got

    def scatter_3(self, groups, after):
        blocks = jnp.concatenate([got for _, got, _ in groups], axis=1)
        return blocks, blocks

    def scatter_34(self, sent, got, more, after):
        return got, ()

    def scatter_4(self, kept, parts, after):
        return kept, kept

    def scatter_5(self, kept, parts, after):
        return kept, kept

    def split(self, blocks, widths):
        parts, row = [], 0
        for rows, slabs in widths:
            taken = []
            for _ in range(slabs):
                taken.append(blocks[:, row : row + rows])
                row += rows
            part = jnp.concatenate(taken, axis=2)
            part = part.reshape(BLOCKS * rows, part.shape[2])
            parts.append(lax.psum_scatter(part, "fsdp", scatter_dimension=0, tiled=True))
        return parts

    def ordered(self, part):
        other = swap(part).astype(wide)
        part = part.astype(wide)
        first = jnp.where(self.core == 0, part, other)
        return first, jnp.where(self.core == 0, other, part)

    def pins(self, arrays):
        return ()

    def finish_ffn(self, chunk_0, chunk_1, shapes, after):
        gates, ups, downs = [], [], []
        for blocks, _ in (chunk_0, chunk_1):
            gate, up, down_w = self.split(blocks, ((96, 2), (96, 2), (64, 3)))
            gates.append(self.ordered(gate))
            ups.append(self.ordered(up))
            downs.append(self.ordered(down_w))

        def columns(pairs):
            parts = [pairs[chunk][owner] for owner in range(2) for chunk in range(CHUNKS)]
            rows = parts[0].shape[0]
            parts = [part.reshape(rows, self.count, self.quarter) for part in parts]
            return jnp.stack(parts, axis=2).reshape(rows, -1)

        grad_down = [downs[chunk][owner] for owner in range(2) for chunk in range(CHUNKS)]
        return columns(gates), columns(ups), jnp.concatenate(grad_down, axis=0)

    def finish_first(self, first, chunk_1, shapes, owned, after):
        mine = first[0]
        (qkv,) = self.split(mine[:, :GAINS], ((96, 3),))
        blocks = chunk_1[0][:, 2 * FFN_HALF :]
        rest = blocks[:, 96:144]
        rest = jnp.concatenate([rest[:, :, :256], rest[:, :, 256:]], axis=1)
        (square,) = self.split(jnp.concatenate([blocks[:, :96], rest], axis=2), ((96, 1),))
        pair = self.ordered(qkv)
        grads, at = [], 0
        for shape in shapes[:3]:
            columns = shape[1] // 2
            grads.append(jnp.concatenate([item[:, at : at + columns] for item in pair], axis=1))
            at += columns
        grads.append(jnp.concatenate(self.ordered(square), axis=1))
        rows = mine[:, GAINS, : 2 * LANES].astype(wide)
        rows = rows + swap(rows)
        gains = []
        for index in range(2):
            gain = rows[:, index * LANES : index * LANES + 96].reshape(-1)
            gains.append(lax.psum_scatter(gain, "fsdp", scatter_dimension=0, tiled=True))
        return grads, gains


def solution(mesh):
    rows = P(("rep", "fsdp"), None)
    split = P("fsdp", None)
    gain = P("fsdp")
    return jax.shard_map(
        functools.partial(on_device, mesh.shape["fsdp"] == BLOCKS),
        mesh=mesh,
        in_specs=(rows, rows, gain) + (split,) * 4 + (gain,) + (split,) * 3 + (rows,),
        out_specs=(rows, rows, gain) + (split,) * 4 + (gain,) + (split,) * 3,
        check_vma=False,
    )
```

```python
import functools

import jax
import jax.numpy as jnp
from jax import lax
from jax.experimental import pallas as pl
from jax.experimental.pallas import tpu as pltpu
from jax.sharding import PartitionSpec as P

H = 16
KV = 8
HD = 96
HALF = HD // 2
LANES = 128
BLOCKS = 16
TILE = 128
SLAB = 512
CHUNKS = 2
COST_SCALE = 0.001

epsilon = 1e-05
rope_base = 100000.0
masked_score = -1e30
low = jnp.bfloat16
wide = jnp.float32


def whole(array, buffers=1):
    zeros = (0,) * array.ndim
    mode = pl.Buffered(buffers)
    return pl.BlockSpec(array.shape, lambda *at: zeros, pipeline_mode=mode)


def rows_of(tile, width, first=0):
    return pl.BlockSpec((tile, width), lambda i, place: (first + i, 0))


def shaped(shape, dtype):
    return jax.ShapeDtypeStruct(shape, dtype)


anywhere = pl.BlockSpec(memory_space=pl.ANY)


def run(kernel, name, place, grid, operands, outs, scratch=(), after=(), vmem=56, us=4):
    after = [item for item in after if isinstance(item, jax.Array)]
    count, extra = len(operands), len(after)

    def body(place_ref, *refs):
        kernel(place_ref, *refs[:count], *refs[count + extra :])

    return pl.pallas_call(
        body,
        grid_spec=pltpu.PrefetchScalarGridSpec(
            num_scalar_prefetch=1,
            grid=grid,
            in_specs=[spec for _, spec in operands] + [anywhere] * extra,
            out_specs=[spec for _, spec in outs],
            scratch_shapes=list(scratch),
        ),
        out_shape=[shape for shape, _ in outs],
        compiler_params=pltpu.CompilerParams(vmem_limit_bytes=vmem * 2**20),
        cost_estimate=pl.CostEstimate(
            flops=0, bytes_accessed=int(us * COST_SCALE * 3.3e6), transcendentals=0
        ),
        name=name,
    )(place, *[array for array, _ in operands], *after)


def across(left, right):
    return lax.dot_general(left, right, (((1,), (1,)), ((), ())), preferred_element_type=wide)


def down(left, right):
    return lax.dot_general(left, right, (((0,), (0,)), ((), ())), preferred_element_type=wide)


def project(left, right):
    return jnp.dot(left, right, preferred_element_type=wide)


class Slab:
    def __init__(self, matrix, row, rows, stride, offset, column, width=SLAB, lane=0):
        self.matrix, self.row, self.rows = matrix, row, rows
        self.stride, self.offset = stride, offset
        self.column, self.width, self.lane = column, width, lane

    def of(self, refs, block):
        rows = pl.ds(pl.multiple_of(block * self.stride + self.offset, 16), self.rows)
        return refs[self.matrix].at[rows, pl.ds(self.column, self.width)]

    def lanes(self):
        return pl.ds(self.lane, self.width)


FIRST_HALF, FFN_HALF, QKV_HALF, OUT_HALF = 224, 288, 160, 80


def square_plan(half):
    plan = []
    for slab in range(3):
        top, bottom = slab * 96, slab * 96 + 96
        for first, last in ((top, min(bottom, half)), (max(top, half), bottom)):
            if first < last:
                plan.append(Slab(0, first, last - first, 96, first - top, slab * SLAB))
    return plan


def out_plan(start, half):
    plan = []
    for first, last in ((start, min(start + 96, half)), (max(start, half), start + 96)):
        if first < last:
            plan.append(Slab(0, first, last - first, LANES, first - start, 0))
    for part in range(2):
        plan.append(Slab(0, start + 96, 48, LANES, part * 48, SLAB, 256, part * 256))
    return plan


GAINS = 288
GAIN_SLAB = Slab(1, GAINS, 16, 16, 0, 0)
FIRST_QKV_PLAN = square_plan(FIRST_HALF) + [GAIN_SLAB]
FIRST_OUT_PLAN = out_plan(GAINS + 16, FIRST_HALF)
QKV_PLAN = square_plan(QKV_HALF) + [GAIN_SLAB]
OUT_PLAN = out_plan(0, OUT_HALF)
FFN_PLAN = [
    Slab(0, 0, 96, 96, 0, 0),
    Slab(0, 96, 96, 96, 0, SLAB),
    Slab(1, 192, 96, 96, 0, 0),
    Slab(1, 288, 96, 96, 0, SLAB),
    Slab(2, 384, 64, 64, 0, 0),
    Slab(2, 448, 64, 64, 0, SLAB),
    Slab(2, 512, 64, 64, 0, 2 * SLAB),
]
UPPER_ROWS = 384
UPPER_PLAN, LOWER_PLAN = FFN_PLAN[:4], [
    Slab(2, slab * 64, 64, 64, 0, slab * SLAB) for slab in range(3)
]


def block_index(place_ref, k, dy, dx):
    z, y, x = place_ref[0], place_ref[1], place_ref[2]
    return ((z ^ k) * 2 + (y ^ dy)) * 2 + (x ^ dx)


def from_pieces(pieces, half):
    def source(k, dy, dx, slab):
        at = pl.ds(slab.row, slab.rows)
        piece = pieces[dy * 2 + dx]
        if dy and dx:
            part = int(slab.row >= half)
            at = pl.ds(slab.row - part * half, slab.rows)
            piece = pieces[3 + part]
        return piece.at[k, at, slab.lanes()]

    return source


def from_planes(pair, other):
    def source(k, dy, dx, slab):
        planes = other if k % 2 else pair
        return planes.at[k // 2, dy * 2 + dx, pl.ds(slab.row, slab.rows), slab.lanes()]

    return source


def fetch(place_ref, source, plan, matrices, sems):
    for k in range(4):
        for dy in range(2):
            for dx in range(2):
                block = block_index(place_ref, k, dy, dx)
                for slab in plan:
                    pltpu.make_async_copy(
                        source(k, dy, dx, slab), slab.of(matrices, block), sems.at[slab.matrix]
                    ).start()


def send_off(place_ref, k, matrices, stride_base, plan, half, outs, sems):
    to_x, to_y, late_x, late_y, own = range(5)
    for dy in range(2):
        for dx in range(2):
            block = block_index(place_ref, place_ref[0], dy, dx) + stride_base
            for slab in plan:
                part = int(slab.row >= half)
                at = pl.ds(slab.row - part * half, slab.rows)
                if (dy, dx) == (0, 0):
                    which, index = own, (k, part)
                elif dy and dx:
                    which, index = (to_y if part else to_x), (0, k)
                elif part == dy:
                    which, index = (to_y if dy else to_x), (1, k)
                else:
                    which, index = (late_y if dy else late_x), (k,)
                target = outs[which].at[(*index, at, slab.lanes())]
                pltpu.make_async_copy(slab.of(matrices, block), target, sems.at[which]).start()


def fill_spare(source, row, rows, half, outs, sems):
    at = pl.ds(row - half, rows)
    for k in range(4):
        for which, index in ((1, (0, k)), (1, (1, k)), (2, (k,)), (4, (k, 1))):
            target = outs[which].at[(*index, at)]
            pltpu.make_async_copy(source, target, sems.at[which]).start()


def drain(refs, sems):
    for index, ref in enumerate(refs):
        pltpu.make_async_copy(ref, ref, sems.at[index]).wait()


def sent_shapes(half, width):
    shapes = [(2, 4, half, width)] * 2 + [(4, half, width)] * 2 + [(4, 2, half, width)]
    return [(shaped(shape, low), anywhere) for shape in shapes]


def gate_kernel(place_ref, *refs):
    pass


def gate(place, arrays, after):
    count, extra = len(arrays), len(after)
    return pl.pallas_call(
        gate_kernel,
        grid_spec=pltpu.PrefetchScalarGridSpec(
            num_scalar_prefetch=1,
            grid=(1,),
            in_specs=[anywhere] * (count + extra),
            out_specs=[anywhere] * count,
        ),
        out_shape=[shaped(array.shape, array.dtype) for array in arrays],
        input_output_aliases={1 + index: index for index in range(count)},
        cost_estimate=pl.CostEstimate(flops=0, bytes_accessed=0, transcendentals=0),
        name="gate",
    )(place, *arrays, *after)


def pair_kernel(place_ref, own, far, out, sems):
    copies = [
        pltpu.make_async_copy(ref, out.at[k], sems.at[k]) for k, ref in enumerate((own, far))
    ]
    for copy in copies:
        copy.start()
    for copy in copies:
        copy.wait()


def pair_up(place, own, far, after=()):
    out = shaped((2, *own.shape), low)
    return run(
        pair_kernel,
        "pair",
        place,
        (1,),
        [(own, anywhere), (far, anywhere)],
        [(out, whole(out))],
        [pltpu.SemaphoreType.DMA((2,))],
        after,
        us=2,
    )[0]


def line_kernel(place_ref, pair, near, out, sems):
    copies = []
    for k in range(4):
        ref = near if k % 2 else pair
        copies.append(pltpu.make_async_copy(ref.at[k // 2], out.at[k], sems.at[k]))
        copies[-1].start()
    for copy in copies:
        copy.wait()


def line_up(place, pair, near, after=()):
    _, rows, width = pair.shape
    out = shaped((4, rows, width), low)
    return run(
        line_kernel,
        "line",
        place,
        (1,),
        [(pair, anywhere), (near, anywhere)],
        [(out, whole(out))],
        [pltpu.SemaphoreType.DMA((4,))],
        after,
        us=4,
    )[0]


def join_kernel(place_ref, *refs):
    *parts, out, sems = refs
    copies = [
        pltpu.make_async_copy(part, out.at[k], sems.at[k]) for k, part in enumerate(parts)
    ]
    for copy in copies:
        copy.start()
    for copy in copies:
        copy.wait()


def join(place, parts, after=()):
    out = shaped((4, *parts[0].shape), low)
    return run(
        join_kernel,
        "join",
        place,
        (1,),
        [(part, anywhere) for part in parts],
        [(out, whole(out))],
        [pltpu.SemaphoreType.DMA((4,))],
        after,
        us=4,
    )[0]


def plane_kernel(place_ref, own, from_x, from_y, upper, lower, out, sems):
    half = upper.shape[1]
    parts = [
        (own, out.at[pl.ds(0, 1)]),
        (from_x, out.at[pl.ds(1, 1)]),
        (from_y, out.at[pl.ds(2, 1)]),
        (upper, out.at[pl.ds(3, 1), pl.ds(0, half)]),
        (lower, out.at[pl.ds(3, 1), pl.ds(half, half)]),
    ]
    copies = [
        pltpu.make_async_copy(source, target, sems.at[index])
        for index, (source, target) in enumerate(parts)
    ]
    for copy in copies:
        copy.start()
    for copy in copies:
        copy.wait()


def plane_up(place, parts, after):
    _, rows, width = parts[0].shape
    out = shaped((4, rows, width), low)
    return run(
        plane_kernel,
        "plane",
        place,
        (1,),
        [(part, anywhere) for part in parts],
        [(out, whole(out))],
        [pltpu.SemaphoreType.DMA((5,))],
        after,
        us=2,
    )[0]


def halves_kernel(place_ref, from_x, from_y, upper, lower, sems):
    half = upper.shape[1]
    copies = (
        pltpu.make_async_copy(from_x.at[:, pl.ds(0, half)], upper, sems.at[0]),
        pltpu.make_async_copy(from_y.at[:, pl.ds(half, half)], lower, sems.at[1]),
    )
    for copy in copies:
        copy.start()
    for copy in copies:
        copy.wait()


def halves(place, from_x, from_y, after):
    count, rows, width = from_x.shape
    out = shaped((count, rows // 2, width), low)
    return run(
        halves_kernel,
        "halves",
        place,
        (1,),
        [(from_x, anywhere), (from_y, anywhere)],
        [(out, whole(out))] * 2,
        [pltpu.SemaphoreType.DMA((2,))],
        after,
        us=2,
    )


def step_rows(half):
    return next(rows for rows in (144, 80, 96, 48, 368) if half % rows == 0)


def merge_kernel(place_ref, late_x, late_y, got_x, got_y, out_x, out_y):
    out_x[...] = late_x[...] + got_y[0]
    out_y[...] = late_y[...] + got_x[0]


def merge(place, late_x, late_y, got_x, got_y, after):
    shape = late_x.shape
    rows = step_rows(shape[1])
    spec = pl.BlockSpec((4, rows, shape[2]), lambda i, place: (0, i, 0))
    got = pl.BlockSpec((1, 4, rows, shape[2]), lambda i, place: (0, 0, i, 0))
    return run(
        merge_kernel,
        "merge",
        place,
        (shape[1] // rows,),
        [(late_x, spec), (late_y, spec), (got_x, got), (got_y, got)],
        [(shaped(shape, low), spec)] * 2,
        after=after,
    )


def sum_kernel(direct, groups, place_ref, *refs):
    ins, (kept, *outs) = refs[: 5 * groups], refs[5 * groups :]
    step = pl.program_id(0)
    for k in range(4):

        @pl.when(step == k)
        def _():
            row = 0
            for group in range(groups):
                own, got_x, got_y, more_x, more_y = ins[5 * group : 5 * group + 5]
                at = slice(row, row + own.shape[2])
                row += own.shape[2]
                upper = own[0, 0].astype(wide) + got_x[0, 0].astype(wide)
                upper = upper + more_y[0].astype(wide)
                lower = own[0, 1].astype(wide) + got_y[0, 0].astype(wide)
                lower = lower + more_x[0].astype(wide)
                if k == 0:
                    ref = kept
                elif direct:
                    ref = outs[k - 1]
                else:
                    ref = outs[1].at[0] if k % 2 else outs[0]
                ref[0, at, :], ref[1, at, :] = upper.astype(ref.dtype), lower.astype(ref.dtype)


def sum_plane(place, groups, direct, after):
    operands = []
    for own, got_x, got_y, more_x, more_y in groups:
        _, _, half, width = own.shape
        got = pl.BlockSpec((1, 1, half, width), lambda k, place: (1, k, 0, 0))
        more = pl.BlockSpec((1, half, width), lambda k, place: (k, 0, 0))
        operands += [
            (own, pl.BlockSpec((1, 2, half, width), lambda k, place: (k, 0, 0, 0))),
            (got_x, got),
            (got_y, got),
            (more_x, more),
            (more_y, more),
        ]
    half = sum(group[0].shape[2] for group in groups)
    out = pl.BlockSpec((2, half, width), lambda k, place: (0, 0, 0))
    both = pl.BlockSpec((1, 2, half, width), lambda k, place: (k // 2, 0, 0, 0))
    outs = [(shaped((2, half, width), wide), out)]
    if direct:
        outs += [(shaped((2, half, width), low), out)] * 3
    else:
        outs += [(shaped((2, half, width), wide), out)]
        outs += [(shaped((2, 2, half, width), low), both)]
    return run(
        functools.partial(sum_kernel, direct, len(groups)),
        "sum_plane",
        place,
        (4,),
        operands,
        outs,
        after=after,
        us=5,
    )


def pass_kernel(place_ref, kept_far, near, out):
    out[...] = (kept_far[...] + near[0].astype(wide)).astype(low)


def sum_pass(place, kept_far, near, after):
    _, half, width = kept_far.shape
    rows = step_rows(half)
    spec = pl.BlockSpec((2, rows, width), lambda i, place: (0, i, 0))
    second = pl.BlockSpec((1, 2, rows, width), lambda i, place: (1, 0, i, 0))
    return run(
        pass_kernel,
        "sum_pass",
        place,
        (half // rows,),
        [(kept_far, spec), (near, second)],
        [(shaped(kept_far.shape, low), spec)],
        after=after,
        us=3,
    )[0]


def total_kernel(place_ref, kept, *refs):
    *received, out, out_low = refs
    total = kept[...]
    for ref in received:
        part = ref[0] if len(ref.shape) > len(kept.shape) else ref[...]
        total = total + part.astype(wide)
    out[...] = total
    out_low[...] = total.astype(low)


def sum_line(place, kept, received, after):
    _, half, width = kept.shape
    rows = step_rows(half)
    spec = pl.BlockSpec((2, rows, width), lambda i, place: (0, i, 0))
    first = pl.BlockSpec((1, 2, rows, width), lambda i, place: (0, 0, i, 0))
    total, total_low = run(
        total_kernel,
        "sum_line",
        place,
        (half // rows,),
        [(kept, spec)] + [(item, first if item.ndim == 4 else spec) for item in received],
        [(shaped(kept.shape, wide), spec), (shaped(kept.shape, low), spec)],
        after=after,
        us=4,
    )
    return total.reshape(2 * half, width), total_low.reshape(2 * half, width)


def pack_first_kernel(place_ref, query, key, value, square, gain_one, gain_two, out):
    core = place_ref[3]

    def mine(ref):
        columns = ref.shape[1] // 2
        return ref[:, pl.ds(pl.multiple_of(core * columns, LANES), columns)]

    packed = jnp.concatenate([mine(query), mine(key), mine(value)], axis=1)
    rows = packed.shape[0]
    for slab in range(3):
        out[slab * rows : (slab + 1) * rows, :] = packed[:, slab * SLAB : (slab + 1) * SLAB]
    row = lax.broadcasted_iota(jnp.int32, (16, LANES), 0)
    gap = jnp.zeros((16, LANES - rows), wide)
    out[GAINS : GAINS + 16, :] = jnp.zeros((16, SLAB), low)
    for index, gain in enumerate((gain_one, gain_two)):
        spread = jnp.broadcast_to(gain[...].astype(wide), (16, rows))
        spread = jnp.where(row == 0, jnp.concatenate([spread, gap], axis=1), 0.0)
        out[GAINS : GAINS + 16, index * LANES : (index + 1) * LANES] = spread.astype(low)
    at, packed = GAINS + 16, mine(square)
    out[at : at + rows, :] = packed[:, :SLAB]
    for part in range(2):
        out[at + rows :, part * 256 : (part + 1) * 256] = packed[
            part * rows // 2 : (part + 1) * rows // 2, SLAB:
        ]


def pack_first(place, query, key, value, square, gain_one, gain_two):
    operands = [query, key, value, square, gain_one.reshape(1, -1), gain_two.reshape(1, -1)]
    out = shaped((2 * FIRST_HALF, SLAB), low)
    return run(
        pack_first_kernel,
        "pack_first",
        place,
        (1,),
        [(item, whole(item)) for item in operands],
        [(out, whole(out))],
    )[0]


def interleave(even, odd):
    lane = lax.broadcasted_iota(jnp.int32, even.shape, 1)
    left = jnp.where(lane < LANES // 2, even, pltpu.roll(odd, LANES // 2, 1))
    right = jnp.where(lane < LANES // 2, pltpu.roll(even, LANES // 2, 1), odd)
    return left, right


def pack_ffn_kernel(chunk, place_ref, gate, up, down_w, *outs):
    core = place_ref[3]
    rows = gate.shape[0]

    def put(at, size, column, part):
        span, width = outs[0].shape[0], part.shape[1]
        out, at = (outs[0], at) if at < span else (outs[1], at - span)
        out[at : at + size, column : column + width] = part

    for matrix, ref in enumerate((gate, up)):
        for pair in range(8):
            windows = [
                ref[:, pl.ds(pl.multiple_of((2 * pair + odd) * 256 + core * LANES, LANES), LANES)]
                for odd in range(2)
            ]
            packed = interleave(windows[0].astype(wide), windows[1].astype(wide))[chunk]
            at = (matrix * 2 + pair // 4) * rows
            column = pair % 4 * LANES
            put(at, rows, column, packed.astype(low))
    units = down_w[pl.ds(pl.multiple_of(core * LANES + chunk * 64, 64), 64), :]
    for slab in range(3):
        at = 4 * rows + slab * 64
        put(at, 64, 0, units[:, slab * SLAB : (slab + 1) * SLAB])


def pack_ffn(place, chunk, parts, gate, up, down_w, after):
    outs = [shaped((rows, SLAB), low) for rows in parts]
    return run(
        functools.partial(pack_ffn_kernel, chunk),
        "pack_ffn",
        place,
        (1,),
        [(item, whole(item)) for item in (gate, up, down_w)],
        [(out, whole(out)) for out in outs],
        after=after,
    )


def rows_in(ref, at, rows):
    if at >= FFN_HALF:
        at += ref.shape[0] // 2 - FFN_HALF
    return ref[at : at + rows, :]


def unpack_ffn_kernel(place_ref, mine_0, mine_1, other_0, other_1, gate, up, down_w):
    core = place_ref[3]
    rows = gate.shape[0]
    for owner, chunks in ((core, (mine_0, mine_1)), (1 - core, (other_0, other_1))):
        for matrix, ref in enumerate((gate, up)):
            for pair in range(8):
                at = (matrix * 2 + pair // 4) * rows
                column = pair % 4 * LANES
                parts = [
                    rows_in(chunk, at, rows)[:, column : column + LANES].astype(wide)
                    for chunk in chunks
                ]
                for odd, window in enumerate(interleave(*parts)):
                    place = (2 * pair + odd) * 256 + owner * LANES
                    ref[:, pl.ds(pl.multiple_of(place, LANES), LANES)] = window
        for index, chunk in enumerate(chunks):
            for slab in range(3):
                at = 4 * rows + slab * 64
                place = pl.multiple_of(owner * LANES + index * 64, 64)
                part = rows_in(chunk, at, 64).astype(wide)
                down_w[pl.ds(place, 64), slab * SLAB : (slab + 1) * SLAB] = part


def unpack_ffn(place, mine, other, shapes, after):
    outs = [shaped(shape, wide) for shape in shapes]
    return run(
        unpack_ffn_kernel,
        "unpack_ffn",
        place,
        (1,),
        [(item, whole(item)) for item in (*mine, *other)],
        [(out, whole(out)) for out in outs],
        after=after,
    )


def unpack_first_kernel(
    place_ref, mine, other, joint_mine, joint_other, query, key, value, square
):
    core = place_ref[3]
    rows = query.shape[0]

    def put(ref, owner, part):
        columns = ref.shape[1] // 2
        at = pl.ds(pl.multiple_of(owner * columns, LANES), columns)
        ref[:, at] = part.astype(wide)

    for owner, qkv, joint in ((core, mine, joint_mine), (1 - core, other, joint_other)):
        slabs = [qkv[slab * rows : (slab + 1) * rows, :] for slab in range(3)]
        put(query, owner, jnp.concatenate([slabs[0], slabs[1][:, :256]], axis=1))
        put(key, owner, jnp.concatenate([slabs[1][:, 256:], slabs[2][:, :128]], axis=1))
        put(value, owner, slabs[2][:, 128:])
        half = FFN_HALF + OUT_HALF
        out = [joint[part * half + FFN_HALF : (part + 1) * half, :] for part in range(2)]
        out = jnp.concatenate(out, axis=0)
        rest = out[rows : rows + rows // 2, :]
        rest = jnp.concatenate([rest[:, :256], rest[:, 256:]], axis=0)
        put(square, owner, jnp.concatenate([out[:rows, :], rest], axis=1))


def unpack_first(place, parts, shapes, after):
    outs = [shaped(shape, wide) for shape in shapes]
    return run(
        unpack_first_kernel,
        "unpack_first",
        place,
        (1,),
        [(item, whole(item)) for item in parts],
        [(out, whole(out)) for out in outs],
        after=after,
    )


def turn_table(position):
    frequency = rope_base ** (-jnp.arange(HALF, dtype=wide) * 2.0 / HD)
    angle = position.astype(wide)[:, None] * frequency[None, :]
    gap = jnp.zeros((position.shape[0], LANES // 2 - HALF), wide)
    cosine, sine = jnp.cos(angle), jnp.sin(angle)
    return (
        jnp.concatenate([cosine, gap, cosine, gap], axis=1),
        jnp.concatenate([-sine, gap, sine, gap], axis=1),
    )


def qkv_kernel(tiles, place_ref, own_ref, far_ref, cos_ref, sin_ref, *refs):
    pieces = refs[:5]
    normed_ref, q_ref, k_ref, v_ref, w_ref, gain_ref, gain_rows, x_ref, sems = refs[5:]
    step = pl.program_id(0)

    @pl.when(step < tiles)
    def _():
        x_ref[...] = own_ref[...]

    @pl.when(step >= tiles)
    def _():
        x_ref[...] = far_ref[...]

    @pl.when(pl.program_id(0) == 0)
    def _():
        fetch(
            place_ref, from_pieces(pieces, FIRST_HALF), FIRST_QKV_PLAN, (w_ref, gain_rows), sems
        )
        drain((w_ref, gain_rows), sems)
        for index in range(2):
            parts = [
                gain_rows[16 * block : 16 * block + 16, index * LANES : (index + 1) * LANES]
                for block in range(BLOCKS)
            ]
            parts = [part.astype(wide)[:8, :HD] for part in parts]
            gain_ref[8 * index : 8 * index + 8, :] = jnp.concatenate(parts, axis=1)

    hidden = x_ref[...].astype(wide)
    scale = lax.rsqrt(jnp.mean(hidden * hidden, axis=-1, keepdims=True) + epsilon)
    normed = (hidden * scale * gain_ref[0:1, :]).astype(low)
    normed_ref[...] = normed
    gap = jnp.zeros((x_ref.shape[0], LANES // 2 - HALF), wide)
    heads = q_ref.shape[1] // LANES
    groups = k_ref.shape[1] // LANES
    count = 4
    for first in range(0, heads + 2 * groups, count):
        part = project(normed, w_ref[:, first * HD : (first + count) * HD])
        for index in range(first, first + count):
            at = (index - first) * HD
            if index >= heads + groups:
                column = (index - heads - groups) * LANES
                padded = jnp.concatenate([part[:, at : at + HD], gap, gap], axis=1)
                v_ref[:, column : column + LANES] = padded.astype(low)
                continue
            padded = jnp.concatenate(
                [part[:, at : at + HALF], gap, part[:, at + HALF : at + HD], gap], axis=1
            )
            turned = pltpu.roll(padded, LANES // 2, 1)
            padded = (padded * cos_ref[...] + turned * sin_ref[...]).astype(low)
            if index < heads:
                q_ref[:, index * LANES : (index + 1) * LANES] = padded
            else:
                column = (index - heads) * LANES
                k_ref[:, column : column + LANES] = padded


def project_qkv(place, own, far, cosine, sine, pieces, after):
    count, width = own.shape
    tile = 320
    tiles = count // tile
    count = 2 * count
    heads, groups = H // 2 * LANES, KV // 2 * LANES
    weight, gains = shaped((width, width), low), shaped((16, width), wide)
    early = pl.BlockSpec((tile, width), lambda i, place: (jnp.minimum(i, tiles - 1), 0))
    late = pl.BlockSpec((tile, width), lambda i, place: (jnp.maximum(i - tiles, 0), 0))
    return run(
        functools.partial(qkv_kernel, tiles),
        "project_qkv",
        place,
        (count // tile,),
        [
            (own, early),
            (far, late),
            (cosine, rows_of(tile, LANES)),
            (sine, rows_of(tile, LANES)),
        ]
        + [(piece, anywhere) for piece in pieces],
        [
            (shaped((count, width), low), rows_of(tile, width)),
            (shaped((count, heads), low), rows_of(tile, heads)),
            (shaped((count, groups), low), rows_of(tile, groups)),
            (shaped((count, groups), low), rows_of(tile, groups)),
            (weight, whole(weight)),
            (gains, whole(gains)),
        ],
        [
            pltpu.VMEM((BLOCKS * 16, SLAB), low),
            pltpu.VMEM((tile, width), low),
            pltpu.SemaphoreType.DMA((2,)),
        ],
        after,
        us=18,
    )


def fill_bias(bias_ref, column_ref, row_ref):
    size = bias_ref.shape[0]
    for start in range(0, size, TILE):
        shape = (TILE, size)
        slots = lax.broadcasted_iota(jnp.int32, shape, 0) + start
        keys = lax.broadcasted_iota(jnp.int32, shape, 1)
        same = column_ref[start : start + TILE, :] == row_ref[0]
        allowed = same & (keys <= slots)
        bias_ref[start : start + TILE, :] = jnp.where(allowed, 0.0, masked_score)


LOG2_E = 1.4426950408889634


def both_heads(ref, start):
    rows = slice(start, start + TILE)
    return jnp.concatenate([ref[rows, :LANES], ref[rows, LANES:]], axis=0)


def attend_kernel(
    place_ref, q_ref, k_ref, v_ref, column_ref, row_ref, out_ref, total_ref, bias_ref
):
    group = pl.program_id(0)
    size = q_ref.shape[0]

    @pl.when(group == 0)
    def _():
        fill_bias(bias_ref, column_ref, row_ref)
        total_ref[...] = jnp.zeros_like(total_ref)

    lane = lax.broadcasted_iota(jnp.int32, (TILE, LANES), 1)
    for start in range(0, size, TILE):
        stop = start + TILE
        raw = across(both_heads(q_ref, start), k_ref[:stop, :])
        bias = bias_ref[start:stop, :stop]
        scores = raw * (HD ** (-0.5) * LOG2_E) + jnp.concatenate([bias, bias], axis=0)
        top = jnp.max(scores, axis=-1, keepdims=True)
        powers = jnp.exp2(scores - top)
        amount = jnp.sum(powers, axis=-1, keepdims=True)
        probs = (powers * (1.0 / amount)).astype(low)
        mixed = project(probs, v_ref[:stop, :]).astype(low)
        total = top + jnp.log2(amount)
        kept = total_ref[start:stop, :]
        for head in range(2):
            rows = slice(head * TILE, (head + 1) * TILE)
            out_ref[start:stop, head * LANES : (head + 1) * LANES] = mixed[rows]
            kept = jnp.where(lane == 2 * group + head, total[rows], kept)
        total_ref[start:stop, :] = kept


def attention_specs(size, block):
    return dict(
        pair=pl.BlockSpec((size, 2 * LANES), lambda g, place: (block, g)),
        one=pl.BlockSpec((size, LANES), lambda g, place: (block, g)),
        pair_alone=pl.BlockSpec((size, 2 * LANES), lambda g, place: (0, g)),
        one_alone=pl.BlockSpec((size, LANES), lambda g, place: (0, g)),
        shared=pl.BlockSpec((size, LANES), lambda g, place: (block, 0)),
        alone=pl.BlockSpec((size, LANES), lambda g, place: (0, 0)),
        column=pl.BlockSpec((size, 1), lambda g, place: (block, 0)),
        row=pl.BlockSpec((1, 1, size), lambda g, place: (block, 0, 0)),
    )


def attend(place, q, k, v, segment, block, after=()):
    blocks, size = segment.shape
    spec = attention_specs(size, block)
    return run(
        attend_kernel,
        "attend",
        place,
        (k.shape[1] // LANES,),
        [
            (q, spec["pair"]),
            (k, spec["one"]),
            (v, spec["one"]),
            (segment.reshape(blocks * size, 1), spec["column"]),
            (segment.reshape(blocks, 1, size), spec["row"]),
        ],
        [
            (shaped((size, q.shape[1]), low), spec["pair_alone"]),
            (shaped((size, LANES), wide), spec["alone"]),
        ],
        [pltpu.VMEM((size, size), wide)],
        after,
        us=17,
    )


def attend_back_kernel(
    place_ref,
    q_ref,
    k_ref,
    v_ref,
    grad_ref,
    out_ref,
    total_ref,
    column_ref,
    row_ref,
    cos_ref,
    sin_ref,
    dq_ref,
    dk_ref,
    dv_ref,
    bias_ref,
    dk_sum,
    dv_sum,
):
    group = pl.program_id(0)
    size = q_ref.shape[0]

    @pl.when(group == 0)
    def _():
        fill_bias(bias_ref, column_ref, row_ref)

    def turned_back(grad, rows):
        turned = pltpu.roll(grad, LANES // 2, 1)
        return (grad * cos_ref[rows, :] - turned * sin_ref[rows, :]).astype(low)

    dk_sum[...] = jnp.zeros_like(dk_sum)
    dv_sum[...] = jnp.zeros_like(dv_sum)
    lane = lax.broadcasted_iota(jnp.int32, (TILE, LANES), 1)
    scale = HD ** (-0.5)
    for start in range(0, size, TILE):
        stop = start + TILE
        queries, grads = both_heads(q_ref, start), both_heads(grad_ref, start)
        mixed = both_heads(out_ref, start)
        delta = jnp.sum(grads.astype(wide) * mixed.astype(wide), axis=-1, keepdims=True)
        totals = [
            jnp.sum(
                jnp.where(lane == 2 * group + head, total_ref[start:stop, :], 0.0),
                axis=-1,
                keepdims=True,
            )
            for head in range(2)
        ]
        bias = bias_ref[start:stop, :stop]
        raw = across(queries, k_ref[:stop, :])
        scores = raw * (scale * LOG2_E) + jnp.concatenate([bias, bias], axis=0)
        probs = jnp.exp2(scores - jnp.concatenate(totals, axis=0))
        dv_sum[:stop, :] += down(probs.astype(low), grads)
        grad_probs = across(grads, v_ref[:stop, :])
        grad_raw = (probs * (grad_probs - delta)).astype(low)
        dq = project(grad_raw, k_ref[:stop, :]) * scale
        for head in range(2):
            part = turned_back(dq[head * TILE : (head + 1) * TILE], slice(start, stop))
            dq_ref[start:stop, head * LANES : (head + 1) * LANES] = part
        dk_sum[:stop, :] += down(grad_raw, queries)
    dv_ref[...] = dv_sum[...].astype(low)
    dk_ref[...] = turned_back(dk_sum[...] * scale, slice(None))


def attend_back(place, q, k, v, grad, out, total, segment, cosine, sine, block, after=()):
    blocks, size = segment.shape
    spec = attention_specs(size, block)
    return run(
        attend_back_kernel,
        "attend_back",
        place,
        (k.shape[1] // LANES,),
        [
            (q, spec["pair"]),
            (k, spec["one"]),
            (v, spec["one"]),
            (grad, spec["pair_alone"]),
            (out, spec["pair_alone"]),
            (total, spec["alone"]),
            (segment.reshape(blocks * size, 1), spec["column"]),
            (segment.reshape(blocks, 1, size), spec["row"]),
            (cosine, spec["shared"]),
            (sine, spec["shared"]),
        ],
        [
            (shaped((size, q.shape[1]), low), spec["pair_alone"]),
            (shaped((size, k.shape[1]), low), spec["one_alone"]),
            (shaped((size, v.shape[1]), low), spec["one_alone"]),
        ],
        [
            pltpu.VMEM((size, size), wide),
            pltpu.VMEM((size, LANES), wide),
            pltpu.VMEM((size, LANES), wide),
        ],
        after,
        us=21,
    )


def out_weight_kernel(place_ref, *refs):
    pieces, weights, whole_weight, sems = refs[:5], refs[5:7], refs[7], refs[8]
    fetch(place_ref, from_pieces(pieces, FIRST_HALF), FIRST_OUT_PLAN, (whole_weight,), sems)
    zeros = jnp.zeros((LANES - HD, whole_weight.shape[1]), low)
    for block in range(BLOCKS):
        whole_weight[pl.ds(block * LANES + HD, LANES - HD), :] = zeros
    drain((whole_weight.at[pl.ds(0, BLOCKS * HD)],), sems)
    rows = weights[0].shape[0]
    for part in range(2):
        weights[part][...] = whole_weight[part * rows : (part + 1) * rows, :]


def out_weight(place, pieces, width, after):
    out = shaped((H // 2 * LANES, width // 2), low)
    return run(
        out_weight_kernel,
        "out_weight",
        place,
        (1,),
        [(piece, anywhere) for piece in pieces],
        [(out, whole(out))] * 2,
        [pltpu.VMEM((H * LANES, width // 2), low), pltpu.SemaphoreType.DMA((1,))],
        after,
    )


def middle_kernel(
    place_ref, x_ref, mine_ref, other_ref, *refs
):
    w_mine, w_other, (gain_ref, middle_ref, out_ref, heads) = refs[:2], refs[2:4], refs[4:]
    core = place_ref[3]
    span = mine_ref.shape[1]
    heads[:, pl.ds(pl.multiple_of(core * span, LANES), span)] = mine_ref[...]
    heads[:, pl.ds(pl.multiple_of((1 - core) * span, LANES), span)] = other_ref[...]
    columns = w_mine[0].shape[1]
    for owner, weight in ((core, w_mine), (1 - core, w_other)):
        at = pl.ds(pl.multiple_of(owner * columns, LANES), columns)
        branch = project(heads[:, :span], weight[0][...])
        branch = branch + project(heads[:, span:], weight[1][...])
        middle_ref[:, at] = x_ref[:, at].astype(wide) + branch
    hidden = middle_ref[...]
    scale = lax.rsqrt(jnp.mean(hidden * hidden, axis=-1, keepdims=True) + epsilon)
    out_ref[...] = (hidden * scale * gain_ref[8:9, :]).astype(low)


def middle_of(place, x, mine, other, w_mine, w_other, gains, after=()):
    count, width = x.shape
    tile, span = count // 2, mine.shape[1]
    return run(
        middle_kernel,
        "middle",
        place,
        (2,),
        [
            (x, rows_of(tile, width)),
            (mine, rows_of(tile, span)),
            (other, rows_of(tile, span)),
            *[(item, whole(item)) for item in (*w_mine, *w_other, gains)],
        ],
        [
            (shaped((count, width), wide), rows_of(tile, width)),
            (shaped((count, width), low), rows_of(tile, width)),
        ],
        [pltpu.VMEM((tile, 2 * span), low)],
        after,
        us=11,
    )


def middle_back_kernel(
    place_ref,
    middle_ref,
    mine_0,
    mine_1,
    other_0,
    other_1,
    cotangent_ref,
    gain_ref,
    *refs,
):
    w_mine, w_other, refs = refs[:2], refs[2:4], refs[4:]
    grad_ref, branch_mine, branch_other, heads_mine, heads_other, gain_grad, branch, heads = refs
    core = place_ref[3]
    hidden = middle_ref[...]
    scale = lax.rsqrt(jnp.mean(hidden * hidden, axis=-1, keepdims=True) + epsilon)
    parts = (mine_0, mine_1, other_0, other_1)
    incoming = sum(ref[...].astype(wide) for ref in parts)
    weighted = incoming * gain_ref[8:9, :]
    inner = jnp.mean(weighted * hidden, axis=-1, keepdims=True)
    grad = cotangent_ref[...].astype(wide) + (scale * weighted - hidden * scale**3 * inner)
    grad_ref[...] = grad
    branch[...] = grad.astype(low)

    @pl.when(pl.program_id(0) == 0)
    def _():
        gain_grad[...] = jnp.zeros_like(gain_grad)

    summed = jnp.sum(incoming * hidden * scale, axis=0, keepdims=True)
    gain_grad[...] += jnp.broadcast_to(summed, gain_grad.shape)
    columns, span = w_mine[0].shape[1], heads_mine.shape[1]

    def part(ref, owner, size):
        return ref[:, pl.ds(pl.multiple_of(owner * size, LANES), size)]

    branch_mine[...] = part(branch, core, columns)
    branch_other[...] = part(branch, 1 - core, columns)
    for at in range(0, 2 * span, SLAB):
        index, rows = at // span, slice(at % span, at % span + SLAB)
        heads[:, at : at + SLAB] = (
            across(branch_mine[...], w_mine[index][rows, :])
            + across(branch_other[...], w_other[index][rows, :])
        ).astype(low)
    heads_mine[...] = part(heads, core, span)
    heads_other[...] = part(heads, 1 - core, span)


def middle_back(place, middle, parts, cotangent, gains, w_mine, w_other, after=()):
    count, width = middle.shape
    tile, columns, span = count // 2, w_mine[0].shape[1], w_mine[0].shape[0]
    gain_grad = shaped((8, width), wide)
    return run(
        middle_back_kernel,
        "middle_back",
        place,
        (2,),
        [
            *[(item, rows_of(tile, width)) for item in (middle, *parts, cotangent)],
            *[(item, whole(item)) for item in (gains, *w_mine, *w_other)],
        ],
        [
            (shaped((count, width), wide), rows_of(tile, width)),
            (shaped((count, columns), low), rows_of(tile, columns)),
            (shaped((count, columns), low), rows_of(tile, columns)),
            (shaped((count, span), low), rows_of(tile, span)),
            (shaped((count, span), low), rows_of(tile, span)),
            (gain_grad, whole(gain_grad)),
        ],
        [pltpu.VMEM((tile, width), low), pltpu.VMEM((tile, 2 * span), low)],
        after,
        us=15,
    )


def out_grad_kernel(
    place_ref,
    own_mine,
    own_other,
    far_mine,
    far_other,
    branch_own,
    branch_far,
    *refs,
):
    outs, (grad, sems) = refs[:5], refs[5:]
    core = place_ref[3]
    span = own_mine.shape[1]
    for owner, own, far in ((core, own_mine, far_mine), (1 - core, own_other, far_other)):
        for at in range(0, span, SLAB):
            part = down(own[:, at : at + SLAB], branch_own[...])
            part = part + down(far[:, at : at + SLAB], branch_far[...])
            grad[pl.ds(pl.multiple_of(owner * span + at, LANES), SLAB), :] = part.astype(low)
    for k in range(4):
        base = (place_ref[0] ^ k) * 4
        send_off(place_ref, k, (grad,), base, OUT_PLAN, OUT_HALF, outs, sems)
    fill_spare(grad.at[pl.ds(0, 16), pl.ds(0, SLAB)], 144, 16, OUT_HALF, outs, sems)
    drain(outs, sems)


def out_grad(place, own_mine, own_other, far_mine, far_other, branch_own, branch_far, after=()):
    columns = branch_own.shape[1]
    operands = (own_mine, own_other, far_mine, far_other, branch_own, branch_far)
    return run(
        out_grad_kernel,
        "out_grad",
        place,
        (1,),
        [(item, whole(item)) for item in operands],
        sent_shapes(OUT_HALF, SLAB),
        [pltpu.VMEM((H * LANES, columns), low), pltpu.SemaphoreType.DMA((5,))],
        after,
        us=10,
    )


FFN_TILE = 640
FFN_STEP = 256
FFN_SPAN = 768


def load_tokens(ref, own, far, sem):
    count = far.shape[0]
    for part, source in enumerate((far, own)):
        pltpu.make_async_copy(source, ref.at[pl.ds(part * count, count)], sem).start()


def ffn_forward(step, tiles, x_ref, c_ref, weights, sums, middles, at_rows):
    gate_w, up_w, down_w = weights
    inner, grad_gate, grad_up = middles
    units, width = gate_w.shape[1], gate_w.shape[0]
    rows = pl.ds(pl.multiple_of(step * FFN_TILE, FFN_TILE), FFN_TILE)

    @pl.loop(0, units // FFN_STEP)
    def _(index):
        at = pl.ds(pl.multiple_of(index * FFN_STEP, FFN_STEP), FFN_STEP)
        gate = project(x_ref[rows, :], gate_w[:, at])
        upward = project(x_ref[rows, :], up_w[:, at])
        grad_inner = across(c_ref[rows, :], down_w[at, :])
        sigma = 1.0 / (1.0 + jnp.exp(-gate))
        silu = gate * sigma
        inner[at_rows, at] = (silu * upward).astype(low)
        grad_up[at_rows, at] = (grad_inner * silu).astype(low)
        grad_gate[at_rows, at] = (
            grad_inner * upward * sigma * (1.0 + gate * (1.0 - sigma))
        ).astype(low)

    for part in range(2):

        @pl.when((step >= part * tiles // 2) & (step < (part + 1) * tiles // 2))
        def _():
            out_ref, normed_ref = sums[2 * part : 2 * part + 2]

            @pl.loop(0, width // SLAB)
            def _(index):
                at = pl.ds(pl.multiple_of(index * SLAB, SLAB), SLAB)
                out = project(inner[at_rows, :], down_w[:, at])
                normed = across(grad_gate[at_rows, :], gate_w[at, :])
                normed = normed + across(grad_up[at_rows, :], up_w[at, :])
                out_ref[:, at] = out.astype(out_ref.dtype)
                normed_ref[:, at] = normed.astype(normed_ref.dtype)


def ffn_backward(
    place_ref, k, x_ref, c_ref, middles, stages, turned, turned_units, sent, sems, wait
):
    inner, grad_gate, grad_up = middles
    stage_gate, stage_up, stage_down = stages
    width, units = x_ref.shape[1], inner.shape[1]
    depth = place_ref[0] ^ k
    rows, span = width // 4, units // 4
    here = pl.ds(pl.multiple_of(depth * rows, LANES), rows)
    there = pl.ds(pl.multiple_of(depth * span, LANES), span)
    wait(x_ref, grad_gate)
    turned[...] = x_ref[:, here].T
    to = pl.ds(pl.multiple_of(k * rows, 16), rows)
    to_units = pl.ds(pl.multiple_of(k * span, 16), span)
    stage_gate[to, :] = project(turned[...], grad_gate[...]).astype(low)
    wait(grad_up)
    stage_up[to, :] = project(turned[...], grad_up[...]).astype(low)
    wait(inner, c_ref)
    turned_units[...] = inner[:, there].T

    @pl.loop(0, width // FFN_SPAN)
    def _(index):
        at = pl.ds(pl.multiple_of(index * FFN_SPAN, FFN_SPAN), FFN_SPAN)
        stage_down[to_units, at] = project(turned_units[...], c_ref[:, at]).astype(low)

    send_off(place_ref, k, stages, k * 4, FFN_PLAN, FFN_HALF, sent, sems)


def ffn_forward_kernel(tiles, pieces, place_ref, *refs):
    tokens, pieces, refs = refs[:4], refs[4 : 4 + pieces], refs[4 + pieces :]
    sums, middles = refs[:4], refs[4:7]
    x_ref, c_ref, *weights, x_sems, in_sems = refs[7:]
    step = pl.program_id(0)

    @pl.when(step == 0)
    def _():
        x_own, x_far, c_own, c_far = tokens
        load_tokens(x_ref, x_own, x_far, x_sems.at[0])
        load_tokens(c_ref, c_own, c_far, x_sems.at[1])
        if len(pieces) == 5:
            fetch(place_ref, from_pieces(pieces, FFN_HALF), FFN_PLAN, weights, in_sems)
        else:
            source = from_pieces(pieces[:5], UPPER_ROWS // 2)
            fetch(place_ref, source, UPPER_PLAN, weights, in_sems)
            fetch(place_ref, from_planes(*pieces[5:]), LOWER_PLAN, weights, in_sems)
        drain((x_ref, c_ref), x_sems)
        drain(weights, in_sems)

    ffn_forward(step, tiles, x_ref, c_ref, weights, sums, middles, slice(None))


def ffn_backward_kernel(place_ref, *refs):
    tokens, sources, sent = refs[:4], refs[4:7], refs[7:12]
    x_ref, c_ref, *rest = refs[12:]
    middles, stages, rest = rest[:3], rest[3:6], rest[6:]
    turned, turned_units, x_sems, in_sems, out_sems = rest
    k = pl.program_id(0)

    x_own, x_far, c_own, c_far = tokens

    def middle(index):
        pltpu.make_async_copy(sources[index], middles[index], in_sems.at[index]).start()

    @pl.when(k == 0)
    def _():
        load_tokens(x_ref, x_own, x_far, x_sems.at[0])
        middle(1)
        middle(2)
        middle(0)
        load_tokens(c_ref, c_own, c_far, x_sems.at[1])

    arrived = [(x_ref, x_sems.at[0]), (c_ref, x_sems.at[1])]
    arrived += [(ref, in_sems.at[index]) for index, ref in enumerate(middles)]

    def wait(*refs):
        @pl.when(k == 0)
        def _():
            for ref, sem in arrived:
                if any(ref is other for other in refs):
                    pltpu.make_async_copy(ref, ref, sem).wait()

    ffn_backward(
        place_ref, k, x_ref, c_ref, middles, stages, turned, turned_units, sent, out_sems, wait
    )

    @pl.when(k == 3)
    def _():
        drain(sent, out_sems)


FFN_UNITS = 1024


def ffn_sums(count, width):
    last = count // FFN_TILE - 1
    early = pl.BlockSpec((FFN_TILE, width), lambda i, place: (jnp.minimum(i, last), 0))
    late = pl.BlockSpec(
        (FFN_TILE, width), lambda i, place: (jnp.clip(i - last - 1, 0, last), 0)
    )
    return [(shaped((count, width), low), spec) for spec in (early, early, late, late)]


def ffn_scratch(count, width, weights=True, middles=True, stages=True):
    weight = [pltpu.VMEM((width, FFN_UNITS), low)] * 2 + [pltpu.VMEM((FFN_UNITS, width), low)]
    shapes = [pltpu.VMEM((count, width), low)] * 2
    shapes += weight if weights else []
    shapes += [pltpu.VMEM((count, FFN_UNITS), low)] * 3 if middles else []
    if stages:
        shapes += weight
        shapes += [pltpu.VMEM((width // 4, count), low)]
        shapes += [pltpu.VMEM((FFN_UNITS // 4, count), low)]
    shapes += [pltpu.SemaphoreType.DMA((2,)), pltpu.SemaphoreType.DMA((3,))]
    return shapes + ([pltpu.SemaphoreType.DMA((5,))] if stages else [])


def ffn_chunk_forward(place, tokens, pieces, after=()):
    count, width = tokens[0].shape
    tiles = 2 * count // FFN_TILE
    middle = pl.BlockSpec((FFN_TILE, FFN_UNITS), lambda i, place: (i, 0))
    results = run(
        functools.partial(ffn_forward_kernel, tiles, len(pieces)),
        "ffn_forward",
        place,
        (tiles,),
        [(item, anywhere) for item in (*tokens, *pieces)],
        ffn_sums(count, width) + [(shaped((2 * count, FFN_UNITS), low), middle)] * 3,
        ffn_scratch(2 * count, width, middles=False, stages=False),
        after,
        us=36,
    )
    return results[:4], results[4:]


def ffn_chunk_backward(place, tokens, middles, after=()):
    count, width = tokens[0].shape
    return run(
        ffn_backward_kernel,
        "ffn_backward",
        place,
        (4,),
        [(item, anywhere) for item in (*tokens, *middles)],
        sent_shapes(FFN_HALF, SLAB),
        ffn_scratch(2 * count, width, weights=False),
        after,
        us=22,
    )


def input_back_kernel(
    tiles, place_ref, own_q, own_k, own_v, far_q, far_k, far_v, x_own, x_far, w_ref, *refs
):
    grad_ref, own_ref, far_ref, gain_grad = refs
    step = pl.program_id(0)

    @pl.when(step == 0)
    def _():
        gain_grad[...] = jnp.zeros_like(gain_grad)

    def squeezed(query, key, value):
        parts = []
        for ref in (query, key):
            for at in range(0, ref.shape[1], LANES):
                head = ref[:, at : at + LANES].astype(wide)
                parts.append(head[:, :HALF])
                parts.append(head[:, LANES // 2 : LANES // 2 + HALF])
        for at in range(0, value.shape[1], LANES):
            parts.append(value[:, at : at + LANES].astype(wide)[:, :HD])
        return jnp.concatenate(parts, axis=1).astype(low)

    def rest(x_ref, incoming):
        hidden = x_ref[...].astype(wide)
        scale = lax.rsqrt(jnp.mean(hidden * hidden, axis=-1, keepdims=True) + epsilon)
        summed = jnp.sum(incoming * hidden * scale, axis=0, keepdims=True)
        gain_grad[...] += jnp.broadcast_to(summed, gain_grad.shape)

    @pl.when(step < tiles)
    def _():
        grad_ref[...] = squeezed(far_q, far_k, far_v)
        incoming = across(grad_ref[...], w_ref[...])
        far_ref[...] = incoming.astype(low)
        rest(x_far, incoming)

    @pl.when(step >= tiles)
    def _():
        grad_ref[...] = squeezed(own_q, own_k, own_v)
        incoming = across(grad_ref[...], w_ref[...])
        own_ref[...] = incoming.astype(low)
        rest(x_own, incoming)


def input_back(place, own, far, x_own, x_far, weight, after=()):
    count, width = 2 * x_own.shape[0], x_own.shape[1]
    tile = 320
    tiles = count // 2 // tile
    gain_grad = shaped((8, width), wide)

    def late(columns):
        return pl.BlockSpec((tile, columns), lambda i, place: (jnp.maximum(i - tiles, 0), 0))

    def early(columns):
        return pl.BlockSpec((tile, columns), lambda i, place: (jnp.minimum(i, tiles - 1), 0))

    def both(columns):
        return pl.BlockSpec((tile, columns), lambda i, place: (lax.rem(i + tiles, 2 * tiles), 0))

    return run(
        functools.partial(input_back_kernel, tiles),
        "input_back",
        place,
        (2 * tiles,),
        [(item, late(item.shape[1])) for item in own]
        + [(item, early(item.shape[1])) for item in far]
        + [(x_own, late(width)), (x_far, early(width)), (weight, whole(weight))],
        [
            (shaped((count, width), low), both(width)),
            (shaped((count // 2, width), low), late(width)),
            (shaped((count // 2, width), low), early(width)),
            (gain_grad, whole(gain_grad)),
        ],
        after=after,
        us=15,
    )


def qkv_grad_kernel(place_ref, x_ref, grad_ref, gain_one, gain_two, *refs):
    outs, (stage, gain_rows, sems) = refs[:5], refs[5:]
    k = pl.program_id(0)
    width = grad_ref.shape[1]

    @pl.when(k == 0)
    def _():
        gap = jnp.zeros((8, LANES - HD), wide)
        row = lax.broadcasted_iota(jnp.int32, (16, LANES), 0)
        gain_rows[...] = jnp.zeros_like(gain_rows)
        for block in range(BLOCKS):
            for index, gain in enumerate((gain_one, gain_two)):
                part = jnp.concatenate([gain[:, block * HD : (block + 1) * HD], gap], axis=1)
                part = jnp.where(row == 0, jnp.concatenate([part, part], axis=0), 0.0)
                gain_rows[
                    16 * block : 16 * block + 16, index * LANES : (index + 1) * LANES
                ] = part.astype(low)

    depth = place_ref[0] ^ k
    rows = width // 4
    to = pl.ds(pl.multiple_of(depth * rows, 16), rows)
    stage[to, :] = project(x_ref[...].T, grad_ref[...]).astype(low)
    send_off(place_ref, k, (stage, gain_rows), depth * 4, QKV_PLAN, QKV_HALF, outs, sems)

    @pl.when(k == 3)
    def _():
        fill_spare(gain_rows.at[pl.ds(0, 16)], GAINS + 16, 16, QKV_HALF, outs, sems)
        drain(outs, sems)


def qkv_grad(place, x, grad, gain_one, gain_two, after=()):
    count, width = x.shape
    column = pl.BlockSpec((count, width // 4), lambda k, place: (0, place[0] ^ k))
    return run(
        qkv_grad_kernel,
        "qkv_grad",
        place,
        (4,),
        [(x, column)] + [(item, whole(item)) for item in (grad, gain_one, gain_two)],
        sent_shapes(QKV_HALF, SLAB),
        [
            pltpu.VMEM((width, width), low),
            pltpu.VMEM((BLOCKS * 16, SLAB), low),
            pltpu.SemaphoreType.DMA((5,)),
        ],
        after,
        us=15,
    )


def tokens_grad_kernel(place_ref, x_ref, middle_ref, mine_ref, other_ref, gain_ref, out_ref):
    hidden = x_ref[...].astype(wide)
    scale = lax.rsqrt(jnp.mean(hidden * hidden, axis=-1, keepdims=True) + epsilon)
    incoming = mine_ref[...].astype(wide) + other_ref[...].astype(wide)
    weighted = incoming * gain_ref[0:1, :]
    inner = jnp.mean(weighted * hidden, axis=-1, keepdims=True)
    out_ref[...] = middle_ref[...] + (scale * weighted - hidden * scale**3 * inner)


def tokens_grad(place, x, grad_middle, mine, other, gains, after=()):
    count, width = x.shape
    tile = 128
    return run(
        tokens_grad_kernel,
        "tokens_grad",
        place,
        (count // tile,),
        [(item, rows_of(tile, width)) for item in (x, grad_middle, mine, other)]
        + [(gains, whole(gains))],
        [(shaped((count, width), wide), rows_of(tile, width))],
        after=after,
    )[0]


def output_kernel(place_ref, middle_ref, mine_0, mine_1, other_0, other_1, out_ref):
    parts = (mine_0, mine_1, other_0, other_1)
    total = middle_ref[...] + sum(ref[...].astype(wide) for ref in parts)
    out_ref[...] = total.astype(low)


def output_of(place, middle, parts, after=()):
    count, width = middle.shape
    tile = 128
    return run(
        output_kernel,
        "output",
        place,
        (count // tile,),
        [(item, rows_of(tile, width)) for item in (middle, *parts)],
        [(shaped((count, width), low), rows_of(tile, width))],
        after=after,
    )[0]


def swap(array):
    return lax.ppermute(array, "rep", [(0, 1), (1, 0)])


def hop(array, z_flip, y_flip, x_flip):
    flip = (z_flip * 2 + y_flip) * 2 + x_flip
    return lax.ppermute(array, "fsdp", [(chip, chip ^ flip) for chip in range(BLOCKS)])


def hop_x(array):
    return hop(array, 0, 0, 1)


def hop_y(array):
    return hop(array, 0, 1, 0)


def near(line):
    return hop_x(line), hop_y(line)


def pieces_of(blocks):
    cut = blocks.reshape(4, 2, 2, *blocks.shape[1:])
    half = blocks.shape[1] // 2
    far = cut[:, 1, 1]
    return cut[:, 0, 0], cut[:, 0, 1], cut[:, 1, 0], far[:, :half], far[:, half:]


def blocks_of(sent):
    to_x, to_y, late_x, late_y, own = sent
    near_x = jnp.stack([to_x[1], late_x], axis=1)
    near_y = jnp.stack([late_y, to_y[1]], axis=1)
    far = jnp.stack([to_x[0], to_y[0]], axis=1)
    cut = jnp.stack([jnp.stack([own, near_x], 1), jnp.stack([near_y, far], 1)], 1)
    return cut.reshape(BLOCKS, 2 * own.shape[2], own.shape[3])


def layout(length_row, count):
    ends = jnp.cumsum(length_row)
    slots = jnp.arange(count, dtype=jnp.int32)
    passed = (slots[:, None] >= ends[None, :]).astype(jnp.int32)
    segment = jnp.sum(passed, axis=1)
    position = slots - jnp.sum(passed * length_row[None, :], axis=1)
    return position, segment


class Direct:
    def __init__(self, place, weights):
        self.place = place
        self.weights = weights

    def pack_first(self):
        return pack_first(self.place, *self.weights[:4], *self.weights[7:])

    def pack_ffn(self, chunk, parts, after):
        return pack_ffn(self.place, chunk, parts, *self.weights[4:7], after)

    def step_0(self, shard):
        return hop(shard, 2, 0, 0)

    def all_z(self, shard):
        return [hop(shard, k, 0, 0) for k in (1, 2, 3)]

    def join(self, shard, received, after):
        return join(self.place, [shard, *received], after)

    def step_1(self, shard, received, after=()):
        return pair_up(self.place, shard, received, after)

    def step_2(self, pair):
        return hop(pair, 1, 0, 0)

    def step_3(self, pair, received, after=()):
        return line_up(self.place, pair, received, after)

    def step_4(self, line):
        return near(line)

    def step_5(self, line, sides, after=()):
        upper, lower = halves(self.place, *sides, after)
        return (line, *sides, hop_y(upper), hop_x(lower)), upper

    def plane(self, parts, after):
        return plane_up(self.place, parts, after)

    def gate(self, sent, pieces):
        return (*gate(self.place, sent[:2], (*pieces[3:5], pieces[6])), *sent[2:])

    def scatter_1(self, sent):
        return hop_x(sent[0]), hop_y(sent[1])

    def scatter_2(self, sent, got, after):
        late_x, late_y = merge(self.place, sent[2], sent[3], got[0], got[1], after)
        return late_x, (hop_x(late_x), hop_y(late_y))

    def scatter_3(self, groups, after):
        groups = [(sent[4], *got, *more) for sent, got, more in groups]
        kept, kept_far, part = sum_plane(self.place, groups, False, after)
        return kept, (kept_far, hop(part, 1, 0, 0))

    def scatter_4(self, kept, parts, after):
        kept_far, near = parts
        token = sum_pass(self.place, kept_far, near, after)
        return token, (near, hop(token, 2, 0, 0))

    def scatter_34(self, sent, got, more, after):
        kept, *parts = sum_plane(self.place, [(sent[4], *got, *more)], True, after)
        return kept, tuple(hop(part, k + 1, 0, 0) for k, part in enumerate(parts))

    def scatter_5(self, kept, parts, after):
        total, total_low = sum_line(self.place, kept, parts, after)
        return total, swap(total_low)

    def pins(self, arrays):
        return tuple(arrays)

    def finish_ffn(self, chunk_0, chunk_1, shapes, after):
        mine, other = zip(chunk_0, chunk_1)
        return unpack_ffn(self.place, mine, other, shapes, after)

    def finish_first(self, first, chunk_1, shapes, owned, after):
        grads = unpack_first(self.place, (*first, *chunk_1), shapes, after)
        both = first[0][GAINS, : 2 * LANES] + first[1][GAINS, : 2 * LANES].astype(wide)
        return grads, (both[:owned], both[LANES : LANES + owned])


def on_device(
    direct,
    tokens,
    lengths,
    attn_gain,
    w_query,
    w_key,
    w_value,
    w_out,
    ffn_gain,
    w_gate,
    w_up,
    w_down,
    cotangent,
):
    count, width = tokens.shape
    owned = attn_gain.shape[0]
    core = lax.axis_index("rep")
    if direct:
        index = lax.axis_index("fsdp")
        spot = (index // 4, (index // 2) % 2, index % 2)
    else:
        spot = (0, 0, 0)
    place = jnp.stack([jnp.int32(item) for item in (*spot, core)])
    weights = (w_query, w_key, w_value, w_out, w_gate, w_up, w_down, attn_gain, ffn_gain)
    routes = Direct(place, weights) if direct else Whole(place, weights)

    first = routes.pack_first()
    far_tokens, far_cotangent = swap(tokens), swap(cotangent)
    laid = [layout(row, count) for row in (lengths[0], swap(lengths)[0])]
    segment = jnp.stack([item[1] for item in laid])
    cosine, sine = turn_table(jnp.concatenate([item[0] for item in laid]))

    received_first = routes.all_z(first)
    whole_rows = 2 * FFN_HALF
    chunk_a, chunk_b = routes.pack_ffn(
        1, (UPPER_ROWS, whole_rows - UPPER_ROWS), (first, far_tokens, far_cotangent)
    )
    if direct:
        chunk_b = chunk_b.reshape(1, *chunk_b.shape)
    sides_b = routes.step_4(chunk_b)
    parts_b, token = routes.step_5(chunk_b, sides_b)
    (chunk_0,) = routes.pack_ffn(0, (whole_rows,), (token,))
    received_0 = routes.step_0(chunk_0)
    plane_b = routes.plane(parts_b, (chunk_0,))
    tables = (far_tokens, far_cotangent, segment, cosine, sine)
    line_first = routes.join(first, received_first, (*tables, plane_b))
    sides_first = routes.step_4(line_first)
    pair_0 = routes.step_1(chunk_0, received_0, (line_first,))
    near_0 = routes.step_2(pair_0)
    received_a = routes.step_0(chunk_a)
    received_b = routes.step_0(plane_b)
    pieces_first, token = routes.step_5(line_first, sides_first, (pair_0,))
    line_0 = routes.step_3(pair_0, near_0, (token,))
    sides_0 = routes.step_4(line_0)
    w_mine = out_weight(place, pieces_first, tokens.shape[1], (line_0,))
    w_other = [swap(part) for part in w_mine]
    normed_low, queries, keys, values, w_qkv, gains = project_qkv(
        place, tokens, far_tokens, cosine, sine, pieces_first, (w_mine[0],)
    )
    far_mine, far_total = attend(place, queries, keys, values, segment, 1, (keys,))
    own_other = swap(far_mine)
    own_mine, own_total = attend(
        place, queries, keys, values, segment, 0, (far_mine, *w_other)
    )
    far_other = swap(own_mine)
    pair_b = routes.step_1(plane_b, received_b, (own_mine,))
    near_b = routes.step_2(pair_b)
    pieces_0, token = routes.step_5(line_0, sides_0, (pair_b, received_a))
    pair_a = routes.step_1(chunk_a, received_a, (token,))
    near_a = routes.step_2(pair_a)
    middle, normed_own = middle_of(
        place, tokens, own_mine, own_other, w_mine, w_other, gains, (pair_a,)
    )
    normed_far = swap(normed_own)
    line_a = routes.step_3(pair_a, near_a, (normed_own, far_other, *pieces_0[3:]))
    sides_a = routes.step_4(line_a)

    inputs = (normed_own, normed_far, cotangent, far_cotangent)
    sums_0, middles_0 = ffn_chunk_forward(place, inputs, pieces_0, (line_a,))
    out_far_0, norm_far_0 = swap(sums_0[0]), swap(sums_0[1])
    pieces_a, token = routes.step_5(line_a, sides_a, (sums_0[0],))
    planes_b = (pair_b, near_b) if direct else chunk_b
    pieces_1 = (*pieces_a, *planes_b)
    sent_0 = ffn_chunk_backward(place, inputs, middles_0, (token,))
    sent_0 = routes.gate(sent_0, pieces_1)
    got_0 = routes.scatter_1(sent_0)
    sums_1, middles_1 = ffn_chunk_forward(place, inputs, pieces_1, (sent_0[0],))
    out_far_1, norm_far_1 = swap(sums_1[0]), swap(sums_1[1])
    token, more_0 = routes.scatter_2(sent_0, got_0, (sums_1[0], out_far_0))
    sent_1 = ffn_chunk_backward(place, inputs, middles_1, (token,))
    got_1 = routes.scatter_1(sent_1)

    norms = (sums_0[3], sums_1[3], norm_far_0, norm_far_1)
    grad_middle, branch_mine, branch_sent, heads_mine, heads_sent, ffn_gain_grad = middle_back(
        place, middle, norms, cotangent, gains, w_mine, w_other, (sent_1[4], *more_0)
    )
    branch_far, heads_far = swap(branch_sent), swap(heads_sent)
    attended = (queries, keys, values)
    tables = (segment, cosine, sine)
    own_grads = attend_back(place, *attended, heads_mine, own_mine, own_total, *tables, 0)
    sent_out = out_grad(
        place,
        own_mine,
        own_other,
        far_mine,
        far_other,
        branch_mine,
        branch_far,
        (own_grads[0],),
    )
    got_out = routes.scatter_1(sent_out)
    kept_0, parts_0 = routes.scatter_3([(sent_0, got_0, more_0)], (sent_out[4],))
    token, more_1 = routes.scatter_2(sent_1, got_1, (kept_0,))
    far_grads = attend_back(
        place, *attended, heads_far, far_mine, far_total, *tables, 1, (token, out_far_1)
    )
    token, more_out = routes.scatter_2(sent_out, got_out, (far_grads[0],))
    token, parts_0 = routes.scatter_4(kept_0, parts_0, (token,))
    grad_qkv, own_part, far_part, attn_gain_grad = input_back(
        place, own_grads, far_grads, tokens, far_tokens, w_qkv, (token,)
    )
    own_rest = swap(far_part)
    sent_qkv = qkv_grad(place, normed_low, grad_qkv, attn_gain_grad, ffn_gain_grad)
    got_qkv = routes.scatter_1(sent_qkv)
    groups = [(sent_1, got_1, more_1), (sent_out, got_out, more_out)]
    kept_1, parts_1 = routes.scatter_3(groups, (sent_qkv[4], *routes.pins(parts_0[1:])))

    owned_0 = routes.scatter_5(kept_0, parts_0, (kept_1,))
    outs = (sums_0[2], sums_1[2], out_far_0, out_far_1)
    output = output_of(place, middle, outs, (owned_0[0],))
    token, more_qkv = routes.scatter_2(sent_qkv, got_qkv, (output,))
    token, parts_1 = routes.scatter_4(kept_1, parts_1, (token,))
    grad_tokens = tokens_grad(place, tokens, grad_middle, own_part, own_rest, gains, (token,))
    kept_qkv, parts_qkv = routes.scatter_34(sent_qkv, got_qkv, more_qkv, (grad_tokens,))
    owned_1 = routes.scatter_5(kept_1, parts_1, (kept_qkv,))
    owned_qkv = routes.scatter_5(kept_qkv, parts_qkv, (owned_1[0],))
    shapes = [w_gate.shape, w_up.shape, w_down.shape]
    grad_gate, grad_up, grad_down = routes.finish_ffn(owned_0, owned_1, shapes, (owned_qkv[0],))
    shapes = [w_query.shape, w_key.shape, w_value.shape, w_out.shape]
    grads, gain_grads = routes.finish_first(owned_qkv, owned_1, shapes, owned, (grad_gate,))
    return (
        output,
        grad_tokens,
        gain_grads[0],
        *grads,
        gain_grads[1],
        grad_gate,
        grad_up,
        grad_down,
    )


class Whole:
    def __init__(self, place, weights):
        self.place = place
        query, key, value, out, gate, up, down_w, gain_one, gain_two = weights
        core = place[3]
        self.core = core
        count = query.shape[1] // query.shape[0]
        self.count = count
        rows = query.shape[1] // BLOCKS

        def full(shard):
            return lax.all_gather(shard, "fsdp", axis=0, tiled=True)

        def mine(weight):
            columns = weight.shape[1] // 2
            return lax.dynamic_slice_in_dim(weight, core * columns, columns, axis=1)

        def slabs(weight):
            blocks = weight.reshape(BLOCKS, -1, weight.shape[1])
            return [blocks[:, :, at : at + SLAB] for at in range(0, weight.shape[1], SLAB)]

        qkv = full(jnp.concatenate([mine(query), mine(key), mine(value)], axis=1))
        gain_rows = jnp.zeros((BLOCKS, 16, SLAB), low)
        for index, gain in enumerate((gain_one, gain_two)):
            part = full(gain).reshape(BLOCKS, rows)
            gain_rows = gain_rows.at[:, 0, index * LANES : index * LANES + rows].set(part)
        square = full(mine(out)).reshape(BLOCKS, rows, -1)
        rest = square[:, :, SLAB:]
        rest = jnp.concatenate([rest[:, : rows // 2], rest[:, rows // 2 :]], axis=2)
        parts = slabs(qkv) + [gain_rows, square[:, :, :SLAB], rest]
        self.first = pieces_of(jnp.concatenate(parts, axis=1))
        quarter = down_w.shape[0] // (2 * CHUNKS)
        self.quarter = quarter

        def units(weight, chunk):
            split = weight.reshape(weight.shape[0], count, 2 * CHUNKS, quarter)
            part = lax.dynamic_index_in_dim(split, CHUNKS * core + chunk, 2, keepdims=False)
            return full(part.reshape(weight.shape[0], count * quarter))

        chunks = []
        for chunk in range(CHUNKS):
            at = (CHUNKS * core + chunk) * quarter
            part = full(lax.dynamic_slice_in_dim(down_w, at, quarter, axis=0))
            parts = slabs(units(gate, chunk)) + slabs(units(up, chunk)) + slabs(part)
            chunks.append(jnp.concatenate(parts, axis=1))
        planes = chunks[1][:, UPPER_ROWS:].reshape(4, 4, -1, SLAB)
        self.ffn_0 = (pieces_of(chunks[0]),)
        self.ffn_1 = pieces_of(chunks[1][:, :UPPER_ROWS]), (planes[0::2], planes[1::2])

    def pack_first(self):
        return self.first

    def pack_ffn(self, chunk, parts, after):
        return (self.ffn_0, self.ffn_1)[chunk]

    def step_0(self, shard):
        return shard

    def all_z(self, shard):
        return ()

    def join(self, shard, received, after):
        return shard

    def step_1(self, shard, received, after=()):
        return shard

    def step_2(self, pair):
        return pair

    def step_3(self, pair, received, after=()):
        return pair

    def step_4(self, line):
        return ()

    def step_5(self, line, sides, after=()):
        return line, line

    def plane(self, parts, after):
        return parts

    def gate(self, sent, pieces):
        return sent

    def scatter_1(self, sent):
        return blocks_of(sent)

    def scatter_2(self, sent, got, after):
        return got, got

    def scatter_3(self, groups, after):
        blocks = jnp.concatenate([got for _, got, _ in groups], axis=1)
        return blocks, blocks

    def scatter_34(self, sent, got, more, after):
        return got, ()

    def scatter_4(self, kept, parts, after):
        return kept, kept

    def scatter_5(self, kept, parts, after):
        return kept, kept

    def split(self, blocks, widths):
        parts, row = [], 0
        for rows, slabs in widths:
            taken = []
            for _ in range(slabs):
                taken.append(blocks[:, row : row + rows])
                row += rows
            part = jnp.concatenate(taken, axis=2)
            part = part.reshape(BLOCKS * rows, part.shape[2])
            parts.append(lax.psum_scatter(part, "fsdp", scatter_dimension=0, tiled=True))
        return parts

    def ordered(self, part):
        other = swap(part).astype(wide)
        part = part.astype(wide)
        first = jnp.where(self.core == 0, part, other)
        return first, jnp.where(self.core == 0, other, part)

    def pins(self, arrays):
        return ()

    def finish_ffn(self, chunk_0, chunk_1, shapes, after):
        gates, ups, downs = [], [], []
        for blocks, _ in (chunk_0, chunk_1):
            gate, up, down_w = self.split(blocks, ((96, 2), (96, 2), (64, 3)))
            gates.append(self.ordered(gate))
            ups.append(self.ordered(up))
            downs.append(self.ordered(down_w))

        def columns(pairs):
            parts = [pairs[chunk][owner] for owner in range(2) for chunk in range(CHUNKS)]
            rows = parts[0].shape[0]
            parts = [part.reshape(rows, self.count, self.quarter) for part in parts]
            return jnp.stack(parts, axis=2).reshape(rows, -1)

        grad_down = [downs[chunk][owner] for owner in range(2) for chunk in range(CHUNKS)]
        return columns(gates), columns(ups), jnp.concatenate(grad_down, axis=0)

    def finish_first(self, first, chunk_1, shapes, owned, after):
        mine = first[0]
        (qkv,) = self.split(mine[:, :GAINS], ((96, 3),))
        blocks = chunk_1[0][:, 2 * FFN_HALF :]
        rest = blocks[:, 96:144]
        rest = jnp.concatenate([rest[:, :, :256], rest[:, :, 256:]], axis=1)
        (square,) = self.split(jnp.concatenate([blocks[:, :96], rest], axis=2), ((96, 1),))
        pair = self.ordered(qkv)
        grads, at = [], 0
        for shape in shapes[:3]:
            columns = shape[1] // 2
            grads.append(jnp.concatenate([item[:, at : at + columns] for item in pair], axis=1))
            at += columns
        grads.append(jnp.concatenate(self.ordered(square), axis=1))
        rows = mine[:, GAINS, : 2 * LANES].astype(wide)
        rows = rows + swap(rows)
        gains = []
        for index in range(2):
            gain = rows[:, index * LANES : index * LANES + 96].reshape(-1)
            gains.append(lax.psum_scatter(gain, "fsdp", scatter_dimension=0, tiled=True))
        return grads, gains


def solution(mesh):
    rows = P(("rep", "fsdp"), None)
    split = P("fsdp", None)
    gain = P("fsdp")
    return jax.shard_map(
        functools.partial(on_device, mesh.shape["fsdp"] == BLOCKS),
        mesh=mesh,
        in_specs=(rows, rows, gain) + (split,) * 4 + (gain,) + (split,) * 3 + (rows,),
        out_specs=(rows, rows, gain) + (split,) * 4 + (gain,) + (split,) * 3,
        check_vma=False,
    )
```

```python
import functools

import jax
import jax.numpy as jnp
from jax import lax
from jax.experimental import pallas as pl
from jax.experimental.pallas import tpu as pltpu
from jax.sharding import PartitionSpec as P

H = 16
KV = 8
HD = 96
HALF = HD // 2
LANES = 128
BLOCKS = 16
TILE = 128
SLAB = 512
CHUNKS = 2
COST_SCALE = 0.001

epsilon = 1e-05
rope_base = 100000.0
masked_score = -1e30
low = jnp.bfloat16
wide = jnp.float32


def whole(array, buffers=1):
    zeros = (0,) * array.ndim
    mode = pl.Buffered(buffers)
    return pl.BlockSpec(array.shape, lambda *at: zeros, pipeline_mode=mode)


def rows_of(tile, width, first=0):
    return pl.BlockSpec((tile, width), lambda i, place: (first + i, 0))


def shaped(shape, dtype):
    return jax.ShapeDtypeStruct(shape, dtype)


anywhere = pl.BlockSpec(memory_space=pl.ANY)


def run(kernel, name, place, grid, operands, outs, scratch=(), after=(), vmem=56, us=4):
    after = [item for item in after if isinstance(item, jax.Array)]
    count, extra = len(operands), len(after)

    def body(place_ref, *refs):
        kernel(place_ref, *refs[:count], *refs[count + extra :])

    return pl.pallas_call(
        body,
        grid_spec=pltpu.PrefetchScalarGridSpec(
            num_scalar_prefetch=1,
            grid=grid,
            in_specs=[spec for _, spec in operands] + [anywhere] * extra,
            out_specs=[spec for _, spec in outs],
            scratch_shapes=list(scratch),
        ),
        out_shape=[shape for shape, _ in outs],
        compiler_params=pltpu.CompilerParams(vmem_limit_bytes=vmem * 2**20),
        cost_estimate=pl.CostEstimate(
            flops=0, bytes_accessed=int(us * COST_SCALE * 3.3e6), transcendentals=0
        ),
        name=name,
    )(place, *[array for array, _ in operands], *after)


def across(left, right):
    return lax.dot_general(left, right, (((1,), (1,)), ((), ())), preferred_element_type=wide)


def down(left, right):
    return lax.dot_general(left, right, (((0,), (0,)), ((), ())), preferred_element_type=wide)


def project(left, right):
    return jnp.dot(left, right, preferred_element_type=wide)


class Slab:
    def __init__(self, matrix, row, rows, stride, offset, column, width=SLAB, lane=0):
        self.matrix, self.row, self.rows = matrix, row, rows
        self.stride, self.offset = stride, offset
        self.column, self.width, self.lane = column, width, lane

    def of(self, refs, block):
        rows = pl.ds(pl.multiple_of(block * self.stride + self.offset, 16), self.rows)
        return refs[self.matrix].at[rows, pl.ds(self.column, self.width)]

    def lanes(self):
        return pl.ds(self.lane, self.width)


FIRST_HALF, FFN_HALF, QKV_HALF, OUT_HALF = 224, 288, 160, 80


def square_plan(half):
    plan = []
    for slab in range(3):
        top, bottom = slab * 96, slab * 96 + 96
        for first, last in ((top, min(bottom, half)), (max(top, half), bottom)):
            if first < last:
                plan.append(Slab(0, first, last - first, 96, first - top, slab * SLAB))
    return plan


def out_plan(start, half):
    plan = []
    for first, last in ((start, min(start + 96, half)), (max(start, half), start + 96)):
        if first < last:
            plan.append(Slab(0, first, last - first, LANES, first - start, 0))
    for part in range(2):
        plan.append(Slab(0, start + 96, 48, LANES, part * 48, SLAB, 256, part * 256))
    return plan


GAINS = 288
GAIN_SLAB = Slab(1, GAINS, 16, 16, 0, 0)
FIRST_QKV_PLAN = square_plan(FIRST_HALF) + [GAIN_SLAB]
FIRST_OUT_PLAN = out_plan(GAINS + 16, FIRST_HALF)
QKV_PLAN = square_plan(QKV_HALF) + [GAIN_SLAB]
OUT_PLAN = out_plan(0, OUT_HALF)
FFN_PLAN = [
    Slab(0, 0, 96, 96, 0, 0),
    Slab(0, 96, 96, 96, 0, SLAB),
    Slab(1, 192, 96, 96, 0, 0),
    Slab(1, 288, 96, 96, 0, SLAB),
    Slab(2, 384, 64, 64, 0, 0),
    Slab(2, 448, 64, 64, 0, SLAB),
    Slab(2, 512, 64, 64, 0, 2 * SLAB),
]
UPPER_ROWS = 384
UPPER_PLAN, LOWER_PLAN = FFN_PLAN[:4], [
    Slab(2, slab * 64, 64, 64, 0, slab * SLAB) for slab in range(3)
]


def block_index(place_ref, k, dy, dx):
    z, y, x = place_ref[0], place_ref[1], place_ref[2]
    return ((z ^ k) * 2 + (y ^ dy)) * 2 + (x ^ dx)


def from_pieces(pieces, half):
    def source(k, dy, dx, slab):
        at = pl.ds(slab.row, slab.rows)
        piece = pieces[dy * 2 + dx]
        if dy and dx:
            part = int(slab.row >= half)
            at = pl.ds(slab.row - part * half, slab.rows)
            piece = pieces[3 + part]
        return piece.at[k, at, slab.lanes()]

    return source


def from_planes(pair, other):
    def source(k, dy, dx, slab):
        planes = other if k % 2 else pair
        return planes.at[k // 2, dy * 2 + dx, pl.ds(slab.row, slab.rows), slab.lanes()]

    return source


def fetch(place_ref, source, plan, matrices, sems):
    for k in range(4):
        for dy in range(2):
            for dx in range(2):
                block = block_index(place_ref, k, dy, dx)
                for slab in plan:
                    pltpu.make_async_copy(
                        source(k, dy, dx, slab), slab.of(matrices, block), sems.at[slab.matrix]
                    ).start()


def send_off(place_ref, k, matrices, stride_base, plan, half, outs, sems):
    to_x, to_y, late_x, late_y, own = range(5)
    for dy in range(2):
        for dx in range(2):
            block = block_index(place_ref, place_ref[0], dy, dx) + stride_base
            for slab in plan:
                part = int(slab.row >= half)
                at = pl.ds(slab.row - part * half, slab.rows)
                if (dy, dx) == (0, 0):
                    which, index = own, (k, part)
                elif dy and dx:
                    which, index = (to_y if part else to_x), (0, k)
                elif part == dy:
                    which, index = (to_y if dy else to_x), (1, k)
                else:
                    which, index = (late_y if dy else late_x), (k,)
                target = outs[which].at[(*index, at, slab.lanes())]
                pltpu.make_async_copy(slab.of(matrices, block), target, sems.at[which]).start()


def fill_spare(source, row, rows, half, outs, sems):
    at = pl.ds(row - half, rows)
    for k in range(4):
        for which, index in ((1, (0, k)), (1, (1, k)), (2, (k,)), (4, (k, 1))):
            target = outs[which].at[(*index, at)]
            pltpu.make_async_copy(source, target, sems.at[which]).start()


def drain(refs, sems):
    for index, ref in enumerate(refs):
        pltpu.make_async_copy(ref, ref, sems.at[index]).wait()


def sent_shapes(half, width):
    shapes = [(2, 4, half, width)] * 2 + [(4, half, width)] * 2 + [(4, 2, half, width)]
    return [(shaped(shape, low), anywhere) for shape in shapes]


def gate_kernel(place_ref, *refs):
    pass


def gate(place, arrays, after):
    count, extra = len(arrays), len(after)
    return pl.pallas_call(
        gate_kernel,
        grid_spec=pltpu.PrefetchScalarGridSpec(
            num_scalar_prefetch=1,
            grid=(1,),
            in_specs=[anywhere] * (count + extra),
            out_specs=[anywhere] * count,
        ),
        out_shape=[shaped(array.shape, array.dtype) for array in arrays],
        input_output_aliases={1 + index: index for index in range(count)},
        cost_estimate=pl.CostEstimate(flops=0, bytes_accessed=0, transcendentals=0),
        name="gate",
    )(place, *arrays, *after)


def pair_kernel(place_ref, own, far, out, sems):
    copies = [
        pltpu.make_async_copy(ref, out.at[k], sems.at[k]) for k, ref in enumerate((own, far))
    ]
    for copy in copies:
        copy.start()
    for copy in copies:
        copy.wait()


def pair_up(place, own, far, after=()):
    out = shaped((2, *own.shape), low)
    return run(
        pair_kernel,
        "pair",
        place,
        (1,),
        [(own, anywhere), (far, anywhere)],
        [(out, whole(out))],
        [pltpu.SemaphoreType.DMA((2,))],
        after,
        us=2,
    )[0]


def line_kernel(place_ref, pair, near, out, sems):
    copies = []
    for k in range(4):
        ref = near if k % 2 else pair
        copies.append(pltpu.make_async_copy(ref.at[k // 2], out.at[k], sems.at[k]))
        copies[-1].start()
    for copy in copies:
        copy.wait()


def line_up(place, pair, near, after=()):
    _, rows, width = pair.shape
    out = shaped((4, rows, width), low)
    return run(
        line_kernel,
        "line",
        place,
        (1,),
        [(pair, anywhere), (near, anywhere)],
        [(out, whole(out))],
        [pltpu.SemaphoreType.DMA((4,))],
        after,
        us=4,
    )[0]


def join_kernel(place_ref, *refs):
    *parts, out, sems = refs
    copies = [
        pltpu.make_async_copy(part, out.at[k], sems.at[k]) for k, part in enumerate(parts)
    ]
    for copy in copies:
        copy.start()
    for copy in copies:
        copy.wait()


def join(place, parts, after=()):
    out = shaped((4, *parts[0].shape), low)
    return run(
        join_kernel,
        "join",
        place,
        (1,),
        [(part, anywhere) for part in parts],
        [(out, whole(out))],
        [pltpu.SemaphoreType.DMA((4,))],
        after,
        us=4,
    )[0]


def plane_kernel(place_ref, own, from_x, from_y, upper, lower, out, sems):
    half = upper.shape[1]
    parts = [
        (own, out.at[pl.ds(0, 1)]),
        (from_x, out.at[pl.ds(1, 1)]),
        (from_y, out.at[pl.ds(2, 1)]),
        (upper, out.at[pl.ds(3, 1), pl.ds(0, half)]),
        (lower, out.at[pl.ds(3, 1), pl.ds(half, half)]),
    ]
    copies = [
        pltpu.make_async_copy(source, target, sems.at[index])
        for index, (source, target) in enumerate(parts)
    ]
    for copy in copies:
        copy.start()
    for copy in copies:
        copy.wait()


def plane_up(place, parts, after):
    _, rows, width = parts[0].shape
    out = shaped((4, rows, width), low)
    return run(
        plane_kernel,
        "plane",
        place,
        (1,),
        [(part, anywhere) for part in parts],
        [(out, whole(out))],
        [pltpu.SemaphoreType.DMA((5,))],
        after,
        us=2,
    )[0]


def halves_kernel(place_ref, from_x, from_y, upper, lower, sems):
    half = upper.shape[1]
    copies = (
        pltpu.make_async_copy(from_x.at[:, pl.ds(0, half)], upper, sems.at[0]),
        pltpu.make_async_copy(from_y.at[:, pl.ds(half, half)], lower, sems.at[1]),
    )
    for copy in copies:
        copy.start()
    for copy in copies:
        copy.wait()


def halves(place, from_x, from_y, after):
    count, rows, width = from_x.shape
    out = shaped((count, rows // 2, width), low)
    return run(
        halves_kernel,
        "halves",
        place,
        (1,),
        [(from_x, anywhere), (from_y, anywhere)],
        [(out, whole(out))] * 2,
        [pltpu.SemaphoreType.DMA((2,))],
        after,
        us=2,
    )


def step_rows(half):
    return next(rows for rows in (144, 80, 96, 48, 368) if half % rows == 0)


def merge_kernel(place_ref, late_x, late_y, got_x, got_y, out_x, out_y):
    out_x[...] = late_x[...] + got_y[0]
    out_y[...] = late_y[...] + got_x[0]


def merge(place, late_x, late_y, got_x, got_y, after):
    shape = late_x.shape
    rows = step_rows(shape[1])
    spec = pl.BlockSpec((4, rows, shape[2]), lambda i, place: (0, i, 0))
    got = pl.BlockSpec((1, 4, rows, shape[2]), lambda i, place: (0, 0, i, 0))
    return run(
        merge_kernel,
        "merge",
        place,
        (shape[1] // rows,),
        [(late_x, spec), (late_y, spec), (got_x, got), (got_y, got)],
        [(shaped(shape, low), spec)] * 2,
        after=after,
    )


def sum_kernel(direct, groups, place_ref, *refs):
    ins, (kept, *outs) = refs[: 5 * groups], refs[5 * groups :]
    step = pl.program_id(0)
    for k in range(4):

        @pl.when(step == k)
        def _():
            row = 0
            for group in range(groups):
                own, got_x, got_y, more_x, more_y = ins[5 * group : 5 * group + 5]
                at = slice(row, row + own.shape[2])
                row += own.shape[2]
                upper = own[0, 0].astype(wide) + got_x[0, 0].astype(wide)
                upper = upper + more_y[0].astype(wide)
                lower = own[0, 1].astype(wide) + got_y[0, 0].astype(wide)
                lower = lower + more_x[0].astype(wide)
                if k == 0:
                    ref = kept
                elif direct:
                    ref = outs[k - 1]
                else:
                    ref = outs[1].at[0] if k % 2 else outs[0]
                ref[0, at, :], ref[1, at, :] = upper.astype(ref.dtype), lower.astype(ref.dtype)


def sum_plane(place, groups, direct, after):
    operands = []
    for own, got_x, got_y, more_x, more_y in groups:
        _, _, half, width = own.shape
        got = pl.BlockSpec((1, 1, half, width), lambda k, place: (1, k, 0, 0))
        more = pl.BlockSpec((1, half, width), lambda k, place: (k, 0, 0))
        operands += [
            (own, pl.BlockSpec((1, 2, half, width), lambda k, place: (k, 0, 0, 0))),
            (got_x, got),
            (got_y, got),
            (more_x, more),
            (more_y, more),
        ]
    half = sum(group[0].shape[2] for group in groups)
    out = pl.BlockSpec((2, half, width), lambda k, place: (0, 0, 0))
    both = pl.BlockSpec((1, 2, half, width), lambda k, place: (k // 2, 0, 0, 0))
    outs = [(shaped((2, half, width), wide), out)]
    if direct:
        outs += [(shaped((2, half, width), low), out)] * 3
    else:
        outs += [(shaped((2, half, width), wide), out)]
        outs += [(shaped((2, 2, half, width), low), both)]
    return run(
        functools.partial(sum_kernel, direct, len(groups)),
        "sum_plane",
        place,
        (4,),
        operands,
        outs,
        after=after,
        us=5,
    )


def pass_kernel(place_ref, kept_far, near, out):
    out[...] = (kept_far[...] + near[0].astype(wide)).astype(low)


def sum_pass(place, kept_far, near, after):
    _, half, width = kept_far.shape
    rows = step_rows(half)
    spec = pl.BlockSpec((2, rows, width), lambda i, place: (0, i, 0))
    second = pl.BlockSpec((1, 2, rows, width), lambda i, place: (1, 0, i, 0))
    return run(
        pass_kernel,
        "sum_pass",
        place,
        (half // rows,),
        [(kept_far, spec), (near, second)],
        [(shaped(kept_far.shape, low), spec)],
        after=after,
        us=3,
    )[0]


def total_kernel(place_ref, kept, *refs):
    *received, out, out_low = refs
    total = kept[...]
    for ref in received:
        part = ref[0] if len(ref.shape) > len(kept.shape) else ref[...]
        total = total + part.astype(wide)
    out[...] = total
    out_low[...] = total.astype(low)


def sum_line(place, kept, received, after):
    _, half, width = kept.shape
    rows = step_rows(half)
    spec = pl.BlockSpec((2, rows, width), lambda i, place: (0, i, 0))
    first = pl.BlockSpec((1, 2, rows, width), lambda i, place: (0, 0, i, 0))
    total, total_low = run(
        total_kernel,
        "sum_line",
        place,
        (half // rows,),
        [(kept, spec)] + [(item, first if item.ndim == 4 else spec) for item in received],
        [(shaped(kept.shape, wide), spec), (shaped(kept.shape, low), spec)],
        after=after,
        us=4,
    )
    return total.reshape(2 * half, width), total_low.reshape(2 * half, width)


def pack_first_kernel(place_ref, query, key, value, square, gain_one, gain_two, out):
    core = place_ref[3]

    def mine(ref):
        columns = ref.shape[1] // 2
        return ref[:, pl.ds(pl.multiple_of(core * columns, LANES), columns)]

    packed = jnp.concatenate([mine(query), mine(key), mine(value)], axis=1)
    rows = packed.shape[0]
    for slab in range(3):
        out[slab * rows : (slab + 1) * rows, :] = packed[:, slab * SLAB : (slab + 1) * SLAB]
    row = lax.broadcasted_iota(jnp.int32, (16, LANES), 0)
    gap = jnp.zeros((16, LANES - rows), wide)
    out[GAINS : GAINS + 16, :] = jnp.zeros((16, SLAB), low)
    for index, gain in enumerate((gain_one, gain_two)):
        spread = jnp.broadcast_to(gain[...].astype(wide), (16, rows))
        spread = jnp.where(row == 0, jnp.concatenate([spread, gap], axis=1), 0.0)
        out[GAINS : GAINS + 16, index * LANES : (index + 1) * LANES] = spread.astype(low)
    at, packed = GAINS + 16, mine(square)
    out[at : at + rows, :] = packed[:, :SLAB]
    for part in range(2):
        out[at + rows :, part * 256 : (part + 1) * 256] = packed[
            part * rows // 2 : (part + 1) * rows // 2, SLAB:
        ]


def pack_first(place, query, key, value, square, gain_one, gain_two):
    operands = [query, key, value, square, gain_one.reshape(1, -1), gain_two.reshape(1, -1)]
    out = shaped((2 * FIRST_HALF, SLAB), low)
    return run(
        pack_first_kernel,
        "pack_first",
        place,
        (1,),
        [(item, whole(item)) for item in operands],
        [(out, whole(out))],
    )[0]


def interleave(even, odd):
    lane = lax.broadcasted_iota(jnp.int32, even.shape, 1)
    left = jnp.where(lane < LANES // 2, even, pltpu.roll(odd, LANES // 2, 1))
    right = jnp.where(lane < LANES // 2, pltpu.roll(even, LANES // 2, 1), odd)
    return left, right


def pack_ffn_kernel(chunk, place_ref, gate, up, down_w, *outs):
    core = place_ref[3]
    rows = gate.shape[0]

    def put(at, size, column, part):
        span, width = outs[0].shape[0], part.shape[1]
        out, at = (outs[0], at) if at < span else (outs[1], at - span)
        out[at : at + size, column : column + width] = part

    for matrix, ref in enumerate((gate, up)):
        for pair in range(8):
            windows = [
                ref[:, pl.ds(pl.multiple_of((2 * pair + odd) * 256 + core * LANES, LANES), LANES)]
                for odd in range(2)
            ]
            packed = interleave(windows[0].astype(wide), windows[1].astype(wide))[chunk]
            at = (matrix * 2 + pair // 4) * rows
            column = pair % 4 * LANES
            put(at, rows, column, packed.astype(low))
    units = down_w[pl.ds(pl.multiple_of(core * LANES + chunk * 64, 64), 64), :]
    for slab in range(3):
        at = 4 * rows + slab * 64
        put(at, 64, 0, units[:, slab * SLAB : (slab + 1) * SLAB])


def pack_ffn(place, chunk, parts, gate, up, down_w, after):
    outs = [shaped((rows, SLAB), low) for rows in parts]
    return run(
        functools.partial(pack_ffn_kernel, chunk),
        "pack_ffn",
        place,
        (1,),
        [(item, whole(item)) for item in (gate, up, down_w)],
        [(out, whole(out)) for out in outs],
        after=after,
    )


def rows_in(ref, at, rows):
    if at >= FFN_HALF:
        at += ref.shape[0] // 2 - FFN_HALF
    return ref[at : at + rows, :]


def unpack_ffn_kernel(place_ref, mine_0, mine_1, other_0, other_1, gate, up, down_w):
    core = place_ref[3]
    rows = gate.shape[0]
    for owner, chunks in ((core, (mine_0, mine_1)), (1 - core, (other_0, other_1))):
        for matrix, ref in enumerate((gate, up)):
            for pair in range(8):
                at = (matrix * 2 + pair // 4) * rows
                column = pair % 4 * LANES
                parts = [
                    rows_in(chunk, at, rows)[:, column : column + LANES].astype(wide)
                    for chunk in chunks
                ]
                for odd, window in enumerate(interleave(*parts)):
                    place = (2 * pair + odd) * 256 + owner * LANES
                    ref[:, pl.ds(pl.multiple_of(place, LANES), LANES)] = window
        for index, chunk in enumerate(chunks):
            for slab in range(3):
                at = 4 * rows + slab * 64
                place = pl.multiple_of(owner * LANES + index * 64, 64)
                part = rows_in(chunk, at, 64).astype(wide)
                down_w[pl.ds(place, 64), slab * SLAB : (slab + 1) * SLAB] = part


def unpack_ffn(place, mine, other, shapes, after):
    outs = [shaped(shape, wide) for shape in shapes]
    return run(
        unpack_ffn_kernel,
        "unpack_ffn",
        place,
        (1,),
        [(item, whole(item)) for item in (*mine, *other)],
        [(out, whole(out)) for out in outs],
        after=after,
    )


def unpack_first_kernel(
    place_ref, mine, other, joint_mine, joint_other, query, key, value, square
):
    core = place_ref[3]
    rows = query.shape[0]

    def put(ref, owner, part):
        columns = ref.shape[1] // 2
        at = pl.ds(pl.multiple_of(owner * columns, LANES), columns)
        ref[:, at] = part.astype(wide)

    for owner, qkv, joint in ((core, mine, joint_mine), (1 - core, other, joint_other)):
        slabs = [qkv[slab * rows : (slab + 1) * rows, :] for slab in range(3)]
        put(query, owner, jnp.concatenate([slabs[0], slabs[1][:, :256]], axis=1))
        put(key, owner, jnp.concatenate([slabs[1][:, 256:], slabs[2][:, :128]], axis=1))
        put(value, owner, slabs[2][:, 128:])
        half = FFN_HALF + OUT_HALF
        out = [joint[part * half + FFN_HALF : (part + 1) * half, :] for part in range(2)]
        out = jnp.concatenate(out, axis=0)
        rest = out[rows : rows + rows // 2, :]
        rest = jnp.concatenate([rest[:, :256], rest[:, 256:]], axis=0)
        put(square, owner, jnp.concatenate([out[:rows, :], rest], axis=1))


def unpack_first(place, parts, shapes, after):
    outs = [shaped(shape, wide) for shape in shapes]
    return run(
        unpack_first_kernel,
        "unpack_first",
        place,
        (1,),
        [(item, whole(item)) for item in parts],
        [(out, whole(out)) for out in outs],
        after=after,
    )


def turn_table(position):
    frequency = rope_base ** (-jnp.arange(HALF, dtype=wide) * 2.0 / HD)
    angle = position.astype(wide)[:, None] * frequency[None, :]
    gap = jnp.zeros((position.shape[0], LANES // 2 - HALF), wide)
    cosine, sine = jnp.cos(angle), jnp.sin(angle)
    return (
        jnp.concatenate([cosine, gap, cosine, gap], axis=1),
        jnp.concatenate([-sine, gap, sine, gap], axis=1),
    )


def qkv_kernel(tiles, place_ref, own_ref, far_ref, cos_ref, sin_ref, *refs):
    pieces = refs[:5]
    normed_ref, q_ref, k_ref, v_ref, w_ref, gain_ref, gain_rows, x_ref, sems = refs[5:]
    step = pl.program_id(0)

    @pl.when(step < tiles)
    def _():
        x_ref[...] = own_ref[...]

    @pl.when(step >= tiles)
    def _():
        x_ref[...] = far_ref[...]

    @pl.when(pl.program_id(0) == 0)
    def _():
        fetch(
            place_ref, from_pieces(pieces, FIRST_HALF), FIRST_QKV_PLAN, (w_ref, gain_rows), sems
        )
        drain((w_ref, gain_rows), sems)
        for index in range(2):
            parts = [
                gain_rows[16 * block : 16 * block + 16, index * LANES : (index + 1) * LANES]
                for block in range(BLOCKS)
            ]
            parts = [part.astype(wide)[:8, :HD] for part in parts]
            gain_ref[8 * index : 8 * index + 8, :] = jnp.concatenate(parts, axis=1)

    hidden = x_ref[...].astype(wide)
    scale = lax.rsqrt(jnp.mean(hidden * hidden, axis=-1, keepdims=True) + epsilon)
    normed = (hidden * scale * gain_ref[0:1, :]).astype(low)
    normed_ref[...] = normed
    gap = jnp.zeros((x_ref.shape[0], LANES // 2 - HALF), wide)
    heads = q_ref.shape[1] // LANES
    groups = k_ref.shape[1] // LANES
    count = 4
    for first in range(0, heads + 2 * groups, count):
        part = project(normed, w_ref[:, first * HD : (first + count) * HD])
        for index in range(first, first + count):
            at = (index - first) * HD
            if index >= heads + groups:
                column = (index - heads - groups) * LANES
                padded = jnp.concatenate([part[:, at : at + HD], gap, gap], axis=1)
                v_ref[:, column : column + LANES] = padded.astype(low)
                continue
            padded = jnp.concatenate(
                [part[:, at : at + HALF], gap, part[:, at + HALF : at + HD], gap], axis=1
            )
            turned = pltpu.roll(padded, LANES // 2, 1)
            padded = (padded * cos_ref[...] + turned * sin_ref[...]).astype(low)
            if index < heads:
                q_ref[:, index * LANES : (index + 1) * LANES] = padded
            else:
                column = (index - heads) * LANES
                k_ref[:, column : column + LANES] = padded


def project_qkv(place, own, far, cosine, sine, pieces, after):
    count, width = own.shape
    tile = 320
    tiles = count // tile
    count = 2 * count
    heads, groups = H // 2 * LANES, KV // 2 * LANES
    weight, gains = shaped((width, width), low), shaped((16, width), wide)
    early = pl.BlockSpec((tile, width), lambda i, place: (jnp.minimum(i, tiles - 1), 0))
    late = pl.BlockSpec((tile, width), lambda i, place: (jnp.maximum(i - tiles, 0), 0))
    return run(
        functools.partial(qkv_kernel, tiles),
        "project_qkv",
        place,
        (count // tile,),
        [
            (own, early),
            (far, late),
            (cosine, rows_of(tile, LANES)),
            (sine, rows_of(tile, LANES)),
        ]
        + [(piece, anywhere) for piece in pieces],
        [
            (shaped((count, width), low), rows_of(tile, width)),
            (shaped((count, heads), low), rows_of(tile, heads)),
            (shaped((count, groups), low), rows_of(tile, groups)),
            (shaped((count, groups), low), rows_of(tile, groups)),
            (weight, whole(weight)),
            (gains, whole(gains)),
        ],
        [
            pltpu.VMEM((BLOCKS * 16, SLAB), low),
            pltpu.VMEM((tile, width), low),
            pltpu.SemaphoreType.DMA((2,)),
        ],
        after,
        us=18,
    )


def fill_bias(bias_ref, column_ref, row_ref):
    size = bias_ref.shape[0]
    for start in range(0, size, TILE):
        shape = (TILE, size)
        slots = lax.broadcasted_iota(jnp.int32, shape, 0) + start
        keys = lax.broadcasted_iota(jnp.int32, shape, 1)
        same = column_ref[start : start + TILE, :] == row_ref[0]
        allowed = same & (keys <= slots)
        bias_ref[start : start + TILE, :] = jnp.where(allowed, 0.0, masked_score)


LOG2_E = 1.4426950408889634


def both_heads(ref, start):
    rows = slice(start, start + TILE)
    return jnp.concatenate([ref[rows, :LANES], ref[rows, LANES:]], axis=0)


def attend_kernel(
    place_ref, q_ref, k_ref, v_ref, column_ref, row_ref, out_ref, total_ref, bias_ref
):
    group = pl.program_id(0)
    size = q_ref.shape[0]

    @pl.when(group == 0)
    def _():
        fill_bias(bias_ref, column_ref, row_ref)
        total_ref[...] = jnp.zeros_like(total_ref)

    lane = lax.broadcasted_iota(jnp.int32, (TILE, LANES), 1)
    for start in range(0, size, TILE):
        stop = start + TILE
        raw = across(both_heads(q_ref, start), k_ref[:stop, :])
        bias = bias_ref[start:stop, :stop]
        scores = raw * (HD ** (-0.5) * LOG2_E) + jnp.concatenate([bias, bias], axis=0)
        top = jnp.max(scores, axis=-1, keepdims=True)
        powers = jnp.exp2(scores - top)
        amount = jnp.sum(powers, axis=-1, keepdims=True)
        probs = (powers * (1.0 / amount)).astype(low)
        mixed = project(probs, v_ref[:stop, :]).astype(low)
        total = top + jnp.log2(amount)
        kept = total_ref[start:stop, :]
        for head in range(2):
            rows = slice(head * TILE, (head + 1) * TILE)
            out_ref[start:stop, head * LANES : (head + 1) * LANES] = mixed[rows]
            kept = jnp.where(lane == 2 * group + head, total[rows], kept)
        total_ref[start:stop, :] = kept


def attention_specs(size, block):
    return dict(
        pair=pl.BlockSpec((size, 2 * LANES), lambda g, place: (block, g)),
        one=pl.BlockSpec((size, LANES), lambda g, place: (block, g)),
        pair_alone=pl.BlockSpec((size, 2 * LANES), lambda g, place: (0, g)),
        one_alone=pl.BlockSpec((size, LANES), lambda g, place: (0, g)),
        shared=pl.BlockSpec((size, LANES), lambda g, place: (block, 0)),
        alone=pl.BlockSpec((size, LANES), lambda g, place: (0, 0)),
        column=pl.BlockSpec((size, 1), lambda g, place: (block, 0)),
        row=pl.BlockSpec((1, 1, size), lambda g, place: (block, 0, 0)),
    )


def attend(place, q, k, v, segment, block, after=()):
    blocks, size = segment.shape
    spec = attention_specs(size, block)
    return run(
        attend_kernel,
        "attend",
        place,
        (k.shape[1] // LANES,),
        [
            (q, spec["pair"]),
            (k, spec["one"]),
            (v, spec["one"]),
            (segment.reshape(blocks * size, 1), spec["column"]),
            (segment.reshape(blocks, 1, size), spec["row"]),
        ],
        [
            (shaped((size, q.shape[1]), low), spec["pair_alone"]),
            (shaped((size, LANES), wide), spec["alone"]),
        ],
        [pltpu.VMEM((size, size), wide)],
        after,
        us=17,
    )


def attend_back_kernel(
    place_ref,
    q_ref,
    k_ref,
    v_ref,
    grad_ref,
    out_ref,
    total_ref,
    column_ref,
    row_ref,
    cos_ref,
    sin_ref,
    dq_ref,
    dk_ref,
    dv_ref,
    bias_ref,
    dk_sum,
    dv_sum,
):
    group = pl.program_id(0)
    size = q_ref.shape[0]

    @pl.when(group == 0)
    def _():
        fill_bias(bias_ref, column_ref, row_ref)

    def turned_back(grad, rows):
        turned = pltpu.roll(grad, LANES // 2, 1)
        return (grad * cos_ref[rows, :] - turned * sin_ref[rows, :]).astype(low)

    dk_sum[...] = jnp.zeros_like(dk_sum)
    dv_sum[...] = jnp.zeros_like(dv_sum)
    lane = lax.broadcasted_iota(jnp.int32, (TILE, LANES), 1)
    scale = HD ** (-0.5)
    for start in range(0, size, TILE):
        stop = start + TILE
        queries, grads = both_heads(q_ref, start), both_heads(grad_ref, start)
        mixed = both_heads(out_ref, start)
        delta = jnp.sum(grads.astype(wide) * mixed.astype(wide), axis=-1, keepdims=True)
        totals = [
            jnp.sum(
                jnp.where(lane == 2 * group + head, total_ref[start:stop, :], 0.0),
                axis=-1,
                keepdims=True,
            )
            for head in range(2)
        ]
        bias = bias_ref[start:stop, :stop]
        raw = across(queries, k_ref[:stop, :])
        scores = raw * (scale * LOG2_E) + jnp.concatenate([bias, bias], axis=0)
        probs = jnp.exp2(scores - jnp.concatenate(totals, axis=0))
        dv_sum[:stop, :] += down(probs.astype(low), grads)
        grad_probs = across(grads, v_ref[:stop, :])
        grad_raw = (probs * (grad_probs - delta)).astype(low)
        dq = project(grad_raw, k_ref[:stop, :]) * scale
        for head in range(2):
            part = turned_back(dq[head * TILE : (head + 1) * TILE], slice(start, stop))
            dq_ref[start:stop, head * LANES : (head + 1) * LANES] = part
        dk_sum[:stop, :] += down(grad_raw, queries)
    dv_ref[...] = dv_sum[...].astype(low)
    dk_ref[...] = turned_back(dk_sum[...] * scale, slice(None))


def attend_back(place, q, k, v, grad, out, total, segment, cosine, sine, block, after=()):
    blocks, size = segment.shape
    spec = attention_specs(size, block)
    return run(
        attend_back_kernel,
        "attend_back",
        place,
        (k.shape[1] // LANES,),
        [
            (q, spec["pair"]),
            (k, spec["one"]),
            (v, spec["one"]),
            (grad, spec["pair_alone"]),
            (out, spec["pair_alone"]),
            (total, spec["alone"]),
            (segment.reshape(blocks * size, 1), spec["column"]),
            (segment.reshape(blocks, 1, size), spec["row"]),
            (cosine, spec["shared"]),
            (sine, spec["shared"]),
        ],
        [
            (shaped((size, q.shape[1]), low), spec["pair_alone"]),
            (shaped((size, k.shape[1]), low), spec["one_alone"]),
            (shaped((size, v.shape[1]), low), spec["one_alone"]),
        ],
        [
            pltpu.VMEM((size, size), wide),
            pltpu.VMEM((size, LANES), wide),
            pltpu.VMEM((size, LANES), wide),
        ],
        after,
        us=21,
    )


def out_weight_kernel(place_ref, *refs):
    pieces, weights, whole_weight, sems = refs[:5], refs[5:7], refs[7], refs[8]
    fetch(place_ref, from_pieces(pieces, FIRST_HALF), FIRST_OUT_PLAN, (whole_weight,), sems)
    zeros = jnp.zeros((LANES - HD, whole_weight.shape[1]), low)
    for block in range(BLOCKS):
        whole_weight[pl.ds(block * LANES + HD, LANES - HD), :] = zeros
    drain((whole_weight.at[pl.ds(0, BLOCKS * HD)],), sems)
    rows = weights[0].shape[0]
    for part in range(2):
        weights[part][...] = whole_weight[part * rows : (part + 1) * rows, :]


def out_weight(place, pieces, width, after):
    out = shaped((H // 2 * LANES, width // 2), low)
    return run(
        out_weight_kernel,
        "out_weight",
        place,
        (1,),
        [(piece, anywhere) for piece in pieces],
        [(out, whole(out))] * 2,
        [pltpu.VMEM((H * LANES, width // 2), low), pltpu.SemaphoreType.DMA((1,))],
        after,
    )


def middle_kernel(
    place_ref, x_ref, mine_ref, other_ref, *refs
):
    w_mine, w_other, (gain_ref, middle_ref, out_ref, heads) = refs[:2], refs[2:4], refs[4:]
    core = place_ref[3]
    span = mine_ref.shape[1]
    heads[:, pl.ds(pl.multiple_of(core * span, LANES), span)] = mine_ref[...]
    heads[:, pl.ds(pl.multiple_of((1 - core) * span, LANES), span)] = other_ref[...]
    columns = w_mine[0].shape[1]
    for owner, weight in ((core, w_mine), (1 - core, w_other)):
        at = pl.ds(pl.multiple_of(owner * columns, LANES), columns)
        branch = project(heads[:, :span], weight[0][...])
        branch = branch + project(heads[:, span:], weight[1][...])
        middle_ref[:, at] = x_ref[:, at].astype(wide) + branch
    hidden = middle_ref[...]
    scale = lax.rsqrt(jnp.mean(hidden * hidden, axis=-1, keepdims=True) + epsilon)
    out_ref[...] = (hidden * scale * gain_ref[8:9, :]).astype(low)


def middle_of(place, x, mine, other, w_mine, w_other, gains, after=()):
    count, width = x.shape
    tile, span = count // 2, mine.shape[1]
    return run(
        middle_kernel,
        "middle",
        place,
        (2,),
        [
            (x, rows_of(tile, width)),
            (mine, rows_of(tile, span)),
            (other, rows_of(tile, span)),
            *[(item, whole(item)) for item in (*w_mine, *w_other, gains)],
        ],
        [
            (shaped((count, width), wide), rows_of(tile, width)),
            (shaped((count, width), low), rows_of(tile, width)),
        ],
        [pltpu.VMEM((tile, 2 * span), low)],
        after,
        us=11,
    )


def middle_back_kernel(
    place_ref,
    middle_ref,
    mine_0,
    mine_1,
    other_0,
    other_1,
    cotangent_ref,
    gain_ref,
    *refs,
):
    w_mine, w_other, refs = refs[:2], refs[2:4], refs[4:]
    grad_ref, branch_mine, branch_other, heads_mine, heads_other, gain_grad, branch, heads = refs
    core = place_ref[3]
    hidden = middle_ref[...]
    scale = lax.rsqrt(jnp.mean(hidden * hidden, axis=-1, keepdims=True) + epsilon)
    parts = (mine_0, mine_1, other_0, other_1)
    incoming = sum(ref[...].astype(wide) for ref in parts)
    weighted = incoming * gain_ref[8:9, :]
    inner = jnp.mean(weighted * hidden, axis=-1, keepdims=True)
    grad = cotangent_ref[...].astype(wide) + (scale * weighted - hidden * scale**3 * inner)
    grad_ref[...] = grad
    branch[...] = grad.astype(low)

    @pl.when(pl.program_id(0) == 0)
    def _():
        gain_grad[...] = jnp.zeros_like(gain_grad)

    summed = jnp.sum(incoming * hidden * scale, axis=0, keepdims=True)
    gain_grad[...] += jnp.broadcast_to(summed, gain_grad.shape)
    columns, span = w_mine[0].shape[1], heads_mine.shape[1]

    def part(ref, owner, size):
        return ref[:, pl.ds(pl.multiple_of(owner * size, LANES), size)]

    branch_mine[...] = part(branch, core, columns)
    branch_other[...] = part(branch, 1 - core, columns)
    for at in range(0, 2 * span, SLAB):
        index, rows = at // span, slice(at % span, at % span + SLAB)
        heads[:, at : at + SLAB] = (
            across(branch_mine[...], w_mine[index][rows, :])
            + across(branch_other[...], w_other[index][rows, :])
        ).astype(low)
    heads_mine[...] = part(heads, core, span)
    heads_other[...] = part(heads, 1 - core, span)


def middle_back(place, middle, parts, cotangent, gains, w_mine, w_other, after=()):
    count, width = middle.shape
    tile, columns, span = count // 2, w_mine[0].shape[1], w_mine[0].shape[0]
    gain_grad = shaped((8, width), wide)
    return run(
        middle_back_kernel,
        "middle_back",
        place,
        (2,),
        [
            *[(item, rows_of(tile, width)) for item in (middle, *parts, cotangent)],
            *[(item, whole(item)) for item in (gains, *w_mine, *w_other)],
        ],
        [
            (shaped((count, width), wide), rows_of(tile, width)),
            (shaped((count, columns), low), rows_of(tile, columns)),
            (shaped((count, columns), low), rows_of(tile, columns)),
            (shaped((count, span), low), rows_of(tile, span)),
            (shaped((count, span), low), rows_of(tile, span)),
            (gain_grad, whole(gain_grad)),
        ],
        [pltpu.VMEM((tile, width), low), pltpu.VMEM((tile, 2 * span), low)],
        after,
        us=15,
    )


def out_grad_kernel(
    place_ref,
    own_mine,
    own_other,
    far_mine,
    far_other,
    branch_own,
    branch_far,
    *refs,
):
    outs, (grad, sems) = refs[:5], refs[5:]
    core = place_ref[3]
    span = own_mine.shape[1]
    for owner, own, far in ((core, own_mine, far_mine), (1 - core, own_other, far_other)):
        for at in range(0, span, SLAB):
            part = down(own[:, at : at + SLAB], branch_own[...])
            part = part + down(far[:, at : at + SLAB], branch_far[...])
            grad[pl.ds(pl.multiple_of(owner * span + at, LANES), SLAB), :] = part.astype(low)
    for k in range(4):
        base = (place_ref[0] ^ k) * 4
        send_off(place_ref, k, (grad,), base, OUT_PLAN, OUT_HALF, outs, sems)
    fill_spare(grad.at[pl.ds(0, 16), pl.ds(0, SLAB)], 144, 16, OUT_HALF, outs, sems)
    drain(outs, sems)


def out_grad(place, own_mine, own_other, far_mine, far_other, branch_own, branch_far, after=()):
    columns = branch_own.shape[1]
    operands = (own_mine, own_other, far_mine, far_other, branch_own, branch_far)
    return run(
        out_grad_kernel,
        "out_grad",
        place,
        (1,),
        [(item, whole(item)) for item in operands],
        sent_shapes(OUT_HALF, SLAB),
        [pltpu.VMEM((H * LANES, columns), low), pltpu.SemaphoreType.DMA((5,))],
        after,
        us=10,
    )


FFN_TILE = 640
FFN_STEP = 256
FFN_SPAN = 768


def load_tokens(ref, own, far, sem):
    count = far.shape[0]
    for part, source in enumerate((far, own)):
        pltpu.make_async_copy(source, ref.at[pl.ds(part * count, count)], sem).start()


def ffn_forward(step, tiles, x_ref, c_ref, weights, sums, middles, at_rows):
    gate_w, up_w, down_w = weights
    inner, grad_gate, grad_up = middles
    units, width = gate_w.shape[1], gate_w.shape[0]
    rows = pl.ds(pl.multiple_of(step * FFN_TILE, FFN_TILE), FFN_TILE)

    @pl.loop(0, units // FFN_STEP)
    def _(index):
        at = pl.ds(pl.multiple_of(index * FFN_STEP, FFN_STEP), FFN_STEP)
        gate = project(x_ref[rows, :], gate_w[:, at])
        upward = project(x_ref[rows, :], up_w[:, at])
        grad_inner = across(c_ref[rows, :], down_w[at, :])
        sigma = 1.0 / (1.0 + jnp.exp(-gate))
        silu = gate * sigma
        inner[at_rows, at] = (silu * upward).astype(low)
        grad_up[at_rows, at] = (grad_inner * silu).astype(low)
        grad_gate[at_rows, at] = (
            grad_inner * upward * sigma * (1.0 + gate * (1.0 - sigma))
        ).astype(low)

    for part in range(2):

        @pl.when((step >= part * tiles // 2) & (step < (part + 1) * tiles // 2))
        def _():
            out_ref, normed_ref = sums[2 * part : 2 * part + 2]

            @pl.loop(0, width // SLAB)
            def _(index):
                at = pl.ds(pl.multiple_of(index * SLAB, SLAB), SLAB)
                out = project(inner[at_rows, :], down_w[:, at])
                normed = across(grad_gate[at_rows, :], gate_w[at, :])
                normed = normed + across(grad_up[at_rows, :], up_w[at, :])
                out_ref[:, at] = out.astype(out_ref.dtype)
                normed_ref[:, at] = normed.astype(normed_ref.dtype)


def ffn_backward(
    place_ref, k, x_ref, c_ref, middles, stages, turned, turned_units, sent, sems, wait
):
    inner, grad_gate, grad_up = middles
    stage_gate, stage_up, stage_down = stages
    width, units = x_ref.shape[1], inner.shape[1]
    depth = place_ref[0] ^ k
    rows, span = width // 4, units // 4
    here = pl.ds(pl.multiple_of(depth * rows, LANES), rows)
    there = pl.ds(pl.multiple_of(depth * span, LANES), span)
    wait(x_ref, grad_gate)
    turned[...] = x_ref[:, here].T
    to = pl.ds(pl.multiple_of(k * rows, 16), rows)
    to_units = pl.ds(pl.multiple_of(k * span, 16), span)
    stage_gate[to, :] = project(turned[...], grad_gate[...]).astype(low)
    wait(grad_up)
    stage_up[to, :] = project(turned[...], grad_up[...]).astype(low)
    wait(inner, c_ref)
    turned_units[...] = inner[:, there].T

    @pl.loop(0, width // FFN_SPAN)
    def _(index):
        at = pl.ds(pl.multiple_of(index * FFN_SPAN, FFN_SPAN), FFN_SPAN)
        stage_down[to_units, at] = project(turned_units[...], c_ref[:, at]).astype(low)

    send_off(place_ref, k, stages, k * 4, FFN_PLAN, FFN_HALF, sent, sems)


def ffn_forward_kernel(tiles, pieces, place_ref, *refs):
    tokens, pieces, refs = refs[:4], refs[4 : 4 + pieces], refs[4 + pieces :]
    sums, middles = refs[:4], refs[4:7]
    x_ref, c_ref, *weights, x_sems, in_sems = refs[7:]
    step = pl.program_id(0)

    @pl.when(step == 0)
    def _():
        x_own, x_far, c_own, c_far = tokens
        load_tokens(x_ref, x_own, x_far, x_sems.at[0])
        load_tokens(c_ref, c_own, c_far, x_sems.at[1])
        if len(pieces) == 5:
            fetch(place_ref, from_pieces(pieces, FFN_HALF), FFN_PLAN, weights, in_sems)
        else:
            source = from_pieces(pieces[:5], UPPER_ROWS // 2)
            fetch(place_ref, source, UPPER_PLAN, weights, in_sems)
            fetch(place_ref, from_planes(*pieces[5:]), LOWER_PLAN, weights, in_sems)
        drain((x_ref, c_ref), x_sems)
        drain(weights, in_sems)

    ffn_forward(step, tiles, x_ref, c_ref, weights, sums, middles, slice(None))


def ffn_backward_kernel(place_ref, *refs):
    tokens, sources, sent = refs[:4], refs[4:7], refs[7:12]
    x_ref, c_ref, *rest = refs[12:]
    middles, stages, rest = rest[:3], rest[3:6], rest[6:]
    turned, turned_units, x_sems, in_sems, out_sems = rest
    k = pl.program_id(0)

    x_own, x_far, c_own, c_far = tokens

    def middle(index):
        pltpu.make_async_copy(sources[index], middles[index], in_sems.at[index]).start()

    @pl.when(k == 0)
    def _():
        load_tokens(x_ref, x_own, x_far, x_sems.at[0])
        middle(1)
        middle(2)
        middle(0)
        load_tokens(c_ref, c_own, c_far, x_sems.at[1])

    arrived = [(x_ref, x_sems.at[0]), (c_ref, x_sems.at[1])]
    arrived += [(ref, in_sems.at[index]) for index, ref in enumerate(middles)]

    def wait(*refs):
        @pl.when(k == 0)
        def _():
            for ref, sem in arrived:
                if any(ref is other for other in refs):
                    pltpu.make_async_copy(ref, ref, sem).wait()

    ffn_backward(
        place_ref, k, x_ref, c_ref, middles, stages, turned, turned_units, sent, out_sems, wait
    )

    @pl.when(k == 3)
    def _():
        drain(sent, out_sems)


FFN_UNITS = 1024


def ffn_sums(count, width):
    last = count // FFN_TILE - 1
    early = pl.BlockSpec((FFN_TILE, width), lambda i, place: (jnp.minimum(i, last), 0))
    late = pl.BlockSpec(
        (FFN_TILE, width), lambda i, place: (jnp.clip(i - last - 1, 0, last), 0)
    )
    return [(shaped((count, width), low), spec) for spec in (early, early, late, late)]


def ffn_scratch(count, width, weights=True, middles=True, stages=True):
    weight = [pltpu.VMEM((width, FFN_UNITS), low)] * 2 + [pltpu.VMEM((FFN_UNITS, width), low)]
    shapes = [pltpu.VMEM((count, width), low)] * 2
    shapes += weight if weights else []
    shapes += [pltpu.VMEM((count, FFN_UNITS), low)] * 3 if middles else []
    if stages:
        shapes += weight
        shapes += [pltpu.VMEM((width // 4, count), low)]
        shapes += [pltpu.VMEM((FFN_UNITS // 4, count), low)]
    shapes += [pltpu.SemaphoreType.DMA((2,)), pltpu.SemaphoreType.DMA((3,))]
    return shapes + ([pltpu.SemaphoreType.DMA((5,))] if stages else [])


def ffn_chunk_forward(place, tokens, pieces, after=()):
    count, width = tokens[0].shape
    tiles = 2 * count // FFN_TILE
    middle = pl.BlockSpec((FFN_TILE, FFN_UNITS), lambda i, place: (i, 0))
    results = run(
        functools.partial(ffn_forward_kernel, tiles, len(pieces)),
        "ffn_forward",
        place,
        (tiles,),
        [(item, anywhere) for item in (*tokens, *pieces)],
        ffn_sums(count, width) + [(shaped((2 * count, FFN_UNITS), low), middle)] * 3,
        ffn_scratch(2 * count, width, middles=False, stages=False),
        after,
        us=36,
    )
    return results[:4], results[4:]


def ffn_chunk_backward(place, tokens, middles, after=()):
    count, width = tokens[0].shape
    return run(
        ffn_backward_kernel,
        "ffn_backward",
        place,
        (4,),
        [(item, anywhere) for item in (*tokens, *middles)],
        sent_shapes(FFN_HALF, SLAB),
        ffn_scratch(2 * count, width, weights=False),
        after,
        us=22,
    )


def input_back_kernel(
    tiles, place_ref, own_q, own_k, own_v, far_q, far_k, far_v, x_own, x_far, w_ref, *refs
):
    grad_ref, own_ref, far_ref, gain_grad = refs
    step = pl.program_id(0)

    @pl.when(step == 0)
    def _():
        gain_grad[...] = jnp.zeros_like(gain_grad)

    def squeezed(query, key, value):
        parts = []
        for ref in (query, key):
            for at in range(0, ref.shape[1], LANES):
                head = ref[:, at : at + LANES].astype(wide)
                parts.append(head[:, :HALF])
                parts.append(head[:, LANES // 2 : LANES // 2 + HALF])
        for at in range(0, value.shape[1], LANES):
            parts.append(value[:, at : at + LANES].astype(wide)[:, :HD])
        return jnp.concatenate(parts, axis=1).astype(low)

    def rest(x_ref, incoming):
        hidden = x_ref[...].astype(wide)
        scale = lax.rsqrt(jnp.mean(hidden * hidden, axis=-1, keepdims=True) + epsilon)
        summed = jnp.sum(incoming * hidden * scale, axis=0, keepdims=True)
        gain_grad[...] += jnp.broadcast_to(summed, gain_grad.shape)

    @pl.when(step < tiles)
    def _():
        grad_ref[...] = squeezed(far_q, far_k, far_v)
        incoming = across(grad_ref[...], w_ref[...])
        far_ref[...] = incoming.astype(low)
        rest(x_far, incoming)

    @pl.when(step >= tiles)
    def _():
        grad_ref[...] = squeezed(own_q, own_k, own_v)
        incoming = across(grad_ref[...], w_ref[...])
        own_ref[...] = incoming.astype(low)
        rest(x_own, incoming)


def input_back(place, own, far, x_own, x_far, weight, after=()):
    count, width = 2 * x_own.shape[0], x_own.shape[1]
    tile = 320
    tiles = count // 2 // tile
    gain_grad = shaped((8, width), wide)

    def late(columns):
        return pl.BlockSpec((tile, columns), lambda i, place: (jnp.maximum(i - tiles, 0), 0))

    def early(columns):
        return pl.BlockSpec((tile, columns), lambda i, place: (jnp.minimum(i, tiles - 1), 0))

    def both(columns):
        return pl.BlockSpec((tile, columns), lambda i, place: (lax.rem(i + tiles, 2 * tiles), 0))

    return run(
        functools.partial(input_back_kernel, tiles),
        "input_back",
        place,
        (2 * tiles,),
        [(item, late(item.shape[1])) for item in own]
        + [(item, early(item.shape[1])) for item in far]
        + [(x_own, late(width)), (x_far, early(width)), (weight, whole(weight))],
        [
            (shaped((count, width), low), both(width)),
            (shaped((count // 2, width), low), late(width)),
            (shaped((count // 2, width), low), early(width)),
            (gain_grad, whole(gain_grad)),
        ],
        after=after,
        us=15,
    )


def qkv_grad_kernel(place_ref, x_ref, grad_ref, gain_one, gain_two, *refs):
    outs, (stage, gain_rows, sems) = refs[:5], refs[5:]
    k = pl.program_id(0)
    width = grad_ref.shape[1]

    @pl.when(k == 0)
    def _():
        gap = jnp.zeros((8, LANES - HD), wide)
        row = lax.broadcasted_iota(jnp.int32, (16, LANES), 0)
        gain_rows[...] = jnp.zeros_like(gain_rows)
        for block in range(BLOCKS):
            for index, gain in enumerate((gain_one, gain_two)):
                part = jnp.concatenate([gain[:, block * HD : (block + 1) * HD], gap], axis=1)
                part = jnp.where(row == 0, jnp.concatenate([part, part], axis=0), 0.0)
                gain_rows[
                    16 * block : 16 * block + 16, index * LANES : (index + 1) * LANES
                ] = part.astype(low)

    depth = place_ref[0] ^ k
    rows = width // 4
    to = pl.ds(pl.multiple_of(depth * rows, 16), rows)
    stage[to, :] = project(x_ref[...].T, grad_ref[...]).astype(low)
    send_off(place_ref, k, (stage, gain_rows), depth * 4, QKV_PLAN, QKV_HALF, outs, sems)

    @pl.when(k == 3)
    def _():
        fill_spare(gain_rows.at[pl.ds(0, 16)], GAINS + 16, 16, QKV_HALF, outs, sems)
        drain(outs, sems)


def qkv_grad(place, x, grad, gain_one, gain_two, after=()):
    count, width = x.shape
    column = pl.BlockSpec((count, width // 4), lambda k, place: (0, place[0] ^ k))
    return run(
        qkv_grad_kernel,
        "qkv_grad",
        place,
        (4,),
        [(x, column)] + [(item, whole(item)) for item in (grad, gain_one, gain_two)],
        sent_shapes(QKV_HALF, SLAB),
        [
            pltpu.VMEM((width, width), low),
            pltpu.VMEM((BLOCKS * 16, SLAB), low),
            pltpu.SemaphoreType.DMA((5,)),
        ],
        after,
        us=15,
    )


def tokens_grad_kernel(place_ref, x_ref, middle_ref, mine_ref, other_ref, gain_ref, out_ref):
    hidden = x_ref[...].astype(wide)
    scale = lax.rsqrt(jnp.mean(hidden * hidden, axis=-1, keepdims=True) + epsilon)
    incoming = mine_ref[...].astype(wide) + other_ref[...].astype(wide)
    weighted = incoming * gain_ref[0:1, :]
    inner = jnp.mean(weighted * hidden, axis=-1, keepdims=True)
    out_ref[...] = middle_ref[...] + (scale * weighted - hidden * scale**3 * inner)


def tokens_grad(place, x, grad_middle, mine, other, gains, after=()):
    count, width = x.shape
    tile = 128
    return run(
        tokens_grad_kernel,
        "tokens_grad",
        place,
        (count // tile,),
        [(item, rows_of(tile, width)) for item in (x, grad_middle, mine, other)]
        + [(gains, whole(gains))],
        [(shaped((count, width), wide), rows_of(tile, width))],
        after=after,
    )[0]


def output_kernel(place_ref, middle_ref, mine_0, mine_1, other_0, other_1, out_ref):
    parts = (mine_0, mine_1, other_0, other_1)
    total = middle_ref[...] + sum(ref[...].astype(wide) for ref in parts)
    out_ref[...] = total.astype(low)


def output_of(place, middle, parts, after=()):
    count, width = middle.shape
    tile = 128
    return run(
        output_kernel,
        "output",
        place,
        (count // tile,),
        [(item, rows_of(tile, width)) for item in (middle, *parts)],
        [(shaped((count, width), low), rows_of(tile, width))],
        after=after,
    )[0]


def swap(array):
    return lax.ppermute(array, "rep", [(0, 1), (1, 0)])


def hop(array, z_flip, y_flip, x_flip):
    flip = (z_flip * 2 + y_flip) * 2 + x_flip
    return lax.ppermute(array, "fsdp", [(chip, chip ^ flip) for chip in range(BLOCKS)])


def hop_x(array):
    return hop(array, 0, 0, 1)


def hop_y(array):
    return hop(array, 0, 1, 0)


def near(line):
    return hop_x(line), hop_y(line)


def pieces_of(blocks):
    cut = blocks.reshape(4, 2, 2, *blocks.shape[1:])
    half = blocks.shape[1] // 2
    far = cut[:, 1, 1]
    return cut[:, 0, 0], cut[:, 0, 1], cut[:, 1, 0], far[:, :half], far[:, half:]


def blocks_of(sent):
    to_x, to_y, late_x, late_y, own = sent
    near_x = jnp.stack([to_x[1], late_x], axis=1)
    near_y = jnp.stack([late_y, to_y[1]], axis=1)
    far = jnp.stack([to_x[0], to_y[0]], axis=1)
    cut = jnp.stack([jnp.stack([own, near_x], 1), jnp.stack([near_y, far], 1)], 1)
    return cut.reshape(BLOCKS, 2 * own.shape[2], own.shape[3])


def layout(length_row, count):
    ends = jnp.cumsum(length_row)
    slots = jnp.arange(count, dtype=jnp.int32)
    passed = (slots[:, None] >= ends[None, :]).astype(jnp.int32)
    segment = jnp.sum(passed, axis=1)
    position = slots - jnp.sum(passed * length_row[None, :], axis=1)
    return position, segment


class Direct:
    def __init__(self, place, weights):
        self.place = place
        self.weights = weights

    def pack_first(self):
        return pack_first(self.place, *self.weights[:4], *self.weights[7:])

    def pack_ffn(self, chunk, parts, after):
        return pack_ffn(self.place, chunk, parts, *self.weights[4:7], after)

    def step_0(self, shard):
        return hop(shard, 2, 0, 0)

    def all_z(self, shard):
        return [hop(shard, k, 0, 0) for k in (1, 2, 3)]

    def join(self, shard, received, after):
        return join(self.place, [shard, *received], after)

    def step_1(self, shard, received, after=()):
        return pair_up(self.place, shard, received, after)

    def step_2(self, pair):
        return hop(pair, 1, 0, 0)

    def step_3(self, pair, received, after=()):
        return line_up(self.place, pair, received, after)

    def step_4(self, line):
        return near(line)

    def step_5(self, line, sides, after=()):
        upper, lower = halves(self.place, *sides, after)
        return (line, *sides, hop_y(upper), hop_x(lower)), upper

    def plane(self, parts, after):
        return plane_up(self.place, parts, after)

    def gate(self, sent, pieces):
        return (*gate(self.place, sent[:2], (*pieces[3:5], pieces[6])), *sent[2:])

    def scatter_1(self, sent):
        return hop_x(sent[0]), hop_y(sent[1])

    def scatter_2(self, sent, got, after):
        late_x, late_y = merge(self.place, sent[2], sent[3], got[0], got[1], after)
        return late_x, (hop_x(late_x), hop_y(late_y))

    def scatter_3(self, groups, after):
        groups = [(sent[4], *got, *more) for sent, got, more in groups]
        kept, kept_far, part = sum_plane(self.place, groups, False, after)
        return kept, (kept_far, hop(part, 1, 0, 0))

    def scatter_4(self, kept, parts, after):
        kept_far, near = parts
        token = sum_pass(self.place, kept_far, near, after)
        return token, (near, hop(token, 2, 0, 0))

    def scatter_34(self, groups, after):
        groups = [(sent[4], *got, *more) for sent, got, more in groups]
        kept, *parts = sum_plane(self.place, groups, True, after)
        return kept, tuple(hop(part, k + 1, 0, 0) for k, part in enumerate(parts))

    def scatter_5(self, kept, parts, after):
        total, total_low = sum_line(self.place, kept, parts, after)
        return total, swap(total_low)

    def pins(self, arrays):
        return tuple(arrays)

    def finish_ffn(self, chunk_0, chunk_1, shapes, after):
        mine, other = zip(chunk_0, chunk_1)
        return unpack_ffn(self.place, mine, other, shapes, after)

    def finish_first(self, first, chunk_1, shapes, owned, after):
        grads = unpack_first(self.place, (*first, *chunk_1), shapes, after)
        both = first[0][GAINS, : 2 * LANES] + first[1][GAINS, : 2 * LANES].astype(wide)
        return grads, (both[:owned], both[LANES : LANES + owned])


def on_device(
    direct,
    tokens,
    lengths,
    attn_gain,
    w_query,
    w_key,
    w_value,
    w_out,
    ffn_gain,
    w_gate,
    w_up,
    w_down,
    cotangent,
):
    count, width = tokens.shape
    owned = attn_gain.shape[0]
    core = lax.axis_index("rep")
    if direct:
        index = lax.axis_index("fsdp")
        spot = (index // 4, (index // 2) % 2, index % 2)
    else:
        spot = (0, 0, 0)
    place = jnp.stack([jnp.int32(item) for item in (*spot, core)])
    weights = (w_query, w_key, w_value, w_out, w_gate, w_up, w_down, attn_gain, ffn_gain)
    routes = Direct(place, weights) if direct else Whole(place, weights)

    first = routes.pack_first()
    far_tokens, far_cotangent = swap(tokens), swap(cotangent)
    laid = [layout(row, count) for row in (lengths[0], swap(lengths)[0])]
    segment = jnp.stack([item[1] for item in laid])
    cosine, sine = turn_table(jnp.concatenate([item[0] for item in laid]))

    received_first = routes.all_z(first)
    whole_rows = 2 * FFN_HALF
    chunk_a, chunk_b = routes.pack_ffn(
        1, (UPPER_ROWS, whole_rows - UPPER_ROWS), (first, far_tokens, far_cotangent)
    )
    if direct:
        chunk_b = chunk_b.reshape(1, *chunk_b.shape)
    sides_b = routes.step_4(chunk_b)
    parts_b, token = routes.step_5(chunk_b, sides_b)
    (chunk_0,) = routes.pack_ffn(0, (whole_rows,), (token,))
    received_0 = routes.step_0(chunk_0)
    plane_b = routes.plane(parts_b, (chunk_0,))
    tables = (far_tokens, far_cotangent, segment, cosine, sine)
    line_first = routes.join(first, received_first, (*tables, plane_b))
    sides_first = routes.step_4(line_first)
    pair_0 = routes.step_1(chunk_0, received_0, (line_first,))
    near_0 = routes.step_2(pair_0)
    received_a = routes.step_0(chunk_a)
    received_b = routes.step_0(plane_b)
    pieces_first, token = routes.step_5(line_first, sides_first, (pair_0,))
    line_0 = routes.step_3(pair_0, near_0, (token,))
    sides_0 = routes.step_4(line_0)
    w_mine = out_weight(place, pieces_first, tokens.shape[1], (line_0,))
    w_other = [swap(part) for part in w_mine]
    normed_low, queries, keys, values, w_qkv, gains = project_qkv(
        place, tokens, far_tokens, cosine, sine, pieces_first, (w_mine[0],)
    )
    far_mine, far_total = attend(place, queries, keys, values, segment, 1, (keys,))
    own_other = swap(far_mine)
    own_mine, own_total = attend(
        place, queries, keys, values, segment, 0, (far_mine, *w_other)
    )
    far_other = swap(own_mine)
    pair_b = routes.step_1(plane_b, received_b, (own_mine,))
    near_b = routes.step_2(pair_b)
    pieces_0, token = routes.step_5(line_0, sides_0, (pair_b, received_a))
    pair_a = routes.step_1(chunk_a, received_a, (token,))
    near_a = routes.step_2(pair_a)
    middle, normed_own = middle_of(
        place, tokens, own_mine, own_other, w_mine, w_other, gains, (pair_a,)
    )
    normed_far = swap(normed_own)
    line_a = routes.step_3(pair_a, near_a, (normed_own, far_other, *pieces_0[3:]))
    sides_a = routes.step_4(line_a)

    inputs = (normed_own, normed_far, cotangent, far_cotangent)
    sums_0, middles_0 = ffn_chunk_forward(place, inputs, pieces_0, (line_a,))
    out_far_0, norm_far_0 = swap(sums_0[0]), swap(sums_0[1])
    pieces_a, token = routes.step_5(line_a, sides_a, (sums_0[0],))
    planes_b = (pair_b, near_b) if direct else chunk_b
    pieces_1 = (*pieces_a, *planes_b)
    sent_0 = ffn_chunk_backward(place, inputs, middles_0, (token,))
    sent_0 = routes.gate(sent_0, pieces_1)
    got_0 = routes.scatter_1(sent_0)
    sums_1, middles_1 = ffn_chunk_forward(place, inputs, pieces_1, (sent_0[0],))
    out_far_1, norm_far_1 = swap(sums_1[0]), swap(sums_1[1])
    token, more_0 = routes.scatter_2(sent_0, got_0, (sums_1[0], out_far_0))
    sent_1 = ffn_chunk_backward(place, inputs, middles_1, (token,))
    got_1 = routes.scatter_1(sent_1)

    norms = (sums_0[3], sums_1[3], norm_far_0, norm_far_1)
    grad_middle, branch_mine, branch_sent, heads_mine, heads_sent, ffn_gain_grad = middle_back(
        place, middle, norms, cotangent, gains, w_mine, w_other, (sent_1[4], *more_0)
    )
    branch_far, heads_far = swap(branch_sent), swap(heads_sent)
    attended = (queries, keys, values)
    tables = (segment, cosine, sine)
    own_grads = attend_back(place, *attended, heads_mine, own_mine, own_total, *tables, 0)
    sent_out = out_grad(
        place,
        own_mine,
        own_other,
        far_mine,
        far_other,
        branch_mine,
        branch_far,
        (own_grads[0],),
    )
    got_out = routes.scatter_1(sent_out)
    kept_0, parts_0 = routes.scatter_3([(sent_0, got_0, more_0)], (sent_out[4],))
    token, more_1 = routes.scatter_2(sent_1, got_1, (kept_0,))
    far_grads = attend_back(
        place, *attended, heads_far, far_mine, far_total, *tables, 1, (token, out_far_1)
    )
    token, more_out = routes.scatter_2(sent_out, got_out, (far_grads[0],))
    token, parts_0 = routes.scatter_4(kept_0, parts_0, (token,))
    grad_qkv, own_part, far_part, attn_gain_grad = input_back(
        place, own_grads, far_grads, tokens, far_tokens, w_qkv, (token,)
    )
    own_rest = swap(far_part)
    sent_qkv = qkv_grad(place, normed_low, grad_qkv, attn_gain_grad, ffn_gain_grad)
    got_qkv = routes.scatter_1(sent_qkv)
    groups = [(sent_1, got_1, more_1), (sent_out, got_out, more_out)]
    kept_1, parts_1 = routes.scatter_34(groups, (sent_qkv[4], *routes.pins(parts_0[1:])))

    owned_0 = routes.scatter_5(kept_0, parts_0, (kept_1,))
    outs = (sums_0[2], sums_1[2], out_far_0, out_far_1)
    output = output_of(place, middle, outs, (owned_0[0],))
    token, more_qkv = routes.scatter_2(sent_qkv, got_qkv, (output,))
    grad_tokens = tokens_grad(place, tokens, grad_middle, own_part, own_rest, gains, (token,))
    kept_qkv, parts_qkv = routes.scatter_34([(sent_qkv, got_qkv, more_qkv)], (grad_tokens,))
    owned_1 = routes.scatter_5(kept_1, parts_1, (kept_qkv,))
    owned_qkv = routes.scatter_5(kept_qkv, parts_qkv, (owned_1[0],))
    shapes = [w_gate.shape, w_up.shape, w_down.shape]
    grad_gate, grad_up, grad_down = routes.finish_ffn(owned_0, owned_1, shapes, (owned_qkv[0],))
    shapes = [w_query.shape, w_key.shape, w_value.shape, w_out.shape]
    grads, gain_grads = routes.finish_first(owned_qkv, owned_1, shapes, owned, (grad_gate,))
    return (
        output,
        grad_tokens,
        gain_grads[0],
        *grads,
        gain_grads[1],
        grad_gate,
        grad_up,
        grad_down,
    )


class Whole:
    def __init__(self, place, weights):
        self.place = place
        query, key, value, out, gate, up, down_w, gain_one, gain_two = weights
        core = place[3]
        self.core = core
        count = query.shape[1] // query.shape[0]
        self.count = count
        rows = query.shape[1] // BLOCKS

        def full(shard):
            return lax.all_gather(shard, "fsdp", axis=0, tiled=True)

        def mine(weight):
            columns = weight.shape[1] // 2
            return lax.dynamic_slice_in_dim(weight, core * columns, columns, axis=1)

        def slabs(weight):
            blocks = weight.reshape(BLOCKS, -1, weight.shape[1])
            return [blocks[:, :, at : at + SLAB] for at in range(0, weight.shape[1], SLAB)]

        qkv = full(jnp.concatenate([mine(query), mine(key), mine(value)], axis=1))
        gain_rows = jnp.zeros((BLOCKS, 16, SLAB), low)
        for index, gain in enumerate((gain_one, gain_two)):
            part = full(gain).reshape(BLOCKS, rows)
            gain_rows = gain_rows.at[:, 0, index * LANES : index * LANES + rows].set(part)
        square = full(mine(out)).reshape(BLOCKS, rows, -1)
        rest = square[:, :, SLAB:]
        rest = jnp.concatenate([rest[:, : rows // 2], rest[:, rows // 2 :]], axis=2)
        parts = slabs(qkv) + [gain_rows, square[:, :, :SLAB], rest]
        self.first = pieces_of(jnp.concatenate(parts, axis=1))
        quarter = down_w.shape[0] // (2 * CHUNKS)
        self.quarter = quarter

        def units(weight, chunk):
            split = weight.reshape(weight.shape[0], count, 2 * CHUNKS, quarter)
            part = lax.dynamic_index_in_dim(split, CHUNKS * core + chunk, 2, keepdims=False)
            return full(part.reshape(weight.shape[0], count * quarter))

        chunks = []
        for chunk in range(CHUNKS):
            at = (CHUNKS * core + chunk) * quarter
            part = full(lax.dynamic_slice_in_dim(down_w, at, quarter, axis=0))
            parts = slabs(units(gate, chunk)) + slabs(units(up, chunk)) + slabs(part)
            chunks.append(jnp.concatenate(parts, axis=1))
        planes = chunks[1][:, UPPER_ROWS:].reshape(4, 4, -1, SLAB)
        self.ffn_0 = (pieces_of(chunks[0]),)
        self.ffn_1 = pieces_of(chunks[1][:, :UPPER_ROWS]), (planes[0::2], planes[1::2])

    def pack_first(self):
        return self.first

    def pack_ffn(self, chunk, parts, after):
        return (self.ffn_0, self.ffn_1)[chunk]

    def step_0(self, shard):
        return shard

    def all_z(self, shard):
        return ()

    def join(self, shard, received, after):
        return shard

    def step_1(self, shard, received, after=()):
        return shard

    def step_2(self, pair):
        return pair

    def step_3(self, pair, received, after=()):
        return pair

    def step_4(self, line):
        return ()

    def step_5(self, line, sides, after=()):
        return line, line

    def plane(self, parts, after):
        return parts

    def gate(self, sent, pieces):
        return sent

    def scatter_1(self, sent):
        return blocks_of(sent)

    def scatter_2(self, sent, got, after):
        return got, got

    def scatter_3(self, groups, after):
        blocks = jnp.concatenate([got for _, got, _ in groups], axis=1)
        return blocks, blocks

    def scatter_34(self, groups, after):
        return self.scatter_3(groups, after)[0], ()

    def scatter_4(self, kept, parts, after):
        return kept, kept

    def scatter_5(self, kept, parts, after):
        return kept, kept

    def split(self, blocks, widths):
        parts, row = [], 0
        for rows, slabs in widths:
            taken = []
            for _ in range(slabs):
                taken.append(blocks[:, row : row + rows])
                row += rows
            part = jnp.concatenate(taken, axis=2)
            part = part.reshape(BLOCKS * rows, part.shape[2])
            parts.append(lax.psum_scatter(part, "fsdp", scatter_dimension=0, tiled=True))
        return parts

    def ordered(self, part):
        other = swap(part).astype(wide)
        part = part.astype(wide)
        first = jnp.where(self.core == 0, part, other)
        return first, jnp.where(self.core == 0, other, part)

    def pins(self, arrays):
        return ()

    def finish_ffn(self, chunk_0, chunk_1, shapes, after):
        gates, ups, downs = [], [], []
        for blocks, _ in (chunk_0, chunk_1):
            gate, up, down_w = self.split(blocks, ((96, 2), (96, 2), (64, 3)))
            gates.append(self.ordered(gate))
            ups.append(self.ordered(up))
            downs.append(self.ordered(down_w))

        def columns(pairs):
            parts = [pairs[chunk][owner] for owner in range(2) for chunk in range(CHUNKS)]
            rows = parts[0].shape[0]
            parts = [part.reshape(rows, self.count, self.quarter) for part in parts]
            return jnp.stack(parts, axis=2).reshape(rows, -1)

        grad_down = [downs[chunk][owner] for owner in range(2) for chunk in range(CHUNKS)]
        return columns(gates), columns(ups), jnp.concatenate(grad_down, axis=0)

    def finish_first(self, first, chunk_1, shapes, owned, after):
        mine = first[0]
        (qkv,) = self.split(mine[:, :GAINS], ((96, 3),))
        blocks = chunk_1[0][:, 2 * FFN_HALF :]
        rest = blocks[:, 96:144]
        rest = jnp.concatenate([rest[:, :, :256], rest[:, :, 256:]], axis=1)
        (square,) = self.split(jnp.concatenate([blocks[:, :96], rest], axis=2), ((96, 1),))
        pair = self.ordered(qkv)
        grads, at = [], 0
        for shape in shapes[:3]:
            columns = shape[1] // 2
            grads.append(jnp.concatenate([item[:, at : at + columns] for item in pair], axis=1))
            at += columns
        grads.append(jnp.concatenate(self.ordered(square), axis=1))
        rows = mine[:, GAINS, : 2 * LANES].astype(wide)
        rows = rows + swap(rows)
        gains = []
        for index in range(2):
            gain = rows[:, index * LANES : index * LANES + 96].reshape(-1)
            gains.append(lax.psum_scatter(gain, "fsdp", scatter_dimension=0, tiled=True))
        return grads, gains


def solution(mesh):
    rows = P(("rep", "fsdp"), None)
    split = P("fsdp", None)
    gain = P("fsdp")
    return jax.shard_map(
        functools.partial(on_device, mesh.shape["fsdp"] == BLOCKS),
        mesh=mesh,
        in_specs=(rows, rows, gain) + (split,) * 4 + (gain,) + (split,) * 3 + (rows,),
        out_specs=(rows, rows, gain) + (split,) * 4 + (gain,) + (split,) * 3,
        check_vma=False,
    )
```
